32 devices in a mesh: dp: 4 (over y, x), pack: 8 (over z, core).
Axes of the slice: x: 2, y: 2, z: 4, core: 2. Of those that a mesh axis runs over, the one named last changes fastest.
Arguments:
- hidden_in: bfloat16 [64, 4096], P('dp', 'pack'), may hold values from -6 to 6
- attn_gain: float32 [4096], P('pack'), may hold values from 0.25 to 1.75
- w_query: bfloat16 [4096, 4096], P(None, 'pack'), may hold values from -0.09375 to 0.09375
- query_gain: float32 [128], replicated, may hold values from 0.25 to 1.75
- cached_keys: bfloat16 [10240, 1024], P(('dp', 'pack')), may hold values from -200 to 200
- cached_values: bfloat16 [10240, 1024], P(('dp', 'pack')), may hold values from -9 to 9
- w_out: bfloat16 [4096, 4096], P('pack'), may hold values from -0.09375 to 0.09375
- final_gain: float32 [4096], P('pack'), may hold values from 0.25 to 1.75
- lengths: int32 [4, 16], P('dp'), may hold values from 16 to 304, as said below
- pack_order: int32 [4, 16], P('dp'), may hold values from 0 to 15, each once within a row
- partner: int32 [64], replicated, may hold values from 0 to 63, as said below
Outputs:
- pooled: bfloat16 [64, 4096], P('dp', 'pack')
- loss_rows: float32 [64], P(('dp', 'pack'))
- grad_hidden: bfloat16 [64, 4096], P('dp', 'pack')
The draws below stay inside these ranges and needn't reach their ends.
Inputs may be any that keep to these rules, and one draw needn't show every extreme that they name: Statements 2k and 2k+1 of a group have lengths that sum to 320, so a group's lengths sum to 320 * 8. `pack_order`: each row is a permutation of the group's statement indices. `partner`: no statement is its own positive.
All inputs are finite; a program needn't handle non-finite values.
Results may differ from the reference program's by a relative error of at most 0.019.
Values may be sent and summed in bfloat16 or wider, within the bound.
No kernel may reach another device: no remote copies, remote signals or barrier semaphores. Data moves between devices by JAX's collectives and lax.ppermute only.
A program may use at most 128 MiB of HBM per device.

```python
import math
import jax
import jax.numpy as jnp
from jax import lax

D = 4096
HEADS = 32
KV_HEADS = 8
HEAD_DIM = 128
MEANLEN = 160
TOK_DEV = 320
STMTS = 16
GROUPS = 4
ALL_STMTS = 64
N_DP = 4
N_PACK = 8


def draw_lengths(key, part):
    pair_sum = 2 * MEANLEN
    shorter = jax.random.randint(key, (GROUPS, STMTS // 2), 16, pair_sum - 15, dtype=jnp.int32)
    first_col = jnp.arange(STMTS // 2, dtype=jnp.int32)[None, :] == 0
    shorter = jnp.where(first_col, 16, shorter).astype(jnp.int32)
    return jnp.stack([shorter, pair_sum - shorter], axis=2).reshape(GROUPS, STMTS).astype(jnp.int32)


def draw_partner(key, part):
    offset = jax.random.randint(key, (ALL_STMTS,), 1, ALL_STMTS, dtype=jnp.int32)
    return ((jnp.arange(ALL_STMTS, dtype=jnp.int32) + offset) % ALL_STMTS).astype(jnp.int32)


def draw_cached_keys(key, part):
    row_count = TOK_DEV * N_PACK * N_DP
    base_key = jax.random.fold_in(key, 11)
    entries = jax.random.truncated_normal(base_key, -6.0, 6.0, (row_count, KV_HEADS, HEAD_DIM), jnp.float32)
    drawn = entries * 2.5
    return drawn.reshape(row_count, KV_HEADS * HEAD_DIM).astype(jnp.bfloat16)


def block_scale(rng, dims, shards, low, high):
    level = 1.0
    for dim, blocks in shards:
        draws = jax.random.uniform(jax.random.fold_in(jax.random.fold_in(rng, 6), dim), (blocks,), jnp.float32, low / len(shards), high / len(shards))
        level = level * jnp.repeat(jnp.exp(draws), dims[dim] // blocks).reshape((-1,) + (1,) * (len(dims) - 1 - dim))
    return level


def normal_values(key, extent, width, most, shards=(), kind=jnp.bfloat16):
    values = width * jax.random.normal(key, extent, jnp.float32)
    if shards:
        values = values * block_scale(key, extent, shards, -0.22, 0.18)
    return jnp.clip(values, -most, most).astype(kind)


def setup_inputs(seed: int = 0) -> dict:
    splits = jax.random.split(jax.random.key(seed), 12)
    return {
        "hidden_in": normal_values(splits[0], (ALL_STMTS, D), 1.0, 6.0, ((0, 4), (1, 8))),
        "attn_gain": jnp.clip(1.0 + 0.15 * jax.random.normal(splits[1], (D,), jnp.float32), 0.25, 1.75),
        "w_query": normal_values(splits[2], (D, HEADS * HEAD_DIM), D ** -0.5, 0.09375, ((1, 8),)),
        "query_gain": jnp.clip(1.0 + 0.15 * jax.random.normal(splits[3], (HEAD_DIM,), jnp.float32), 0.25, 1.75),
        "cached_keys": draw_cached_keys(jax.random.fold_in(splits[11], 71), 0),
        "cached_values": normal_values(splits[5], (TOK_DEV * N_PACK * N_DP, KV_HEADS * HEAD_DIM), 1.5, 9.0, ((0, 32),)),
        "w_out": normal_values(splits[6], (HEADS * HEAD_DIM, D), (HEADS * HEAD_DIM) ** -0.5, 0.09375, ((0, 8),)),
        "final_gain": jnp.clip(1.0 + 0.15 * jax.random.normal(splits[7], (D,), jnp.float32), 0.25, 1.75),
        "lengths": draw_lengths(jax.random.fold_in(splits[11], 71), 0),
        "pack_order": jax.vmap(lambda own: jax.random.permutation(own, STMTS))(jax.random.split(splits[9], GROUPS)).reshape((GROUPS, STMTS)).astype(jnp.int32),
        "partner": draw_partner(jax.random.fold_in(splits[11], 71), 0),
    }


EPSILON = 1e-06
SOFTMAX_WARMTH = 0.05
ROPE_BASE = 1000000.0
MASKED_LOGIT = -1e+30

def rotate_heads(queries, position):
    head_dim = queries.shape[-1]
    half_dim = head_dim // 2
    frequency = jnp.power(jnp.float32(ROPE_BASE), -jnp.arange(half_dim).astype(jnp.float32) * 2.0 / head_dim)
    angles = position[:, None] * frequency[None, :]
    cosine = jnp.concatenate([jnp.cos(angles), jnp.cos(angles)], axis=1)[:, None, :]
    sine_part = jnp.concatenate([jnp.sin(angles), jnp.sin(angles)], axis=1)[:, None, :]
    turned = jnp.concatenate([-queries[..., half_dim:], queries[..., :half_dim]], axis=-1)
    return queries * cosine + turned * sine_part

def token_owner(lengths_row, order_row, first_token, token_count):
    stmt_count = order_row.shape[0]
    picked = order_row[:, None] == jnp.arange(stmt_count, dtype=jnp.int32)[None, :]
    packed_len = lax.optimization_barrier(jnp.sum(jnp.where(picked, lengths_row[None, :], 0), axis=1)).astype(jnp.int32)
    range_end = jnp.cumsum(packed_len).astype(jnp.int32)
    token_index = first_token + jnp.arange(token_count, dtype=jnp.int32)
    slot_index = lax.optimization_barrier(jnp.sum((token_index[:, None] >= range_end[None, :]).astype(jnp.int32), axis=1)).astype(jnp.int32)
    return jnp.take(order_row, slot_index)

def shard_attention(group_queries, shard_keys, shard_values, token_owners):
    stmt_count = group_queries.shape[0]
    grouped = group_queries.astype(jnp.float32).reshape(stmt_count, KV_HEADS, HEADS // KV_HEADS, HEAD_DIM)
    key_heads = shard_keys.astype(jnp.float32).reshape(-1, KV_HEADS, HEAD_DIM)
    value_heads = shard_values.astype(jnp.float32).reshape(-1, KV_HEADS, HEAD_DIM)
    scores = jnp.einsum('skgd,tkd->skgt', grouped, key_heads) * HEAD_DIM ** (-0.5)
    token_mask = (token_owners[None, :] == jnp.arange(stmt_count, dtype=jnp.int32)[:, None])[:, None, None, :]
    block_max = lax.optimization_barrier(jnp.max(jnp.where(token_mask, scores, MASKED_LOGIT), axis=3))
    softmax_weights = jnp.where(token_mask, jnp.exp(scores - block_max[..., None]), 0.0)
    block_sum = lax.optimization_barrier(jnp.sum(softmax_weights, axis=3))
    rounded = lax.optimization_barrier(softmax_weights.astype(jnp.bfloat16)).astype(jnp.float32)
    numerators = jnp.einsum('skgt,tkd->skgd', rounded, value_heads)
    return (block_max.reshape(stmt_count, HEADS), block_sum.reshape(stmt_count, HEADS), numerators.reshape(stmt_count, HEADS, HEAD_DIM))

def reference(hidden_in, attn_gain, w_query, query_gain, cached_keys, cached_values, w_out, final_gain, lengths, pack_order, partner):
    group_tokens = TOK_DEV * N_PACK
    inputs32 = hidden_in.astype(jnp.float32)
    input_rms = lax.rsqrt(lax.optimization_barrier(jnp.sum(inputs32 * inputs32, axis=1, keepdims=True)) / D + EPSILON)
    normed = (inputs32 * input_rms * attn_gain[None, :]).astype(jnp.bfloat16)
    projected = jnp.dot(normed, w_query, preferred_element_type=jnp.float32).reshape(ALL_STMTS, HEADS, HEAD_DIM)
    queries = projected * lax.rsqrt(lax.optimization_barrier(jnp.mean(projected * projected, axis=2, keepdims=True)) + EPSILON) * query_gain
    position = (lengths.reshape(ALL_STMTS) - 1).astype(jnp.float32)
    queries = rotate_heads(queries, position).astype(jnp.bfloat16)

    def one_group(packed):
        group_queries, group_keys, group_values, lengths_row, order_row = packed
        owners = token_owner(lengths_row, order_row, 0, group_tokens).reshape(N_PACK, TOK_DEV)

        def one_shard(shard_data):
            return shard_attention(group_queries, shard_data[0], shard_data[1], shard_data[2])
        block_max, block_sum, numerators = lax.map(one_shard, (group_keys.reshape(N_PACK, TOK_DEV, -1), group_values.reshape(N_PACK, TOK_DEV, -1), owners))
        highest = lax.optimization_barrier(jnp.max(block_max, axis=0))
        factor = jnp.exp(block_max - highest[None])
        denominator = lax.optimization_barrier(jnp.sum(block_sum * factor, axis=0))
        summed = lax.optimization_barrier(jnp.sum(numerators * factor[..., None], axis=0))
        return (summed / denominator[..., None]).astype(jnp.bfloat16)
    attended = lax.map(one_group, (queries.reshape(N_DP, STMTS, HEADS, HEAD_DIM), cached_keys.reshape(N_DP, group_tokens, -1), cached_values.reshape(N_DP, group_tokens, -1), lengths, pack_order))
    attended = attended.reshape(ALL_STMTS, HEADS * HEAD_DIM)
    hidden = inputs32 + jnp.dot(attended, w_out, preferred_element_type=jnp.float32)
    hidden_rms = jnp.sqrt(lax.optimization_barrier(jnp.sum(hidden * hidden, axis=1, keepdims=True)) / D + EPSILON)
    pooled = (hidden / hidden_rms * final_gain[None, :]).astype(jnp.bfloat16)
    pooled32 = pooled.astype(jnp.float32)
    pooled_norm = jnp.sqrt(lax.optimization_barrier(jnp.sum(pooled32 * pooled32, axis=1, keepdims=True)))
    premise_vectors = (pooled32 / pooled_norm).astype(jnp.bfloat16)
    unscaled_logits = jnp.dot(premise_vectors, premise_vectors.T, preferred_element_type=jnp.float32)
    identity_matrix = jnp.arange(ALL_STMTS, dtype=jnp.int32)
    similarity_logits = jnp.where(identity_matrix[None, :] == identity_matrix[:, None], MASKED_LOGIT, unscaled_logits / SOFTMAX_WARMTH)
    highest = lax.optimization_barrier(jnp.max(similarity_logits, axis=1))
    row_lse = highest + jnp.log(lax.optimization_barrier(jnp.sum(jnp.exp(similarity_logits - highest[:, None]), axis=1)))
    is_partner = identity_matrix[None, :] == partner[:, None]
    target = lax.optimization_barrier(jnp.sum(jnp.where(is_partner, similarity_logits, 0.0), axis=1))
    loss_rows = row_lse - target
    pair_weight = jnp.exp(similarity_logits - row_lse[:, None]) + jnp.exp(similarity_logits - row_lse[None, :]) - is_partner.astype(jnp.float32) - is_partner.T.astype(jnp.float32)
    softmax_weights = pair_weight.astype(jnp.bfloat16)
    embedding_gradient = jnp.dot(softmax_weights, premise_vectors, preferred_element_type=jnp.float32) / SOFTMAX_WARMTH
    embed32 = premise_vectors.astype(jnp.float32)
    inner_sum = lax.optimization_barrier(jnp.sum(embed32 * embedding_gradient, axis=1, keepdims=True))
    grad_pooled = (embedding_gradient - embed32 * inner_sum) / pooled_norm
    grad_hidden = (math.sqrt(D) * final_gain[None, :] * grad_pooled / hidden_rms).astype(jnp.bfloat16)
    return (pooled, loss_rows, grad_hidden)
```

```python
import numpy as np
import jax
import jax.numpy as jnp
from jax import lax
from jax.sharding import PartitionSpec as P

EPSILON = 1e-06
SOFTMAX_WARMTH = 0.05
ROPE_BASE = 1000000.0
MASKED_LOGIT = -1e30


def gather_blocks(block, axis):
    size = lax.axis_size(axis)
    return lax.all_to_all(jnp.broadcast_to(block[None], (size,) + block.shape), axis, 0, 0)


def split_float(value, pieces):
    out = []
    for _ in range(pieces):
        piece = lax.reduce_precision(value, 8, 7)
        out.append(piece.astype(jnp.bfloat16))
        value = value - piece
    return out


def cosine_and_sine(angles):
    turns = jnp.round(angles * np.float32(2.0 / np.pi))
    rest = angles - turns * np.float32(1.5703125)
    rest = rest - turns * np.float32(4.837512969970703125e-4)
    rest = rest - turns * np.float32(7.549789948768648e-8)
    square = rest * rest
    sine = rest + rest * square * (
        np.float32(-1.6666654611e-1)
        + square * (np.float32(8.3321608736e-3) + square * np.float32(-1.9515295891e-4))
    )
    cosine = (
        1.0
        - 0.5 * square
        + square
        * square
        * (
            np.float32(4.166664568298827e-2)
            + square
            * (np.float32(-1.388731625493765e-3) + square * np.float32(2.443315711809948e-5))
        )
    )
    quarter = turns.astype(jnp.int32) & 3
    swap = (quarter & 1) == 1
    cos_out = jnp.where(swap, sine, cosine)
    sin_out = jnp.where(swap, cosine, sine)
    cos_out = jnp.where((quarter == 1) | (quarter == 2), -cos_out, cos_out)
    sin_out = jnp.where(quarter >= 2, -sin_out, sin_out)
    return cos_out, sin_out


def rotate_heads(queries, position):
    head_dim = queries.shape[-1]
    half_dim = head_dim // 2
    frequency = (ROPE_BASE ** (-np.arange(half_dim) * 2.0 / head_dim)).astype(np.float32)
    cosine, sine = cosine_and_sine(position[:, None] * frequency[None, :])
    cosine = jnp.concatenate([cosine, cosine], axis=1)[:, None, :]
    sine = jnp.concatenate([-sine, sine], axis=1)[:, None, :]
    turned = jnp.concatenate([queries[..., half_dim:], queries[..., :half_dim]], axis=-1)
    return queries * cosine + turned * sine


def statement_ranges(lengths_row, order_row):
    stmt_count = order_row.shape[0]
    index = jnp.arange(stmt_count, dtype=jnp.int32)
    slot = jnp.sum(jnp.where(order_row[None, :] == index[:, None], index[None, :], 0), axis=1)
    start = jnp.sum(jnp.where(slot[None, :] < slot[:, None], lengths_row[None, :], 0), axis=1)
    return start, start + lengths_row


def block_attention(all_queries, cached_keys, cached_values, token_mask, score_scale):
    stmt_count, head_count, head_dim = all_queries.shape
    kv_heads = cached_keys.shape[1] // head_dim
    group_size = head_count // kv_heads
    grouped = all_queries.reshape(stmt_count, kv_heads, group_size, head_dim)
    key_heads = cached_keys.reshape(-1, kv_heads, head_dim)
    value_heads = cached_values.reshape(-1, kv_heads, head_dim)
    scores = (
        jnp.einsum("skgd,tkd->skgt", grouped, key_heads, preferred_element_type=jnp.float32)
        * score_scale
    )
    token_mask = token_mask[:, None, None, :]
    block_max = jnp.max(jnp.where(token_mask, scores, MASKED_LOGIT), axis=3)
    softmax_weights = jnp.where(token_mask, jnp.exp(scores - block_max[..., None]), 0.0)
    block_sum = jnp.sum(softmax_weights, axis=3)
    numerators = jnp.einsum(
        "skgt,tkd->skgd",
        softmax_weights.astype(jnp.bfloat16),
        value_heads,
        preferred_element_type=jnp.float32,
    )
    return (
        block_max.reshape(stmt_count, head_count),
        block_sum.reshape(stmt_count, head_count),
        numerators.reshape(stmt_count, head_count, head_dim),
    )


def local(
    hidden_in,
    attn_gain,
    w_query,
    query_gain,
    cached_keys,
    cached_values,
    w_out,
    final_gain,
    lengths,
    pack_order,
    partner,
):
    pack_size = lax.axis_size("pack")
    pack_index = lax.axis_index("pack")
    group_index = lax.axis_index("dp")
    stmt_count, feature_count = hidden_in.shape
    model_width = feature_count * pack_size
    head_dim = query_gain.shape[0]
    local_heads = w_query.shape[1] // head_dim
    token_count = cached_keys.shape[0]
    total_stmts = partner.shape[0]
    lengths_row = lengths[0]
    order_row = pack_order[0]
    inputs32 = hidden_in.astype(jnp.float32)

    scaled = (inputs32 * attn_gain[None, :]).astype(jnp.bfloat16)
    squares = split_float(jnp.sum(inputs32 * inputs32, axis=1), 3)
    extra = jnp.stack(squares + [jnp.zeros_like(squares[0])] * 125, axis=1)
    arrived = gather_blocks(jnp.concatenate([scaled, extra], axis=1), "pack")
    input_squares = jnp.sum(arrived[:, :, feature_count : feature_count + 3].astype(jnp.float32), axis=(0, 2))
    input_rms = lax.rsqrt(input_squares / model_width + EPSILON)
    features = jnp.moveaxis(arrived[:, :, :feature_count], 0, 1).reshape(stmt_count, model_width)
    projected = jnp.dot(features, w_query, preferred_element_type=jnp.float32)
    queries = (projected * input_rms[:, None]).reshape(stmt_count, local_heads, head_dim)
    queries = (
        queries
        * lax.rsqrt(jnp.mean(queries * queries, axis=2, keepdims=True) + EPSILON)
        * query_gain
    )
    queries = rotate_heads(queries, (lengths_row - 1).astype(jnp.float32)).astype(jnp.bfloat16)
    all_queries = jnp.moveaxis(gather_blocks(queries, "pack"), 0, 1).reshape(
        stmt_count, pack_size * local_heads, head_dim
    )
    start, end = statement_ranges(lengths_row, order_row)
    tokens = pack_index * token_count + jnp.arange(token_count, dtype=jnp.int32)
    token_mask = (tokens[None, :] >= start[:, None]) & (tokens[None, :] < end[:, None])
    block_max, block_sum, numerators = block_attention(
        all_queries, cached_keys, cached_values, token_mask, head_dim ** (-0.5)
    )

    def by_owner(part):
        return jnp.moveaxis(part.reshape((stmt_count, pack_size, -1)), 1, 0)

    message = jnp.concatenate(
        [by_owner(numerators.astype(jnp.bfloat16))]
        + [by_owner(piece) for piece in split_float(block_max, 3) + split_float(block_sum, 2)],
        axis=2,
    )
    message = lax.all_to_all(message, "pack", 0, 0)
    width = local_heads * head_dim
    stats = message[:, :, width:].astype(jnp.float32).reshape(pack_size, stmt_count, 5, local_heads)
    maxima = stats[:, :, 0] + stats[:, :, 1] + stats[:, :, 2]
    factor = jnp.exp(maxima - jnp.max(maxima, axis=0, keepdims=True))
    denominator = jnp.sum((stats[:, :, 3] + stats[:, :, 4]) * factor, axis=0)
    numerators = message[:, :, :width].astype(jnp.float32).reshape(pack_size, stmt_count, local_heads, head_dim)
    summed = jnp.sum(numerators * factor[..., None], axis=0)
    attended = (summed / denominator[..., None]).astype(jnp.bfloat16)
    partial_out = jnp.dot(
        attended.reshape(stmt_count, width), w_out, preferred_element_type=jnp.float32
    )
    partial_out = jnp.moveaxis(
        partial_out.astype(jnp.bfloat16).reshape(stmt_count, pack_size, feature_count), 1, 0
    )
    partial_out = lax.all_to_all(partial_out, "pack", 0, 0)
    hidden = inputs32 + jnp.sum(partial_out.astype(jnp.float32), axis=0)
    scaled_out = hidden * final_gain[None, :]
    vectors = lax.all_gather(scaled_out.astype(jnp.bfloat16), "dp", axis=0, tiled=True)
    gram = lax.dot_general(
        vectors, vectors, (((1,), (1,)), ((), ())), preferred_element_type=jnp.float32
    )
    own_squares = jnp.sum(hidden * hidden, axis=1)
    extra = jnp.zeros((total_stmts,), jnp.float32).at[:stmt_count].set(own_squares)
    gram = jnp.concatenate([gram, extra[:, None]], axis=1)
    if total_stmts <= 128:
        gram = jnp.sum(gather_blocks(gram, "pack"), axis=0)
    else:
        gram = lax.psum(gram, "pack")
    hidden_rms = jnp.sqrt(gram[:stmt_count, total_stmts] / model_width + EPSILON)
    gram = gram[:, :total_stmts]
    column_ids = jnp.arange(total_stmts, dtype=jnp.int32)
    diagonal = column_ids[:, None] == column_ids[None, :]
    norms_row = lax.rsqrt(jnp.sum(jnp.where(diagonal, gram, 0.0), axis=0))
    norms_column = lax.rsqrt(jnp.sum(jnp.where(diagonal, gram, 0.0), axis=1))
    cosines = gram * norms_column[:, None] * norms_row[None, :]
    logits = jnp.where(diagonal, MASKED_LOGIT, cosines / SOFTMAX_WARMTH)
    highest = jnp.max(logits, axis=1)
    all_lse = highest + jnp.log(jnp.sum(jnp.exp(logits - highest[:, None]), axis=1))
    is_partner = column_ids[None, :] == partner[:, None]
    all_loss = all_lse - jnp.sum(jnp.where(is_partner, logits, 0.0), axis=1)
    own_count = stmt_count // pack_size
    row_base = group_index * stmt_count
    loss_rows = lax.dynamic_slice_in_dim(all_loss, row_base + pack_index * own_count, own_count, 0)
    weights = (
        jnp.exp(logits - all_lse[:, None])
        + jnp.exp(logits - all_lse[None, :])
        - is_partner.astype(jnp.float32)
        - is_partner.T.astype(jnp.float32)
    ).astype(jnp.bfloat16)
    own_weights = lax.dynamic_slice_in_dim(weights, row_base, stmt_count, 0)
    own_cosines = lax.dynamic_slice_in_dim(cosines, row_base, stmt_count, 0)
    own_norm = lax.dynamic_slice_in_dim(norms_column, row_base, stmt_count, 0)
    inner = jnp.sum(own_weights.astype(jnp.float32) * own_cosines, axis=1)
    own_norm = own_norm[:, None]
    embeddings = (vectors.astype(jnp.float32) * norms_column[:, None]).astype(jnp.bfloat16)
    gradient = jnp.dot(own_weights, embeddings, preferred_element_type=jnp.float32)
    scale = model_width**0.5 / SOFTMAX_WARMTH
    pooled = (scaled_out / hidden_rms[:, None]).astype(jnp.bfloat16)
    grad_hidden = (
        scale * final_gain[None, :] * (gradient - scaled_out * own_norm * inner[:, None]) * own_norm
    ).astype(jnp.bfloat16)
    return (pooled, loss_rows, grad_hidden)


def solution(mesh):
    in_specs = (
        P("dp", "pack"),
        P("pack"),
        P(None, "pack"),
        P(),
        P(("dp", "pack"), None),
        P(("dp", "pack"), None),
        P("pack", None),
        P("pack"),
        P("dp", None),
        P("dp", None),
        P(),
    )
    out_specs = (P("dp", "pack"), P(("dp", "pack")), P("dp", "pack"))
    return jax.shard_map(local, mesh=mesh, in_specs=in_specs, out_specs=out_specs, check_vma=False)
```

```python
import numpy as np
import jax
import jax.numpy as jnp
from jax import lax
from jax.experimental import pallas as pl
from jax.experimental.pallas import tpu as pltpu
from jax.sharding import PartitionSpec as P

EPSILON = 1e-06
SOFTMAX_WARMTH = 0.05
ROPE_BASE = 1000000.0
MASKED_LOGIT = -1e30


def gather_blocks(block, axis):
    size = lax.axis_size(axis)
    return lax.all_to_all(jnp.broadcast_to(block[None], (size,) + block.shape), axis, 0, 0)


def split_float(value, pieces):
    out = []
    for _ in range(pieces):
        piece = lax.reduce_precision(value, 8, 7)
        out.append(piece.astype(jnp.bfloat16))
        value = value - piece
    return out


def cosine_and_sine(angles):
    turns = jnp.round(angles * np.float32(2.0 / np.pi))
    rest = angles - turns * np.float32(1.5703125)
    rest = rest - turns * np.float32(4.837512969970703125e-4)
    rest = rest - turns * np.float32(7.549789948768648e-8)
    square = rest * rest
    sine = rest + rest * square * (
        np.float32(-1.6666654611e-1)
        + square * (np.float32(8.3321608736e-3) + square * np.float32(-1.9515295891e-4))
    )
    cosine = (
        1.0
        - 0.5 * square
        + square
        * square
        * (
            np.float32(4.166664568298827e-2)
            + square
            * (np.float32(-1.388731625493765e-3) + square * np.float32(2.443315711809948e-5))
        )
    )
    quarter = turns.astype(jnp.int32) & 3
    swap = (quarter & 1) == 1
    cos_out = jnp.where(swap, sine, cosine)
    sin_out = jnp.where(swap, cosine, sine)
    cos_out = jnp.where((quarter == 1) | (quarter == 2), -cos_out, cos_out)
    sin_out = jnp.where(quarter >= 2, -sin_out, sin_out)
    return cos_out, sin_out


def rotate_heads(queries, position):
    head_dim = queries.shape[-1]
    half_dim = head_dim // 2
    frequency = (ROPE_BASE ** (-np.arange(half_dim) * 2.0 / head_dim)).astype(np.float32)
    cosine, sine = cosine_and_sine(position[:, None] * frequency[None, :])
    cosine = jnp.concatenate([cosine, cosine], axis=1)[:, None, :]
    sine = jnp.concatenate([-sine, sine], axis=1)[:, None, :]
    turned = jnp.concatenate([queries[..., half_dim:], queries[..., :half_dim]], axis=-1)
    return queries * cosine + turned * sine


def statement_ranges(lengths_row, order_row):
    stmt_count = order_row.shape[0]
    index = jnp.arange(stmt_count, dtype=jnp.int32)
    slot = jnp.sum(jnp.where(order_row[None, :] == index[:, None], index[None, :], 0), axis=1)
    start = jnp.sum(jnp.where(slot[None, :] < slot[:, None], lengths_row[None, :], 0), axis=1)
    return start, start + lengths_row


def block_attention(all_queries, cached_keys, cached_values, token_mask, score_scale):
    stmt_count, head_count, head_dim = all_queries.shape
    kv_heads = cached_keys.shape[1] // head_dim
    group_size = head_count // kv_heads
    grouped = all_queries.reshape(stmt_count, kv_heads, group_size, head_dim)
    key_heads = cached_keys.reshape(-1, kv_heads, head_dim)
    value_heads = cached_values.reshape(-1, kv_heads, head_dim)
    scores = (
        jnp.einsum("skgd,tkd->skgt", grouped, key_heads, preferred_element_type=jnp.float32)
        * score_scale
    )
    token_mask = token_mask[:, None, None, :]
    block_max = jnp.max(jnp.where(token_mask, scores, MASKED_LOGIT), axis=3)
    softmax_weights = jnp.where(token_mask, jnp.exp(scores - block_max[..., None]), 0.0)
    block_sum = jnp.sum(softmax_weights, axis=3)
    numerators = jnp.einsum(
        "skgt,tkd->skgd",
        softmax_weights.astype(jnp.bfloat16),
        value_heads,
        preferred_element_type=jnp.float32,
    )
    return (
        block_max.reshape(stmt_count, head_count),
        block_sum.reshape(stmt_count, head_count),
        numerators.reshape(stmt_count, head_count, head_dim),
    )


def flip(array, axis, offset):
    size = lax.axis_size(axis)
    return lax.ppermute(array, axis, [(i, i ^ offset) for i in range(size)])


def in_vmem(body, outputs, *operands, limit=8, flops=1_000_000):
    whole = pl.BlockSpec(memory_space=pltpu.VMEM)
    moved = sum(operand.size * operand.dtype.itemsize for operand in operands)
    return pl.pallas_call(
        body,
        out_shape=outputs,
        in_specs=[whole] * len(operands),
        out_specs=jax.tree.map(lambda _: whole, outputs),
        compiler_params=pltpu.CompilerParams(vmem_limit_bytes=limit << 20),
        cost_estimate=pl.CostEstimate(flops=flops, bytes_accessed=moved, transcendentals=0),
    )(*operands)


def shaped(shape, kind):
    return jax.ShapeDtypeStruct(shape, kind)


def lane_pieces(values, width=128):
    rows = values[0].shape[0]
    lane = lax.broadcasted_iota(jnp.int32, (rows, width), 1)
    out = jnp.zeros((rows, width), jnp.float32)
    for place, value in enumerate(values):
        rest = value
        for part in range(3):
            piece = rest.astype(jnp.bfloat16).astype(jnp.float32)
            out = jnp.where(lane == 3 * place + part, piece, out)
            rest = rest - piece
    return out.astype(jnp.bfloat16)


def lane_sum(block, place):
    lane = lax.broadcasted_iota(jnp.int32, block.shape, 1)
    own = (lane >= 3 * place) & (lane < 3 * place + 3)
    return jnp.sum(jnp.where(own, block, 0.0), axis=1, keepdims=True)


def prepare_inputs(hidden_ref, gain_ref, message_ref):
    inputs = hidden_ref[...].astype(jnp.float32)
    width = inputs.shape[1]
    message_ref[:, :width] = (inputs * gain_ref[...]).astype(jnp.bfloat16)
    message_ref[:, width:] = lane_pieces([jnp.sum(inputs * inputs, axis=1, keepdims=True)])


def positions_and_ranges(frequency_ref, lengths_ref, order_ref, rope_ref, range_ref):
    count = lengths_ref.shape[1]
    half = frequency_ref.shape[1] // 2
    row = lax.broadcasted_iota(jnp.int32, (count, count), 0)
    column = lax.broadcasted_iota(jnp.int32, (count, count), 1)
    lengths = jnp.broadcast_to(lengths_ref[...], (count, count)).astype(jnp.float32)
    length = jnp.sum(jnp.where(row == column, lengths, 0.0), axis=1, keepdims=True)
    order = jnp.broadcast_to(order_ref[...], (count, count))
    placed = order == row
    slot = jnp.sum(jnp.where(placed, column, 0).astype(jnp.float32), axis=1, keepdims=True)
    packed = jnp.sum(jnp.where(placed, length, 0.0), axis=0, keepdims=True)
    earlier = column.astype(jnp.float32) < slot
    start = jnp.sum(jnp.where(earlier, packed, 0.0), axis=1, keepdims=True)
    range_ref[:, :128] = jnp.broadcast_to(start, (count, 128))
    range_ref[:, 128:] = jnp.broadcast_to(start + length, (count, 128))
    cosine, sine = cosine_and_sine((length - 1.0) * frequency_ref[...])
    lane = lax.broadcasted_iota(jnp.int32, cosine.shape, 1)
    rope_ref[:, : 2 * half] = cosine
    rope_ref[:, 2 * half :] = jnp.where(lane < half, -sine, sine)


def send_heads(key_ref, value_ref, out_ref, semaphore):
    me = lax.axis_index("pack")
    heads = out_ref.shape[1] // 256
    copies = []
    for i in range(heads):
        column = pl.multiple_of((me ^ 1 ^ (2 * i)) * 128, 128)
        for place, source in enumerate((key_ref, value_ref)):
            copies.append(
                pltpu.make_async_copy(
                    source.at[:, pl.ds(column, 128)],
                    out_ref.at[:, pl.ds((place * heads + i) * 128, 128)],
                    semaphore.at[place * heads + i],
                )
            )
    for copy in copies:
        copy.start()
    for copy in copies:
        copy.wait()


def project_blocks(offsets, blocks, weight_ref, width):
    me = lax.axis_index("pack")
    total = None
    for offset, block in zip(offsets, blocks):
        rows = pl.ds(pl.multiple_of((me ^ offset) * width, width), width)
        part = jnp.dot(
            block[:, :width].astype(jnp.bfloat16),
            weight_ref[rows, :],
            preferred_element_type=jnp.float32,
        )
        total = part if total is None else total + part
    return total


def join_blocks(*refs):
    out_ref = refs[-1]
    for i, ref in enumerate(refs[:-1]):
        out_ref[i] = ref[...]


def first_half(blocks_ref, weight_ref, total_ref):
    width = weight_ref.shape[1]
    blocks = [blocks_ref[i] for i in range(blocks_ref.shape[0])]
    total_ref[...] = project_blocks((0, 2, 4, 6), blocks, weight_ref, width)


def second_half(
    own_ref, other_ref, total_ref, weight_ref, gain_ref, rope_ref, query_ref, *, model_width
):
    width = weight_ref.shape[1]
    count = own_ref.shape[0]
    blocks = [other_ref[i] for i in range(count)]
    projected = total_ref[...] + project_blocks((1, 3, 5, 7), blocks, weight_ref, width)
    squares = sum(
        lane_sum(ref[i, :, width:].astype(jnp.float32), 0)
        for ref in (own_ref, other_ref)
        for i in range(count)
    )
    projected = projected * lax.rsqrt(squares / model_width + EPSILON)
    head_dim = gain_ref.shape[1]
    cosine = rope_ref[:, :head_dim]
    sine = rope_ref[:, head_dim:]
    for head in range(width // head_dim):
        place = slice(head * head_dim, (head + 1) * head_dim)
        query = projected[:, place]
        mean = jnp.mean(query * query, axis=1, keepdims=True)
        query = query * lax.rsqrt(mean + EPSILON) * gain_ref[...]
        turned = pltpu.roll(query, head_dim // 2, 1)
        query_ref[:, place] = (query * cosine + turned * sine).astype(jnp.bfloat16)


def attend_head(i, query, key_ref, value_ref, swapped_ref, range_ref):
    me = lax.axis_index("pack")
    tokens = key_ref.shape[0]
    head_dim = 128
    heads = swapped_ref.shape[1] // (2 * head_dim)
    grouped = jnp.concatenate(
        [query[:, h * head_dim : (h + 1) * head_dim] for h in range(query.shape[1] // head_dim)],
        axis=0,
    )
    group = query.shape[1] // head_dim
    column = pl.ds(pl.multiple_of((me ^ (2 * i)) * head_dim, head_dim), head_dim)
    keys = (key_ref[:, column], swapped_ref[:, i * head_dim : (i + 1) * head_dim])
    values = (
        value_ref[:, column],
        swapped_ref[:, (heads + i) * head_dim : (heads + i + 1) * head_dim],
    )
    scores = []
    masks = []
    for part, owner in enumerate((me, me ^ 1)):
        index = lax.broadcasted_iota(jnp.int32, (query.shape[0], tokens), 1) + owner * tokens
        index = index.astype(jnp.float32)
        mask = (index >= range_ref[:, :1]) & (index < range_ref[:, 128:129])
        mask = jnp.concatenate([mask.astype(jnp.float32)] * group, axis=0) > 0.5
        raw = lax.dot_general(
            grouped, keys[part], (((1,), (1,)), ((), ())), preferred_element_type=jnp.float32
        )
        scores.append(jnp.where(mask, raw * (head_dim**-0.5), MASKED_LOGIT))
        masks.append(mask)
    highest = jnp.maximum(
        jnp.max(scores[0], axis=1, keepdims=True), jnp.max(scores[1], axis=1, keepdims=True)
    )
    total = 0.0
    numerators = 0.0
    for part in range(2):
        weights = jnp.where(masks[part], jnp.exp(scores[part] - highest), 0.0)
        total = total + jnp.sum(weights, axis=1, keepdims=True)
        numerators = numerators + jnp.dot(
            weights.astype(jnp.bfloat16), values[part], preferred_element_type=jnp.float32
        )
    return highest, total, numerators


def attend_others(*refs):
    query_refs, refs = refs[:3], refs[3:]
    key_ref, value_ref, swapped_ref, range_ref = refs[:4]
    rows = query_refs[0].shape[0]
    for i, (query_ref, out_ref) in enumerate(zip(query_refs, refs[4:])):
        highest, total, numerators = attend_head(
            i + 1, query_ref[...], key_ref, value_ref, swapped_ref, range_ref
        )
        stats = []
        for h in range(query_ref.shape[1] // 128):
            part = slice(h * rows, (h + 1) * rows)
            out_ref[:, h * 128 : (h + 1) * 128] = numerators[part].astype(jnp.bfloat16)
            stats += [highest[part], total[part]]
        out_ref[:, query_ref.shape[1] :] = lane_pieces(stats)


def attend_own(query_ref, key_ref, value_ref, swapped_ref, range_ref, out_ref, stats_ref):
    highest, total, numerators = attend_head(
        0, query_ref[...], key_ref, value_ref, swapped_ref, range_ref
    )
    out_ref[...] = numerators
    stats_ref[:, :128] = jnp.broadcast_to(highest, (highest.shape[0], 128))
    stats_ref[:, 128:] = jnp.broadcast_to(total, (highest.shape[0], 128))


def join_and_project(
    own_ref, stats_ref, first_ref, second_ref, third_ref, weight_ref, attended_ref, out_ref
):
    me = lax.axis_index("pack")
    rows, width = attended_ref.shape
    others = (first_ref, second_ref, third_ref)
    for h in range(width // 128):
        part = slice(h * rows, (h + 1) * rows)
        place = slice(h * 128, (h + 1) * 128)
        maxima = [stats_ref[part, :1]]
        totals = [stats_ref[part, 128:129]]
        numerators = [own_ref[part, :]]
        for ref in others:
            stats = ref[:, width:].astype(jnp.float32)
            maxima.append(lane_sum(stats, 2 * h))
            totals.append(lane_sum(stats, 2 * h + 1))
            numerators.append(ref[:, place].astype(jnp.float32))
        highest = maxima[0]
        for value in maxima[1:]:
            highest = jnp.maximum(highest, value)
        denominator = 0.0
        summed = 0.0
        for value, total, numerator in zip(maxima, totals, numerators):
            factor = jnp.exp(value - highest)
            denominator = denominator + total * factor
            summed = summed + numerator * factor
        attended_ref[:, place] = (summed / denominator).astype(jnp.bfloat16)
    attended = attended_ref[...]
    for i in range(out_ref.shape[0]):
        column = pl.ds(pl.multiple_of((me ^ 1 ^ (2 * i)) * width, width), width)
        out_ref[i] = jnp.dot(
            attended, weight_ref[:, column], preferred_element_type=jnp.float32
        ).astype(jnp.bfloat16)


def project_own(attended_ref, weight_ref, out_ref):
    me = lax.axis_index("pack")
    width = attended_ref.shape[1]
    attended = attended_ref[...]
    for i in range(out_ref.shape[0]):
        column = pl.ds(pl.multiple_of((me ^ (2 * i)) * width, width), width)
        out_ref[i] = jnp.dot(attended, weight_ref[:, column], preferred_element_type=jnp.float32)


def add_cores(own_ref, other_ref, hidden_ref, kept_ref, *sent_refs):
    kept_ref[...] = (
        hidden_ref[...].astype(jnp.float32) + own_ref[0] + other_ref[0].astype(jnp.float32)
    )
    for i, ref in enumerate(sent_refs):
        ref[...] = (own_ref[i + 1] + other_ref[i + 1].astype(jnp.float32)).astype(jnp.bfloat16)


def finish_hidden(kept_ref, first_ref, second_ref, third_ref, gain_ref, sent_ref, scaled_ref, square_ref):
    hidden = kept_ref[...]
    for ref in (first_ref, second_ref, third_ref):
        hidden = hidden + ref[...].astype(jnp.float32)
    scaled = hidden * gain_ref[...]
    scaled_ref[...] = scaled
    sent_ref[...] = scaled.astype(jnp.bfloat16)
    square_ref[...] = jnp.broadcast_to(
        jnp.sum(hidden * hidden, axis=1, keepdims=True), square_ref.shape
    )


def gram_part(first_ref, second_ref, third_ref, fourth_ref, square_ref, vectors_ref, out_ref):
    rows = first_ref.shape[0]
    for i, ref in enumerate((first_ref, second_ref, third_ref, fourth_ref)):
        vectors_ref[i * rows : (i + 1) * rows, :] = ref[...]
    vectors = vectors_ref[...]
    gram = lax.dot_general(
        vectors, vectors, (((1,), (1,)), ((), ())), preferred_element_type=jnp.float32
    )
    half = gram.shape[0] // 2
    out_ref[:half, : 2 * half] = gram[:half]
    out_ref[:half, 2 * half :] = gram[half:]
    out_ref[half:, :] = square_ref[...]


def add_two(first_ref, second_ref, out_ref):
    out_ref[...] = first_ref[...] + second_ref[...]


def losses_and_gradient(
    a_ref,
    b_ref,
    c_ref,
    d_ref,
    vectors_ref,
    scaled_ref,
    gain_ref,
    partner_ref,
    pooled_ref,
    loss_ref,
    grad_ref,
    *,
    model_width,
):
    group = lax.axis_index("dp")
    me = lax.axis_index("pack")
    count = vectors_ref.shape[0]
    rows = scaled_ref.shape[0]
    half = count // 2
    summed = a_ref[...] + b_ref[...] + c_ref[...] + d_ref[...]
    gram = jnp.concatenate([summed[:half, :count], summed[:half, count:]], axis=0)
    squares = summed[half:, :1]
    shape = (count, count)
    row = lax.broadcasted_iota(jnp.int32, shape, 0)
    column = lax.broadcasted_iota(jnp.int32, shape, 1)
    row_id = ((group ^ (row // rows)) * rows) + row % rows
    column_id = ((group ^ (column // rows)) * rows) + column % rows
    partners = jnp.broadcast_to(partner_ref[...], shape)
    row_partner = jnp.sum(
        jnp.where(column == row_id, partners, 0).astype(jnp.float32), axis=1, keepdims=True
    )
    column_partner = jnp.sum(
        jnp.where(row_id == column_id, row_partner, 0.0), axis=0, keepdims=True
    )
    own_partner = column_id.astype(jnp.float32) == row_partner
    other_partner = row_id.astype(jnp.float32) == column_partner
    diagonal = row == column
    on_diagonal = jnp.where(diagonal, gram, 0.0)
    row_scale = lax.rsqrt(jnp.sum(on_diagonal, axis=1, keepdims=True))
    column_scale = lax.rsqrt(jnp.sum(on_diagonal, axis=0, keepdims=True))
    cosines = gram * row_scale * column_scale
    scaled_cosines = cosines * (1.0 / SOFTMAX_WARMTH)
    logits = jnp.where(diagonal, MASKED_LOGIT, scaled_cosines)
    row_high = jnp.max(logits, axis=1, keepdims=True)
    row_lse = row_high + jnp.log(jnp.sum(jnp.exp(logits - row_high), axis=1, keepdims=True))
    column_high = jnp.max(logits, axis=0, keepdims=True)
    column_lse = column_high + jnp.log(
        jnp.sum(jnp.exp(logits - column_high), axis=0, keepdims=True)
    )
    loss = row_lse - jnp.sum(jnp.where(own_partner, logits, 0.0), axis=1, keepdims=True)
    own = loss_ref.shape[0]
    index = lax.broadcasted_iota(jnp.int32, (count, 1), 0)
    for i in range(own):
        loss_ref[i] = jnp.sum(jnp.where(index == me * own + i, loss, 0.0))
    weights = (
        jnp.exp(logits - row_lse)
        + jnp.exp(logits - column_lse)
        - own_partner.astype(jnp.float32)
        - other_partner.astype(jnp.float32)
    )[:rows]
    inner = jnp.sum(weights * cosines[:rows], axis=1, keepdims=True)
    scaled_weights = weights * column_scale
    upper = scaled_weights.astype(jnp.bfloat16)
    lower = (scaled_weights - upper.astype(jnp.float32)).astype(jnp.bfloat16)
    vectors = vectors_ref[...]
    gradient = jnp.dot(upper, vectors, preferred_element_type=jnp.float32) + jnp.dot(
        lower, vectors, preferred_element_type=jnp.float32
    )
    own_scale = row_scale[:rows]
    scaled = scaled_ref[...]
    gradient = (gradient - scaled * (own_scale * inner)) * own_scale
    grad_ref[...] = (gradient * (gain_ref[...] * (model_width**0.5 / SOFTMAX_WARMTH))).astype(
        jnp.bfloat16
    )
    pooled_ref[...] = (scaled * lax.rsqrt(squares / model_width + EPSILON)).astype(jnp.bfloat16)


def chip_pairs(
    hidden_in,
    attn_gain,
    w_query,
    query_gain,
    cached_keys,
    cached_values,
    w_out,
    final_gain,
    lengths,
    pack_order,
    partner,
):
    pack_size = lax.axis_size("pack")
    stmts, width = hidden_in.shape
    model_width = width * pack_size
    head_dim = query_gain.shape[0]
    tokens = cached_keys.shape[0]
    chips = pack_size // 2
    total = partner.shape[0]
    bf16 = jnp.bfloat16
    f32 = jnp.float32
    attn_gain = attn_gain[None]
    final_gain = final_gain[None]
    query_gain = query_gain[None]
    half = np.arange(head_dim // 2)
    frequency = (ROPE_BASE ** (-half * 2.0 / head_dim)).astype(np.float32)
    frequency = jnp.asarray(np.concatenate([frequency, frequency])[None])

    message = in_vmem(
        prepare_inputs, shaped((stmts, width + 128), bf16), hidden_in, attn_gain
    )
    blocks = [message] + [flip(message, "pack", 2 * i) for i in range(1, chips)]
    blocks = in_vmem(join_blocks, shaped((chips,) + message.shape, bf16), *blocks)
    others = flip(blocks, "pack", 1)
    rope, ranges = in_vmem(
        positions_and_ranges,
        (shaped((stmts, 2 * head_dim), f32), shaped((stmts, 256), f32)),
        frequency,
        lengths,
        pack_order,
    )
    anywhere = pl.BlockSpec(memory_space=pl.ANY)
    swapped = pl.pallas_call(
        send_heads,
        out_shape=shaped((tokens, 2 * chips * head_dim), bf16),
        in_specs=[anywhere] * 2,
        out_specs=anywhere,
        scratch_shapes=[pltpu.SemaphoreType.DMA((2 * chips,))],
        compiler_params=pltpu.CompilerParams(vmem_limit_bytes=4 << 20),
        cost_estimate=pl.CostEstimate(flops=0, bytes_accessed=2 << 20, transcendentals=0),
    )(cached_keys, cached_values)
    swapped = flip(swapped, "pack", 1)
    projected = in_vmem(
        first_half, shaped((stmts, width), f32), blocks, w_query, limit=16, flops=1 << 27
    )
    queries = in_vmem(
        lambda *refs: second_half(*refs, model_width=model_width),
        shaped((stmts, width), bf16),
        blocks,
        others,
        projected,
        w_query,
        query_gain,
        rope,
        limit=16,
        flops=1 << 27,
    )
    received = [flip(queries, "pack", 2 * i) for i in range(1, chips)]
    sent = in_vmem(
        attend_others,
        (shaped((stmts, width + 128), bf16),) * (chips - 1),
        *received,
        cached_keys,
        cached_values,
        swapped,
        ranges,
        flops=1 << 27,
    )
    partials = [flip(part, "pack", 2 * (i + 1)) for i, part in enumerate(sent)]
    group_rows = stmts * (width // head_dim)
    own_part, own_stats = in_vmem(
        attend_own,
        (shaped((group_rows, head_dim), f32), shaped((group_rows, 256), f32)),
        queries,
        cached_keys,
        cached_values,
        swapped,
        ranges,
        flops=1 << 26,
    )
    attended, to_core = in_vmem(
        join_and_project,
        (shaped((stmts, width), bf16), shaped((chips, stmts, width), bf16)),
        own_part,
        own_stats,
        *partials,
        w_out,
        limit=16,
        flops=1 << 27,
    )
    from_core = flip(to_core, "pack", 1)
    own_out = in_vmem(
        project_own,
        shaped((chips, stmts, width), f32),
        attended,
        w_out,
        limit=16,
        flops=1 << 27,
    )
    kept, *to_chips = in_vmem(
        add_cores,
        (shaped((stmts, width), f32),) + (shaped((stmts, width), bf16),) * (chips - 1),
        own_out,
        from_core,
        hidden_in,
    )
    from_chips = [flip(part, "pack", 2 * (i + 1)) for i, part in enumerate(to_chips)]
    vector, scaled, squares = in_vmem(
        finish_hidden,
        (shaped((stmts, width), bf16), shaped((stmts, width), f32), shaped((stmts, 128), f32)),
        kept,
        *from_chips,
        final_gain,
    )
    vectors = [vector] + [flip(vector, "dp", i) for i in range(1, lax.axis_size("dp"))]
    vectors, gram = in_vmem(
        gram_part,
        (shaped((total, width), bf16), shaped((total // 2 + stmts, 128), f32)),
        *vectors,
        squares,
    )
    gram = in_vmem(add_two, shaped(gram.shape, f32), gram, flip(gram, "pack", 1))
    grams = [gram] + [flip(gram, "pack", 2 * i) for i in range(1, chips)]
    whole = pl.BlockSpec(memory_space=pltpu.VMEM)
    pooled, loss_rows, grad_hidden = pl.pallas_call(
        lambda *refs: losses_and_gradient(*refs, model_width=model_width),
        out_shape=(
            shaped((stmts, width), bf16),
            shaped((stmts // pack_size,), f32),
            shaped((stmts, width), bf16),
        ),
        in_specs=[whole] * 8,
        out_specs=(whole, pl.BlockSpec(memory_space=pltpu.SMEM), whole),
        compiler_params=pltpu.CompilerParams(vmem_limit_bytes=8 << 20),
    )(*grams, vectors, scaled, final_gain, partner[None])
    return (pooled, loss_rows, grad_hidden)


def local(
    hidden_in,
    attn_gain,
    w_query,
    query_gain,
    cached_keys,
    cached_values,
    w_out,
    final_gain,
    lengths,
    pack_order,
    partner,
):
    pack_size = lax.axis_size("pack")
    pack_index = lax.axis_index("pack")
    group_index = lax.axis_index("dp")
    stmt_count, feature_count = hidden_in.shape
    model_width = feature_count * pack_size
    head_dim = query_gain.shape[0]
    local_heads = w_query.shape[1] // head_dim
    token_count = cached_keys.shape[0]
    total_stmts = partner.shape[0]
    lengths_row = lengths[0]
    order_row = pack_order[0]
    inputs32 = hidden_in.astype(jnp.float32)

    scaled = (inputs32 * attn_gain[None, :]).astype(jnp.bfloat16)
    squares = split_float(jnp.sum(inputs32 * inputs32, axis=1), 3)
    extra = jnp.stack(squares + [jnp.zeros_like(squares[0])] * 125, axis=1)
    arrived = gather_blocks(jnp.concatenate([scaled, extra], axis=1), "pack")
    input_squares = jnp.sum(arrived[:, :, feature_count : feature_count + 3].astype(jnp.float32), axis=(0, 2))
    input_rms = lax.rsqrt(input_squares / model_width + EPSILON)
    features = jnp.moveaxis(arrived[:, :, :feature_count], 0, 1).reshape(stmt_count, model_width)
    projected = jnp.dot(features, w_query, preferred_element_type=jnp.float32)
    queries = (projected * input_rms[:, None]).reshape(stmt_count, local_heads, head_dim)
    queries = (
        queries
        * lax.rsqrt(jnp.mean(queries * queries, axis=2, keepdims=True) + EPSILON)
        * query_gain
    )
    queries = rotate_heads(queries, (lengths_row - 1).astype(jnp.float32)).astype(jnp.bfloat16)
    all_queries = jnp.moveaxis(gather_blocks(queries, "pack"), 0, 1).reshape(
        stmt_count, pack_size * local_heads, head_dim
    )
    start, end = statement_ranges(lengths_row, order_row)
    tokens = pack_index * token_count + jnp.arange(token_count, dtype=jnp.int32)
    token_mask = (tokens[None, :] >= start[:, None]) & (tokens[None, :] < end[:, None])
    block_max, block_sum, numerators = block_attention(
        all_queries, cached_keys, cached_values, token_mask, head_dim ** (-0.5)
    )

    def by_owner(part):
        return jnp.moveaxis(part.reshape((stmt_count, pack_size, -1)), 1, 0)

    message = jnp.concatenate(
        [by_owner(numerators.astype(jnp.bfloat16))]
        + [by_owner(piece) for piece in split_float(block_max, 3) + split_float(block_sum, 2)],
        axis=2,
    )
    message = lax.all_to_all(message, "pack", 0, 0)
    width = local_heads * head_dim
    stats = message[:, :, width:].astype(jnp.float32).reshape(pack_size, stmt_count, 5, local_heads)
    maxima = stats[:, :, 0] + stats[:, :, 1] + stats[:, :, 2]
    factor = jnp.exp(maxima - jnp.max(maxima, axis=0, keepdims=True))
    denominator = jnp.sum((stats[:, :, 3] + stats[:, :, 4]) * factor, axis=0)
    numerators = message[:, :, :width].astype(jnp.float32).reshape(pack_size, stmt_count, local_heads, head_dim)
    summed = jnp.sum(numerators * factor[..., None], axis=0)
    attended = (summed / denominator[..., None]).astype(jnp.bfloat16)
    partial_out = jnp.dot(
        attended.reshape(stmt_count, width), w_out, preferred_element_type=jnp.float32
    )
    partial_out = jnp.moveaxis(
        partial_out.astype(jnp.bfloat16).reshape(stmt_count, pack_size, feature_count), 1, 0
    )
    partial_out = lax.all_to_all(partial_out, "pack", 0, 0)
    hidden = inputs32 + jnp.sum(partial_out.astype(jnp.float32), axis=0)
    scaled_out = hidden * final_gain[None, :]
    vectors = lax.all_gather(scaled_out.astype(jnp.bfloat16), "dp", axis=0, tiled=True)
    gram = lax.dot_general(
        vectors, vectors, (((1,), (1,)), ((), ())), preferred_element_type=jnp.float32
    )
    own_squares = jnp.sum(hidden * hidden, axis=1)
    extra = jnp.zeros((total_stmts,), jnp.float32).at[:stmt_count].set(own_squares)
    gram = jnp.concatenate([gram, extra[:, None]], axis=1)
    if total_stmts <= 128:
        gram = jnp.sum(gather_blocks(gram, "pack"), axis=0)
    else:
        gram = lax.psum(gram, "pack")
    hidden_rms = jnp.sqrt(gram[:stmt_count, total_stmts] / model_width + EPSILON)
    gram = gram[:, :total_stmts]
    column_ids = jnp.arange(total_stmts, dtype=jnp.int32)
    diagonal = column_ids[:, None] == column_ids[None, :]
    norms_row = lax.rsqrt(jnp.sum(jnp.where(diagonal, gram, 0.0), axis=0))
    norms_column = lax.rsqrt(jnp.sum(jnp.where(diagonal, gram, 0.0), axis=1))
    cosines = gram * norms_column[:, None] * norms_row[None, :]
    logits = jnp.where(diagonal, MASKED_LOGIT, cosines / SOFTMAX_WARMTH)
    highest = jnp.max(logits, axis=1)
    all_lse = highest + jnp.log(jnp.sum(jnp.exp(logits - highest[:, None]), axis=1))
    is_partner = column_ids[None, :] == partner[:, None]
    all_loss = all_lse - jnp.sum(jnp.where(is_partner, logits, 0.0), axis=1)
    own_count = stmt_count // pack_size
    row_base = group_index * stmt_count
    loss_rows = lax.dynamic_slice_in_dim(all_loss, row_base + pack_index * own_count, own_count, 0)
    weights = (
        jnp.exp(logits - all_lse[:, None])
        + jnp.exp(logits - all_lse[None, :])
        - is_partner.astype(jnp.float32)
        - is_partner.T.astype(jnp.float32)
    ).astype(jnp.bfloat16)
    own_weights = lax.dynamic_slice_in_dim(weights, row_base, stmt_count, 0)
    own_cosines = lax.dynamic_slice_in_dim(cosines, row_base, stmt_count, 0)
    own_norm = lax.dynamic_slice_in_dim(norms_column, row_base, stmt_count, 0)
    inner = jnp.sum(own_weights.astype(jnp.float32) * own_cosines, axis=1)
    own_norm = own_norm[:, None]
    embeddings = (vectors.astype(jnp.float32) * norms_column[:, None]).astype(jnp.bfloat16)
    gradient = jnp.dot(own_weights, embeddings, preferred_element_type=jnp.float32)
    scale = model_width**0.5 / SOFTMAX_WARMTH
    pooled = (scaled_out / hidden_rms[:, None]).astype(jnp.bfloat16)
    grad_hidden = (
        scale * final_gain[None, :] * (gradient - scaled_out * own_norm * inner[:, None]) * own_norm
    ).astype(jnp.bfloat16)
    return (pooled, loss_rows, grad_hidden)


def solution(mesh):
    body = chip_pairs if mesh.shape["pack"] == 8 and mesh.shape["dp"] == 4 else local
    in_specs = (
        P("dp", "pack"),
        P("pack"),
        P(None, "pack"),
        P(),
        P(("dp", "pack"), None),
        P(("dp", "pack"), None),
        P("pack", None),
        P("pack"),
        P("dp", None),
        P("dp", None),
        P(),
    )
    out_specs = (P("dp", "pack"), P(("dp", "pack")), P("dp", "pack"))
    return jax.shard_map(body, mesh=mesh, in_specs=in_specs, out_specs=out_specs, check_vma=False)
```

```python
import numpy as np
import jax
import jax.numpy as jnp
from jax import lax
from jax.experimental import pallas as pl
from jax.experimental.pallas import tpu as pltpu
from jax.sharding import PartitionSpec as P

EPSILON = 1e-06
SOFTMAX_WARMTH = 0.05
ROPE_BASE = 1000000.0
MASKED_LOGIT = -1e30


def gather_blocks(block, axis):
    size = lax.axis_size(axis)
    return lax.all_to_all(jnp.broadcast_to(block[None], (size,) + block.shape), axis, 0, 0)


def split_float(value, pieces):
    out = []
    for _ in range(pieces):
        piece = lax.reduce_precision(value, 8, 7)
        out.append(piece.astype(jnp.bfloat16))
        value = value - piece
    return out


def cosine_and_sine(angles):
    turns = jnp.round(angles * np.float32(2.0 / np.pi))
    rest = angles - turns * np.float32(1.5703125)
    rest = rest - turns * np.float32(4.837512969970703125e-4)
    rest = rest - turns * np.float32(7.549789948768648e-8)
    square = rest * rest
    sine = rest + rest * square * (
        np.float32(-1.6666654611e-1)
        + square * (np.float32(8.3321608736e-3) + square * np.float32(-1.9515295891e-4))
    )
    cosine = (
        1.0
        - 0.5 * square
        + square
        * square
        * (
            np.float32(4.166664568298827e-2)
            + square
            * (np.float32(-1.388731625493765e-3) + square * np.float32(2.443315711809948e-5))
        )
    )
    quarter = turns.astype(jnp.int32) & 3
    swap = (quarter & 1) == 1
    cos_out = jnp.where(swap, sine, cosine)
    sin_out = jnp.where(swap, cosine, sine)
    cos_out = jnp.where((quarter == 1) | (quarter == 2), -cos_out, cos_out)
    sin_out = jnp.where(quarter >= 2, -sin_out, sin_out)
    return cos_out, sin_out


def rotate_heads(queries, position):
    head_dim = queries.shape[-1]
    half_dim = head_dim // 2
    frequency = (ROPE_BASE ** (-np.arange(half_dim) * 2.0 / head_dim)).astype(np.float32)
    cosine, sine = cosine_and_sine(position[:, None] * frequency[None, :])
    cosine = jnp.concatenate([cosine, cosine], axis=1)[:, None, :]
    sine = jnp.concatenate([-sine, sine], axis=1)[:, None, :]
    turned = jnp.concatenate([queries[..., half_dim:], queries[..., :half_dim]], axis=-1)
    return queries * cosine + turned * sine


def statement_ranges(lengths_row, order_row):
    stmt_count = order_row.shape[0]
    index = jnp.arange(stmt_count, dtype=jnp.int32)
    slot = jnp.sum(jnp.where(order_row[None, :] == index[:, None], index[None, :], 0), axis=1)
    start = jnp.sum(jnp.where(slot[None, :] < slot[:, None], lengths_row[None, :], 0), axis=1)
    return start, start + lengths_row


def block_attention(all_queries, cached_keys, cached_values, token_mask, score_scale):
    stmt_count, head_count, head_dim = all_queries.shape
    kv_heads = cached_keys.shape[1] // head_dim
    group_size = head_count // kv_heads
    grouped = all_queries.reshape(stmt_count, kv_heads, group_size, head_dim)
    key_heads = cached_keys.reshape(-1, kv_heads, head_dim)
    value_heads = cached_values.reshape(-1, kv_heads, head_dim)
    scores = (
        jnp.einsum("skgd,tkd->skgt", grouped, key_heads, preferred_element_type=jnp.float32)
        * score_scale
    )
    token_mask = token_mask[:, None, None, :]
    block_max = jnp.max(jnp.where(token_mask, scores, MASKED_LOGIT), axis=3)
    softmax_weights = jnp.where(token_mask, jnp.exp(scores - block_max[..., None]), 0.0)
    block_sum = jnp.sum(softmax_weights, axis=3)
    numerators = jnp.einsum(
        "skgt,tkd->skgd",
        softmax_weights.astype(jnp.bfloat16),
        value_heads,
        preferred_element_type=jnp.float32,
    )
    return (
        block_max.reshape(stmt_count, head_count),
        block_sum.reshape(stmt_count, head_count),
        numerators.reshape(stmt_count, head_count, head_dim),
    )


def flip(array, axis, offset):
    size = lax.axis_size(axis)
    return lax.ppermute(array, axis, [(i, i ^ offset) for i in range(size)])


def in_vmem(body, outputs, *operands, limit=8, flops=1_000_000):
    whole = pl.BlockSpec(memory_space=pltpu.VMEM)
    moved = sum(operand.size * operand.dtype.itemsize for operand in operands)
    return pl.pallas_call(
        body,
        out_shape=outputs,
        in_specs=[whole] * len(operands),
        out_specs=jax.tree.map(lambda _: whole, outputs),
        compiler_params=pltpu.CompilerParams(vmem_limit_bytes=limit << 20),
        cost_estimate=pl.CostEstimate(flops=flops, bytes_accessed=moved, transcendentals=0),
    )(*operands)


def shaped(shape, kind):
    return jax.ShapeDtypeStruct(shape, kind)


def lane_pieces(values, width=128):
    rows = values[0].shape[0]
    lane = lax.broadcasted_iota(jnp.int32, (rows, width), 1)
    out = jnp.zeros((rows, width), jnp.float32)
    for place, value in enumerate(values):
        rest = value
        for part in range(3):
            piece = rest.astype(jnp.bfloat16).astype(jnp.float32)
            out = jnp.where(lane == 3 * place + part, piece, out)
            rest = rest - piece
    return out.astype(jnp.bfloat16)


def lane_sum(block, place):
    lane = lax.broadcasted_iota(jnp.int32, block.shape, 1)
    own = (lane >= 3 * place) & (lane < 3 * place + 3)
    return jnp.sum(jnp.where(own, block, 0.0), axis=1, keepdims=True)


def open_window(out_ref):
    out_ref[...] = jnp.zeros_like(out_ref)


def prepare_inputs(window_ref, hidden_ref, gain_ref, message_ref):
    del window_ref
    inputs = hidden_ref[...].astype(jnp.float32)
    width = inputs.shape[1]
    message_ref[:, :width] = (inputs * gain_ref[...]).astype(jnp.bfloat16)
    message_ref[:, width:] = lane_pieces([jnp.sum(inputs * inputs, axis=1, keepdims=True)])


def positions_and_ranges(
    message_ref, frequency_ref, lengths_ref, order_ref, rope_ref, range_ref
):
    del message_ref
    count = lengths_ref.shape[1]
    half = frequency_ref.shape[1] // 2
    row = lax.broadcasted_iota(jnp.int32, (count, count), 0)
    column = lax.broadcasted_iota(jnp.int32, (count, count), 1)
    lengths = jnp.broadcast_to(lengths_ref[...], (count, count)).astype(jnp.float32)
    length = jnp.sum(jnp.where(row == column, lengths, 0.0), axis=1, keepdims=True)
    order = jnp.broadcast_to(order_ref[...], (count, count))
    placed = order == row
    slot = jnp.sum(jnp.where(placed, column, 0).astype(jnp.float32), axis=1, keepdims=True)
    packed = jnp.sum(jnp.where(placed, length, 0.0), axis=0, keepdims=True)
    earlier = column.astype(jnp.float32) < slot
    start = jnp.sum(jnp.where(earlier, packed, 0.0), axis=1, keepdims=True)
    range_ref[:, :128] = jnp.broadcast_to(start, (count, 128))
    range_ref[:, 128:] = jnp.broadcast_to(start + length, (count, 128))
    cosine, sine = cosine_and_sine((length - 1.0) * frequency_ref[...])
    lane = lax.broadcasted_iota(jnp.int32, cosine.shape, 1)
    rope_ref[:, : 2 * half] = cosine
    rope_ref[:, 2 * half :] = jnp.where(lane < half, -sine, sine)


def send_heads(message_ref, key_ref, value_ref, out_ref, semaphore):
    del message_ref
    me = lax.axis_index("pack")
    heads = out_ref.shape[1] // 256
    copies = []
    for i in range(heads):
        column = pl.multiple_of((me ^ 1 ^ (2 * i)) * 128, 128)
        for place, source in enumerate((key_ref, value_ref)):
            copies.append(
                pltpu.make_async_copy(
                    source.at[:, pl.ds(column, 128)],
                    out_ref.at[:, pl.ds((place * heads + i) * 128, 128)],
                    semaphore.at[place * heads + i],
                )
            )
    for copy in copies:
        copy.start()
    for copy in copies:
        copy.wait()


def project_blocks(offsets, blocks, weight_ref):
    me = lax.axis_index("pack")
    width = weight_ref.shape[1]
    total = 0.0
    for offset, block in zip(offsets, blocks):
        rows = pl.ds(pl.multiple_of((me ^ offset) * width, width), width)
        total = total + jnp.dot(
            block[:, :width], weight_ref[rows, :], preferred_element_type=jnp.float32
        )
    return total


def project_first(message_ref, weight_ref, total_ref):
    total_ref[...] = project_blocks((0,), [message_ref], weight_ref)


def join_blocks(*refs):
    out_ref = refs[-1]
    for i in range(out_ref.shape[0]):
        out_ref[i] = refs[i][...]


def first_half(blocks_ref, own_ref, weight_ref, total_ref):
    blocks = [blocks_ref.at[i] for i in range(1, blocks_ref.shape[0])]
    total_ref[...] = own_ref[...] + project_blocks((2, 4, 6), blocks, weight_ref)


def second_half(
    own_ref, other_ref, total_ref, weight_ref, gain_ref, rope_ref, query_ref, *, model_width
):
    width = total_ref.shape[1]
    count = own_ref.shape[0]
    blocks = [other_ref.at[i] for i in range(count)]
    projected = total_ref[...] + project_blocks((1, 3, 5, 7), blocks, weight_ref)
    squares = sum(
        lane_sum(ref[i, :, width:].astype(jnp.float32), 0)
        for ref in (own_ref, other_ref)
        for i in range(count)
    )
    projected = projected * lax.rsqrt(squares / model_width + EPSILON)
    head_dim = gain_ref.shape[1]
    cosine = rope_ref[:, :head_dim]
    sine = rope_ref[:, head_dim:]
    for head in range(width // head_dim):
        place = slice(head * head_dim, (head + 1) * head_dim)
        query = projected[:, place]
        mean = jnp.mean(query * query, axis=1, keepdims=True)
        query = query * lax.rsqrt(mean + EPSILON) * gain_ref[...]
        turned = pltpu.roll(query, head_dim // 2, 1)
        query_ref[:, place] = (query * cosine + turned * sine).astype(jnp.bfloat16)


def attend_head(i, query, key_ref, value_ref, swapped_ref, range_ref):
    me = lax.axis_index("pack")
    tokens = key_ref.shape[0]
    head_dim = 128
    heads = swapped_ref.shape[1] // (2 * head_dim)
    grouped = jnp.concatenate(
        [query[:, h * head_dim : (h + 1) * head_dim] for h in range(query.shape[1] // head_dim)],
        axis=0,
    )
    group = query.shape[1] // head_dim
    column = pl.ds(pl.multiple_of((me ^ (2 * i)) * head_dim, head_dim), head_dim)
    keys = (key_ref[:, column], swapped_ref[:, i * head_dim : (i + 1) * head_dim])
    values = (
        value_ref[:, column],
        swapped_ref[:, (heads + i) * head_dim : (heads + i + 1) * head_dim],
    )
    scores = []
    masks = []
    for part, owner in enumerate((me, me ^ 1)):
        index = lax.broadcasted_iota(jnp.int32, (query.shape[0], tokens), 1) + owner * tokens
        index = index.astype(jnp.float32)
        mask = (index >= range_ref[:, :1]) & (index < range_ref[:, 128:129])
        mask = jnp.concatenate([mask.astype(jnp.float32)] * group, axis=0) > 0.5
        raw = lax.dot_general(
            grouped, keys[part], (((1,), (1,)), ((), ())), preferred_element_type=jnp.float32
        )
        scores.append(jnp.where(mask, raw * (head_dim**-0.5), MASKED_LOGIT))
        masks.append(mask)
    highest = jnp.maximum(
        jnp.max(scores[0], axis=1, keepdims=True), jnp.max(scores[1], axis=1, keepdims=True)
    )
    total = 0.0
    numerators = 0.0
    for part in range(2):
        weights = jnp.where(masks[part], jnp.exp(scores[part] - highest), 0.0)
        total = total + jnp.sum(weights, axis=1, keepdims=True)
        numerators = numerators + jnp.dot(
            weights.astype(jnp.bfloat16), values[part], preferred_element_type=jnp.float32
        )
    return highest, total, numerators


def attend_others(*refs):
    query_refs, refs = refs[:3], refs[3:]
    key_ref, value_ref, swapped_ref, range_ref = refs[:4]
    rows = query_refs[0].shape[0]
    for i, (query_ref, out_ref) in enumerate(zip(query_refs, refs[4:])):
        highest, total, numerators = attend_head(
            i + 1, query_ref[...], key_ref, value_ref, swapped_ref, range_ref
        )
        stats = []
        for h in range(query_ref.shape[1] // 128):
            part = slice(h * rows, (h + 1) * rows)
            out_ref[:, h * 128 : (h + 1) * 128] = numerators[part].astype(jnp.bfloat16)
            stats += [highest[part], total[part]]
        out_ref[:, query_ref.shape[1] :] = lane_pieces(stats)


def attend_own(query_ref, key_ref, value_ref, swapped_ref, range_ref, out_ref, stats_ref):
    highest, total, numerators = attend_head(
        0, query_ref[...], key_ref, value_ref, swapped_ref, range_ref
    )
    out_ref[...] = numerators
    stats_ref[:, :128] = jnp.broadcast_to(highest, (highest.shape[0], 128))
    stats_ref[:, 128:] = jnp.broadcast_to(total, (highest.shape[0], 128))


def join_and_project(
    own_ref, stats_ref, first_ref, second_ref, third_ref, weight_ref, attended_ref, out_ref
):
    me = lax.axis_index("pack")
    rows, width = attended_ref.shape
    others = (first_ref, second_ref, third_ref)
    for h in range(width // 128):
        part = slice(h * rows, (h + 1) * rows)
        place = slice(h * 128, (h + 1) * 128)
        maxima = [stats_ref[part, :1]]
        totals = [stats_ref[part, 128:129]]
        numerators = [own_ref[part, :]]
        for ref in others:
            stats = ref[:, width:].astype(jnp.float32)
            maxima.append(lane_sum(stats, 2 * h))
            totals.append(lane_sum(stats, 2 * h + 1))
            numerators.append(ref[:, place].astype(jnp.float32))
        highest = maxima[0]
        for value in maxima[1:]:
            highest = jnp.maximum(highest, value)
        denominator = 0.0
        summed = 0.0
        for value, total, numerator in zip(maxima, totals, numerators):
            factor = jnp.exp(value - highest)
            denominator = denominator + total * factor
            summed = summed + numerator * factor
        attended_ref[:, place] = (summed / denominator).astype(jnp.bfloat16)
    attended = attended_ref[...]
    for i in range(out_ref.shape[0]):
        column = pl.ds(pl.multiple_of((me ^ 1 ^ (2 * i)) * width, width), width)
        out_ref[i] = jnp.dot(
            attended, weight_ref[:, column], preferred_element_type=jnp.float32
        ).astype(jnp.bfloat16)


def project_own(attended_ref, weight_ref, out_ref):
    me = lax.axis_index("pack")
    width = attended_ref.shape[1]
    attended = attended_ref[...]
    for i in range(out_ref.shape[0]):
        column = pl.ds(pl.multiple_of((me ^ (2 * i)) * width, width), width)
        out_ref[i] = jnp.dot(attended, weight_ref[:, column], preferred_element_type=jnp.float32)


def add_cores(own_ref, other_ref, hidden_ref, kept_ref, *sent_refs):
    kept_ref[...] = (
        hidden_ref[...].astype(jnp.float32) + own_ref[0] + other_ref[0].astype(jnp.float32)
    )
    for i, ref in enumerate(sent_refs):
        ref[...] = (own_ref[i + 1] + other_ref[i + 1].astype(jnp.float32)).astype(jnp.bfloat16)


def finish_hidden(kept_ref, first_ref, second_ref, third_ref, gain_ref, sent_ref, scaled_ref, square_ref):
    hidden = kept_ref[...]
    for ref in (first_ref, second_ref, third_ref):
        hidden = hidden + ref[...].astype(jnp.float32)
    scaled = hidden * gain_ref[...]
    scaled_ref[...] = scaled
    sent_ref[...] = scaled.astype(jnp.bfloat16)
    square_ref[...] = jnp.broadcast_to(
        jnp.sum(hidden * hidden, axis=1, keepdims=True), square_ref.shape
    )


def gram_part(first_ref, second_ref, third_ref, fourth_ref, square_ref, vectors_ref, out_ref):
    rows = first_ref.shape[0]
    for i, ref in enumerate((first_ref, second_ref, third_ref, fourth_ref)):
        vectors_ref[i * rows : (i + 1) * rows, :] = ref[...]
    vectors = vectors_ref[...]
    gram = lax.dot_general(
        vectors, vectors, (((1,), (1,)), ((), ())), preferred_element_type=jnp.float32
    )
    half = gram.shape[0] // 2
    out_ref[:half, : 2 * half] = gram[:half]
    out_ref[:half, 2 * half :] = gram[half:]
    out_ref[half:, :] = square_ref[...]


def add_two(first_ref, second_ref, out_ref):
    out_ref[...] = first_ref[...] + second_ref[...]


def losses_and_gradient(
    a_ref,
    b_ref,
    c_ref,
    d_ref,
    vectors_ref,
    scaled_ref,
    gain_ref,
    partner_ref,
    pooled_ref,
    loss_ref,
    grad_ref,
    *,
    model_width,
):
    group = lax.axis_index("dp")
    me = lax.axis_index("pack")
    count = vectors_ref.shape[0]
    rows = scaled_ref.shape[0]
    half = count // 2
    summed = a_ref[...] + b_ref[...] + c_ref[...] + d_ref[...]
    gram = jnp.concatenate([summed[:half, :count], summed[:half, count:]], axis=0)
    squares = summed[half:, :1]
    shape = (count, count)
    row = lax.broadcasted_iota(jnp.int32, shape, 0)
    column = lax.broadcasted_iota(jnp.int32, shape, 1)
    row_id = ((group ^ (row // rows)) * rows) + row % rows
    column_id = ((group ^ (column // rows)) * rows) + column % rows
    partners = jnp.broadcast_to(partner_ref[...], shape)
    row_partner = jnp.sum(
        jnp.where(column == row_id, partners, 0).astype(jnp.float32), axis=1, keepdims=True
    )
    column_partner = jnp.sum(
        jnp.where(row_id == column_id, row_partner, 0.0), axis=0, keepdims=True
    )
    own_partner = column_id.astype(jnp.float32) == row_partner
    other_partner = row_id.astype(jnp.float32) == column_partner
    diagonal = row == column
    on_diagonal = jnp.where(diagonal, gram, 0.0)
    row_scale = lax.rsqrt(jnp.sum(on_diagonal, axis=1, keepdims=True))
    column_scale = lax.rsqrt(jnp.sum(on_diagonal, axis=0, keepdims=True))
    cosines = gram * row_scale * column_scale
    scaled_cosines = cosines * (1.0 / SOFTMAX_WARMTH)
    logits = jnp.where(diagonal, MASKED_LOGIT, scaled_cosines)
    row_high = jnp.max(logits, axis=1, keepdims=True)
    row_lse = row_high + jnp.log(jnp.sum(jnp.exp(logits - row_high), axis=1, keepdims=True))
    column_high = jnp.max(logits, axis=0, keepdims=True)
    column_lse = column_high + jnp.log(
        jnp.sum(jnp.exp(logits - column_high), axis=0, keepdims=True)
    )
    loss = row_lse - jnp.sum(jnp.where(own_partner, logits, 0.0), axis=1, keepdims=True)
    own = loss_ref.shape[0]
    index = lax.broadcasted_iota(jnp.int32, (count, 1), 0)
    for i in range(own):
        loss_ref[i] = jnp.sum(jnp.where(index == me * own + i, loss, 0.0))
    weights = (
        jnp.exp(logits - row_lse)
        + jnp.exp(logits - column_lse)
        - own_partner.astype(jnp.float32)
        - other_partner.astype(jnp.float32)
    )[:rows]
    inner = jnp.sum(weights * cosines[:rows], axis=1, keepdims=True)
    scaled_weights = weights * column_scale
    upper = scaled_weights.astype(jnp.bfloat16)
    lower = (scaled_weights - upper.astype(jnp.float32)).astype(jnp.bfloat16)
    vectors = vectors_ref[...]
    gradient = jnp.dot(upper, vectors, preferred_element_type=jnp.float32) + jnp.dot(
        lower, vectors, preferred_element_type=jnp.float32
    )
    own_scale = row_scale[:rows]
    scaled = scaled_ref[...]
    gradient = (gradient - scaled * (own_scale * inner)) * own_scale
    grad_ref[...] = (gradient * (gain_ref[...] * (model_width**0.5 / SOFTMAX_WARMTH))).astype(
        jnp.bfloat16
    )
    pooled_ref[...] = (scaled * lax.rsqrt(squares / model_width + EPSILON)).astype(jnp.bfloat16)


def chip_pairs(
    hidden_in,
    attn_gain,
    w_query,
    query_gain,
    cached_keys,
    cached_values,
    w_out,
    final_gain,
    lengths,
    pack_order,
    partner,
):
    pack_size = lax.axis_size("pack")
    stmts, width = hidden_in.shape
    model_width = width * pack_size
    head_dim = query_gain.shape[0]
    tokens = cached_keys.shape[0]
    chips = pack_size // 2
    total = partner.shape[0]
    bf16 = jnp.bfloat16
    f32 = jnp.float32
    attn_gain = attn_gain[None]
    final_gain = final_gain[None]
    query_gain = query_gain[None]
    half = np.arange(head_dim // 2)
    frequency = (ROPE_BASE ** (-half * 2.0 / head_dim)).astype(np.float32)
    frequency = jnp.asarray(np.concatenate([frequency, frequency])[None])

    whole = pl.BlockSpec(memory_space=pltpu.VMEM)
    anywhere = pl.BlockSpec(memory_space=pl.ANY)
    window = pl.pallas_call(
        open_window,
        out_shape=shaped((8, 128), f32),
        out_specs=whole,
        compiler_params=pltpu.CompilerParams(vmem_limit_bytes=1 << 20),
        cost_estimate=pl.CostEstimate(flops=1 << 34, bytes_accessed=0, transcendentals=0),
    )()
    message = in_vmem(
        prepare_inputs, shaped((stmts, width + 128), bf16), window, hidden_in, attn_gain
    )
    blocks = [message] + [flip(message, "pack", 2 * i) for i in range(1, chips)]
    own_projected = in_vmem(
        project_first, shaped((stmts, width), f32), message, w_query, limit=16, flops=1 << 26
    )
    rope, ranges = in_vmem(
        positions_and_ranges,
        (shaped((stmts, 2 * head_dim), f32), shaped((stmts, 256), f32)),
        message,
        frequency,
        lengths,
        pack_order,
    )
    blocks = in_vmem(
        join_blocks,
        shaped((chips,) + message.shape, bf16),
        *blocks,
        own_projected,
        rope,
    )
    others = flip(blocks, "pack", 1)
    projected = in_vmem(
        first_half,
        shaped((stmts, width), f32),
        blocks,
        own_projected,
        w_query,
        limit=16,
        flops=1 << 27,
    )
    swapped = pl.pallas_call(
        send_heads,
        out_shape=shaped((tokens, 2 * chips * head_dim), bf16),
        in_specs=[whole] + [anywhere] * 2,
        out_specs=whole,
        scratch_shapes=[pltpu.SemaphoreType.DMA((2 * chips,))],
        compiler_params=pltpu.CompilerParams(vmem_limit_bytes=4 << 20),
        cost_estimate=pl.CostEstimate(flops=0, bytes_accessed=2 << 20, transcendentals=0),
    )(projected, cached_keys, cached_values)
    swapped = flip(swapped, "pack", 1)
    queries = in_vmem(
        lambda *refs: second_half(*refs, model_width=model_width),
        shaped((stmts, width), bf16),
        blocks,
        others,
        projected,
        w_query,
        query_gain,
        rope,
        limit=16,
        flops=1 << 36,
    )
    received = [flip(queries, "pack", 2 * i) for i in range(1, chips)]
    sent = in_vmem(
        attend_others,
        (shaped((stmts, width + 128), bf16),) * (chips - 1),
        *received,
        cached_keys,
        cached_values,
        swapped,
        ranges,
        flops=1 << 27,
    )
    partials = [flip(part, "pack", 2 * (i + 1)) for i, part in enumerate(sent)]
    group_rows = stmts * (width // head_dim)
    own_part, own_stats = in_vmem(
        attend_own,
        (shaped((group_rows, head_dim), f32), shaped((group_rows, 256), f32)),
        queries,
        cached_keys,
        cached_values,
        swapped,
        ranges,
        flops=1 << 26,
    )
    attended, to_core = in_vmem(
        join_and_project,
        (shaped((stmts, width), bf16), shaped((chips, stmts, width), bf16)),
        own_part,
        own_stats,
        *partials,
        w_out,
        limit=16,
        flops=1 << 27,
    )
    from_core = flip(to_core, "pack", 1)
    own_out = in_vmem(
        project_own,
        shaped((chips, stmts, width), f32),
        attended,
        w_out,
        limit=16,
        flops=1 << 27,
    )
    kept, *to_chips = in_vmem(
        add_cores,
        (shaped((stmts, width), f32),) + (shaped((stmts, width), bf16),) * (chips - 1),
        own_out,
        from_core,
        hidden_in,
    )
    from_chips = [flip(part, "pack", 2 * (i + 1)) for i, part in enumerate(to_chips)]
    vector, scaled, squares = in_vmem(
        finish_hidden,
        (shaped((stmts, width), bf16), shaped((stmts, width), f32), shaped((stmts, 128), f32)),
        kept,
        *from_chips,
        final_gain,
    )
    vectors = [vector] + [flip(vector, "dp", i) for i in range(1, lax.axis_size("dp"))]
    vectors, gram = in_vmem(
        gram_part,
        (shaped((total, width), bf16), shaped((total // 2 + stmts, 128), f32)),
        *vectors,
        squares,
    )
    gram = in_vmem(add_two, shaped(gram.shape, f32), gram, flip(gram, "pack", 1))
    grams = [gram] + [flip(gram, "pack", 2 * i) for i in range(1, chips)]
    pooled, loss_rows, grad_hidden = pl.pallas_call(
        lambda *refs: losses_and_gradient(*refs, model_width=model_width),
        out_shape=(
            shaped((stmts, width), bf16),
            shaped((stmts // pack_size,), f32),
            shaped((stmts, width), bf16),
        ),
        in_specs=[whole] * 8,
        out_specs=(whole, pl.BlockSpec(memory_space=pltpu.SMEM), whole),
        compiler_params=pltpu.CompilerParams(vmem_limit_bytes=8 << 20),
    )(*grams, vectors, scaled, final_gain, partner[None])
    return (pooled, loss_rows, grad_hidden)


def local(
    hidden_in,
    attn_gain,
    w_query,
    query_gain,
    cached_keys,
    cached_values,
    w_out,
    final_gain,
    lengths,
    pack_order,
    partner,
):
    pack_size = lax.axis_size("pack")
    pack_index = lax.axis_index("pack")
    group_index = lax.axis_index("dp")
    stmt_count, feature_count = hidden_in.shape
    model_width = feature_count * pack_size
    head_dim = query_gain.shape[0]
    local_heads = w_query.shape[1] // head_dim
    token_count = cached_keys.shape[0]
    total_stmts = partner.shape[0]
    lengths_row = lengths[0]
    order_row = pack_order[0]
    inputs32 = hidden_in.astype(jnp.float32)

    scaled = (inputs32 * attn_gain[None, :]).astype(jnp.bfloat16)
    squares = split_float(jnp.sum(inputs32 * inputs32, axis=1), 3)
    extra = jnp.stack(squares + [jnp.zeros_like(squares[0])] * 125, axis=1)
    arrived = gather_blocks(jnp.concatenate([scaled, extra], axis=1), "pack")
    input_squares = jnp.sum(arrived[:, :, feature_count : feature_count + 3].astype(jnp.float32), axis=(0, 2))
    input_rms = lax.rsqrt(input_squares / model_width + EPSILON)
    features = jnp.moveaxis(arrived[:, :, :feature_count], 0, 1).reshape(stmt_count, model_width)
    projected = jnp.dot(features, w_query, preferred_element_type=jnp.float32)
    queries = (projected * input_rms[:, None]).reshape(stmt_count, local_heads, head_dim)
    queries = (
        queries
        * lax.rsqrt(jnp.mean(queries * queries, axis=2, keepdims=True) + EPSILON)
        * query_gain
    )
    queries = rotate_heads(queries, (lengths_row - 1).astype(jnp.float32)).astype(jnp.bfloat16)
    all_queries = jnp.moveaxis(gather_blocks(queries, "pack"), 0, 1).reshape(
        stmt_count, pack_size * local_heads, head_dim
    )
    start, end = statement_ranges(lengths_row, order_row)
    tokens = pack_index * token_count + jnp.arange(token_count, dtype=jnp.int32)
    token_mask = (tokens[None, :] >= start[:, None]) & (tokens[None, :] < end[:, None])
    block_max, block_sum, numerators = block_attention(
        all_queries, cached_keys, cached_values, token_mask, head_dim ** (-0.5)
    )

    def by_owner(part):
        return jnp.moveaxis(part.reshape((stmt_count, pack_size, -1)), 1, 0)

    message = jnp.concatenate(
        [by_owner(numerators.astype(jnp.bfloat16))]
        + [by_owner(piece) for piece in split_float(block_max, 3) + split_float(block_sum, 2)],
        axis=2,
    )
    message = lax.all_to_all(message, "pack", 0, 0)
    width = local_heads * head_dim
    stats = message[:, :, width:].astype(jnp.float32).reshape(pack_size, stmt_count, 5, local_heads)
    maxima = stats[:, :, 0] + stats[:, :, 1] + stats[:, :, 2]
    factor = jnp.exp(maxima - jnp.max(maxima, axis=0, keepdims=True))
    denominator = jnp.sum((stats[:, :, 3] + stats[:, :, 4]) * factor, axis=0)
    numerators = message[:, :, :width].astype(jnp.float32).reshape(pack_size, stmt_count, local_heads, head_dim)
    summed = jnp.sum(numerators * factor[..., None], axis=0)
    attended = (summed / denominator[..., None]).astype(jnp.bfloat16)
    partial_out = jnp.dot(
        attended.reshape(stmt_count, width), w_out, preferred_element_type=jnp.float32
    )
    partial_out = jnp.moveaxis(
        partial_out.astype(jnp.bfloat16).reshape(stmt_count, pack_size, feature_count), 1, 0
    )
    partial_out = lax.all_to_all(partial_out, "pack", 0, 0)
    hidden = inputs32 + jnp.sum(partial_out.astype(jnp.float32), axis=0)
    scaled_out = hidden * final_gain[None, :]
    vectors = lax.all_gather(scaled_out.astype(jnp.bfloat16), "dp", axis=0, tiled=True)
    gram = lax.dot_general(
        vectors, vectors, (((1,), (1,)), ((), ())), preferred_element_type=jnp.float32
    )
    own_squares = jnp.sum(hidden * hidden, axis=1)
    extra = jnp.zeros((total_stmts,), jnp.float32).at[:stmt_count].set(own_squares)
    gram = jnp.concatenate([gram, extra[:, None]], axis=1)
    if total_stmts <= 128:
        gram = jnp.sum(gather_blocks(gram, "pack"), axis=0)
    else:
        gram = lax.psum(gram, "pack")
    hidden_rms = jnp.sqrt(gram[:stmt_count, total_stmts] / model_width + EPSILON)
    gram = gram[:, :total_stmts]
    column_ids = jnp.arange(total_stmts, dtype=jnp.int32)
    diagonal = column_ids[:, None] == column_ids[None, :]
    norms_row = lax.rsqrt(jnp.sum(jnp.where(diagonal, gram, 0.0), axis=0))
    norms_column = lax.rsqrt(jnp.sum(jnp.where(diagonal, gram, 0.0), axis=1))
    cosines = gram * norms_column[:, None] * norms_row[None, :]
    logits = jnp.where(diagonal, MASKED_LOGIT, cosines / SOFTMAX_WARMTH)
    highest = jnp.max(logits, axis=1)
    all_lse = highest + jnp.log(jnp.sum(jnp.exp(logits - highest[:, None]), axis=1))
    is_partner = column_ids[None, :] == partner[:, None]
    all_loss = all_lse - jnp.sum(jnp.where(is_partner, logits, 0.0), axis=1)
    own_count = stmt_count // pack_size
    row_base = group_index * stmt_count
    loss_rows = lax.dynamic_slice_in_dim(all_loss, row_base + pack_index * own_count, own_count, 0)
    weights = (
        jnp.exp(logits - all_lse[:, None])
        + jnp.exp(logits - all_lse[None, :])
        - is_partner.astype(jnp.float32)
        - is_partner.T.astype(jnp.float32)
    ).astype(jnp.bfloat16)
    own_weights = lax.dynamic_slice_in_dim(weights, row_base, stmt_count, 0)
    own_cosines = lax.dynamic_slice_in_dim(cosines, row_base, stmt_count, 0)
    own_norm = lax.dynamic_slice_in_dim(norms_column, row_base, stmt_count, 0)
    inner = jnp.sum(own_weights.astype(jnp.float32) * own_cosines, axis=1)
    own_norm = own_norm[:, None]
    embeddings = (vectors.astype(jnp.float32) * norms_column[:, None]).astype(jnp.bfloat16)
    gradient = jnp.dot(own_weights, embeddings, preferred_element_type=jnp.float32)
    scale = model_width**0.5 / SOFTMAX_WARMTH
    pooled = (scaled_out / hidden_rms[:, None]).astype(jnp.bfloat16)
    grad_hidden = (
        scale * final_gain[None, :] * (gradient - scaled_out * own_norm * inner[:, None]) * own_norm
    ).astype(jnp.bfloat16)
    return (pooled, loss_rows, grad_hidden)


def solution(mesh):
    body = chip_pairs if mesh.shape["pack"] == 8 and mesh.shape["dp"] == 4 else local
    in_specs = (
        P("dp", "pack"),
        P("pack"),
        P(None, "pack"),
        P(),
        P(("dp", "pack"), None),
        P(("dp", "pack"), None),
        P("pack", None),
        P("pack"),
        P("dp", None),
        P("dp", None),
        P(),
    )
    out_specs = (P("dp", "pack"), P(("dp", "pack")), P("dp", "pack"))
    return jax.shard_map(body, mesh=mesh, in_specs=in_specs, out_specs=out_specs, check_vma=False)
```

```python
import numpy as np
import jax
import jax.numpy as jnp
from jax import lax
from jax.experimental import pallas as pl
from jax.experimental.pallas import tpu as pltpu
from jax.sharding import PartitionSpec as P

EPSILON = 1e-06
SOFTMAX_WARMTH = 0.05
ROPE_BASE = 1000000.0
MASKED_LOGIT = -1e30


def gather_blocks(block, axis):
    size = lax.axis_size(axis)
    return lax.all_to_all(jnp.broadcast_to(block[None], (size,) + block.shape), axis, 0, 0)


def split_float(value, pieces):
    out = []
    for _ in range(pieces):
        piece = lax.reduce_precision(value, 8, 7)
        out.append(piece.astype(jnp.bfloat16))
        value = value - piece
    return out


def cosine_and_sine(angles):
    turns = jnp.round(angles * np.float32(2.0 / np.pi))
    rest = angles - turns * np.float32(1.5703125)
    rest = rest - turns * np.float32(4.837512969970703125e-4)
    rest = rest - turns * np.float32(7.549789948768648e-8)
    square = rest * rest
    sine = rest + rest * square * (
        np.float32(-1.6666654611e-1)
        + square * (np.float32(8.3321608736e-3) + square * np.float32(-1.9515295891e-4))
    )
    cosine = (
        1.0
        - 0.5 * square
        + square
        * square
        * (
            np.float32(4.166664568298827e-2)
            + square
            * (np.float32(-1.388731625493765e-3) + square * np.float32(2.443315711809948e-5))
        )
    )
    quarter = turns.astype(jnp.int32) & 3
    swap = (quarter & 1) == 1
    cos_out = jnp.where(swap, sine, cosine)
    sin_out = jnp.where(swap, cosine, sine)
    cos_out = jnp.where((quarter == 1) | (quarter == 2), -cos_out, cos_out)
    sin_out = jnp.where(quarter >= 2, -sin_out, sin_out)
    return cos_out, sin_out


def rotate_heads(queries, position):
    head_dim = queries.shape[-1]
    half_dim = head_dim // 2
    frequency = (ROPE_BASE ** (-np.arange(half_dim) * 2.0 / head_dim)).astype(np.float32)
    cosine, sine = cosine_and_sine(position[:, None] * frequency[None, :])
    cosine = jnp.concatenate([cosine, cosine], axis=1)[:, None, :]
    sine = jnp.concatenate([-sine, sine], axis=1)[:, None, :]
    turned = jnp.concatenate([queries[..., half_dim:], queries[..., :half_dim]], axis=-1)
    return queries * cosine + turned * sine


def statement_ranges(lengths_row, order_row):
    stmt_count = order_row.shape[0]
    index = jnp.arange(stmt_count, dtype=jnp.int32)
    slot = jnp.sum(jnp.where(order_row[None, :] == index[:, None], index[None, :], 0), axis=1)
    start = jnp.sum(jnp.where(slot[None, :] < slot[:, None], lengths_row[None, :], 0), axis=1)
    return start, start + lengths_row


def block_attention(all_queries, cached_keys, cached_values, token_mask, score_scale):
    stmt_count, head_count, head_dim = all_queries.shape
    kv_heads = cached_keys.shape[1] // head_dim
    group_size = head_count // kv_heads
    grouped = all_queries.reshape(stmt_count, kv_heads, group_size, head_dim)
    key_heads = cached_keys.reshape(-1, kv_heads, head_dim)
    value_heads = cached_values.reshape(-1, kv_heads, head_dim)
    scores = (
        jnp.einsum("skgd,tkd->skgt", grouped, key_heads, preferred_element_type=jnp.float32)
        * score_scale
    )
    token_mask = token_mask[:, None, None, :]
    block_max = jnp.max(jnp.where(token_mask, scores, MASKED_LOGIT), axis=3)
    softmax_weights = jnp.where(token_mask, jnp.exp(scores - block_max[..., None]), 0.0)
    block_sum = jnp.sum(softmax_weights, axis=3)
    numerators = jnp.einsum(
        "skgt,tkd->skgd",
        softmax_weights.astype(jnp.bfloat16),
        value_heads,
        preferred_element_type=jnp.float32,
    )
    return (
        block_max.reshape(stmt_count, head_count),
        block_sum.reshape(stmt_count, head_count),
        numerators.reshape(stmt_count, head_count, head_dim),
    )


def flip(array, axis, offset):
    size = lax.axis_size(axis)
    return lax.ppermute(array, axis, [(i, i ^ offset) for i in range(size)])


def in_vmem(body, outputs, *operands, limit=8, flops=1_000_000):
    whole = pl.BlockSpec(memory_space=pltpu.VMEM)
    moved = sum(operand.size * operand.dtype.itemsize for operand in operands)
    return pl.pallas_call(
        body,
        out_shape=outputs,
        in_specs=[whole] * len(operands),
        out_specs=jax.tree.map(lambda _: whole, outputs),
        compiler_params=pltpu.CompilerParams(vmem_limit_bytes=limit << 20),
        cost_estimate=pl.CostEstimate(flops=flops, bytes_accessed=moved, transcendentals=0),
    )(*operands)


def shaped(shape, kind):
    return jax.ShapeDtypeStruct(shape, kind)


def lane_pieces(values, width=128):
    rows = values[0].shape[0]
    lane = lax.broadcasted_iota(jnp.int32, (rows, width), 1)
    out = jnp.zeros((rows, width), jnp.float32)
    for place, value in enumerate(values):
        rest = value
        for part in range(3):
            piece = rest.astype(jnp.bfloat16).astype(jnp.float32)
            out = jnp.where(lane == 3 * place + part, piece, out)
            rest = rest - piece
    return out.astype(jnp.bfloat16)


def lane_sum(block, place):
    lane = lax.broadcasted_iota(jnp.int32, block.shape, 1)
    own = (lane >= 3 * place) & (lane < 3 * place + 3)
    return jnp.sum(jnp.where(own, block, 0.0), axis=1, keepdims=True)


def open_window(out_ref):
    out_ref[...] = jnp.zeros_like(out_ref)


def prepare_inputs(window_ref, hidden_ref, gain_ref, message_ref):
    del window_ref
    inputs = hidden_ref[...].astype(jnp.float32)
    width = inputs.shape[1]
    message_ref[:, :width] = (inputs * gain_ref[...]).astype(jnp.bfloat16)
    message_ref[:, width:] = lane_pieces([jnp.sum(inputs * inputs, axis=1, keepdims=True)])


def positions_and_ranges(
    message_ref, frequency_ref, lengths_ref, order_ref, rope_ref, range_ref
):
    del message_ref
    count = lengths_ref.shape[1]
    half = frequency_ref.shape[1] // 2
    row = lax.broadcasted_iota(jnp.int32, (count, count), 0)
    column = lax.broadcasted_iota(jnp.int32, (count, count), 1)
    lengths = jnp.broadcast_to(lengths_ref[...], (count, count)).astype(jnp.float32)
    length = jnp.sum(jnp.where(row == column, lengths, 0.0), axis=1, keepdims=True)
    order = jnp.broadcast_to(order_ref[...], (count, count))
    placed = order == row
    slot = jnp.sum(jnp.where(placed, column, 0).astype(jnp.float32), axis=1, keepdims=True)
    packed = jnp.sum(jnp.where(placed, length, 0.0), axis=0, keepdims=True)
    earlier = column.astype(jnp.float32) < slot
    start = jnp.sum(jnp.where(earlier, packed, 0.0), axis=1, keepdims=True)
    range_ref[:, :128] = jnp.broadcast_to(start, (count, 128))
    range_ref[:, 128:] = jnp.broadcast_to(start + length, (count, 128))
    cosine, sine = cosine_and_sine((length - 1.0) * frequency_ref[...])
    lane = lax.broadcasted_iota(jnp.int32, cosine.shape, 1)
    rope_ref[:, : 2 * half] = cosine
    rope_ref[:, 2 * half :] = jnp.where(lane < half, -sine, sine)


def core_number():
    return lax.axis_index("pack") & 1


def chip_number():
    return lax.axis_index("pack") >> 1


def send_across(array, axis, offset, sender):
    groups, pack = lax.axis_size("dp"), lax.axis_size("pack")
    pairs = []
    for group in range(groups):
        for place in range(pack):
            if place % 2 != sender:
                target = (group, place ^ 1)
            elif axis == "dp":
                target = (group ^ offset, place ^ 1)
            else:
                target = (group, place ^ (2 * offset) ^ 1)
            pairs.append((group * pack + place, target[0] * pack + target[1]))
    return lax.ppermute(array, ("dp", "pack"), pairs)


def copy_tokens(_, key_ref, value_ref, out_ref):
    out_ref[0] = key_ref[...]
    out_ref[1] = value_ref[...]


def join_cores(own_ref, other_ref, pair_ref):
    core = core_number()
    pair_ref[core] = own_ref[...]
    pair_ref[1 - core] = other_ref[...]


def join_blocks(*refs):
    out_ref = refs[-1]
    for i in range(out_ref.shape[0]):
        out_ref[i] = refs[i][...]


def project_pair(pair_ref, offset, weight_ref):
    chip = chip_number() ^ offset
    width = weight_ref.shape[1]
    total = 0.0
    for core in range(2):
        rows = pl.ds(pl.multiple_of((2 * chip + core) * width, width), width)
        total = total + jnp.dot(
            pair_ref[core, :, :width], weight_ref[rows, :], preferred_element_type=jnp.float32
        )
    return total


def project_own_pair(pair_ref, weight_ref, total_ref):
    total_ref[...] = project_pair(pair_ref, 0, weight_ref)


def make_queries(
    pair_ref, blocks_ref, total_ref, weight_ref, gain_ref, rope_ref, query_ref, *, core, model_width
):
    width = total_ref.shape[1]
    head_dim = gain_ref.shape[1]

    @pl.when(core_number() == core)
    def _():
        projected = total_ref[...]
        squares = jnp.zeros((total_ref.shape[0], 1), jnp.float32)
        for j in range(2):
            squares = squares + lane_sum(pair_ref[j, :, width:].astype(jnp.float32), 0)
        for i in range(blocks_ref.shape[0]):
            projected = projected + project_pair(blocks_ref.at[i], i + 1, weight_ref)
            for j in range(2):
                squares = squares + lane_sum(blocks_ref[i, j, :, width:].astype(jnp.float32), 0)
        projected = projected * lax.rsqrt(squares / model_width + EPSILON)
        cosine = rope_ref[:, :head_dim]
        sine = rope_ref[:, head_dim:]
        for head in range(width // head_dim):
            place = slice(head * head_dim, (head + 1) * head_dim)
            query = projected[:, place]
            mean = jnp.mean(query * query, axis=1, keepdims=True)
            query = query * lax.rsqrt(mean + EPSILON) * gain_ref[...]
            turned = pltpu.roll(query, head_dim // 2, 1)
            query_ref[:, place] = (query * cosine + turned * sine).astype(jnp.bfloat16)


def join_queries(first_ref, second_ref, out_ref):
    width = first_ref.shape[1]
    out_ref[:, :width] = first_ref[...]
    out_ref[:, width:] = second_ref[...]


def token_masks(range_ref, tokens, group):
    me = lax.axis_index("pack")
    masks = []
    for owner in (me, me ^ 1):
        index = lax.broadcasted_iota(jnp.int32, (range_ref.shape[0], tokens), 1) + owner * tokens
        index = index.astype(jnp.float32)
        mask = (index >= range_ref[:, :1]) & (index < range_ref[:, 128:129])
        masks.append(jnp.concatenate([mask.astype(jnp.float32)] * group, axis=0) > 0.5)
    return masks


def attend_head(query, head, key_ref, value_ref, other_ref, masks):
    head_dim = 128
    group = query.shape[1] // head_dim
    grouped = jnp.concatenate(
        [query[:, h * head_dim : (h + 1) * head_dim] for h in range(group)], axis=0
    )
    column = pl.ds(pl.multiple_of(head * head_dim, head_dim), head_dim)
    keys = (key_ref[:, column], other_ref[0, :, column])
    values = (value_ref[:, column], other_ref[1, :, column])
    scores = []
    for part in range(2):
        raw = lax.dot_general(
            grouped, keys[part], (((1,), (1,)), ((), ())), preferred_element_type=jnp.float32
        )
        scores.append(jnp.where(masks[part], raw * (head_dim**-0.5), MASKED_LOGIT))
    highest = jnp.maximum(
        jnp.max(scores[0], axis=1, keepdims=True), jnp.max(scores[1], axis=1, keepdims=True)
    )
    total = 0.0
    numerators = 0.0
    for part in range(2):
        weights = jnp.exp(scores[part] - highest)
        total = total + jnp.sum(weights, axis=1, keepdims=True)
        numerators = numerators + jnp.dot(
            weights.astype(jnp.bfloat16), values[part], preferred_element_type=jnp.float32
        )
    return highest, total, numerators


def attend_remote(*refs):
    query_refs, refs = refs[:3], refs[3:]
    key_ref, value_ref, other_ref, range_ref = refs[:4]

    @pl.when(core_number() == 1)
    def _():
        rows = query_refs[0].shape[0]
        width = query_refs[0].shape[1] // 2
        masks = token_masks(range_ref, key_ref.shape[0], width // 128)
        for i, (query_ref, out_ref) in enumerate(zip(query_refs, refs[4:])):
            stats = []
            for j in range(2):
                head = 2 * (chip_number() ^ (i + 1)) + j
                query = query_ref[:, j * width : (j + 1) * width]
                highest, total, numerators = attend_head(
                    query, head, key_ref, value_ref, other_ref, masks
                )
                for h in range(width // 128):
                    part = slice(h * rows, (h + 1) * rows)
                    place = slice(j * width + h * 128, j * width + (h + 1) * 128)
                    out_ref[:, place] = numerators[part].astype(jnp.bfloat16)
                    stats += [highest[part], total[part]]
            out_ref[:, 2 * width :] = lane_pieces(stats)


def attend_own(query_ref, key_ref, value_ref, other_ref, range_ref, out_ref, stats_ref):
    @pl.when(core_number() == 0)
    def _():
        width = query_ref.shape[1] // 2
        masks = token_masks(range_ref, key_ref.shape[0], width // 128)
        for j in range(2):
            query = query_ref[:, j * width : (j + 1) * width]
            highest, total, numerators = attend_head(
                query, 2 * chip_number() + j, key_ref, value_ref, other_ref, masks
            )
            out_ref[j] = numerators
            stats_ref[j, :, :128] = jnp.broadcast_to(highest, (highest.shape[0], 128))
            stats_ref[j, :, 128:] = jnp.broadcast_to(total, (highest.shape[0], 128))


def merge_partials(
    own_ref, stats_ref, first_ref, second_ref, third_ref, attended_ref, other_attended_ref
):
    @pl.when(core_number() == 0)
    def _():
        rows, width = attended_ref.shape
        others = (first_ref, second_ref, third_ref)
        stats = [ref[:, 2 * width :].astype(jnp.float32) for ref in others]
        for j, out_ref in enumerate((attended_ref, other_attended_ref)):
            for h in range(width // 128):
                part = slice(h * rows, (h + 1) * rows)
                place = slice(h * 128, (h + 1) * 128)
                far_place = slice(j * width + h * 128, j * width + (h + 1) * 128)
                slot = 2 * (j * (width // 128) + h)
                maxima = [stats_ref[j, part, :1]] + [lane_sum(s, slot) for s in stats]
                totals = [stats_ref[j, part, 128:129]] + [lane_sum(s, slot + 1) for s in stats]
                numerators = [own_ref[j, part, :]]
                numerators += [ref[:, far_place].astype(jnp.float32) for ref in others]
                highest = maxima[0]
                for value in maxima[1:]:
                    highest = jnp.maximum(highest, value)
                denominator = 0.0
                summed = 0.0
                for value, total, numerator in zip(maxima, totals, numerators):
                    factor = jnp.exp(value - highest)
                    denominator = denominator + total * factor
                    summed = summed + numerator * factor
                out_ref[:, place] = (summed / denominator).astype(jnp.bfloat16)


def project_out(attended_ref, weight_ref, *refs, core, offsets):
    out_ref = refs[-1]

    @pl.when(core_number() == core)
    def _():
        width = out_ref.shape[2]
        attended = attended_ref[...]
        for i, offset in enumerate(offsets):
            column = pl.ds(pl.multiple_of((chip_number() ^ offset) * width, width), width)
            out_ref[i] = jnp.dot(
                attended, weight_ref[:, column], preferred_element_type=jnp.float32
            ).astype(out_ref.dtype)


def add_partials(own_ref, other_ref, *out_refs, first):
    for i, out_ref in enumerate(out_refs):
        total = own_ref[first + i] + other_ref[i].astype(jnp.float32)
        out_ref[...] = total.astype(out_ref.dtype)


def finish_hidden(
    kept_ref,
    first_ref,
    second_ref,
    third_ref,
    own_ref,
    other_ref,
    own_gain_ref,
    other_gain_ref,
    sent_ref,
    state_ref,
):
    width = own_ref.shape[1]

    @pl.when(core_number() == 1)
    def _():
        squares = 0.0
        inputs = (other_ref, own_ref)
        gains = (other_gain_ref, own_gain_ref)
        for core in range(2):
            place = slice(core * width, (core + 1) * width)
            hidden = inputs[core][...].astype(jnp.float32) + kept_ref[:, place]
            for ref in (first_ref, second_ref, third_ref):
                hidden = hidden + ref[:, place].astype(jnp.float32)
            scaled = hidden * gains[core][...]
            state_ref[:, place] = scaled
            sent_ref[:, place] = scaled.astype(jnp.bfloat16)
            squares = squares + jnp.sum(hidden * hidden, axis=1, keepdims=True)
        state_ref[:, 2 * width :] = jnp.broadcast_to(squares, (squares.shape[0], 128))


def gram_part(state_ref, first_ref, second_ref, third_ref, out_ref, near_ref, far_ref):
    @pl.when(core_number() == 0)
    def _():
        rows = first_ref.shape[0]
        width = near_ref.shape[1]
        near_ref[:rows] = state_ref[:, :width].astype(jnp.bfloat16)
        far_ref[:rows] = state_ref[:, width : 2 * width].astype(jnp.bfloat16)
        for i, ref in enumerate((first_ref, second_ref, third_ref)):
            near_ref[(i + 1) * rows : (i + 2) * rows] = ref[:, :width]
            far_ref[(i + 1) * rows : (i + 2) * rows] = ref[:, width:]
        gram = 0.0
        for ref in (near_ref, far_ref):
            vectors = ref[...]
            gram = gram + lax.dot_general(
                vectors, vectors, (((1,), (1,)), ((), ())), preferred_element_type=jnp.float32
            )
        half = gram.shape[0] // 2
        out_ref[:half, : 2 * half] = gram[:half]
        out_ref[:half, 2 * half :] = gram[half:]
        out_ref[half:, :] = state_ref[:, 2 * width :]


def sum_grams(own_ref, first_ref, second_ref, third_ref, out_ref):
    out_ref[...] = own_ref[...] + first_ref[...] + second_ref[...] + third_ref[...]


def losses_and_gradient(
    summed_ref,
    other_summed_ref,
    near_ref,
    other_far_ref,
    state_ref,
    other_state_ref,
    gain_ref,
    partner_ref,
    pooled_ref,
    loss_ref,
    grad_ref,
    *,
    model_width,
):
    group = lax.axis_index("dp")
    me = lax.axis_index("pack")
    first_core = core_number() == 0
    count, width = near_ref.shape
    rows = state_ref.shape[0]
    half = count // 2
    summed = jnp.where(first_core, other_summed_ref[...], summed_ref[...])
    gram = jnp.concatenate([summed[:half, :count], summed[:half, count:]], axis=0)
    squares = summed[half:, :1]
    shape = (count, count)
    row = lax.broadcasted_iota(jnp.int32, shape, 0)
    column = lax.broadcasted_iota(jnp.int32, shape, 1)
    row_id = ((group ^ (row // rows)) * rows) + row % rows
    column_id = ((group ^ (column // rows)) * rows) + column % rows
    partners = jnp.broadcast_to(partner_ref[...], shape)
    row_partner = jnp.sum(
        jnp.where(column == row_id, partners, 0).astype(jnp.float32), axis=1, keepdims=True
    )
    column_partner = jnp.sum(
        jnp.where(row_id == column_id, row_partner, 0.0), axis=0, keepdims=True
    )
    own_partner = column_id.astype(jnp.float32) == row_partner
    other_partner = row_id.astype(jnp.float32) == column_partner
    diagonal = row == column
    on_diagonal = jnp.where(diagonal, gram, 0.0)
    row_scale = lax.rsqrt(jnp.sum(on_diagonal, axis=1, keepdims=True))
    column_scale = lax.rsqrt(jnp.sum(on_diagonal, axis=0, keepdims=True))
    cosines = gram * row_scale * column_scale
    logits = jnp.where(diagonal, MASKED_LOGIT, cosines * (1.0 / SOFTMAX_WARMTH))
    row_high = jnp.max(logits, axis=1, keepdims=True)
    row_lse = row_high + jnp.log(jnp.sum(jnp.exp(logits - row_high), axis=1, keepdims=True))
    column_high = jnp.max(logits, axis=0, keepdims=True)
    column_lse = column_high + jnp.log(
        jnp.sum(jnp.exp(logits - column_high), axis=0, keepdims=True)
    )
    loss = row_lse - jnp.sum(jnp.where(own_partner, logits, 0.0), axis=1, keepdims=True)
    own = loss_ref.shape[0]
    index = lax.broadcasted_iota(jnp.int32, (count, 1), 0)
    for i in range(own):
        loss_ref[i] = jnp.sum(jnp.where(index == me * own + i, loss, 0.0))
    weights = (
        jnp.exp(logits - row_lse)
        + jnp.exp(logits - column_lse)
        - own_partner.astype(jnp.float32)
        - other_partner.astype(jnp.float32)
    )[:rows]
    inner = jnp.sum(weights * cosines[:rows], axis=1, keepdims=True)
    scaled_weights = weights * column_scale
    upper = scaled_weights.astype(jnp.bfloat16)
    lower = (scaled_weights - upper.astype(jnp.float32)).astype(jnp.bfloat16)
    own_scale = row_scale[:rows]
    pooled_scale = lax.rsqrt(squares / model_width + EPSILON)
    grad_gain = gain_ref[...] * (model_width**0.5 / SOFTMAX_WARMTH)

    def write(vectors, scaled):
        gradient = jnp.dot(upper, vectors, preferred_element_type=jnp.float32) + jnp.dot(
            lower, vectors, preferred_element_type=jnp.float32
        )
        gradient = (gradient - scaled * (own_scale * inner)) * own_scale
        grad_ref[...] = (gradient * grad_gain).astype(jnp.bfloat16)
        pooled_ref[...] = (scaled * pooled_scale).astype(jnp.bfloat16)

    @pl.when(first_core)
    def _():
        write(near_ref[...], other_state_ref[:, :width])

    @pl.when(core_number() == 1)
    def _():
        write(other_far_ref[...], state_ref[:, width : 2 * width])


def core_roles(
    hidden_in,
    attn_gain,
    w_query,
    query_gain,
    cached_keys,
    cached_values,
    w_out,
    final_gain,
    lengths,
    pack_order,
    partner,
):
    pack_size = lax.axis_size("pack")
    stmts, width = hidden_in.shape
    model_width = width * pack_size
    head_dim = query_gain.shape[0]
    tokens = cached_keys.shape[0]
    chips = pack_size // 2
    others = range(1, chips)
    total = partner.shape[0]
    bf16 = jnp.bfloat16
    f32 = jnp.float32
    final_gain = final_gain[None]
    query_gain = query_gain[None]
    half = np.arange(head_dim // 2)
    frequency = (ROPE_BASE ** (-half * 2.0 / head_dim)).astype(np.float32)
    frequency = jnp.asarray(np.concatenate([frequency, frequency])[None])
    whole = pl.BlockSpec(memory_space=pltpu.VMEM)

    window = pl.pallas_call(
        open_window,
        out_shape=shaped((8, 128), f32),
        out_specs=whole,
        compiler_params=pltpu.CompilerParams(vmem_limit_bytes=1 << 20),
        cost_estimate=pl.CostEstimate(flops=1 << 34, bytes_accessed=0, transcendentals=0),
    )()
    message = in_vmem(
        prepare_inputs, shaped((stmts, width + 128), bf16), window, hidden_in, attn_gain[None]
    )
    pair = in_vmem(
        join_cores, shaped((2,) + message.shape, bf16), message, flip(message, "pack", 1)
    )
    received = [send_across(pair, "pack", k, 0) for k in others]
    own_projected = in_vmem(
        project_own_pair, shaped((stmts, width), f32), pair, w_query, limit=16, flops=1 << 26
    )
    rope, ranges = in_vmem(
        positions_and_ranges,
        (shaped((stmts, 2 * head_dim), f32), shaped((stmts, 256), f32)),
        message,
        frequency,
        lengths,
        pack_order,
    )
    blocks = in_vmem(
        join_blocks, shaped((chips - 1,) + pair.shape, bf16), *received, own_projected, rope
    )
    flipped_blocks = flip(blocks, "pack", 1)

    def queries_on(core, blocks, flops):
        return in_vmem(
            lambda *refs: make_queries(*refs, core=core, model_width=model_width),
            shaped((stmts, width), bf16),
            pair,
            blocks,
            own_projected,
            w_query,
            query_gain,
            rope,
            limit=16,
            flops=flops,
        )

    late_queries = queries_on(1, blocks, 1 << 27)
    held = in_vmem(
        copy_tokens,
        shaped((2,) + cached_keys.shape, bf16),
        late_queries,
        cached_keys,
        cached_values,
    )
    other_held = flip(held, "pack", 1)
    second_queries = flip(late_queries, "pack", 1)
    first_queries = queries_on(0, flipped_blocks, 1 << 36)
    queries = in_vmem(
        join_queries, shaped((stmts, 2 * width), bf16), first_queries, second_queries
    )
    received = [send_across(queries, "pack", k, 0) for k in others]
    group_rows = stmts * (width // head_dim)
    own_part, own_stats = in_vmem(
        attend_own,
        (shaped((2, group_rows, head_dim), f32), shaped((2, group_rows, 256), f32)),
        queries,
        cached_keys,
        cached_values,
        other_held,
        ranges,
        flops=1 << 27,
    )
    partials = in_vmem(
        attend_remote,
        (shaped((stmts, 2 * width + 128), bf16),) * (chips - 1),
        *received,
        cached_keys,
        cached_values,
        other_held,
        ranges,
        flops=1 << 28,
    )
    received = [send_across(part, "pack", k, 1) for k, part in zip(others, partials)]
    attended, other_attended = in_vmem(
        merge_partials,
        (shaped((stmts, width), bf16),) * 2,
        own_part,
        own_stats,
        *received,
    )
    other_attended = flip(other_attended, "pack", 1)

    def projected_on(core, attended, offsets, kind, *after):
        return in_vmem(
            lambda *refs: project_out(*refs, core=core, offsets=offsets),
            shaped((len(offsets), stmts, 2 * width), kind),
            attended,
            w_out,
            *after,
            limit=16,
            flops=1 << 27,
        )

    own_out = projected_on(0, attended, (1, 2, 3, 0), f32)
    early = projected_on(1, other_attended, (1, 2), bf16, own_out)
    late = projected_on(1, other_attended, (3, 0), bf16, early)
    early = flip(early, "pack", 1)
    late = flip(late, "pack", 1)
    chip_part = shaped((stmts, 2 * width), bf16)
    to_chips = in_vmem(
        lambda *refs: add_partials(*refs, first=0), (chip_part, chip_part), own_out, early
    )
    last, kept = in_vmem(
        lambda *refs: add_partials(*refs, first=2),
        (chip_part, shaped((stmts, 2 * width), f32)),
        own_out,
        late,
    )
    other_kept = flip(kept, "pack", 1)
    received = [send_across(part, "pack", k, 0) for k, part in zip(others, (*to_chips, last))]
    vector, state = in_vmem(
        finish_hidden,
        (shaped((stmts, 2 * width), bf16), shaped((stmts, 2 * width + 128), f32)),
        other_kept,
        *received,
        hidden_in,
        flip(hidden_in, "pack", 1),
        final_gain,
        flip(final_gain, "pack", 1),
    )
    other_state = flip(state, "pack", 1)
    received = [send_across(vector, "dp", k, 1) for k in range(1, lax.axis_size("dp"))]
    gram, near, far = in_vmem(
        gram_part,
        (shaped((total // 2 + stmts, 128), f32),) + (shaped((total, width), bf16),) * 2,
        other_state,
        *received,
    )
    other_far = flip(far, "pack", 1)
    other_gram = flip(gram, "pack", 1)
    received = [send_across(gram, "pack", k, 0) for k in others]
    summed = in_vmem(sum_grams, shaped(gram.shape, f32), other_gram, *received)
    pooled, loss_rows, grad_hidden = pl.pallas_call(
        lambda *refs: losses_and_gradient(*refs, model_width=model_width),
        out_shape=(
            shaped((stmts, width), bf16),
            shaped((stmts // pack_size,), f32),
            shaped((stmts, width), bf16),
        ),
        in_specs=[whole] * 8,
        out_specs=(whole, pl.BlockSpec(memory_space=pltpu.SMEM), whole),
        compiler_params=pltpu.CompilerParams(vmem_limit_bytes=8 << 20),
    )(
        summed,
        flip(summed, "pack", 1),
        near,
        other_far,
        state,
        other_state,
        final_gain,
        partner[None],
    )
    return (pooled, loss_rows, grad_hidden)


def local(
    hidden_in,
    attn_gain,
    w_query,
    query_gain,
    cached_keys,
    cached_values,
    w_out,
    final_gain,
    lengths,
    pack_order,
    partner,
):
    pack_size = lax.axis_size("pack")
    pack_index = lax.axis_index("pack")
    group_index = lax.axis_index("dp")
    stmt_count, feature_count = hidden_in.shape
    model_width = feature_count * pack_size
    head_dim = query_gain.shape[0]
    local_heads = w_query.shape[1] // head_dim
    token_count = cached_keys.shape[0]
    total_stmts = partner.shape[0]
    lengths_row = lengths[0]
    order_row = pack_order[0]
    inputs32 = hidden_in.astype(jnp.float32)

    scaled = (inputs32 * attn_gain[None, :]).astype(jnp.bfloat16)
    squares = split_float(jnp.sum(inputs32 * inputs32, axis=1), 3)
    extra = jnp.stack(squares + [jnp.zeros_like(squares[0])] * 125, axis=1)
    arrived = gather_blocks(jnp.concatenate([scaled, extra], axis=1), "pack")
    input_squares = jnp.sum(arrived[:, :, feature_count : feature_count + 3].astype(jnp.float32), axis=(0, 2))
    input_rms = lax.rsqrt(input_squares / model_width + EPSILON)
    features = jnp.moveaxis(arrived[:, :, :feature_count], 0, 1).reshape(stmt_count, model_width)
    projected = jnp.dot(features, w_query, preferred_element_type=jnp.float32)
    queries = (projected * input_rms[:, None]).reshape(stmt_count, local_heads, head_dim)
    queries = (
        queries
        * lax.rsqrt(jnp.mean(queries * queries, axis=2, keepdims=True) + EPSILON)
        * query_gain
    )
    queries = rotate_heads(queries, (lengths_row - 1).astype(jnp.float32)).astype(jnp.bfloat16)
    all_queries = jnp.moveaxis(gather_blocks(queries, "pack"), 0, 1).reshape(
        stmt_count, pack_size * local_heads, head_dim
    )
    start, end = statement_ranges(lengths_row, order_row)
    tokens = pack_index * token_count + jnp.arange(token_count, dtype=jnp.int32)
    token_mask = (tokens[None, :] >= start[:, None]) & (tokens[None, :] < end[:, None])
    block_max, block_sum, numerators = block_attention(
        all_queries, cached_keys, cached_values, token_mask, head_dim ** (-0.5)
    )

    def by_owner(part):
        return jnp.moveaxis(part.reshape((stmt_count, pack_size, -1)), 1, 0)

    message = jnp.concatenate(
        [by_owner(numerators.astype(jnp.bfloat16))]
        + [by_owner(piece) for piece in split_float(block_max, 3) + split_float(block_sum, 2)],
        axis=2,
    )
    message = lax.all_to_all(message, "pack", 0, 0)
    width = local_heads * head_dim
    stats = message[:, :, width:].astype(jnp.float32).reshape(pack_size, stmt_count, 5, local_heads)
    maxima = stats[:, :, 0] + stats[:, :, 1] + stats[:, :, 2]
    factor = jnp.exp(maxima - jnp.max(maxima, axis=0, keepdims=True))
    denominator = jnp.sum((stats[:, :, 3] + stats[:, :, 4]) * factor, axis=0)
    numerators = message[:, :, :width].astype(jnp.float32).reshape(pack_size, stmt_count, local_heads, head_dim)
    summed = jnp.sum(numerators * factor[..., None], axis=0)
    attended = (summed / denominator[..., None]).astype(jnp.bfloat16)
    partial_out = jnp.dot(
        attended.reshape(stmt_count, width), w_out, preferred_element_type=jnp.float32
    )
    partial_out = jnp.moveaxis(
        partial_out.astype(jnp.bfloat16).reshape(stmt_count, pack_size, feature_count), 1, 0
    )
    partial_out = lax.all_to_all(partial_out, "pack", 0, 0)
    hidden = inputs32 + jnp.sum(partial_out.astype(jnp.float32), axis=0)
    scaled_out = hidden * final_gain[None, :]
    vectors = lax.all_gather(scaled_out.astype(jnp.bfloat16), "dp", axis=0, tiled=True)
    gram = lax.dot_general(
        vectors, vectors, (((1,), (1,)), ((), ())), preferred_element_type=jnp.float32
    )
    own_squares = jnp.sum(hidden * hidden, axis=1)
    extra = jnp.zeros((total_stmts,), jnp.float32).at[:stmt_count].set(own_squares)
    gram = jnp.concatenate([gram, extra[:, None]], axis=1)
    if total_stmts <= 128:
        gram = jnp.sum(gather_blocks(gram, "pack"), axis=0)
    else:
        gram = lax.psum(gram, "pack")
    hidden_rms = jnp.sqrt(gram[:stmt_count, total_stmts] / model_width + EPSILON)
    gram = gram[:, :total_stmts]
    column_ids = jnp.arange(total_stmts, dtype=jnp.int32)
    diagonal = column_ids[:, None] == column_ids[None, :]
    norms_row = lax.rsqrt(jnp.sum(jnp.where(diagonal, gram, 0.0), axis=0))
    norms_column = lax.rsqrt(jnp.sum(jnp.where(diagonal, gram, 0.0), axis=1))
    cosines = gram * norms_column[:, None] * norms_row[None, :]
    logits = jnp.where(diagonal, MASKED_LOGIT, cosines / SOFTMAX_WARMTH)
    highest = jnp.max(logits, axis=1)
    all_lse = highest + jnp.log(jnp.sum(jnp.exp(logits - highest[:, None]), axis=1))
    is_partner = column_ids[None, :] == partner[:, None]
    all_loss = all_lse - jnp.sum(jnp.where(is_partner, logits, 0.0), axis=1)
    own_count = stmt_count // pack_size
    row_base = group_index * stmt_count
    loss_rows = lax.dynamic_slice_in_dim(all_loss, row_base + pack_index * own_count, own_count, 0)
    weights = (
        jnp.exp(logits - all_lse[:, None])
        + jnp.exp(logits - all_lse[None, :])
        - is_partner.astype(jnp.float32)
        - is_partner.T.astype(jnp.float32)
    ).astype(jnp.bfloat16)
    own_weights = lax.dynamic_slice_in_dim(weights, row_base, stmt_count, 0)
    own_cosines = lax.dynamic_slice_in_dim(cosines, row_base, stmt_count, 0)
    own_norm = lax.dynamic_slice_in_dim(norms_column, row_base, stmt_count, 0)
    inner = jnp.sum(own_weights.astype(jnp.float32) * own_cosines, axis=1)
    own_norm = own_norm[:, None]
    embeddings = (vectors.astype(jnp.float32) * norms_column[:, None]).astype(jnp.bfloat16)
    gradient = jnp.dot(own_weights, embeddings, preferred_element_type=jnp.float32)
    scale = model_width**0.5 / SOFTMAX_WARMTH
    pooled = (scaled_out / hidden_rms[:, None]).astype(jnp.bfloat16)
    grad_hidden = (
        scale * final_gain[None, :] * (gradient - scaled_out * own_norm * inner[:, None]) * own_norm
    ).astype(jnp.bfloat16)
    return (pooled, loss_rows, grad_hidden)


def solution(mesh):
    body = core_roles if mesh.shape["pack"] == 8 and mesh.shape["dp"] == 4 else local
    in_specs = (
        P("dp", "pack"),
        P("pack"),
        P(None, "pack"),
        P(),
        P(("dp", "pack"), None),
        P(("dp", "pack"), None),
        P("pack", None),
        P("pack"),
        P("dp", None),
        P("dp", None),
        P(),
    )
    out_specs = (P("dp", "pack"), P(("dp", "pack")), P("dp", "pack"))
    return jax.shard_map(body, mesh=mesh, in_specs=in_specs, out_specs=out_specs, check_vma=False)
```

```python
import numpy as np
import jax
import jax.numpy as jnp
from jax import lax
from jax.experimental import pallas as pl
from jax.experimental.pallas import tpu as pltpu
from jax.sharding import PartitionSpec as P

EPSILON = 1e-06
SOFTMAX_WARMTH = 0.05
ROPE_BASE = 1000000.0
MASKED_LOGIT = -1e30


def gather_blocks(block, axis):
    size = lax.axis_size(axis)
    return lax.all_to_all(jnp.broadcast_to(block[None], (size,) + block.shape), axis, 0, 0)


def split_float(value, pieces):
    out = []
    for _ in range(pieces):
        piece = lax.reduce_precision(value, 8, 7)
        out.append(piece.astype(jnp.bfloat16))
        value = value - piece
    return out


def cosine_and_sine(angles):
    turns = jnp.round(angles * np.float32(2.0 / np.pi))
    rest = angles - turns * np.float32(1.5703125)
    rest = rest - turns * np.float32(4.837512969970703125e-4)
    rest = rest - turns * np.float32(7.549789948768648e-8)
    square = rest * rest
    sine = rest + rest * square * (
        np.float32(-1.6666654611e-1)
        + square * (np.float32(8.3321608736e-3) + square * np.float32(-1.9515295891e-4))
    )
    cosine = (
        1.0
        - 0.5 * square
        + square
        * square
        * (
            np.float32(4.166664568298827e-2)
            + square
            * (np.float32(-1.388731625493765e-3) + square * np.float32(2.443315711809948e-5))
        )
    )
    quarter = turns.astype(jnp.int32) & 3
    swap = (quarter & 1) == 1
    cos_out = jnp.where(swap, sine, cosine)
    sin_out = jnp.where(swap, cosine, sine)
    cos_out = jnp.where((quarter == 1) | (quarter == 2), -cos_out, cos_out)
    sin_out = jnp.where(quarter >= 2, -sin_out, sin_out)
    return cos_out, sin_out


def rotate_heads(queries, position):
    head_dim = queries.shape[-1]
    half_dim = head_dim // 2
    frequency = (ROPE_BASE ** (-np.arange(half_dim) * 2.0 / head_dim)).astype(np.float32)
    cosine, sine = cosine_and_sine(position[:, None] * frequency[None, :])
    cosine = jnp.concatenate([cosine, cosine], axis=1)[:, None, :]
    sine = jnp.concatenate([-sine, sine], axis=1)[:, None, :]
    turned = jnp.concatenate([queries[..., half_dim:], queries[..., :half_dim]], axis=-1)
    return queries * cosine + turned * sine


def statement_ranges(lengths_row, order_row):
    stmt_count = order_row.shape[0]
    index = jnp.arange(stmt_count, dtype=jnp.int32)
    slot = jnp.sum(jnp.where(order_row[None, :] == index[:, None], index[None, :], 0), axis=1)
    start = jnp.sum(jnp.where(slot[None, :] < slot[:, None], lengths_row[None, :], 0), axis=1)
    return start, start + lengths_row


def block_attention(all_queries, cached_keys, cached_values, token_mask, score_scale):
    stmt_count, head_count, head_dim = all_queries.shape
    kv_heads = cached_keys.shape[1] // head_dim
    group_size = head_count // kv_heads
    grouped = all_queries.reshape(stmt_count, kv_heads, group_size, head_dim)
    key_heads = cached_keys.reshape(-1, kv_heads, head_dim)
    value_heads = cached_values.reshape(-1, kv_heads, head_dim)
    scores = (
        jnp.einsum("skgd,tkd->skgt", grouped, key_heads, preferred_element_type=jnp.float32)
        * score_scale
    )
    token_mask = token_mask[:, None, None, :]
    block_max = jnp.max(jnp.where(token_mask, scores, MASKED_LOGIT), axis=3)
    softmax_weights = jnp.where(token_mask, jnp.exp(scores - block_max[..., None]), 0.0)
    block_sum = jnp.sum(softmax_weights, axis=3)
    numerators = jnp.einsum(
        "skgt,tkd->skgd",
        softmax_weights.astype(jnp.bfloat16),
        value_heads,
        preferred_element_type=jnp.float32,
    )
    return (
        block_max.reshape(stmt_count, head_count),
        block_sum.reshape(stmt_count, head_count),
        numerators.reshape(stmt_count, head_count, head_dim),
    )


def flip(array, axis, offset):
    size = lax.axis_size(axis)
    return lax.ppermute(array, axis, [(i, i ^ offset) for i in range(size)])


def in_vmem(body, outputs, *operands, limit=8, flops=1_000_000):
    whole = pl.BlockSpec(memory_space=pltpu.VMEM)
    moved = sum(operand.size * operand.dtype.itemsize for operand in operands)
    return pl.pallas_call(
        body,
        out_shape=outputs,
        in_specs=[whole] * len(operands),
        out_specs=jax.tree.map(lambda _: whole, outputs),
        compiler_params=pltpu.CompilerParams(vmem_limit_bytes=limit << 20),
        cost_estimate=pl.CostEstimate(flops=flops, bytes_accessed=moved, transcendentals=0),
    )(*operands)


def shaped(shape, kind):
    return jax.ShapeDtypeStruct(shape, kind)


def lane_pieces(values, width=128):
    rows = values[0].shape[0]
    lane = lax.broadcasted_iota(jnp.int32, (rows, width), 1)
    out = jnp.zeros((rows, width), jnp.float32)
    for place, value in enumerate(values):
        rest = value
        for part in range(3):
            piece = rest.astype(jnp.bfloat16).astype(jnp.float32)
            out = jnp.where(lane == 3 * place + part, piece, out)
            rest = rest - piece
    return out.astype(jnp.bfloat16)


def lane_sum(block, place):
    lane = lax.broadcasted_iota(jnp.int32, block.shape, 1)
    own = (lane >= 3 * place) & (lane < 3 * place + 3)
    return jnp.sum(jnp.where(own, block, 0.0), axis=1, keepdims=True)


def open_window(out_ref):
    out_ref[...] = jnp.zeros_like(out_ref)


def prepare_inputs(window_ref, hidden_ref, gain_ref, message_ref):
    del window_ref
    inputs = hidden_ref[...].astype(jnp.float32)
    width = inputs.shape[1]
    message_ref[:, :width] = (inputs * gain_ref[...]).astype(jnp.bfloat16)
    message_ref[:, width:] = lane_pieces([jnp.sum(inputs * inputs, axis=1, keepdims=True)])


def positions_and_ranges(
    message_ref, frequency_ref, lengths_ref, order_ref, rope_ref, range_ref
):
    del message_ref
    count = lengths_ref.shape[1]
    half = frequency_ref.shape[1] // 2
    row = lax.broadcasted_iota(jnp.int32, (count, count), 0)
    column = lax.broadcasted_iota(jnp.int32, (count, count), 1)
    lengths = jnp.broadcast_to(lengths_ref[...], (count, count)).astype(jnp.float32)
    length = jnp.sum(jnp.where(row == column, lengths, 0.0), axis=1, keepdims=True)
    order = jnp.broadcast_to(order_ref[...], (count, count))
    placed = order == row
    slot = jnp.sum(jnp.where(placed, column, 0).astype(jnp.float32), axis=1, keepdims=True)
    packed = jnp.sum(jnp.where(placed, length, 0.0), axis=0, keepdims=True)
    earlier = column.astype(jnp.float32) < slot
    start = jnp.sum(jnp.where(earlier, packed, 0.0), axis=1, keepdims=True)
    range_ref[:, :128] = jnp.broadcast_to(start, (count, 128))
    range_ref[:, 128:] = jnp.broadcast_to(start + length, (count, 128))
    cosine, sine = cosine_and_sine((length - 1.0) * frequency_ref[...])
    lane = lax.broadcasted_iota(jnp.int32, cosine.shape, 1)
    rope_ref[:, : 2 * half] = cosine
    rope_ref[:, 2 * half :] = jnp.where(lane < half, -sine, sine)


LOG2_E = 1.4426950408889634


def core_number():
    return lax.axis_index("pack") & 1


def chip_number():
    return lax.axis_index("pack") >> 1


def send_across(array, axis, offset, sender):
    groups, pack = lax.axis_size("dp"), lax.axis_size("pack")
    pairs = []
    for group in range(groups):
        for place in range(pack):
            if place % 2 != sender:
                target = (group, place ^ 1)
            elif axis == "dp":
                target = (group ^ offset, place ^ 1)
            else:
                target = (group, place ^ (2 * offset) ^ 1)
            pairs.append((group * pack + place, target[0] * pack + target[1]))
    return lax.ppermute(array, ("dp", "pack"), pairs)


def copy_tokens(_, key_ref, value_ref, out_ref):
    out_ref[0] = key_ref[...]
    out_ref[1] = value_ref[...]


def join_cores(own_ref, other_ref, pair_ref):
    core = core_number()
    pair_ref[core] = own_ref[...]
    pair_ref[1 - core] = other_ref[...]


def join_blocks(*refs):
    out_ref = refs[-1]
    count = out_ref.shape[0]
    for i in range(count):
        out_ref[count - 1 - i] = refs[i][...]


def project_pair(pair_ref, offset, weight_ref):
    chip = chip_number() ^ offset
    width = weight_ref.shape[1]
    total = 0.0
    for core in range(2):
        rows = pl.ds(pl.multiple_of((2 * chip + core) * width, width), width)
        total = total + jnp.dot(
            pair_ref[core, :, :width], weight_ref[rows, :], preferred_element_type=jnp.float32
        )
    return total


def project_own_pair(pair_ref, weight_ref, total_ref):
    total_ref[...] = project_pair(pair_ref, 0, weight_ref)


def make_queries(
    pair_ref, blocks_ref, total_ref, weight_ref, gain_ref, rope_ref, query_ref, *, core, model_width
):
    width = total_ref.shape[1]
    head_dim = gain_ref.shape[1]

    @pl.when(core_number() == core)
    def _():
        projected = total_ref[...]
        squares = jnp.zeros((total_ref.shape[0], 1), jnp.float32)
        for j in range(2):
            squares = squares + lane_sum(pair_ref[j, :, width:].astype(jnp.float32), 0)
        for i in range(blocks_ref.shape[0]):
            projected = projected + project_pair(blocks_ref.at[i], i + 1, weight_ref)
            for j in range(2):
                squares = squares + lane_sum(blocks_ref[i, j, :, width:].astype(jnp.float32), 0)
        projected = projected * lax.rsqrt(squares / model_width + EPSILON)
        cosine = rope_ref[:, :head_dim]
        sine = rope_ref[:, head_dim:]
        for head in range(width // head_dim):
            place = slice(head * head_dim, (head + 1) * head_dim)
            query = projected[:, place]
            mean = jnp.mean(query * query, axis=1, keepdims=True)
            query = query * lax.rsqrt(mean + EPSILON) * gain_ref[...]
            turned = pltpu.roll(query, head_dim // 2, 1)
            query_ref[:, place] = (query * cosine + turned * sine).astype(jnp.bfloat16)


def join_queries(first_ref, second_ref, out_ref):
    width = first_ref.shape[1]
    out_ref[:, :width] = first_ref[...]
    out_ref[:, width:] = second_ref[...]


def token_masks(range_ref, tokens, group):
    me = lax.axis_index("pack")
    masks = []
    for owner in (me, me ^ 1):
        index = lax.broadcasted_iota(jnp.int32, (range_ref.shape[0], tokens), 1) + owner * tokens
        index = index.astype(jnp.float32)
        mask = (index >= range_ref[:, :1]) & (index < range_ref[:, 128:129])
        masks.append(jnp.concatenate([mask.astype(jnp.float32)] * group, axis=0) > 0.5)
    return masks


def attend_heads(queries, heads, key_ref, value_ref, other_ref, masks):
    head_dim = 128
    scale = head_dim**-0.5
    scores = []
    columns = []
    for query, head in zip(queries, heads):
        grouped = jnp.concatenate(
            [query[:, i : i + head_dim] for i in range(0, query.shape[1], head_dim)], axis=0
        )
        column = pl.ds(pl.multiple_of(head * head_dim, head_dim), head_dim)
        columns.append(column)
        raw = [
            lax.dot_general(
                grouped, keys, (((1,), (1,)), ((), ())), preferred_element_type=jnp.float32
            )
            for keys in (key_ref[:, column], other_ref[0, :, column])
        ]
        scores.append([jnp.where(mask, part, MASKED_LOGIT) for mask, part in zip(masks, raw)])
    maxima = [
        jnp.maximum(
            jnp.max(first, axis=1, keepdims=True), jnp.max(second, axis=1, keepdims=True)
        )
        for first, second in scores
    ]
    weights = [
        [jnp.exp2((part - highest) * (scale * LOG2_E)) for part in parts]
        for parts, highest in zip(scores, maxima)
    ]
    out = []
    for parts, highest, column in zip(weights, maxima, columns):
        total = jnp.sum(parts[0], axis=1, keepdims=True) + jnp.sum(
            parts[1], axis=1, keepdims=True
        )
        numerators = jnp.dot(
            parts[0].astype(jnp.bfloat16), value_ref[:, column], preferred_element_type=jnp.float32
        ) + jnp.dot(
            parts[1].astype(jnp.bfloat16),
            other_ref[1, :, column],
            preferred_element_type=jnp.float32,
        )
        out.append((highest * scale, total, numerators))
    return out


def attend_remote(*refs):
    query_refs, refs = refs[:3], refs[3:]
    key_ref, value_ref, other_ref, range_ref = refs[:4]
    out_refs = refs[4:]

    @pl.when(core_number() == 1)
    def _():
        rows = query_refs[0].shape[0]
        width = query_refs[0].shape[1] // 2
        masks = token_masks(range_ref, key_ref.shape[0], width // 128)
        for i, (query_ref, out_ref) in enumerate(zip(query_refs, out_refs)):
            chip = chip_number() ^ (3 - i)
            queries = [query_ref[:, :width], query_ref[:, width:]]
            parts = attend_heads(
                queries, (2 * chip, 2 * chip + 1), key_ref, value_ref, other_ref, masks
            )
            stats = []
            for j, (highest, total, numerators) in enumerate(parts):
                for h in range(width // 128):
                    part = slice(h * rows, (h + 1) * rows)
                    place = slice(j * width + h * 128, j * width + (h + 1) * 128)
                    out_ref[:, place] = numerators[part].astype(jnp.bfloat16)
                    stats += [highest[part], total[part]]
            out_ref[:, 2 * width :] = lane_pieces(stats)


def attend_own(query_ref, key_ref, value_ref, other_ref, range_ref, out_ref, stats_ref):
    @pl.when(core_number() == 0)
    def _():
        width = query_ref.shape[1] // 2
        masks = token_masks(range_ref, key_ref.shape[0], width // 128)
        chip = chip_number()
        parts = attend_heads(
            [query_ref[:, :width], query_ref[:, width:]],
            (2 * chip, 2 * chip + 1),
            key_ref,
            value_ref,
            other_ref,
            masks,
        )
        for j, (highest, total, numerators) in enumerate(parts):
            out_ref[j] = numerators
            stats_ref[j, :, :128] = jnp.broadcast_to(highest, (highest.shape[0], 128))
            stats_ref[j, :, 128:] = jnp.broadcast_to(total, (highest.shape[0], 128))


def merge_partials(third_ref, second_ref, first_ref, own_ref, stats_ref, *refs):
    attended_ref = refs[-1]

    @pl.when(core_number() == 0)
    def _():
        rows = attended_ref.shape[0]
        width = attended_ref.shape[1] // 2
        others = (first_ref, second_ref, third_ref)
        stats = [ref[:, 2 * width :].astype(jnp.float32) for ref in others]
        for j in range(2):
            for h in range(width // 128):
                part = slice(h * rows, (h + 1) * rows)
                place = slice(j * width + h * 128, j * width + (h + 1) * 128)
                slot = 2 * (j * (width // 128) + h)
                maxima = [stats_ref[j, part, :1]] + [lane_sum(s, slot) for s in stats]
                totals = [stats_ref[j, part, 128:129]] + [lane_sum(s, slot + 1) for s in stats]
                numerators = [own_ref[j, part, :]]
                numerators += [ref[:, place].astype(jnp.float32) for ref in others]
                highest = maxima[0]
                for value in maxima[1:]:
                    highest = jnp.maximum(highest, value)
                denominator = 0.0
                summed = 0.0
                for value, total, numerator in zip(maxima, totals, numerators):
                    factor = jnp.exp(value - highest)
                    denominator = denominator + total * factor
                    summed = summed + numerator * factor
                attended_ref[:, place] = (summed / denominator).astype(jnp.bfloat16)


def copy_weights(_, weight_ref, out_ref):
    out_ref[...] = weight_ref[...]


def project_out(attended_ref, weight_ref, other_weight_ref, *refs, offset):
    out_ref = refs[-1]

    @pl.when(core_number() == 0)
    def _():
        width = attended_ref.shape[1] // 2
        column = pl.ds(pl.multiple_of((chip_number() ^ offset) * 2 * width, 2 * width), 2 * width)
        total = jnp.dot(
            attended_ref[:, :width], weight_ref[:, column], preferred_element_type=jnp.float32
        ) + jnp.dot(
            attended_ref[:, width:], other_weight_ref[:, column], preferred_element_type=jnp.float32
        )
        out_ref[...] = total.astype(out_ref.dtype)


def finish_hidden(
    third_ref,
    second_ref,
    first_ref,
    kept_ref,
    own_ref,
    other_ref,
    own_gain_ref,
    other_gain_ref,
    sent_ref,
    scaled_ref,
    other_scaled_ref,
):
    width = own_ref.shape[1]

    @pl.when(core_number() == 1)
    def _():
        squares = 0.0
        inputs = (other_ref, own_ref)
        gains = (other_gain_ref, own_gain_ref)
        for core in range(2):
            place = slice(core * width, (core + 1) * width)
            hidden = inputs[core][...].astype(jnp.float32)
            for ref in (kept_ref, first_ref, second_ref, third_ref):
                hidden = hidden + ref[:, place].astype(jnp.float32)
            scaled = hidden * gains[core][...]
            (other_scaled_ref, scaled_ref)[core][...] = scaled
            sent_ref[:, place] = scaled.astype(jnp.bfloat16)
            squares = squares + jnp.sum(hidden * hidden, axis=1, keepdims=True)
        sent_ref[:, 2 * width :] = lane_pieces([squares])


def gram_part(third_ref, second_ref, first_ref, own_ref, _, out_ref, near_ref, far_ref):
    @pl.when(core_number() == 0)
    def _():
        rows = own_ref.shape[0]
        width = far_ref.shape[1]
        refs = (own_ref, first_ref, second_ref, third_ref)
        for i, ref in enumerate(refs):
            near_ref[i * rows : (i + 1) * rows] = ref[:, :width]
        for i, ref in enumerate(refs[1:]):
            far_ref[i * rows : (i + 1) * rows] = ref[:, width : 2 * width]
        far = jnp.concatenate([ref[:, width : 2 * width] for ref in refs], axis=0)
        squares = lane_sum(own_ref[:, 2 * width :].astype(jnp.float32), 0)
        gram = 0.0
        for vectors in (near_ref[...], far):
            gram = gram + lax.dot_general(
                vectors, vectors, (((1,), (1,)), ((), ())), preferred_element_type=jnp.float32
            )
        half = gram.shape[0] // 2
        out_ref[:half, : 2 * half] = gram[:half]
        out_ref[:half, 2 * half :] = gram[half:]
        out_ref[half:, :] = jnp.broadcast_to(squares, (rows, 128))


def sum_grams(third_ref, second_ref, first_ref, own_ref, *refs):
    out_ref = refs[-1]
    out_ref[...] = own_ref[...] + first_ref[...] + second_ref[...] + third_ref[...]


def partner_masks(partner_ref, out_ref, *, rows):
    group = lax.axis_index("dp")
    shape = out_ref.shape[1:]
    row = lax.broadcasted_iota(jnp.int32, shape, 0)
    column = lax.broadcasted_iota(jnp.int32, shape, 1)
    row_id = ((group ^ (row // rows)) * rows) + row % rows
    column_id = ((group ^ (column // rows)) * rows) + column % rows
    partners = jnp.broadcast_to(partner_ref[...], shape)
    row_partner = jnp.sum(
        jnp.where(column == row_id, partners, 0).astype(jnp.float32), axis=1, keepdims=True
    )
    column_partner = jnp.sum(
        jnp.where(row_id == column_id, row_partner, 0.0), axis=0, keepdims=True
    )
    own_partner = column_id.astype(jnp.float32) == row_partner
    other_partner = row_id.astype(jnp.float32) == column_partner
    own_partner = own_partner.astype(jnp.float32)
    out_ref[0] = own_partner
    out_ref[1] = own_partner + other_partner.astype(jnp.float32)


def losses_and_gradient(
    summed_ref,
    other_summed_ref,
    near_ref,
    sent_ref,
    other_far_ref,
    scaled_ref,
    other_scaled_ref,
    gain_ref,
    partner_ref,
    pooled_ref,
    loss_ref,
    grad_ref,
    *,
    model_width,
):
    me = lax.axis_index("pack")
    first_core = core_number() == 0
    count, width = near_ref.shape
    rows = scaled_ref.shape[0]
    half = count // 2
    summed = jnp.where(first_core, other_summed_ref[...], summed_ref[...])
    gram = jnp.concatenate([summed[:half, :count], summed[:half, count:]], axis=0)
    squares = summed[half:, :1]
    shape = (count, count)
    row = lax.broadcasted_iota(jnp.int32, shape, 0)
    column = lax.broadcasted_iota(jnp.int32, shape, 1)
    diagonal = row == column
    on_diagonal = jnp.where(diagonal, gram, 0.0)
    row_scale = lax.rsqrt(jnp.sum(on_diagonal, axis=1, keepdims=True))
    column_scale = lax.rsqrt(jnp.sum(on_diagonal, axis=0, keepdims=True))
    cosines = gram * row_scale * column_scale
    logits = jnp.where(diagonal, MASKED_LOGIT, cosines * (1.0 / SOFTMAX_WARMTH))
    row_high = jnp.max(logits, axis=1, keepdims=True)
    row_lse = row_high + jnp.log(jnp.sum(jnp.exp(logits - row_high), axis=1, keepdims=True))
    column_high = jnp.max(logits, axis=0, keepdims=True)
    column_lse = column_high + jnp.log(
        jnp.sum(jnp.exp(logits - column_high), axis=0, keepdims=True)
    )
    target = jnp.sum(partner_ref[0] * logits, axis=1, keepdims=True)
    loss = row_lse - target
    own = loss_ref.shape[0]
    index = lax.broadcasted_iota(jnp.int32, (count, 1), 0)
    for i in range(own):
        loss_ref[i] = jnp.sum(jnp.where(index == me * own + i, loss, 0.0))
    weights = (
        jnp.exp(logits - row_lse)
        + jnp.exp(logits - column_lse)
        - partner_ref[1]
    )[:rows]
    inner = jnp.sum(weights * cosines[:rows], axis=1, keepdims=True)
    scaled_weights = weights * column_scale
    upper = scaled_weights.astype(jnp.bfloat16)
    lower = (scaled_weights - upper.astype(jnp.float32)).astype(jnp.bfloat16)
    own_scale = row_scale[:rows]
    pooled_scale = lax.rsqrt(squares / model_width + EPSILON)
    grad_gain = gain_ref[...] * (model_width**0.5 / SOFTMAX_WARMTH)

    def write(vectors, scaled):
        gradient = jnp.dot(upper, vectors, preferred_element_type=jnp.float32) + jnp.dot(
            lower, vectors, preferred_element_type=jnp.float32
        )
        gradient = (gradient - scaled * (own_scale * inner)) * own_scale
        grad_ref[...] = (gradient * grad_gain).astype(jnp.bfloat16)
        pooled_ref[...] = (scaled * pooled_scale).astype(jnp.bfloat16)

    @pl.when(first_core)
    def _():
        write(near_ref[...], other_scaled_ref[...])

    @pl.when(core_number() == 1)
    def _():
        vectors = jnp.concatenate((sent_ref[:, width : 2 * width], other_far_ref[...]), axis=0)
        write(vectors, scaled_ref[...])


def core_roles(
    hidden_in,
    attn_gain,
    w_query,
    query_gain,
    cached_keys,
    cached_values,
    w_out,
    final_gain,
    lengths,
    pack_order,
    partner,
):
    pack_size = lax.axis_size("pack")
    stmts, width = hidden_in.shape
    model_width = width * pack_size
    head_dim = query_gain.shape[0]
    tokens = cached_keys.shape[0]
    chips = pack_size // 2
    others = range(1, chips)
    total = partner.shape[0]
    bf16 = jnp.bfloat16
    f32 = jnp.float32
    final_gain = final_gain[None]
    query_gain = query_gain[None]
    half = np.arange(head_dim // 2)
    frequency = (ROPE_BASE ** (-half * 2.0 / head_dim)).astype(np.float32)
    frequency = jnp.asarray(np.concatenate([frequency, frequency])[None])
    whole = pl.BlockSpec(memory_space=pltpu.VMEM)

    window = pl.pallas_call(
        open_window,
        out_shape=shaped((8, 128), f32),
        out_specs=whole,
        compiler_params=pltpu.CompilerParams(vmem_limit_bytes=1 << 20),
        cost_estimate=pl.CostEstimate(flops=1 << 34, bytes_accessed=0, transcendentals=0),
    )()
    message = in_vmem(
        prepare_inputs, shaped((stmts, width + 128), bf16), window, hidden_in, attn_gain[None]
    )
    pair = in_vmem(
        join_cores, shaped((2,) + message.shape, bf16), message, flip(message, "pack", 1)
    )
    received = [send_across(pair, "pack", k, 0) for k in others]
    own_projected = in_vmem(
        project_own_pair, shaped((stmts, width), f32), pair, w_query, limit=16, flops=1 << 26
    )
    rope, ranges = in_vmem(
        positions_and_ranges,
        (shaped((stmts, 2 * head_dim), f32), shaped((stmts, 256), f32)),
        message,
        frequency,
        lengths,
        pack_order,
    )
    blocks = in_vmem(
        join_blocks, shaped((chips - 1,) + pair.shape, bf16), *received[::-1], own_projected, rope
    )
    flipped_blocks = flip(blocks, "pack", 1)

    def queries_on(core, blocks, flops):
        return in_vmem(
            lambda *refs: make_queries(*refs, core=core, model_width=model_width),
            shaped((stmts, width), bf16),
            pair,
            blocks,
            own_projected,
            w_query,
            query_gain,
            rope,
            limit=16,
            flops=flops,
        )

    late_queries = queries_on(1, blocks, 1 << 27)
    held = in_vmem(
        copy_tokens,
        shaped((2,) + cached_keys.shape, bf16),
        late_queries,
        cached_keys,
        cached_values,
    )
    other_held = flip(held, "pack", 1)
    second_queries = flip(late_queries, "pack", 1)
    first_queries = queries_on(0, flipped_blocks, 1 << 36)
    queries = in_vmem(
        join_queries, shaped((stmts, 2 * width), bf16), first_queries, second_queries
    )
    other_weights = flip(
        in_vmem(copy_weights, shaped(w_out.shape, bf16), queries, w_out, limit=16), "pack", 1
    )
    received = [send_across(queries, "pack", k, 0) for k in others]
    group_rows = stmts * (width // head_dim)
    own_part, own_stats = in_vmem(
        attend_own,
        (shaped((2, group_rows, head_dim), f32), shaped((2, group_rows, 256), f32)),
        queries,
        cached_keys,
        cached_values,
        other_held,
        ranges,
        flops=1 << 27,
    )
    partials = in_vmem(
        attend_remote,
        (shaped((stmts, 2 * width + 128), bf16),) * (chips - 1),
        *received[::-1],
        cached_keys,
        cached_values,
        other_held,
        ranges,
        flops=1 << 36,
    )
    received = [send_across(part, "pack", k, 1) for k, part in zip(others, partials[::-1])]
    other_hidden_in = flip(hidden_in, "pack", 1)
    other_gain = flip(final_gain, "pack", 1)
    attended = in_vmem(
        merge_partials,
        shaped((stmts, 2 * width), bf16),
        *received[::-1],
        own_part,
        own_stats,
        other_hidden_in,
        other_gain,
    )

    def projected_to(offset, kind, *after):
        return in_vmem(
            lambda *refs: project_out(*refs, offset=offset),
            shaped((stmts, 2 * width), kind),
            attended,
            w_out,
            other_weights,
            *after,
            limit=16,
            flops=1 << 27,
        )

    third = projected_to(3, bf16)
    second = projected_to(2, bf16, third)
    first = projected_to(1, bf16, second)
    kept = projected_to(0, bf16, first)
    received = [send_across(part, "pack", k, 0) for k, part in zip(others, (first, second, third))]
    vector, scaled, far_scaled = in_vmem(
        finish_hidden,
        (shaped((stmts, 2 * width + 128), bf16),) + (shaped((stmts, width), f32),) * 2,
        *received[::-1],
        flip(kept, "pack", 1),
        hidden_in,
        other_hidden_in,
        final_gain,
        other_gain,
    )
    received = [send_across(vector, "dp", k, 1) for k in range(1, lax.axis_size("dp"))]
    other_scaled = flip(far_scaled, "pack", 1)
    gram, near, far = in_vmem(
        gram_part,
        (
            shaped((total // 2 + stmts, 128), f32),
            shaped((total, width), bf16),
            shaped((total - stmts, width), bf16),
        ),
        *received[::-1],
        flip(vector, "pack", 1),
        other_scaled,
    )
    received = [send_across(gram, "pack", k, 0) for k in others]
    other_far = flip(far, "pack", 1)
    summed = in_vmem(
        sum_grams,
        shaped(gram.shape, f32),
        *received[::-1],
        flip(gram, "pack", 1),
    )
    masks = in_vmem(
        lambda *refs: partner_masks(*refs, rows=stmts),
        shaped((2, total, total), f32),
        partner[None],
    )
    pooled, loss_rows, grad_hidden = pl.pallas_call(
        lambda *refs: losses_and_gradient(*refs, model_width=model_width),
        out_shape=(
            shaped((stmts, width), bf16),
            shaped((stmts // pack_size,), f32),
            shaped((stmts, width), bf16),
        ),
        in_specs=[whole] * 9,
        out_specs=(whole, pl.BlockSpec(memory_space=pltpu.SMEM), whole),
        compiler_params=pltpu.CompilerParams(vmem_limit_bytes=8 << 20),
    )(
        summed,
        flip(summed, "pack", 1),
        near,
        vector,
        other_far,
        scaled,
        other_scaled,
        final_gain,
        masks,
    )
    return (pooled, loss_rows, grad_hidden)


def local(
    hidden_in,
    attn_gain,
    w_query,
    query_gain,
    cached_keys,
    cached_values,
    w_out,
    final_gain,
    lengths,
    pack_order,
    partner,
):
    pack_size = lax.axis_size("pack")
    pack_index = lax.axis_index("pack")
    group_index = lax.axis_index("dp")
    stmt_count, feature_count = hidden_in.shape
    model_width = feature_count * pack_size
    head_dim = query_gain.shape[0]
    local_heads = w_query.shape[1] // head_dim
    token_count = cached_keys.shape[0]
    total_stmts = partner.shape[0]
    lengths_row = lengths[0]
    order_row = pack_order[0]
    inputs32 = hidden_in.astype(jnp.float32)

    scaled = (inputs32 * attn_gain[None, :]).astype(jnp.bfloat16)
    squares = split_float(jnp.sum(inputs32 * inputs32, axis=1), 3)
    extra = jnp.stack(squares + [jnp.zeros_like(squares[0])] * 125, axis=1)
    arrived = gather_blocks(jnp.concatenate([scaled, extra], axis=1), "pack")
    input_squares = jnp.sum(arrived[:, :, feature_count : feature_count + 3].astype(jnp.float32), axis=(0, 2))
    input_rms = lax.rsqrt(input_squares / model_width + EPSILON)
    features = jnp.moveaxis(arrived[:, :, :feature_count], 0, 1).reshape(stmt_count, model_width)
    projected = jnp.dot(features, w_query, preferred_element_type=jnp.float32)
    queries = (projected * input_rms[:, None]).reshape(stmt_count, local_heads, head_dim)
    queries = (
        queries
        * lax.rsqrt(jnp.mean(queries * queries, axis=2, keepdims=True) + EPSILON)
        * query_gain
    )
    queries = rotate_heads(queries, (lengths_row - 1).astype(jnp.float32)).astype(jnp.bfloat16)
    all_queries = jnp.moveaxis(gather_blocks(queries, "pack"), 0, 1).reshape(
        stmt_count, pack_size * local_heads, head_dim
    )
    start, end = statement_ranges(lengths_row, order_row)
    tokens = pack_index * token_count + jnp.arange(token_count, dtype=jnp.int32)
    token_mask = (tokens[None, :] >= start[:, None]) & (tokens[None, :] < end[:, None])
    block_max, block_sum, numerators = block_attention(
        all_queries, cached_keys, cached_values, token_mask, head_dim ** (-0.5)
    )

    def by_owner(part):
        return jnp.moveaxis(part.reshape((stmt_count, pack_size, -1)), 1, 0)

    message = jnp.concatenate(
        [by_owner(numerators.astype(jnp.bfloat16))]
        + [by_owner(piece) for piece in split_float(block_max, 3) + split_float(block_sum, 2)],
        axis=2,
    )
    message = lax.all_to_all(message, "pack", 0, 0)
    width = local_heads * head_dim
    stats = message[:, :, width:].astype(jnp.float32).reshape(pack_size, stmt_count, 5, local_heads)
    maxima = stats[:, :, 0] + stats[:, :, 1] + stats[:, :, 2]
    factor = jnp.exp(maxima - jnp.max(maxima, axis=0, keepdims=True))
    denominator = jnp.sum((stats[:, :, 3] + stats[:, :, 4]) * factor, axis=0)
    numerators = message[:, :, :width].astype(jnp.float32).reshape(pack_size, stmt_count, local_heads, head_dim)
    summed = jnp.sum(numerators * factor[..., None], axis=0)
    attended = (summed / denominator[..., None]).astype(jnp.bfloat16)
    partial_out = jnp.dot(
        attended.reshape(stmt_count, width), w_out, preferred_element_type=jnp.float32
    )
    partial_out = jnp.moveaxis(
        partial_out.astype(jnp.bfloat16).reshape(stmt_count, pack_size, feature_count), 1, 0
    )
    partial_out = lax.all_to_all(partial_out, "pack", 0, 0)
    hidden = inputs32 + jnp.sum(partial_out.astype(jnp.float32), axis=0)
    scaled_out = hidden * final_gain[None, :]
    vectors = lax.all_gather(scaled_out.astype(jnp.bfloat16), "dp", axis=0, tiled=True)
    gram = lax.dot_general(
        vectors, vectors, (((1,), (1,)), ((), ())), preferred_element_type=jnp.float32
    )
    own_squares = jnp.sum(hidden * hidden, axis=1)
    extra = jnp.zeros((total_stmts,), jnp.float32).at[:stmt_count].set(own_squares)
    gram = jnp.concatenate([gram, extra[:, None]], axis=1)
    if total_stmts <= 128:
        gram = jnp.sum(gather_blocks(gram, "pack"), axis=0)
    else:
        gram = lax.psum(gram, "pack")
    hidden_rms = jnp.sqrt(gram[:stmt_count, total_stmts] / model_width + EPSILON)
    gram = gram[:, :total_stmts]
    column_ids = jnp.arange(total_stmts, dtype=jnp.int32)
    diagonal = column_ids[:, None] == column_ids[None, :]
    norms_row = lax.rsqrt(jnp.sum(jnp.where(diagonal, gram, 0.0), axis=0))
    norms_column = lax.rsqrt(jnp.sum(jnp.where(diagonal, gram, 0.0), axis=1))
    cosines = gram * norms_column[:, None] * norms_row[None, :]
    logits = jnp.where(diagonal, MASKED_LOGIT, cosines / SOFTMAX_WARMTH)
    highest = jnp.max(logits, axis=1)
    all_lse = highest + jnp.log(jnp.sum(jnp.exp(logits - highest[:, None]), axis=1))
    is_partner = column_ids[None, :] == partner[:, None]
    all_loss = all_lse - jnp.sum(jnp.where(is_partner, logits, 0.0), axis=1)
    own_count = stmt_count // pack_size
    row_base = group_index * stmt_count
    loss_rows = lax.dynamic_slice_in_dim(all_loss, row_base + pack_index * own_count, own_count, 0)
    weights = (
        jnp.exp(logits - all_lse[:, None])
        + jnp.exp(logits - all_lse[None, :])
        - is_partner.astype(jnp.float32)
        - is_partner.T.astype(jnp.float32)
    ).astype(jnp.bfloat16)
    own_weights = lax.dynamic_slice_in_dim(weights, row_base, stmt_count, 0)
    own_cosines = lax.dynamic_slice_in_dim(cosines, row_base, stmt_count, 0)
    own_norm = lax.dynamic_slice_in_dim(norms_column, row_base, stmt_count, 0)
    inner = jnp.sum(own_weights.astype(jnp.float32) * own_cosines, axis=1)
    own_norm = own_norm[:, None]
    embeddings = (vectors.astype(jnp.float32) * norms_column[:, None]).astype(jnp.bfloat16)
    gradient = jnp.dot(own_weights, embeddings, preferred_element_type=jnp.float32)
    scale = model_width**0.5 / SOFTMAX_WARMTH
    pooled = (scaled_out / hidden_rms[:, None]).astype(jnp.bfloat16)
    grad_hidden = (
        scale * final_gain[None, :] * (gradient - scaled_out * own_norm * inner[:, None]) * own_norm
    ).astype(jnp.bfloat16)
    return (pooled, loss_rows, grad_hidden)


def solution(mesh):
    body = core_roles if mesh.shape["pack"] == 8 and mesh.shape["dp"] == 4 else local
    in_specs = (
        P("dp", "pack"),
        P("pack"),
        P(None, "pack"),
        P(),
        P(("dp", "pack"), None),
        P(("dp", "pack"), None),
        P("pack", None),
        P("pack"),
        P("dp", None),
        P("dp", None),
        P(),
    )
    out_specs = (P("dp", "pack"), P(("dp", "pack")), P("dp", "pack"))
    return jax.shard_map(body, mesh=mesh, in_specs=in_specs, out_specs=out_specs, check_vma=False)
```

```python
import numpy as np
import jax
import jax.numpy as jnp
from jax import lax
from jax.experimental import pallas as pl
from jax.experimental.pallas import tpu as pltpu
from jax.sharding import PartitionSpec as P

EPSILON = 1e-06
SOFTMAX_WARMTH = 0.05
ROPE_BASE = 1000000.0
MASKED_LOGIT = -1e30


def gather_blocks(block, axis):
    size = lax.axis_size(axis)
    return lax.all_to_all(jnp.broadcast_to(block[None], (size,) + block.shape), axis, 0, 0)


def split_float(value, pieces):
    out = []
    for _ in range(pieces):
        piece = lax.reduce_precision(value, 8, 7)
        out.append(piece.astype(jnp.bfloat16))
        value = value - piece
    return out


def cosine_and_sine(angles):
    turns = jnp.round(angles * np.float32(2.0 / np.pi))
    rest = angles - turns * np.float32(1.5703125)
    rest = rest - turns * np.float32(4.837512969970703125e-4)
    rest = rest - turns * np.float32(7.549789948768648e-8)
    square = rest * rest
    sine = rest + rest * square * (
        np.float32(-1.6666654611e-1)
        + square * (np.float32(8.3321608736e-3) + square * np.float32(-1.9515295891e-4))
    )
    cosine = (
        1.0
        - 0.5 * square
        + square
        * square
        * (
            np.float32(4.166664568298827e-2)
            + square
            * (np.float32(-1.388731625493765e-3) + square * np.float32(2.443315711809948e-5))
        )
    )
    quarter = turns.astype(jnp.int32) & 3
    swap = (quarter & 1) == 1
    cos_out = jnp.where(swap, sine, cosine)
    sin_out = jnp.where(swap, cosine, sine)
    cos_out = jnp.where((quarter == 1) | (quarter == 2), -cos_out, cos_out)
    sin_out = jnp.where(quarter >= 2, -sin_out, sin_out)
    return cos_out, sin_out


def rotate_heads(queries, position):
    head_dim = queries.shape[-1]
    half_dim = head_dim // 2
    frequency = (ROPE_BASE ** (-np.arange(half_dim) * 2.0 / head_dim)).astype(np.float32)
    cosine, sine = cosine_and_sine(position[:, None] * frequency[None, :])
    cosine = jnp.concatenate([cosine, cosine], axis=1)[:, None, :]
    sine = jnp.concatenate([-sine, sine], axis=1)[:, None, :]
    turned = jnp.concatenate([queries[..., half_dim:], queries[..., :half_dim]], axis=-1)
    return queries * cosine + turned * sine


def statement_ranges(lengths_row, order_row):
    stmt_count = order_row.shape[0]
    index = jnp.arange(stmt_count, dtype=jnp.int32)
    slot = jnp.sum(jnp.where(order_row[None, :] == index[:, None], index[None, :], 0), axis=1)
    start = jnp.sum(jnp.where(slot[None, :] < slot[:, None], lengths_row[None, :], 0), axis=1)
    return start, start + lengths_row


def block_attention(all_queries, cached_keys, cached_values, token_mask, score_scale):
    stmt_count, head_count, head_dim = all_queries.shape
    kv_heads = cached_keys.shape[1] // head_dim
    group_size = head_count // kv_heads
    grouped = all_queries.reshape(stmt_count, kv_heads, group_size, head_dim)
    key_heads = cached_keys.reshape(-1, kv_heads, head_dim)
    value_heads = cached_values.reshape(-1, kv_heads, head_dim)
    scores = (
        jnp.einsum("skgd,tkd->skgt", grouped, key_heads, preferred_element_type=jnp.float32)
        * score_scale
    )
    token_mask = token_mask[:, None, None, :]
    block_max = jnp.max(jnp.where(token_mask, scores, MASKED_LOGIT), axis=3)
    softmax_weights = jnp.where(token_mask, jnp.exp(scores - block_max[..., None]), 0.0)
    block_sum = jnp.sum(softmax_weights, axis=3)
    numerators = jnp.einsum(
        "skgt,tkd->skgd",
        softmax_weights.astype(jnp.bfloat16),
        value_heads,
        preferred_element_type=jnp.float32,
    )
    return (
        block_max.reshape(stmt_count, head_count),
        block_sum.reshape(stmt_count, head_count),
        numerators.reshape(stmt_count, head_count, head_dim),
    )


def flip(array, axis, offset):
    size = lax.axis_size(axis)
    return lax.ppermute(array, axis, [(i, i ^ offset) for i in range(size)])


def in_vmem(body, outputs, *operands, limit=8, flops=1_000_000):
    whole = pl.BlockSpec(memory_space=pltpu.VMEM)
    moved = sum(operand.size * operand.dtype.itemsize for operand in operands)
    return pl.pallas_call(
        body,
        out_shape=outputs,
        in_specs=[whole] * len(operands),
        out_specs=jax.tree.map(lambda _: whole, outputs),
        compiler_params=pltpu.CompilerParams(vmem_limit_bytes=limit << 20),
        cost_estimate=pl.CostEstimate(flops=flops, bytes_accessed=moved, transcendentals=0),
    )(*operands)


def shaped(shape, kind):
    return jax.ShapeDtypeStruct(shape, kind)


def open_window(out_ref):
    out_ref[...] = jnp.zeros_like(out_ref)


def prepare_inputs(window_ref, hidden_ref, gain_ref, message_ref):
    del window_ref
    inputs = hidden_ref[...].astype(jnp.float32)
    width = inputs.shape[1]
    message_ref[:, :width] = (inputs * gain_ref[...]).astype(jnp.bfloat16)
    message_ref[:, width:] = pack_statistics([jnp.sum(inputs * inputs, axis=1, keepdims=True)])


def positions_and_ranges(
    message_ref, frequency_ref, lengths_ref, order_ref, rope_ref, range_ref
):
    del message_ref
    count = lengths_ref.shape[1]
    half = frequency_ref.shape[1] // 2
    row = lax.broadcasted_iota(jnp.int32, (count, count), 0)
    column = lax.broadcasted_iota(jnp.int32, (count, count), 1)
    lengths = jnp.broadcast_to(lengths_ref[...], (count, count)).astype(jnp.float32)
    length = jnp.sum(jnp.where(row == column, lengths, 0.0), axis=1, keepdims=True)
    order = jnp.broadcast_to(order_ref[...], (count, count))
    placed = order == row
    slot = jnp.sum(jnp.where(placed, column, 0).astype(jnp.float32), axis=1, keepdims=True)
    packed = jnp.sum(jnp.where(placed, length, 0.0), axis=0, keepdims=True)
    earlier = column.astype(jnp.float32) < slot
    start = jnp.sum(jnp.where(earlier, packed, 0.0), axis=1, keepdims=True)
    range_ref[:, :128] = jnp.broadcast_to(start, (count, 128))
    range_ref[:, 128:] = jnp.broadcast_to(start + length, (count, 128))
    cosine, sine = cosine_and_sine((length - 1.0) * frequency_ref[...])
    lane = lax.broadcasted_iota(jnp.int32, cosine.shape, 1)
    rope_ref[:, : 2 * half] = cosine
    rope_ref[:, 2 * half :] = jnp.where(lane < half, -sine, sine)


LOG2_E = 1.4426950408889634


def pack_statistics(values):
    rows = values[0].shape[0]
    lane = lax.broadcasted_iota(jnp.int32, (rows, 128), 1)
    rest = jnp.zeros((rows, 128), jnp.float32)
    for place, value in enumerate(values):
        rest = jnp.where(lane == place, value, rest)
    out = rest.astype(jnp.bfloat16).astype(jnp.float32)
    for part in (1, 2):
        rest = rest - rest.astype(jnp.bfloat16).astype(jnp.float32)
        out = out + pltpu.roll(rest.astype(jnp.bfloat16).astype(jnp.float32), 32 * part, 1)
    return out.astype(jnp.bfloat16)


def unpack_statistics(block):
    block = block.astype(jnp.float32)
    return block + pltpu.roll(block, 96, 1) + pltpu.roll(block, 64, 1)


def core_number():
    return lax.axis_index("pack") & 1


def chip_number():
    return lax.axis_index("pack") >> 1


def send_across(array, axis, offset, sender):
    groups, pack = lax.axis_size("dp"), lax.axis_size("pack")
    pairs = []
    for group in range(groups):
        for place in range(pack):
            if place % 2 != sender:
                target = (group, place ^ 1)
            elif axis == "dp":
                target = (group ^ offset, place ^ 1)
            else:
                target = (group, place ^ (2 * offset) ^ 1)
            pairs.append((group * pack + place, target[0] * pack + target[1]))
    return lax.ppermute(array, ("dp", "pack"), pairs)


def copy_tokens(_, key_ref, value_ref, out_ref):
    out_ref[0] = key_ref[...]
    out_ref[1] = value_ref[...]


def join_cores(own_ref, other_ref, pair_ref):
    core = core_number()
    width = own_ref.shape[1] - 128
    refs = (own_ref, other_ref)
    squares = sum(unpack_statistics(ref[:, width:])[:, :1] for ref in refs)
    pair_ref[:, 2 * width :] = pack_statistics([squares])
    for first in range(2):

        @pl.when(core == first)
        def _():
            pair_ref[:, :width] = refs[first][:, :width]
            pair_ref[:, width : 2 * width] = refs[1 - first][:, :width]


def join_blocks(*refs):
    out_ref = refs[-1]
    count = out_ref.shape[0]
    for i in range(count):
        out_ref[count - 1 - i] = refs[i][...]


def project_pair(pair_ref, offset, weight_ref):
    chip = chip_number() ^ offset
    width = 2 * weight_ref.shape[1]
    rows = pl.ds(pl.multiple_of(chip * width, width), width)
    return jnp.dot(
        pair_ref[:, :width], weight_ref[rows, :], preferred_element_type=jnp.float32
    )


def project_own_pair(pair_ref, weight_ref, total_ref):
    total_ref[...] = project_pair(pair_ref, 0, weight_ref)


def make_queries(
    pair_ref, blocks_ref, total_ref, weight_ref, gain_ref, rope_ref, query_ref, *, core, model_width
):
    width = total_ref.shape[1]
    head_dim = gain_ref.shape[1]

    @pl.when(core_number() == core)
    def _():
        projected = total_ref[...]
        squares = unpack_statistics(pair_ref[:, 2 * width :])
        for i in range(blocks_ref.shape[0]):
            projected = projected + project_pair(blocks_ref.at[i], i + 1, weight_ref)
            squares = squares + unpack_statistics(blocks_ref[i, :, 2 * width :])
        squares = squares[:, :1]
        projected = projected * lax.rsqrt(squares / model_width + EPSILON)
        cosine = rope_ref[:, :head_dim]
        sine = rope_ref[:, head_dim:]
        for head in range(width // head_dim):
            place = slice(head * head_dim, (head + 1) * head_dim)
            query = projected[:, place]
            mean = jnp.mean(query * query, axis=1, keepdims=True)
            query = query * lax.rsqrt(mean + EPSILON) * gain_ref[...]
            turned = pltpu.roll(query, head_dim // 2, 1)
            query_ref[:, place] = (query * cosine + turned * sine).astype(jnp.bfloat16)


def join_queries(first_ref, second_ref, out_ref):
    width = first_ref.shape[1]
    out_ref[:, :width] = first_ref[...]
    out_ref[:, width:] = second_ref[...]


def token_masks(range_ref, tokens, group):
    me = lax.axis_index("pack")
    masks = []
    for owner in (me, me ^ 1):
        index = lax.broadcasted_iota(jnp.int32, (range_ref.shape[0], tokens), 1) + owner * tokens
        index = index.astype(jnp.float32)
        mask = (index >= range_ref[:, :1]) & (index < range_ref[:, 128:129])
        masks.append(jnp.concatenate([mask.astype(jnp.float32)] * group, axis=0) > 0.5)
    return masks


def attend_heads(queries, heads, key_ref, value_ref, other_ref, masks):
    head_dim = 128
    scale = head_dim**-0.5
    scores = []
    columns = []
    for query, head in zip(queries, heads):
        grouped = jnp.concatenate(
            [query[:, i : i + head_dim] for i in range(0, query.shape[1], head_dim)], axis=0
        )
        column = pl.ds(pl.multiple_of(head * head_dim, head_dim), head_dim)
        columns.append(column)
        raw = [
            lax.dot_general(
                grouped, keys, (((1,), (1,)), ((), ())), preferred_element_type=jnp.float32
            )
            for keys in (key_ref[:, column], other_ref[0, :, column])
        ]
        scores.append([jnp.where(mask, part, MASKED_LOGIT) for mask, part in zip(masks, raw)])
    maxima = [
        jnp.maximum(
            jnp.max(first, axis=1, keepdims=True), jnp.max(second, axis=1, keepdims=True)
        )
        for first, second in scores
    ]
    weights = [
        [jnp.exp2((part - highest) * (scale * LOG2_E)) for part in parts]
        for parts, highest in zip(scores, maxima)
    ]
    out = []
    for parts, highest, column in zip(weights, maxima, columns):
        total = jnp.sum(parts[0], axis=1, keepdims=True) + jnp.sum(
            parts[1], axis=1, keepdims=True
        )
        numerators = jnp.dot(
            parts[0].astype(jnp.bfloat16), value_ref[:, column], preferred_element_type=jnp.float32
        ) + jnp.dot(
            parts[1].astype(jnp.bfloat16),
            other_ref[1, :, column],
            preferred_element_type=jnp.float32,
        )
        out.append((highest * scale, total, numerators))
    return out


def attend_remote(query_ref, key_ref, value_ref, other_ref, range_ref, *refs, offset):
    out_ref = refs[-1]

    @pl.when(core_number() == 1)
    def _():
        rows = query_ref.shape[0]
        width = query_ref.shape[1] // 2
        masks = token_masks(range_ref, key_ref.shape[0], width // 128)
        chip = chip_number() ^ offset
        queries = [query_ref[:, :width], query_ref[:, width:]]
        heads = (2 * chip, 2 * chip + 1)
        parts = attend_heads(queries, heads, key_ref, value_ref, other_ref, masks)
        stats = []
        for j, (highest, total, numerators) in enumerate(parts):
            for h in range(width // 128):
                part = slice(h * rows, (h + 1) * rows)
                place = slice(j * width + h * 128, j * width + (h + 1) * 128)
                out_ref[:, place] = numerators[part].astype(jnp.bfloat16)
                stats += [highest[part], total[part]]
        out_ref[:, 2 * width :] = pack_statistics(stats)


def attend_own(query_ref, key_ref, value_ref, other_ref, range_ref, out_ref, stats_ref):
    @pl.when(core_number() == 0)
    def _():
        width = query_ref.shape[1] // 2
        masks = token_masks(range_ref, key_ref.shape[0], width // 128)
        chip = chip_number()
        parts = attend_heads(
            [query_ref[:, :width], query_ref[:, width:]],
            (2 * chip, 2 * chip + 1),
            key_ref,
            value_ref,
            other_ref,
            masks,
        )
        for j, (highest, total, numerators) in enumerate(parts):
            out_ref[j] = numerators
            stats_ref[j, :, :128] = jnp.broadcast_to(highest, (highest.shape[0], 128))
            stats_ref[j, :, 128:] = jnp.broadcast_to(total, (highest.shape[0], 128))


def merge_partials(third_ref, second_ref, first_ref, own_ref, stats_ref, *refs):
    attended_ref = refs[-1]

    @pl.when(core_number() == 0)
    def _():
        rows = attended_ref.shape[0]
        width = attended_ref.shape[1] // 2
        others = (first_ref, second_ref, third_ref)
        stats = [unpack_statistics(ref[:, 2 * width :]) for ref in others]
        for j in range(2):
            for h in range(width // 128):
                part = slice(h * rows, (h + 1) * rows)
                place = slice(j * width + h * 128, j * width + (h + 1) * 128)
                slot = 2 * (j * (width // 128) + h)
                maxima = [stats_ref[j, part, :1]] + [s[:, slot : slot + 1] for s in stats]
                totals = [stats_ref[j, part, 128:129]]
                totals += [s[:, slot + 1 : slot + 2] for s in stats]
                numerators = [own_ref[j, part, :]]
                numerators += [ref[:, place].astype(jnp.float32) for ref in others]
                highest = maxima[0]
                for value in maxima[1:]:
                    highest = jnp.maximum(highest, value)
                denominator = 0.0
                summed = 0.0
                for value, total, numerator in zip(maxima, totals, numerators):
                    factor = jnp.exp(value - highest)
                    denominator = denominator + total * factor
                    summed = summed + numerator * factor
                attended_ref[:, place] = (summed / denominator).astype(jnp.bfloat16)


def copy_weights(_, weight_ref, out_ref):
    out_ref[...] = weight_ref[...]


def project_out(attended_ref, weight_ref, other_weight_ref, *refs, offset):
    out_ref = refs[-1]

    @pl.when(core_number() == 0)
    def _():
        width = attended_ref.shape[1] // 2
        column = pl.ds(pl.multiple_of((chip_number() ^ offset) * 2 * width, 2 * width), 2 * width)
        total = jnp.dot(
            attended_ref[:, :width], weight_ref[:, column], preferred_element_type=jnp.float32
        ) + jnp.dot(
            attended_ref[:, width:], other_weight_ref[:, column], preferred_element_type=jnp.float32
        )
        out_ref[...] = total.astype(out_ref.dtype)


def finish_hidden(
    third_ref,
    second_ref,
    first_ref,
    kept_ref,
    own_ref,
    other_ref,
    own_gain_ref,
    other_gain_ref,
    sent_ref,
    scaled_ref,
    other_scaled_ref,
):
    width = own_ref.shape[1]

    @pl.when(core_number() == 1)
    def _():
        squares = 0.0
        inputs = (other_ref, own_ref)
        gains = (other_gain_ref, own_gain_ref)
        for core in range(2):
            place = slice(core * width, (core + 1) * width)
            hidden = inputs[core][...].astype(jnp.float32)
            for ref in (kept_ref, first_ref, second_ref, third_ref):
                hidden = hidden + ref[:, place].astype(jnp.float32)
            scaled = hidden * gains[core][...]
            (other_scaled_ref, scaled_ref)[core][...] = scaled
            sent_ref[:, place] = scaled.astype(jnp.bfloat16)
            squares = squares + jnp.sum(hidden * hidden, axis=1, keepdims=True)
        sent_ref[:, 2 * width :] = pack_statistics([squares])


def gram_part(third_ref, second_ref, first_ref, own_ref, _, out_ref, near_ref, far_ref):
    @pl.when(core_number() == 0)
    def _():
        rows = own_ref.shape[0]
        width = far_ref.shape[1]
        refs = (own_ref, first_ref, second_ref, third_ref)
        for i, ref in enumerate(refs):
            near_ref[i * rows : (i + 1) * rows] = ref[:, :width]
        for i, ref in enumerate(refs[1:]):
            far_ref[i * rows : (i + 1) * rows] = ref[:, width : 2 * width]
        far = jnp.concatenate([ref[:, width : 2 * width] for ref in refs], axis=0)
        squares = unpack_statistics(own_ref[:, 2 * width :])[:, :1]
        gram = 0.0
        for vectors in (near_ref[...], far):
            gram = gram + lax.dot_general(
                vectors, vectors, (((1,), (1,)), ((), ())), preferred_element_type=jnp.float32
            )
        half = gram.shape[0] // 2
        out_ref[:half, : 2 * half] = gram[:half]
        out_ref[:half, 2 * half :] = gram[half:]
        out_ref[half:, :] = jnp.broadcast_to(squares, (rows, 128))


def sum_grams(third_ref, second_ref, first_ref, own_ref, *refs):
    out_ref = refs[-1]
    out_ref[...] = own_ref[...] + first_ref[...] + second_ref[...] + third_ref[...]


def partner_masks(partner_ref, out_ref, *, rows):
    group = lax.axis_index("dp")
    shape = out_ref.shape[1:]
    row = lax.broadcasted_iota(jnp.int32, shape, 0)
    column = lax.broadcasted_iota(jnp.int32, shape, 1)
    row_id = ((group ^ (row // rows)) * rows) + row % rows
    column_id = ((group ^ (column // rows)) * rows) + column % rows
    partners = jnp.broadcast_to(partner_ref[...], shape)
    row_partner = jnp.sum(
        jnp.where(column == row_id, partners, 0).astype(jnp.float32), axis=1, keepdims=True
    )
    column_partner = jnp.sum(
        jnp.where(row_id == column_id, row_partner, 0.0), axis=0, keepdims=True
    )
    own_partner = column_id.astype(jnp.float32) == row_partner
    other_partner = row_id.astype(jnp.float32) == column_partner
    own_partner = own_partner.astype(jnp.float32)
    out_ref[0] = own_partner
    out_ref[1] = own_partner + other_partner.astype(jnp.float32)


def losses_and_gradient(
    summed_ref,
    other_summed_ref,
    near_ref,
    sent_ref,
    other_far_ref,
    scaled_ref,
    other_scaled_ref,
    gain_ref,
    partner_ref,
    pooled_ref,
    loss_ref,
    grad_ref,
    *,
    model_width,
):
    me = lax.axis_index("pack")
    first_core = core_number() == 0
    count, width = near_ref.shape
    rows = scaled_ref.shape[0]
    half = count // 2
    summed = jnp.where(first_core, other_summed_ref[...], summed_ref[...])
    gram = jnp.concatenate([summed[:half, :count], summed[:half, count:]], axis=0)
    squares = summed[half:, :1]
    shape = (count, count)
    row = lax.broadcasted_iota(jnp.int32, shape, 0)
    column = lax.broadcasted_iota(jnp.int32, shape, 1)
    diagonal = row == column
    on_diagonal = jnp.where(diagonal, gram, 0.0)
    row_scale = lax.rsqrt(jnp.sum(on_diagonal, axis=1, keepdims=True))
    column_scale = lax.rsqrt(jnp.sum(on_diagonal, axis=0, keepdims=True))
    cosines = gram * row_scale * column_scale
    logits = cosines * (1.0 / SOFTMAX_WARMTH)
    powers = jnp.where(diagonal, 0.0, jnp.exp(logits))
    row_sum = jnp.sum(powers, axis=1, keepdims=True)
    column_sum = jnp.sum(powers, axis=0, keepdims=True)
    weights = (powers * (1.0 / row_sum + 1.0 / column_sum) - partner_ref[1])[:rows]
    target = jnp.sum(partner_ref[0] * logits, axis=1, keepdims=True)
    loss = jnp.log(row_sum) - target
    own = loss_ref.shape[0]
    index = lax.broadcasted_iota(jnp.int32, (count, 1), 0)
    for i in range(own):
        loss_ref[i] = jnp.sum(jnp.where(index == me * own + i, loss, 0.0))
    inner = jnp.sum(weights * cosines[:rows], axis=1, keepdims=True)
    scaled_weights = weights * column_scale
    upper = scaled_weights.astype(jnp.bfloat16)
    lower = (scaled_weights - upper.astype(jnp.float32)).astype(jnp.bfloat16)
    own_scale = row_scale[:rows]
    pooled_scale = lax.rsqrt(squares / model_width + EPSILON)
    grad_gain = gain_ref[...] * (model_width**0.5 / SOFTMAX_WARMTH)

    def write(vectors, scaled):
        gradient = jnp.dot(upper, vectors, preferred_element_type=jnp.float32) + jnp.dot(
            lower, vectors, preferred_element_type=jnp.float32
        )
        gradient = (gradient - scaled * (own_scale * inner)) * own_scale
        grad_ref[...] = (gradient * grad_gain).astype(jnp.bfloat16)
        pooled_ref[...] = (scaled * pooled_scale).astype(jnp.bfloat16)

    @pl.when(first_core)
    def _():
        write(near_ref[...], other_scaled_ref[...])

    @pl.when(core_number() == 1)
    def _():
        vectors = jnp.concatenate((sent_ref[:, width : 2 * width], other_far_ref[...]), axis=0)
        write(vectors, scaled_ref[...])


def core_roles(
    hidden_in,
    attn_gain,
    w_query,
    query_gain,
    cached_keys,
    cached_values,
    w_out,
    final_gain,
    lengths,
    pack_order,
    partner,
):
    pack_size = lax.axis_size("pack")
    stmts, width = hidden_in.shape
    model_width = width * pack_size
    head_dim = query_gain.shape[0]
    tokens = cached_keys.shape[0]
    chips = pack_size // 2
    others = range(1, chips)
    total = partner.shape[0]
    bf16 = jnp.bfloat16
    f32 = jnp.float32
    final_gain = final_gain[None]
    query_gain = query_gain[None]
    half = np.arange(head_dim // 2)
    frequency = (ROPE_BASE ** (-half * 2.0 / head_dim)).astype(np.float32)
    frequency = jnp.asarray(np.concatenate([frequency, frequency])[None])
    whole = pl.BlockSpec(memory_space=pltpu.VMEM)

    window = pl.pallas_call(
        open_window,
        out_shape=shaped((8, 128), f32),
        out_specs=whole,
        compiler_params=pltpu.CompilerParams(vmem_limit_bytes=1 << 20),
        cost_estimate=pl.CostEstimate(flops=1 << 34, bytes_accessed=0, transcendentals=0),
    )()
    message = in_vmem(
        prepare_inputs, shaped((stmts, width + 128), bf16), window, hidden_in, attn_gain[None]
    )
    pair = in_vmem(
        join_cores, shaped((stmts, 2 * width + 128), bf16), message, flip(message, "pack", 1)
    )
    received = [send_across(pair, "pack", k, 0) for k in others]
    own_projected = in_vmem(
        project_own_pair, shaped((stmts, width), f32), pair, w_query, limit=16, flops=1 << 26
    )
    rope, ranges = in_vmem(
        positions_and_ranges,
        (shaped((stmts, 2 * head_dim), f32), shaped((stmts, 256), f32)),
        message,
        frequency,
        lengths,
        pack_order,
    )
    blocks = in_vmem(
        join_blocks, shaped((chips - 1,) + pair.shape, bf16), *received[::-1], own_projected, rope
    )
    flipped_blocks = flip(blocks, "pack", 1)

    def queries_on(core, blocks, flops):
        return in_vmem(
            lambda *refs: make_queries(*refs, core=core, model_width=model_width),
            shaped((stmts, width), bf16),
            pair,
            blocks,
            own_projected,
            w_query,
            query_gain,
            rope,
            limit=16,
            flops=flops,
        )

    late_queries = queries_on(1, blocks, 1 << 27)
    held = in_vmem(
        copy_tokens,
        shaped((2,) + cached_keys.shape, bf16),
        late_queries,
        cached_keys,
        cached_values,
    )
    other_held = flip(held, "pack", 1)
    second_queries = flip(late_queries, "pack", 1)
    first_queries = queries_on(0, flipped_blocks, 1 << 36)
    queries = in_vmem(
        join_queries, shaped((stmts, 2 * width), bf16), first_queries, second_queries
    )
    other_weights = flip(
        in_vmem(copy_weights, shaped(w_out.shape, bf16), queries, w_out, limit=16), "pack", 1
    )
    received = [send_across(queries, "pack", k, 0) for k in others]
    group_rows = stmts * (width // head_dim)
    own_part, own_stats = in_vmem(
        attend_own,
        (shaped((2, group_rows, head_dim), f32), shaped((2, group_rows, 256), f32)),
        queries,
        cached_keys,
        cached_values,
        other_held,
        ranges,
        flops=1 << 27,
    )
    partials = []
    for k, part in zip(others[::-1], received[::-1]):
        partials.append(
            in_vmem(
                lambda *refs, offset=k: attend_remote(*refs, offset=offset),
                shaped((stmts, 2 * width + 128), bf16),
                part,
                cached_keys,
                cached_values,
                other_held,
                ranges,
                *partials[-1:],
                flops=1 << 34,
            )
        )
    received = [send_across(part, "pack", k, 1) for k, part in zip(others, partials[::-1])]
    other_hidden_in = flip(hidden_in, "pack", 1)
    other_gain = flip(final_gain, "pack", 1)
    attended = in_vmem(
        merge_partials,
        shaped((stmts, 2 * width), bf16),
        *received[::-1],
        own_part,
        own_stats,
        other_hidden_in,
        other_gain,
    )

    def projected_to(offset, kind, *after):
        return in_vmem(
            lambda *refs: project_out(*refs, offset=offset),
            shaped((stmts, 2 * width), kind),
            attended,
            w_out,
            other_weights,
            *after,
            limit=16,
            flops=1 << 27,
        )

    third = projected_to(3, bf16)
    second = projected_to(2, bf16, third)
    first = projected_to(1, bf16, second)
    kept = projected_to(0, bf16, first)
    received = [send_across(part, "pack", k, 0) for k, part in zip(others, (first, second, third))]
    vector, scaled, far_scaled = in_vmem(
        finish_hidden,
        (shaped((stmts, 2 * width + 128), bf16),) + (shaped((stmts, width), f32),) * 2,
        *received[::-1],
        flip(kept, "pack", 1),
        hidden_in,
        other_hidden_in,
        final_gain,
        other_gain,
    )
    received = [send_across(vector, "dp", k, 1) for k in range(1, lax.axis_size("dp"))]
    other_scaled = flip(far_scaled, "pack", 1)
    gram, near, far = in_vmem(
        gram_part,
        (
            shaped((total // 2 + stmts, 128), f32),
            shaped((total, width), bf16),
            shaped((total - stmts, width), bf16),
        ),
        *received[::-1],
        flip(vector, "pack", 1),
        other_scaled,
    )
    received = [send_across(gram, "pack", k, 0) for k in others]
    other_far = flip(far, "pack", 1)
    summed = in_vmem(
        sum_grams,
        shaped(gram.shape, f32),
        *received[::-1],
        flip(gram, "pack", 1),
    )
    masks = in_vmem(
        lambda *refs: partner_masks(*refs, rows=stmts),
        shaped((2, total, total), f32),
        partner[None],
    )
    pooled, loss_rows, grad_hidden = pl.pallas_call(
        lambda *refs: losses_and_gradient(*refs, model_width=model_width),
        out_shape=(
            shaped((stmts, width), bf16),
            shaped((stmts // pack_size,), f32),
            shaped((stmts, width), bf16),
        ),
        in_specs=[whole] * 9,
        out_specs=(whole, pl.BlockSpec(memory_space=pltpu.SMEM), whole),
        compiler_params=pltpu.CompilerParams(vmem_limit_bytes=8 << 20),
    )(
        summed,
        flip(summed, "pack", 1),
        near,
        vector,
        other_far,
        scaled,
        other_scaled,
        final_gain,
        masks,
    )
    return (pooled, loss_rows, grad_hidden)


def local(
    hidden_in,
    attn_gain,
    w_query,
    query_gain,
    cached_keys,
    cached_values,
    w_out,
    final_gain,
    lengths,
    pack_order,
    partner,
):
    pack_size = lax.axis_size("pack")
    pack_index = lax.axis_index("pack")
    group_index = lax.axis_index("dp")
    stmt_count, feature_count = hidden_in.shape
    model_width = feature_count * pack_size
    head_dim = query_gain.shape[0]
    local_heads = w_query.shape[1] // head_dim
    token_count = cached_keys.shape[0]
    total_stmts = partner.shape[0]
    lengths_row = lengths[0]
    order_row = pack_order[0]
    inputs32 = hidden_in.astype(jnp.float32)

    scaled = (inputs32 * attn_gain[None, :]).astype(jnp.bfloat16)
    squares = split_float(jnp.sum(inputs32 * inputs32, axis=1), 3)
    extra = jnp.stack(squares + [jnp.zeros_like(squares[0])] * 125, axis=1)
    arrived = gather_blocks(jnp.concatenate([scaled, extra], axis=1), "pack")
    input_squares = jnp.sum(arrived[:, :, feature_count : feature_count + 3].astype(jnp.float32), axis=(0, 2))
    input_rms = lax.rsqrt(input_squares / model_width + EPSILON)
    features = jnp.moveaxis(arrived[:, :, :feature_count], 0, 1).reshape(stmt_count, model_width)
    projected = jnp.dot(features, w_query, preferred_element_type=jnp.float32)
    queries = (projected * input_rms[:, None]).reshape(stmt_count, local_heads, head_dim)
    queries = (
        queries
        * lax.rsqrt(jnp.mean(queries * queries, axis=2, keepdims=True) + EPSILON)
        * query_gain
    )
    queries = rotate_heads(queries, (lengths_row - 1).astype(jnp.float32)).astype(jnp.bfloat16)
    all_queries = jnp.moveaxis(gather_blocks(queries, "pack"), 0, 1).reshape(
        stmt_count, pack_size * local_heads, head_dim
    )
    start, end = statement_ranges(lengths_row, order_row)
    tokens = pack_index * token_count + jnp.arange(token_count, dtype=jnp.int32)
    token_mask = (tokens[None, :] >= start[:, None]) & (tokens[None, :] < end[:, None])
    block_max, block_sum, numerators = block_attention(
        all_queries, cached_keys, cached_values, token_mask, head_dim ** (-0.5)
    )

    def by_owner(part):
        return jnp.moveaxis(part.reshape((stmt_count, pack_size, -1)), 1, 0)

    message = jnp.concatenate(
        [by_owner(numerators.astype(jnp.bfloat16))]
        + [by_owner(piece) for piece in split_float(block_max, 3) + split_float(block_sum, 2)],
        axis=2,
    )
    message = lax.all_to_all(message, "pack", 0, 0)
    width = local_heads * head_dim
    stats = message[:, :, width:].astype(jnp.float32).reshape(pack_size, stmt_count, 5, local_heads)
    maxima = stats[:, :, 0] + stats[:, :, 1] + stats[:, :, 2]
    factor = jnp.exp(maxima - jnp.max(maxima, axis=0, keepdims=True))
    denominator = jnp.sum((stats[:, :, 3] + stats[:, :, 4]) * factor, axis=0)
    numerators = message[:, :, :width].astype(jnp.float32).reshape(pack_size, stmt_count, local_heads, head_dim)
    summed = jnp.sum(numerators * factor[..., None], axis=0)
    attended = (summed / denominator[..., None]).astype(jnp.bfloat16)
    partial_out = jnp.dot(
        attended.reshape(stmt_count, width), w_out, preferred_element_type=jnp.float32
    )
    partial_out = jnp.moveaxis(
        partial_out.astype(jnp.bfloat16).reshape(stmt_count, pack_size, feature_count), 1, 0
    )
    partial_out = lax.all_to_all(partial_out, "pack", 0, 0)
    hidden = inputs32 + jnp.sum(partial_out.astype(jnp.float32), axis=0)
    scaled_out = hidden * final_gain[None, :]
    vectors = lax.all_gather(scaled_out.astype(jnp.bfloat16), "dp", axis=0, tiled=True)
    gram = lax.dot_general(
        vectors, vectors, (((1,), (1,)), ((), ())), preferred_element_type=jnp.float32
    )
    own_squares = jnp.sum(hidden * hidden, axis=1)
    extra = jnp.zeros((total_stmts,), jnp.float32).at[:stmt_count].set(own_squares)
    gram = jnp.concatenate([gram, extra[:, None]], axis=1)
    if total_stmts <= 128:
        gram = jnp.sum(gather_blocks(gram, "pack"), axis=0)
    else:
        gram = lax.psum(gram, "pack")
    hidden_rms = jnp.sqrt(gram[:stmt_count, total_stmts] / model_width + EPSILON)
    gram = gram[:, :total_stmts]
    column_ids = jnp.arange(total_stmts, dtype=jnp.int32)
    diagonal = column_ids[:, None] == column_ids[None, :]
    norms_row = lax.rsqrt(jnp.sum(jnp.where(diagonal, gram, 0.0), axis=0))
    norms_column = lax.rsqrt(jnp.sum(jnp.where(diagonal, gram, 0.0), axis=1))
    cosines = gram * norms_column[:, None] * norms_row[None, :]
    logits = jnp.where(diagonal, MASKED_LOGIT, cosines / SOFTMAX_WARMTH)
    highest = jnp.max(logits, axis=1)
    all_lse = highest + jnp.log(jnp.sum(jnp.exp(logits - highest[:, None]), axis=1))
    is_partner = column_ids[None, :] == partner[:, None]
    all_loss = all_lse - jnp.sum(jnp.where(is_partner, logits, 0.0), axis=1)
    own_count = stmt_count // pack_size
    row_base = group_index * stmt_count
    loss_rows = lax.dynamic_slice_in_dim(all_loss, row_base + pack_index * own_count, own_count, 0)
    weights = (
        jnp.exp(logits - all_lse[:, None])
        + jnp.exp(logits - all_lse[None, :])
        - is_partner.astype(jnp.float32)
        - is_partner.T.astype(jnp.float32)
    ).astype(jnp.bfloat16)
    own_weights = lax.dynamic_slice_in_dim(weights, row_base, stmt_count, 0)
    own_cosines = lax.dynamic_slice_in_dim(cosines, row_base, stmt_count, 0)
    own_norm = lax.dynamic_slice_in_dim(norms_column, row_base, stmt_count, 0)
    inner = jnp.sum(own_weights.astype(jnp.float32) * own_cosines, axis=1)
    own_norm = own_norm[:, None]
    embeddings = (vectors.astype(jnp.float32) * norms_column[:, None]).astype(jnp.bfloat16)
    gradient = jnp.dot(own_weights, embeddings, preferred_element_type=jnp.float32)
    scale = model_width**0.5 / SOFTMAX_WARMTH
    pooled = (scaled_out / hidden_rms[:, None]).astype(jnp.bfloat16)
    grad_hidden = (
        scale * final_gain[None, :] * (gradient - scaled_out * own_norm * inner[:, None]) * own_norm
    ).astype(jnp.bfloat16)
    return (pooled, loss_rows, grad_hidden)


def solution(mesh):
    body = core_roles if mesh.shape["pack"] == 8 and mesh.shape["dp"] == 4 else local
    in_specs = (
        P("dp", "pack"),
        P("pack"),
        P(None, "pack"),
        P(),
        P(("dp", "pack"), None),
        P(("dp", "pack"), None),
        P("pack", None),
        P("pack"),
        P("dp", None),
        P("dp", None),
        P(),
    )
    out_specs = (P("dp", "pack"), P(("dp", "pack")), P("dp", "pack"))
    return jax.shard_map(body, mesh=mesh, in_specs=in_specs, out_specs=out_specs, check_vma=False)
```

```python
import numpy as np
import jax
import jax.numpy as jnp
from jax import lax
from jax.experimental import pallas as pl
from jax.experimental.pallas import tpu as pltpu
from jax.sharding import PartitionSpec as P

EPSILON = 1e-06
SOFTMAX_WARMTH = 0.05
ROPE_BASE = 1000000.0
MASKED_LOGIT = -1e30


def gather_blocks(block, axis):
    size = lax.axis_size(axis)
    return lax.all_to_all(jnp.broadcast_to(block[None], (size,) + block.shape), axis, 0, 0)


def split_float(value, pieces):
    out = []
    for _ in range(pieces):
        piece = lax.reduce_precision(value, 8, 7)
        out.append(piece.astype(jnp.bfloat16))
        value = value - piece
    return out


def cosine_and_sine(angles):
    turns = jnp.round(angles * np.float32(2.0 / np.pi))
    rest = angles - turns * np.float32(1.5703125)
    rest = rest - turns * np.float32(4.837512969970703125e-4)
    rest = rest - turns * np.float32(7.549789948768648e-8)
    square = rest * rest
    sine = rest + rest * square * (
        np.float32(-1.6666654611e-1)
        + square * (np.float32(8.3321608736e-3) + square * np.float32(-1.9515295891e-4))
    )
    cosine = (
        1.0
        - 0.5 * square
        + square
        * square
        * (
            np.float32(4.166664568298827e-2)
            + square
            * (np.float32(-1.388731625493765e-3) + square * np.float32(2.443315711809948e-5))
        )
    )
    quarter = turns.astype(jnp.int32) & 3
    swap = (quarter & 1) == 1
    cos_out = jnp.where(swap, sine, cosine)
    sin_out = jnp.where(swap, cosine, sine)
    cos_out = jnp.where((quarter == 1) | (quarter == 2), -cos_out, cos_out)
    sin_out = jnp.where(quarter >= 2, -sin_out, sin_out)
    return cos_out, sin_out


def rotate_heads(queries, position):
    head_dim = queries.shape[-1]
    half_dim = head_dim // 2
    frequency = (ROPE_BASE ** (-np.arange(half_dim) * 2.0 / head_dim)).astype(np.float32)
    cosine, sine = cosine_and_sine(position[:, None] * frequency[None, :])
    cosine = jnp.concatenate([cosine, cosine], axis=1)[:, None, :]
    sine = jnp.concatenate([-sine, sine], axis=1)[:, None, :]
    turned = jnp.concatenate([queries[..., half_dim:], queries[..., :half_dim]], axis=-1)
    return queries * cosine + turned * sine


def statement_ranges(lengths_row, order_row):
    stmt_count = order_row.shape[0]
    index = jnp.arange(stmt_count, dtype=jnp.int32)
    slot = jnp.sum(jnp.where(order_row[None, :] == index[:, None], index[None, :], 0), axis=1)
    start = jnp.sum(jnp.where(slot[None, :] < slot[:, None], lengths_row[None, :], 0), axis=1)
    return start, start + lengths_row


def block_attention(all_queries, cached_keys, cached_values, token_mask, score_scale):
    stmt_count, head_count, head_dim = all_queries.shape
    kv_heads = cached_keys.shape[1] // head_dim
    group_size = head_count // kv_heads
    grouped = all_queries.reshape(stmt_count, kv_heads, group_size, head_dim)
    key_heads = cached_keys.reshape(-1, kv_heads, head_dim)
    value_heads = cached_values.reshape(-1, kv_heads, head_dim)
    scores = (
        jnp.einsum("skgd,tkd->skgt", grouped, key_heads, preferred_element_type=jnp.float32)
        * score_scale
    )
    token_mask = token_mask[:, None, None, :]
    block_max = jnp.max(jnp.where(token_mask, scores, MASKED_LOGIT), axis=3)
    softmax_weights = jnp.where(token_mask, jnp.exp(scores - block_max[..., None]), 0.0)
    block_sum = jnp.sum(softmax_weights, axis=3)
    numerators = jnp.einsum(
        "skgt,tkd->skgd",
        softmax_weights.astype(jnp.bfloat16),
        value_heads,
        preferred_element_type=jnp.float32,
    )
    return (
        block_max.reshape(stmt_count, head_count),
        block_sum.reshape(stmt_count, head_count),
        numerators.reshape(stmt_count, head_count, head_dim),
    )


def flip(array, axis, offset):
    size = lax.axis_size(axis)
    return lax.ppermute(array, axis, [(i, i ^ offset) for i in range(size)])


def in_vmem(body, outputs, *operands, limit=8, flops=1_000_000):
    whole = pl.BlockSpec(memory_space=pltpu.VMEM)
    moved = sum(operand.size * operand.dtype.itemsize for operand in operands)
    return pl.pallas_call(
        body,
        out_shape=outputs,
        in_specs=[whole] * len(operands),
        out_specs=jax.tree.map(lambda _: whole, outputs),
        compiler_params=pltpu.CompilerParams(vmem_limit_bytes=limit << 20),
        cost_estimate=pl.CostEstimate(flops=flops, bytes_accessed=moved, transcendentals=0),
    )(*operands)


def shaped(shape, kind):
    return jax.ShapeDtypeStruct(shape, kind)


def open_window(out_ref):
    out_ref[...] = jnp.zeros_like(out_ref)


def prepare_inputs(window_ref, hidden_ref, gain_ref, message_ref):
    del window_ref
    inputs = hidden_ref[...].astype(jnp.float32)
    width = inputs.shape[1]
    message_ref[:, :width] = (inputs * gain_ref[...]).astype(jnp.bfloat16)
    message_ref[:, width:] = pack_statistics(
        [jnp.sum(inputs * inputs, axis=1, keepdims=True)], core_number()
    )


def positions_and_ranges(
    message_ref, frequency_ref, lengths_ref, order_ref, rope_ref, range_ref
):
    del message_ref
    count = lengths_ref.shape[1]
    half = frequency_ref.shape[1] // 2
    row = lax.broadcasted_iota(jnp.int32, (count, count), 0)
    column = lax.broadcasted_iota(jnp.int32, (count, count), 1)
    lengths = jnp.broadcast_to(lengths_ref[...], (count, count)).astype(jnp.float32)
    length = jnp.sum(jnp.where(row == column, lengths, 0.0), axis=1, keepdims=True)
    order = jnp.broadcast_to(order_ref[...], (count, count))
    placed = order == row
    slot = jnp.sum(jnp.where(placed, column, 0).astype(jnp.float32), axis=1, keepdims=True)
    packed = jnp.sum(jnp.where(placed, length, 0.0), axis=0, keepdims=True)
    earlier = column.astype(jnp.float32) < slot
    start = jnp.sum(jnp.where(earlier, packed, 0.0), axis=1, keepdims=True)
    range_ref[:, :128] = jnp.broadcast_to(start, (count, 128))
    range_ref[:, 128:] = jnp.broadcast_to(start + length, (count, 128))
    cosine, sine = cosine_and_sine((length - 1.0) * frequency_ref[...])
    lane = lax.broadcasted_iota(jnp.int32, cosine.shape, 1)
    rope_ref[:, : 2 * half] = cosine
    rope_ref[:, 2 * half :] = jnp.where(lane < half, -sine, sine)


LOG2_E = 1.4426950408889634


def pack_statistics(values, first=0):
    rows = values[0].shape[0]
    lane = lax.broadcasted_iota(jnp.int32, (rows, 128), 1)
    rest = jnp.zeros((rows, 128), jnp.float32)
    for place, value in enumerate(values):
        rest = jnp.where(lane == first + place, value, rest)
    out = rest.astype(jnp.bfloat16).astype(jnp.float32)
    for part in (1, 2):
        rest = rest - rest.astype(jnp.bfloat16).astype(jnp.float32)
        out = out + pltpu.roll(rest.astype(jnp.bfloat16).astype(jnp.float32), 32 * part, 1)
    return out.astype(jnp.bfloat16)


def read_statistic(block, first, count=1):
    lane = lax.broadcasted_iota(jnp.int32, block.shape, 1)
    place = (lane & 31) - first
    mine = (place >= 0) & (place < count) & (lane < 96)
    return jnp.sum(jnp.where(mine, block.astype(jnp.float32), 0.0), axis=1, keepdims=True)


def core_number():
    return lax.axis_index("pack") & 1


def chip_number():
    return lax.axis_index("pack") >> 1


def send_across(array, axis, offset, sender):
    groups, pack = lax.axis_size("dp"), lax.axis_size("pack")
    pairs = []
    for group in range(groups):
        for place in range(pack):
            if place % 2 != sender:
                target = (group, place ^ 1)
            elif axis == "dp":
                target = (group ^ offset, place ^ 1)
            else:
                target = (group, place ^ (2 * offset) ^ 1)
            pairs.append((group * pack + place, target[0] * pack + target[1]))
    return lax.ppermute(array, ("dp", "pack"), pairs)


def copy_tokens(_, key_ref, value_ref, out_ref):
    out_ref[0] = key_ref[...]
    out_ref[1] = value_ref[...]


def join_cores(own_ref, other_ref, pair_ref):
    core = core_number()
    width = own_ref.shape[1] - 128
    refs = (own_ref, other_ref)
    pair_ref[:, 2 * width :] = own_ref[:, width:] + other_ref[:, width:]
    for first in range(2):

        @pl.when(core == first)
        def _():
            pair_ref[:, :width] = refs[first][:, :width]
            pair_ref[:, width : 2 * width] = refs[1 - first][:, :width]


def join_blocks(*refs):
    out_ref = refs[-1]
    count = out_ref.shape[0]
    for i in range(count):
        out_ref[count - 1 - i] = refs[i][...]


def project_pair(pair_ref, offset, weight_ref):
    chip = chip_number() ^ offset
    width = 2 * weight_ref.shape[1]
    rows = pl.ds(pl.multiple_of(chip * width, width), width)
    return jnp.dot(
        pair_ref[:, :width], weight_ref[rows, :], preferred_element_type=jnp.float32
    )


def project_own_pair(pair_ref, weight_ref, total_ref):
    total_ref[...] = project_pair(pair_ref, 0, weight_ref)


def make_queries(
    pair_ref, blocks_ref, total_ref, weight_ref, gain_ref, rope_ref, query_ref, *, core, model_width
):
    width = total_ref.shape[1]
    head_dim = gain_ref.shape[1]

    @pl.when(core_number() == core)
    def _():
        projected = total_ref[...]
        squares = pair_ref[:, 2 * width :].astype(jnp.float32)
        for i in range(blocks_ref.shape[0]):
            projected = projected + project_pair(blocks_ref.at[i], i + 1, weight_ref)
            squares = squares + blocks_ref[i, :, 2 * width :].astype(jnp.float32)
        squares = read_statistic(squares, 0, 2)
        projected = projected * lax.rsqrt(squares / model_width + EPSILON)
        cosine = rope_ref[:, :head_dim]
        sine = rope_ref[:, head_dim:]
        for head in range(width // head_dim):
            place = slice(head * head_dim, (head + 1) * head_dim)
            query = projected[:, place]
            mean = jnp.mean(query * query, axis=1, keepdims=True)
            query = query * lax.rsqrt(mean + EPSILON) * gain_ref[...]
            turned = pltpu.roll(query, head_dim // 2, 1)
            query_ref[:, place] = (query * cosine + turned * sine).astype(jnp.bfloat16)


def join_queries(first_ref, second_ref, out_ref):
    width = first_ref.shape[1]
    out_ref[:, :width] = first_ref[...]
    out_ref[:, width:] = second_ref[...]


def token_masks(range_ref, tokens, group):
    me = lax.axis_index("pack")
    masks = []
    for owner in (me, me ^ 1):
        index = lax.broadcasted_iota(jnp.int32, (range_ref.shape[0], tokens), 1) + owner * tokens
        index = index.astype(jnp.float32)
        mask = (index >= range_ref[:, :1]) & (index < range_ref[:, 128:129])
        masks.append(jnp.concatenate([mask.astype(jnp.float32)] * group, axis=0) > 0.5)
    return masks


def attend_heads(queries, heads, key_ref, value_ref, other_ref, masks):
    head_dim = 128
    scale = head_dim**-0.5
    scores = []
    columns = []
    for query, head in zip(queries, heads):
        grouped = jnp.concatenate(
            [query[:, i : i + head_dim] for i in range(0, query.shape[1], head_dim)], axis=0
        )
        column = pl.ds(pl.multiple_of(head * head_dim, head_dim), head_dim)
        columns.append(column)
        raw = [
            lax.dot_general(
                grouped, keys, (((1,), (1,)), ((), ())), preferred_element_type=jnp.float32
            )
            for keys in (key_ref[:, column], other_ref[0, :, column])
        ]
        scores.append([jnp.where(mask, part, MASKED_LOGIT) for mask, part in zip(masks, raw)])
    maxima = [
        jnp.maximum(
            jnp.max(first, axis=1, keepdims=True), jnp.max(second, axis=1, keepdims=True)
        )
        for first, second in scores
    ]
    weights = [
        [jnp.exp2((part - highest) * (scale * LOG2_E)) for part in parts]
        for parts, highest in zip(scores, maxima)
    ]
    out = []
    for parts, highest, column in zip(weights, maxima, columns):
        total = jnp.sum(parts[0], axis=1, keepdims=True) + jnp.sum(
            parts[1], axis=1, keepdims=True
        )
        numerators = jnp.dot(
            parts[0].astype(jnp.bfloat16), value_ref[:, column], preferred_element_type=jnp.float32
        ) + jnp.dot(
            parts[1].astype(jnp.bfloat16),
            other_ref[1, :, column],
            preferred_element_type=jnp.float32,
        )
        out.append((highest * scale, total, numerators))
    return out


def attend_remote(query_ref, key_ref, value_ref, other_ref, range_ref, *refs, offset):
    out_ref = refs[-1]

    @pl.when(core_number() == 1)
    def _():
        rows = query_ref.shape[0]
        width = query_ref.shape[1] // 2
        masks = token_masks(range_ref, key_ref.shape[0], width // 128)
        chip = chip_number() ^ offset
        queries = [query_ref[:, :width], query_ref[:, width:]]
        heads = (2 * chip, 2 * chip + 1)
        parts = attend_heads(queries, heads, key_ref, value_ref, other_ref, masks)
        stats = []
        for j, (highest, total, numerators) in enumerate(parts):
            for h in range(width // 128):
                part = slice(h * rows, (h + 1) * rows)
                place = slice(j * width + h * 128, j * width + (h + 1) * 128)
                out_ref[:, place] = numerators[part].astype(jnp.bfloat16)
                stats += [highest[part], total[part]]
        out_ref[:, 2 * width :] = pack_statistics(stats)


def attend_own(query_ref, key_ref, value_ref, other_ref, range_ref, out_ref, stats_ref):
    @pl.when(core_number() == 0)
    def _():
        width = query_ref.shape[1] // 2
        masks = token_masks(range_ref, key_ref.shape[0], width // 128)
        chip = chip_number()
        parts = attend_heads(
            [query_ref[:, :width], query_ref[:, width:]],
            (2 * chip, 2 * chip + 1),
            key_ref,
            value_ref,
            other_ref,
            masks,
        )
        for j, (highest, total, numerators) in enumerate(parts):
            out_ref[j] = numerators
            stats_ref[j, :, :128] = jnp.broadcast_to(highest, (highest.shape[0], 128))
            stats_ref[j, :, 128:] = jnp.broadcast_to(total, (highest.shape[0], 128))


def merge_partials(third_ref, second_ref, first_ref, own_ref, stats_ref, *refs):
    attended_ref = refs[-1]

    @pl.when(core_number() == 0)
    def _():
        rows = attended_ref.shape[0]
        width = attended_ref.shape[1] // 2
        others = (first_ref, second_ref, third_ref)
        stats = [ref[:, 2 * width :] for ref in others]
        for j in range(2):
            for h in range(width // 128):
                part = slice(h * rows, (h + 1) * rows)
                place = slice(j * width + h * 128, j * width + (h + 1) * 128)
                slot = 2 * (j * (width // 128) + h)
                maxima = [stats_ref[j, part, :1]] + [read_statistic(s, slot) for s in stats]
                totals = [stats_ref[j, part, 128:129]]
                totals += [read_statistic(s, slot + 1) for s in stats]
                numerators = [own_ref[j, part, :]]
                numerators += [ref[:, place].astype(jnp.float32) for ref in others]
                highest = maxima[0]
                for value in maxima[1:]:
                    highest = jnp.maximum(highest, value)
                denominator = 0.0
                summed = 0.0
                for value, total, numerator in zip(maxima, totals, numerators):
                    factor = jnp.exp(value - highest)
                    denominator = denominator + total * factor
                    summed = summed + numerator * factor
                attended_ref[:, place] = (summed / denominator).astype(jnp.bfloat16)


def copy_weights(_, weight_ref, out_ref):
    out_ref[...] = weight_ref[...]


def project_out(attended_ref, weight_ref, other_weight_ref, *refs, offset):
    out_ref = refs[-1]

    @pl.when(core_number() == 0)
    def _():
        width = attended_ref.shape[1] // 2
        column = pl.ds(pl.multiple_of((chip_number() ^ offset) * 2 * width, 2 * width), 2 * width)
        total = jnp.dot(
            attended_ref[:, :width], weight_ref[:, column], preferred_element_type=jnp.float32
        ) + jnp.dot(
            attended_ref[:, width:], other_weight_ref[:, column], preferred_element_type=jnp.float32
        )
        out_ref[...] = total.astype(out_ref.dtype)


def finish_hidden(
    third_ref,
    second_ref,
    first_ref,
    kept_ref,
    own_ref,
    other_ref,
    own_gain_ref,
    other_gain_ref,
    sent_ref,
    scaled_ref,
    other_scaled_ref,
):
    width = own_ref.shape[1]

    @pl.when(core_number() == 1)
    def _():
        squares = 0.0
        inputs = (other_ref, own_ref)
        gains = (other_gain_ref, own_gain_ref)
        for core in range(2):
            place = slice(core * width, (core + 1) * width)
            hidden = inputs[core][...].astype(jnp.float32)
            for ref in (kept_ref, first_ref, second_ref, third_ref):
                hidden = hidden + ref[:, place].astype(jnp.float32)
            scaled = hidden * gains[core][...]
            (other_scaled_ref, scaled_ref)[core][...] = scaled
            sent_ref[:, place] = scaled.astype(jnp.bfloat16)
            squares = squares + jnp.sum(hidden * hidden, axis=1, keepdims=True)
        sent_ref[:, 2 * width :] = pack_statistics([squares])


def gram_part(third_ref, second_ref, first_ref, own_ref, _, out_ref, near_ref, far_ref):
    @pl.when(core_number() == 0)
    def _():
        rows = own_ref.shape[0]
        width = far_ref.shape[1]
        refs = (own_ref, first_ref, second_ref, third_ref)
        for i, ref in enumerate(refs):
            near_ref[i * rows : (i + 1) * rows] = ref[:, :width]
        for i, ref in enumerate(refs[1:]):
            far_ref[i * rows : (i + 1) * rows] = ref[:, width : 2 * width]
        far = jnp.concatenate([ref[:, width : 2 * width] for ref in refs], axis=0)
        squares = read_statistic(own_ref[:, 2 * width :], 0)
        gram = 0.0
        for vectors in (near_ref[...], far):
            gram = gram + lax.dot_general(
                vectors, vectors, (((1,), (1,)), ((), ())), preferred_element_type=jnp.float32
            )
        half = gram.shape[0] // 2
        out_ref[:half, : 2 * half] = gram[:half]
        out_ref[:half, 2 * half :] = gram[half:]
        out_ref[half:, :] = jnp.broadcast_to(squares, (rows, 128))


def sum_grams(third_ref, second_ref, first_ref, own_ref, *refs):
    out_ref = refs[-1]
    out_ref[...] = own_ref[...] + first_ref[...] + second_ref[...] + third_ref[...]


def partner_masks(partner_ref, out_ref, *, rows):
    group = lax.axis_index("dp")
    shape = out_ref.shape[1:]
    row = lax.broadcasted_iota(jnp.int32, shape, 0)
    column = lax.broadcasted_iota(jnp.int32, shape, 1)
    row_id = ((group ^ (row // rows)) * rows) + row % rows
    column_id = ((group ^ (column // rows)) * rows) + column % rows
    partners = jnp.broadcast_to(partner_ref[...], shape)
    row_partner = jnp.sum(
        jnp.where(column == row_id, partners, 0).astype(jnp.float32), axis=1, keepdims=True
    )
    column_partner = jnp.sum(
        jnp.where(row_id == column_id, row_partner, 0.0), axis=0, keepdims=True
    )
    own_partner = column_id.astype(jnp.float32) == row_partner
    other_partner = row_id.astype(jnp.float32) == column_partner
    own_partner = own_partner.astype(jnp.float32)
    out_ref[0] = own_partner
    out_ref[1] = own_partner + other_partner.astype(jnp.float32)


def losses_and_gradient(
    summed_ref,
    other_summed_ref,
    near_ref,
    sent_ref,
    other_far_ref,
    scaled_ref,
    other_scaled_ref,
    gain_ref,
    partner_ref,
    pooled_ref,
    loss_ref,
    grad_ref,
    *,
    model_width,
):
    me = lax.axis_index("pack")
    first_core = core_number() == 0
    count, width = near_ref.shape
    rows = scaled_ref.shape[0]
    half = count // 2
    summed = jnp.where(first_core, other_summed_ref[...], summed_ref[...])
    gram = jnp.concatenate([summed[:half, :count], summed[:half, count:]], axis=0)
    squares = summed[half:, :1]
    shape = (count, count)
    row = lax.broadcasted_iota(jnp.int32, shape, 0)
    column = lax.broadcasted_iota(jnp.int32, shape, 1)
    diagonal = row == column
    on_diagonal = jnp.where(diagonal, gram, 0.0)
    row_scale = lax.rsqrt(jnp.sum(on_diagonal, axis=1, keepdims=True))
    column_scale = lax.rsqrt(jnp.sum(on_diagonal, axis=0, keepdims=True))
    cosines = gram * row_scale * column_scale
    logits = cosines * (1.0 / SOFTMAX_WARMTH)
    powers = jnp.where(diagonal, 0.0, jnp.exp(logits))
    row_sum = jnp.sum(powers, axis=1, keepdims=True)
    column_sum = jnp.sum(powers, axis=0, keepdims=True)
    weights = (powers * (1.0 / row_sum + 1.0 / column_sum) - partner_ref[1])[:rows]
    target = jnp.sum(partner_ref[0] * logits, axis=1, keepdims=True)
    loss = jnp.log(row_sum) - target
    own = loss_ref.shape[0]
    index = lax.broadcasted_iota(jnp.int32, (count, 1), 0)
    for i in range(own):
        loss_ref[i] = jnp.sum(jnp.where(index == me * own + i, loss, 0.0))
    inner = jnp.sum(weights * cosines[:rows], axis=1, keepdims=True)
    scaled_weights = weights * column_scale
    upper = scaled_weights.astype(jnp.bfloat16)
    lower = (scaled_weights - upper.astype(jnp.float32)).astype(jnp.bfloat16)
    own_scale = row_scale[:rows]
    pooled_scale = lax.rsqrt(squares / model_width + EPSILON)
    grad_gain = gain_ref[...] * (model_width**0.5 / SOFTMAX_WARMTH)

    def write(vectors, scaled):
        gradient = jnp.dot(upper, vectors, preferred_element_type=jnp.float32) + jnp.dot(
            lower, vectors, preferred_element_type=jnp.float32
        )
        gradient = (gradient - scaled * (own_scale * inner)) * own_scale
        grad_ref[...] = (gradient * grad_gain).astype(jnp.bfloat16)
        pooled_ref[...] = (scaled * pooled_scale).astype(jnp.bfloat16)

    @pl.when(first_core)
    def _():
        write(near_ref[...], other_scaled_ref[...])

    @pl.when(core_number() == 1)
    def _():
        vectors = jnp.concatenate((sent_ref[:, width : 2 * width], other_far_ref[...]), axis=0)
        write(vectors, scaled_ref[...])


def core_roles(
    hidden_in,
    attn_gain,
    w_query,
    query_gain,
    cached_keys,
    cached_values,
    w_out,
    final_gain,
    lengths,
    pack_order,
    partner,
):
    pack_size = lax.axis_size("pack")
    stmts, width = hidden_in.shape
    model_width = width * pack_size
    head_dim = query_gain.shape[0]
    tokens = cached_keys.shape[0]
    chips = pack_size // 2
    others = range(1, chips)
    total = partner.shape[0]
    bf16 = jnp.bfloat16
    f32 = jnp.float32
    final_gain = final_gain[None]
    query_gain = query_gain[None]
    half = np.arange(head_dim // 2)
    frequency = (ROPE_BASE ** (-half * 2.0 / head_dim)).astype(np.float32)
    frequency = jnp.asarray(np.concatenate([frequency, frequency])[None])
    whole = pl.BlockSpec(memory_space=pltpu.VMEM)

    window = pl.pallas_call(
        open_window,
        out_shape=shaped((8, 128), f32),
        out_specs=whole,
        compiler_params=pltpu.CompilerParams(vmem_limit_bytes=1 << 20),
        cost_estimate=pl.CostEstimate(flops=1 << 34, bytes_accessed=0, transcendentals=0),
    )()
    message = in_vmem(
        prepare_inputs, shaped((stmts, width + 128), bf16), window, hidden_in, attn_gain[None]
    )
    pair = in_vmem(
        join_cores, shaped((stmts, 2 * width + 128), bf16), message, flip(message, "pack", 1)
    )
    received = [send_across(pair, "pack", k, 0) for k in others]
    own_projected = in_vmem(
        project_own_pair, shaped((stmts, width), f32), pair, w_query, limit=16, flops=1 << 26
    )
    rope, ranges = in_vmem(
        positions_and_ranges,
        (shaped((stmts, 2 * head_dim), f32), shaped((stmts, 256), f32)),
        message,
        frequency,
        lengths,
        pack_order,
    )
    other_hidden_in = flip(hidden_in, "pack", 1)
    other_gain = flip(final_gain, "pack", 1)
    blocks = in_vmem(
        join_blocks,
        shaped((chips - 1,) + pair.shape, bf16),
        *received[::-1],
        other_hidden_in,
        other_gain,
        own_projected,
        rope,
    )
    flipped_blocks = flip(blocks, "pack", 1)

    def queries_on(core, blocks, flops):
        return in_vmem(
            lambda *refs: make_queries(*refs, core=core, model_width=model_width),
            shaped((stmts, width), bf16),
            pair,
            blocks,
            own_projected,
            w_query,
            query_gain,
            rope,
            limit=16,
            flops=flops,
        )

    late_queries = queries_on(1, blocks, 1 << 27)
    held = in_vmem(
        copy_tokens,
        shaped((2,) + cached_keys.shape, bf16),
        late_queries,
        cached_keys,
        cached_values,
    )
    other_held = flip(held, "pack", 1)
    second_queries = flip(late_queries, "pack", 1)
    first_queries = queries_on(0, flipped_blocks, 1 << 36)
    queries = in_vmem(
        join_queries, shaped((stmts, 2 * width), bf16), first_queries, second_queries
    )
    other_weights = flip(
        in_vmem(copy_weights, shaped(w_out.shape, bf16), queries, w_out, limit=16), "pack", 1
    )
    received = [send_across(queries, "pack", k, 0) for k in others]
    group_rows = stmts * (width // head_dim)
    own_part, own_stats = in_vmem(
        attend_own,
        (shaped((2, group_rows, head_dim), f32), shaped((2, group_rows, 256), f32)),
        queries,
        cached_keys,
        cached_values,
        other_held,
        ranges,
        flops=1 << 27,
    )
    partials = []
    for k, part in zip(others[::-1], received[::-1]):
        partials.append(
            in_vmem(
                lambda *refs, offset=k: attend_remote(*refs, offset=offset),
                shaped((stmts, 2 * width + 128), bf16),
                part,
                cached_keys,
                cached_values,
                other_held,
                ranges,
                *(partials[-1:] or (own_stats,)),
                flops=1 << 34,
            )
        )
    received = [send_across(part, "pack", k, 1) for k, part in zip(others, partials[::-1])]
    attended = in_vmem(
        merge_partials,
        shaped((stmts, 2 * width), bf16),
        *received[::-1],
        own_part,
        own_stats,
    )

    def projected_to(offset, kind, *after):
        return in_vmem(
            lambda *refs: project_out(*refs, offset=offset),
            shaped((stmts, 2 * width), kind),
            attended,
            w_out,
            other_weights,
            *after,
            limit=16,
            flops=1 << 27,
        )

    third = projected_to(3, bf16)
    second = projected_to(2, bf16, third)
    first = projected_to(1, bf16, second)
    kept = projected_to(0, bf16, first)
    received = [send_across(part, "pack", k, 0) for k, part in zip(others, (first, second, third))]
    vector, scaled, far_scaled = in_vmem(
        finish_hidden,
        (shaped((stmts, 2 * width + 128), bf16),) + (shaped((stmts, width), f32),) * 2,
        *received[::-1],
        flip(kept, "pack", 1),
        hidden_in,
        other_hidden_in,
        final_gain,
        other_gain,
    )
    received = [send_across(vector, "dp", k, 1) for k in range(1, lax.axis_size("dp"))]
    other_scaled = flip(far_scaled, "pack", 1)
    gram, near, far = in_vmem(
        gram_part,
        (
            shaped((total // 2 + stmts, 128), f32),
            shaped((total, width), bf16),
            shaped((total - stmts, width), bf16),
        ),
        *received[::-1],
        flip(vector, "pack", 1),
        other_scaled,
    )
    received = [send_across(gram, "pack", k, 0) for k in others]
    other_far = flip(far, "pack", 1)
    summed = in_vmem(
        sum_grams,
        shaped(gram.shape, f32),
        *received[::-1],
        flip(gram, "pack", 1),
    )
    masks = in_vmem(
        lambda *refs: partner_masks(*refs, rows=stmts),
        shaped((2, total, total), f32),
        partner[None],
    )
    pooled, loss_rows, grad_hidden = pl.pallas_call(
        lambda *refs: losses_and_gradient(*refs, model_width=model_width),
        out_shape=(
            shaped((stmts, width), bf16),
            shaped((stmts // pack_size,), f32),
            shaped((stmts, width), bf16),
        ),
        in_specs=[whole] * 9,
        out_specs=(whole, pl.BlockSpec(memory_space=pltpu.SMEM), whole),
        compiler_params=pltpu.CompilerParams(vmem_limit_bytes=8 << 20),
    )(
        summed,
        flip(summed, "pack", 1),
        near,
        vector,
        other_far,
        scaled,
        other_scaled,
        final_gain,
        masks,
    )
    return (pooled, loss_rows, grad_hidden)


def local(
    hidden_in,
    attn_gain,
    w_query,
    query_gain,
    cached_keys,
    cached_values,
    w_out,
    final_gain,
    lengths,
    pack_order,
    partner,
):
    pack_size = lax.axis_size("pack")
    pack_index = lax.axis_index("pack")
    group_index = lax.axis_index("dp")
    stmt_count, feature_count = hidden_in.shape
    model_width = feature_count * pack_size
    head_dim = query_gain.shape[0]
    local_heads = w_query.shape[1] // head_dim
    token_count = cached_keys.shape[0]
    total_stmts = partner.shape[0]
    lengths_row = lengths[0]
    order_row = pack_order[0]
    inputs32 = hidden_in.astype(jnp.float32)

    scaled = (inputs32 * attn_gain[None, :]).astype(jnp.bfloat16)
    squares = split_float(jnp.sum(inputs32 * inputs32, axis=1), 3)
    extra = jnp.stack(squares + [jnp.zeros_like(squares[0])] * 125, axis=1)
    arrived = gather_blocks(jnp.concatenate([scaled, extra], axis=1), "pack")
    input_squares = jnp.sum(arrived[:, :, feature_count : feature_count + 3].astype(jnp.float32), axis=(0, 2))
    input_rms = lax.rsqrt(input_squares / model_width + EPSILON)
    features = jnp.moveaxis(arrived[:, :, :feature_count], 0, 1).reshape(stmt_count, model_width)
    projected = jnp.dot(features, w_query, preferred_element_type=jnp.float32)
    queries = (projected * input_rms[:, None]).reshape(stmt_count, local_heads, head_dim)
    queries = (
        queries
        * lax.rsqrt(jnp.mean(queries * queries, axis=2, keepdims=True) + EPSILON)
        * query_gain
    )
    queries = rotate_heads(queries, (lengths_row - 1).astype(jnp.float32)).astype(jnp.bfloat16)
    all_queries = jnp.moveaxis(gather_blocks(queries, "pack"), 0, 1).reshape(
        stmt_count, pack_size * local_heads, head_dim
    )
    start, end = statement_ranges(lengths_row, order_row)
    tokens = pack_index * token_count + jnp.arange(token_count, dtype=jnp.int32)
    token_mask = (tokens[None, :] >= start[:, None]) & (tokens[None, :] < end[:, None])
    block_max, block_sum, numerators = block_attention(
        all_queries, cached_keys, cached_values, token_mask, head_dim ** (-0.5)
    )

    def by_owner(part):
        return jnp.moveaxis(part.reshape((stmt_count, pack_size, -1)), 1, 0)

    message = jnp.concatenate(
        [by_owner(numerators.astype(jnp.bfloat16))]
        + [by_owner(piece) for piece in split_float(block_max, 3) + split_float(block_sum, 2)],
        axis=2,
    )
    message = lax.all_to_all(message, "pack", 0, 0)
    width = local_heads * head_dim
    stats = message[:, :, width:].astype(jnp.float32).reshape(pack_size, stmt_count, 5, local_heads)
    maxima = stats[:, :, 0] + stats[:, :, 1] + stats[:, :, 2]
    factor = jnp.exp(maxima - jnp.max(maxima, axis=0, keepdims=True))
    denominator = jnp.sum((stats[:, :, 3] + stats[:, :, 4]) * factor, axis=0)
    numerators = message[:, :, :width].astype(jnp.float32).reshape(pack_size, stmt_count, local_heads, head_dim)
    summed = jnp.sum(numerators * factor[..., None], axis=0)
    attended = (summed / denominator[..., None]).astype(jnp.bfloat16)
    partial_out = jnp.dot(
        attended.reshape(stmt_count, width), w_out, preferred_element_type=jnp.float32
    )
    partial_out = jnp.moveaxis(
        partial_out.astype(jnp.bfloat16).reshape(stmt_count, pack_size, feature_count), 1, 0
    )
    partial_out = lax.all_to_all(partial_out, "pack", 0, 0)
    hidden = inputs32 + jnp.sum(partial_out.astype(jnp.float32), axis=0)
    scaled_out = hidden * final_gain[None, :]
    vectors = lax.all_gather(scaled_out.astype(jnp.bfloat16), "dp", axis=0, tiled=True)
    gram = lax.dot_general(
        vectors, vectors, (((1,), (1,)), ((), ())), preferred_element_type=jnp.float32
    )
    own_squares = jnp.sum(hidden * hidden, axis=1)
    extra = jnp.zeros((total_stmts,), jnp.float32).at[:stmt_count].set(own_squares)
    gram = jnp.concatenate([gram, extra[:, None]], axis=1)
    if total_stmts <= 128:
        gram = jnp.sum(gather_blocks(gram, "pack"), axis=0)
    else:
        gram = lax.psum(gram, "pack")
    hidden_rms = jnp.sqrt(gram[:stmt_count, total_stmts] / model_width + EPSILON)
    gram = gram[:, :total_stmts]
    column_ids = jnp.arange(total_stmts, dtype=jnp.int32)
    diagonal = column_ids[:, None] == column_ids[None, :]
    norms_row = lax.rsqrt(jnp.sum(jnp.where(diagonal, gram, 0.0), axis=0))
    norms_column = lax.rsqrt(jnp.sum(jnp.where(diagonal, gram, 0.0), axis=1))
    cosines = gram * norms_column[:, None] * norms_row[None, :]
    logits = jnp.where(diagonal, MASKED_LOGIT, cosines / SOFTMAX_WARMTH)
    highest = jnp.max(logits, axis=1)
    all_lse = highest + jnp.log(jnp.sum(jnp.exp(logits - highest[:, None]), axis=1))
    is_partner = column_ids[None, :] == partner[:, None]
    all_loss = all_lse - jnp.sum(jnp.where(is_partner, logits, 0.0), axis=1)
    own_count = stmt_count // pack_size
    row_base = group_index * stmt_count
    loss_rows = lax.dynamic_slice_in_dim(all_loss, row_base + pack_index * own_count, own_count, 0)
    weights = (
        jnp.exp(logits - all_lse[:, None])
        + jnp.exp(logits - all_lse[None, :])
        - is_partner.astype(jnp.float32)
        - is_partner.T.astype(jnp.float32)
    ).astype(jnp.bfloat16)
    own_weights = lax.dynamic_slice_in_dim(weights, row_base, stmt_count, 0)
    own_cosines = lax.dynamic_slice_in_dim(cosines, row_base, stmt_count, 0)
    own_norm = lax.dynamic_slice_in_dim(norms_column, row_base, stmt_count, 0)
    inner = jnp.sum(own_weights.astype(jnp.float32) * own_cosines, axis=1)
    own_norm = own_norm[:, None]
    embeddings = (vectors.astype(jnp.float32) * norms_column[:, None]).astype(jnp.bfloat16)
    gradient = jnp.dot(own_weights, embeddings, preferred_element_type=jnp.float32)
    scale = model_width**0.5 / SOFTMAX_WARMTH
    pooled = (scaled_out / hidden_rms[:, None]).astype(jnp.bfloat16)
    grad_hidden = (
        scale * final_gain[None, :] * (gradient - scaled_out * own_norm * inner[:, None]) * own_norm
    ).astype(jnp.bfloat16)
    return (pooled, loss_rows, grad_hidden)


def solution(mesh):
    body = core_roles if mesh.shape["pack"] == 8 and mesh.shape["dp"] == 4 else local
    in_specs = (
        P("dp", "pack"),
        P("pack"),
        P(None, "pack"),
        P(),
        P(("dp", "pack"), None),
        P(("dp", "pack"), None),
        P("pack", None),
        P("pack"),
        P("dp", None),
        P("dp", None),
        P(),
    )
    out_specs = (P("dp", "pack"), P(("dp", "pack")), P("dp", "pack"))
    return jax.shard_map(body, mesh=mesh, in_specs=in_specs, out_specs=out_specs, check_vma=False)
```

```python
import numpy as np
import jax
import jax.numpy as jnp
from jax import lax
from jax.experimental import pallas as pl
from jax.experimental.pallas import tpu as pltpu
from jax.sharding import PartitionSpec as P

EPSILON = 1e-06
SOFTMAX_WARMTH = 0.05
ROPE_BASE = 1000000.0
MASKED_LOGIT = -1e30


def gather_blocks(block, axis):
    size = lax.axis_size(axis)
    return lax.all_to_all(jnp.broadcast_to(block[None], (size,) + block.shape), axis, 0, 0)


def split_float(value, pieces):
    out = []
    for _ in range(pieces):
        piece = lax.reduce_precision(value, 8, 7)
        out.append(piece.astype(jnp.bfloat16))
        value = value - piece
    return out


def cosine_and_sine(angles):
    turns = jnp.round(angles * np.float32(2.0 / np.pi))
    rest = angles - turns * np.float32(1.5703125)
    rest = rest - turns * np.float32(4.837512969970703125e-4)
    rest = rest - turns * np.float32(7.549789948768648e-8)
    square = rest * rest
    sine = rest + rest * square * (
        np.float32(-1.6666654611e-1)
        + square * (np.float32(8.3321608736e-3) + square * np.float32(-1.9515295891e-4))
    )
    cosine = (
        1.0
        - 0.5 * square
        + square
        * square
        * (
            np.float32(4.166664568298827e-2)
            + square
            * (np.float32(-1.388731625493765e-3) + square * np.float32(2.443315711809948e-5))
        )
    )
    quarter = turns.astype(jnp.int32) & 3
    swap = (quarter & 1) == 1
    cos_out = jnp.where(swap, sine, cosine)
    sin_out = jnp.where(swap, cosine, sine)
    cos_out = jnp.where((quarter == 1) | (quarter == 2), -cos_out, cos_out)
    sin_out = jnp.where(quarter >= 2, -sin_out, sin_out)
    return cos_out, sin_out


def rotate_heads(queries, position):
    head_dim = queries.shape[-1]
    half_dim = head_dim // 2
    frequency = (ROPE_BASE ** (-np.arange(half_dim) * 2.0 / head_dim)).astype(np.float32)
    cosine, sine = cosine_and_sine(position[:, None] * frequency[None, :])
    cosine = jnp.concatenate([cosine, cosine], axis=1)[:, None, :]
    sine = jnp.concatenate([-sine, sine], axis=1)[:, None, :]
    turned = jnp.concatenate([queries[..., half_dim:], queries[..., :half_dim]], axis=-1)
    return queries * cosine + turned * sine


def statement_ranges(lengths_row, order_row):
    stmt_count = order_row.shape[0]
    index = jnp.arange(stmt_count, dtype=jnp.int32)
    slot = jnp.sum(jnp.where(order_row[None, :] == index[:, None], index[None, :], 0), axis=1)
    start = jnp.sum(jnp.where(slot[None, :] < slot[:, None], lengths_row[None, :], 0), axis=1)
    return start, start + lengths_row


def block_attention(all_queries, cached_keys, cached_values, token_mask, score_scale):
    stmt_count, head_count, head_dim = all_queries.shape
    kv_heads = cached_keys.shape[1] // head_dim
    group_size = head_count // kv_heads
    grouped = all_queries.reshape(stmt_count, kv_heads, group_size, head_dim)
    key_heads = cached_keys.reshape(-1, kv_heads, head_dim)
    value_heads = cached_values.reshape(-1, kv_heads, head_dim)
    scores = (
        jnp.einsum("skgd,tkd->skgt", grouped, key_heads, preferred_element_type=jnp.float32)
        * score_scale
    )
    token_mask = token_mask[:, None, None, :]
    block_max = jnp.max(jnp.where(token_mask, scores, MASKED_LOGIT), axis=3)
    softmax_weights = jnp.where(token_mask, jnp.exp(scores - block_max[..., None]), 0.0)
    block_sum = jnp.sum(softmax_weights, axis=3)
    numerators = jnp.einsum(
        "skgt,tkd->skgd",
        softmax_weights.astype(jnp.bfloat16),
        value_heads,
        preferred_element_type=jnp.float32,
    )
    return (
        block_max.reshape(stmt_count, head_count),
        block_sum.reshape(stmt_count, head_count),
        numerators.reshape(stmt_count, head_count, head_dim),
    )


def flip(array, axis, offset):
    size = lax.axis_size(axis)
    return lax.ppermute(array, axis, [(i, i ^ offset) for i in range(size)])


def in_vmem(body, outputs, *operands, limit=8, flops=1_000_000):
    whole = pl.BlockSpec(memory_space=pltpu.VMEM)
    moved = sum(operand.size * operand.dtype.itemsize for operand in operands)
    return pl.pallas_call(
        body,
        out_shape=outputs,
        in_specs=[whole] * len(operands),
        out_specs=jax.tree.map(lambda _: whole, outputs),
        compiler_params=pltpu.CompilerParams(vmem_limit_bytes=limit << 20),
        cost_estimate=pl.CostEstimate(flops=flops, bytes_accessed=moved, transcendentals=0),
    )(*operands)


def shaped(shape, kind):
    return jax.ShapeDtypeStruct(shape, kind)


def open_window(out_ref):
    out_ref[...] = jnp.zeros_like(out_ref)


def positions_and_ranges(
    message_ref, frequency_ref, lengths_ref, order_ref, rope_ref, range_ref
):
    del message_ref
    count = lengths_ref.shape[1]
    half = frequency_ref.shape[1] // 2
    row = lax.broadcasted_iota(jnp.int32, (count, count), 0)
    column = lax.broadcasted_iota(jnp.int32, (count, count), 1)
    lengths = jnp.broadcast_to(lengths_ref[...], (count, count)).astype(jnp.float32)
    length = jnp.sum(jnp.where(row == column, lengths, 0.0), axis=1, keepdims=True)
    order = jnp.broadcast_to(order_ref[...], (count, count))
    placed = order == row
    slot = jnp.sum(jnp.where(placed, column, 0).astype(jnp.float32), axis=1, keepdims=True)
    packed = jnp.sum(jnp.where(placed, length, 0.0), axis=0, keepdims=True)
    earlier = column.astype(jnp.float32) < slot
    start = jnp.sum(jnp.where(earlier, packed, 0.0), axis=1, keepdims=True)
    range_ref[:, :128] = jnp.broadcast_to(start, (count, 128))
    range_ref[:, 128:] = jnp.broadcast_to(start + length, (count, 128))
    cosine, sine = cosine_and_sine((length - 1.0) * frequency_ref[...])
    lane = lax.broadcasted_iota(jnp.int32, cosine.shape, 1)
    rope_ref[:, : 2 * half] = cosine
    rope_ref[:, 2 * half :] = jnp.where(lane < half, -sine, sine)


LOG2_E = 1.4426950408889634


def pack_statistics(values):
    rows = values[0].shape[0]
    lane = lax.broadcasted_iota(jnp.int32, (rows, 128), 1)
    rest = jnp.zeros((rows, 128), jnp.float32)
    for place, value in enumerate(values):
        rest = jnp.where(lane == place, value, rest)
    out = rest.astype(jnp.bfloat16).astype(jnp.float32)
    for part in (1, 2):
        rest = rest - rest.astype(jnp.bfloat16).astype(jnp.float32)
        out = out + pltpu.roll(rest.astype(jnp.bfloat16).astype(jnp.float32), 32 * part, 1)
    return out.astype(jnp.bfloat16)


def read_statistic(block, first):
    lane = lax.broadcasted_iota(jnp.int32, block.shape, 1)
    mine = ((lane & 31) == first) & (lane < 96)
    return jnp.sum(jnp.where(mine, block.astype(jnp.float32), 0.0), axis=1, keepdims=True)


def core_number():
    return lax.axis_index("pack") & 1


def chip_number():
    return lax.axis_index("pack") >> 1


def send_across(array, axis, offset, sender):
    groups, pack = lax.axis_size("dp"), lax.axis_size("pack")
    pairs = []
    for group in range(groups):
        for place in range(pack):
            if place % 2 != sender:
                target = (group, place ^ 1)
            elif axis == "dp":
                target = (group ^ offset, place ^ 1)
            else:
                target = (group, place ^ (2 * offset) ^ 1)
            pairs.append((group * pack + place, target[0] * pack + target[1]))
    return lax.ppermute(array, ("dp", "pack"), pairs)


def copy_tokens(_, key_ref, value_ref, out_ref):
    out_ref[0] = key_ref[...]
    out_ref[1] = value_ref[...]


def prepare_pair(_, own_ref, other_ref, own_gain_ref, other_gain_ref, pair_ref):
    width = own_ref.shape[1]
    squares = 0.0
    scaled = []
    for ref, factor_ref in ((own_ref, own_gain_ref), (other_ref, other_gain_ref)):
        inputs = ref[...].astype(jnp.float32)
        squares = squares + jnp.sum(inputs * inputs, axis=1, keepdims=True)
        scaled.append((inputs * factor_ref[...]).astype(jnp.bfloat16))
    pair_ref[:, 2 * width :] = pack_statistics([squares])
    for first in range(2):

        @pl.when(core_number() == first)
        def _():
            pair_ref[:, :width] = scaled[first]
            pair_ref[:, width : 2 * width] = scaled[1 - first]


def project_pair(pair_ref, offset, weight_ref):
    chip = chip_number() ^ offset
    width = 2 * weight_ref.shape[1]
    rows = pl.ds(pl.multiple_of(chip * width, width), width)
    return jnp.dot(
        pair_ref[:, :width], weight_ref[rows, :], preferred_element_type=jnp.float32
    )


def project_own_pair(pair_ref, weight_ref, total_ref):
    total_ref[...] = project_pair(pair_ref, 0, weight_ref)


def project_early(third_ref, second_ref, own_ref, weight_ref, *refs, core):
    total_ref = refs[-1]

    @pl.when(core_number() == core)
    def _():
        total_ref[...] = (
            own_ref[...]
            + project_pair(third_ref, 3, weight_ref)
            + project_pair(second_ref, 2, weight_ref)
        )


def make_queries(
    third_ref,
    second_ref,
    first_ref,
    pair_ref,
    total_ref,
    weight_ref,
    gain_ref,
    rope_ref,
    *refs,
    core,
    model_width,
):
    query_ref = refs[-1]
    width = total_ref.shape[1]
    head_dim = gain_ref.shape[1]

    @pl.when(core_number() == core)
    def _():
        projected = total_ref[...] + project_pair(first_ref, 1, weight_ref)
        squares = sum(
            ref[:, 2 * width :].astype(jnp.float32)
            for ref in (pair_ref, first_ref, second_ref, third_ref)
        )
        squares = read_statistic(squares, 0)
        projected = projected * lax.rsqrt(squares / model_width + EPSILON)
        cosine = rope_ref[:, :head_dim]
        sine = rope_ref[:, head_dim:]
        for head in range(width // head_dim):
            place = slice(head * head_dim, (head + 1) * head_dim)
            query = projected[:, place]
            mean = jnp.mean(query * query, axis=1, keepdims=True)
            query = query * lax.rsqrt(mean + EPSILON) * gain_ref[...]
            turned = pltpu.roll(query, head_dim // 2, 1)
            query_ref[:, place] = (query * cosine + turned * sine).astype(jnp.bfloat16)


def join_queries(first_ref, second_ref, out_ref):
    width = first_ref.shape[1]
    out_ref[:, :width] = first_ref[...]
    out_ref[:, width:] = second_ref[...]


def token_masks(range_ref, tokens, group):
    me = lax.axis_index("pack")
    masks = []
    for owner in (me, me ^ 1):
        index = lax.broadcasted_iota(jnp.int32, (range_ref.shape[0], tokens), 1) + owner * tokens
        index = index.astype(jnp.float32)
        mask = (index >= range_ref[:, :1]) & (index < range_ref[:, 128:129])
        masks.append(jnp.concatenate([mask.astype(jnp.float32)] * group, axis=0) > 0.5)
    return masks


def attend_heads(queries, heads, key_ref, value_ref, other_ref, masks):
    head_dim = 128
    scale = head_dim**-0.5
    scores = []
    columns = []
    for query, head in zip(queries, heads):
        grouped = jnp.concatenate(
            [query[:, i : i + head_dim] for i in range(0, query.shape[1], head_dim)], axis=0
        )
        column = pl.ds(pl.multiple_of(head * head_dim, head_dim), head_dim)
        columns.append(column)
        raw = [
            lax.dot_general(
                grouped, keys, (((1,), (1,)), ((), ())), preferred_element_type=jnp.float32
            )
            for keys in (key_ref[:, column], other_ref[0, :, column])
        ]
        scores.append([jnp.where(mask, part, MASKED_LOGIT) for mask, part in zip(masks, raw)])
    maxima = [
        jnp.maximum(
            jnp.max(first, axis=1, keepdims=True), jnp.max(second, axis=1, keepdims=True)
        )
        for first, second in scores
    ]
    weights = [
        [jnp.exp2((part - highest) * (scale * LOG2_E)) for part in parts]
        for parts, highest in zip(scores, maxima)
    ]
    out = []
    for parts, highest, column in zip(weights, maxima, columns):
        total = jnp.sum(parts[0], axis=1, keepdims=True) + jnp.sum(
            parts[1], axis=1, keepdims=True
        )
        numerators = jnp.dot(
            parts[0].astype(jnp.bfloat16), value_ref[:, column], preferred_element_type=jnp.float32
        ) + jnp.dot(
            parts[1].astype(jnp.bfloat16),
            other_ref[1, :, column],
            preferred_element_type=jnp.float32,
        )
        out.append((highest * scale, total, numerators))
    return out


def attend_remote(query_ref, key_ref, value_ref, other_ref, range_ref, *refs, offset):
    out_ref = refs[-1]

    @pl.when(core_number() == 1)
    def _():
        rows = query_ref.shape[0]
        width = query_ref.shape[1] // 2
        masks = token_masks(range_ref, key_ref.shape[0], width // 128)
        chip = chip_number() ^ offset
        queries = [query_ref[:, :width], query_ref[:, width:]]
        heads = (2 * chip, 2 * chip + 1)
        parts = attend_heads(queries, heads, key_ref, value_ref, other_ref, masks)
        stats = []
        for j, (highest, total, numerators) in enumerate(parts):
            for h in range(width // 128):
                part = slice(h * rows, (h + 1) * rows)
                place = slice(j * width + h * 128, j * width + (h + 1) * 128)
                out_ref[:, place] = numerators[part].astype(jnp.bfloat16)
                stats += [highest[part], total[part]]
        out_ref[:, 2 * width :] = pack_statistics(stats)


def attend_own(query_ref, key_ref, value_ref, other_ref, range_ref, _, out_ref, stats_ref):
    @pl.when(core_number() == 0)
    def _():
        width = query_ref.shape[1] // 2
        masks = token_masks(range_ref, key_ref.shape[0], width // 128)
        chip = chip_number()
        parts = attend_heads(
            [query_ref[:, :width], query_ref[:, width:]],
            (2 * chip, 2 * chip + 1),
            key_ref,
            value_ref,
            other_ref,
            masks,
        )
        for j, (highest, total, numerators) in enumerate(parts):
            out_ref[j] = numerators
            stats_ref[j, :, :128] = jnp.broadcast_to(highest, (highest.shape[0], 128))
            stats_ref[j, :, 128:] = jnp.broadcast_to(total, (highest.shape[0], 128))


def merge_partials(third_ref, second_ref, first_ref, own_ref, stats_ref, *refs):
    attended_ref = refs[-1]

    @pl.when(core_number() == 0)
    def _():
        rows = attended_ref.shape[0]
        width = attended_ref.shape[1] // 2
        others = (first_ref, second_ref, third_ref)
        stats = [ref[:, 2 * width :] for ref in others]
        for j in range(2):
            for h in range(width // 128):
                part = slice(h * rows, (h + 1) * rows)
                place = slice(j * width + h * 128, j * width + (h + 1) * 128)
                slot = 2 * (j * (width // 128) + h)
                maxima = [stats_ref[j, part, :1]] + [read_statistic(s, slot) for s in stats]
                totals = [stats_ref[j, part, 128:129]]
                totals += [read_statistic(s, slot + 1) for s in stats]
                numerators = [own_ref[j, part, :]]
                numerators += [ref[:, place].astype(jnp.float32) for ref in others]
                highest = maxima[0]
                for value in maxima[1:]:
                    highest = jnp.maximum(highest, value)
                denominator = 0.0
                summed = 0.0
                for value, total, numerator in zip(maxima, totals, numerators):
                    factor = jnp.exp(value - highest)
                    denominator = denominator + total * factor
                    summed = summed + numerator * factor
                attended_ref[:, place] = (summed / denominator).astype(jnp.bfloat16)


def copy_weights(_, weight_ref, out_ref):
    out_ref[...] = weight_ref[...]


def project_out(attended_ref, weight_ref, other_weight_ref, *refs, offset):
    out_ref = refs[-1]

    @pl.when(core_number() == 0)
    def _():
        width = attended_ref.shape[1] // 2
        column = pl.ds(pl.multiple_of((chip_number() ^ offset) * 2 * width, 2 * width), 2 * width)
        total = jnp.dot(
            attended_ref[:, :width], weight_ref[:, column], preferred_element_type=jnp.float32
        ) + jnp.dot(
            attended_ref[:, width:], other_weight_ref[:, column], preferred_element_type=jnp.float32
        )
        out_ref[...] = total.astype(out_ref.dtype)


def finish_hidden(
    third_ref,
    second_ref,
    first_ref,
    kept_ref,
    own_ref,
    other_ref,
    own_gain_ref,
    other_gain_ref,
    sent_ref,
    scaled_ref,
    other_scaled_ref,
):
    width = own_ref.shape[1]

    @pl.when(core_number() == 1)
    def _():
        squares = 0.0
        inputs = (other_ref, own_ref)
        gains = (other_gain_ref, own_gain_ref)
        for core in range(2):
            place = slice(core * width, (core + 1) * width)
            hidden = inputs[core][...].astype(jnp.float32)
            for ref in (kept_ref, first_ref, second_ref, third_ref):
                hidden = hidden + ref[:, place].astype(jnp.float32)
            scaled = hidden * gains[core][...]
            (other_scaled_ref, scaled_ref)[core][...] = scaled
            sent_ref[:, place] = scaled.astype(jnp.bfloat16)
            squares = squares + jnp.sum(hidden * hidden, axis=1, keepdims=True)
        sent_ref[:, 2 * width :] = pack_statistics([squares])


def gram_part(third_ref, second_ref, first_ref, own_ref, _, out_ref, near_ref, far_ref):
    @pl.when(core_number() == 0)
    def _():
        rows = own_ref.shape[0]
        width = far_ref.shape[1]
        refs = (own_ref, first_ref, second_ref, third_ref)
        for i, ref in enumerate(refs):
            near_ref[i * rows : (i + 1) * rows] = ref[:, :width]
        for i, ref in enumerate(refs[1:]):
            far_ref[i * rows : (i + 1) * rows] = ref[:, width : 2 * width]
        far = jnp.concatenate([ref[:, width : 2 * width] for ref in refs], axis=0)
        squares = read_statistic(own_ref[:, 2 * width :], 0)
        gram = 0.0
        for vectors in (near_ref[...], far):
            gram = gram + lax.dot_general(
                vectors, vectors, (((1,), (1,)), ((), ())), preferred_element_type=jnp.float32
            )
        half = gram.shape[0] // 2
        out_ref[:half, : 2 * half] = gram[:half]
        out_ref[:half, 2 * half :] = gram[half:]
        out_ref[half:, :] = jnp.broadcast_to(squares, (rows, 128))


def sum_grams(third_ref, second_ref, first_ref, own_ref, *refs):
    out_ref = refs[-1]
    out_ref[...] = own_ref[...] + first_ref[...] + second_ref[...] + third_ref[...]


def partner_masks(partner_ref, out_ref, *, rows):
    group = lax.axis_index("dp")
    shape = out_ref.shape[1:]
    row = lax.broadcasted_iota(jnp.int32, shape, 0)
    column = lax.broadcasted_iota(jnp.int32, shape, 1)
    row_id = ((group ^ (row // rows)) * rows) + row % rows
    column_id = ((group ^ (column // rows)) * rows) + column % rows
    partners = jnp.broadcast_to(partner_ref[...], shape)
    row_partner = jnp.sum(
        jnp.where(column == row_id, partners, 0).astype(jnp.float32), axis=1, keepdims=True
    )
    column_partner = jnp.sum(
        jnp.where(row_id == column_id, row_partner, 0.0), axis=0, keepdims=True
    )
    own_partner = column_id.astype(jnp.float32) == row_partner
    other_partner = row_id.astype(jnp.float32) == column_partner
    own_partner = own_partner.astype(jnp.float32)
    out_ref[0] = own_partner
    out_ref[1] = own_partner + other_partner.astype(jnp.float32)


def losses_and_gradient(
    summed_ref,
    other_summed_ref,
    near_ref,
    sent_ref,
    other_far_ref,
    scaled_ref,
    other_scaled_ref,
    gain_ref,
    partner_ref,
    pooled_ref,
    loss_ref,
    grad_ref,
    *,
    model_width,
):
    me = lax.axis_index("pack")
    first_core = core_number() == 0
    count, width = near_ref.shape
    rows = scaled_ref.shape[0]
    half = count // 2
    summed = jnp.where(first_core, other_summed_ref[...], summed_ref[...])
    gram = jnp.concatenate([summed[:half, :count], summed[:half, count:]], axis=0)
    squares = summed[half:, :1]
    shape = (count, count)
    row = lax.broadcasted_iota(jnp.int32, shape, 0)
    column = lax.broadcasted_iota(jnp.int32, shape, 1)
    diagonal = row == column
    on_diagonal = jnp.where(diagonal, gram, 0.0)
    row_scale = lax.rsqrt(jnp.sum(on_diagonal, axis=1, keepdims=True))
    column_scale = lax.rsqrt(jnp.sum(on_diagonal, axis=0, keepdims=True))
    cosines = gram * row_scale * column_scale
    logits = cosines * (1.0 / SOFTMAX_WARMTH)
    powers = jnp.where(diagonal, 0.0, jnp.exp(logits))
    row_sum = jnp.sum(powers, axis=1, keepdims=True)
    column_sum = jnp.sum(powers, axis=0, keepdims=True)
    weights = (powers * (1.0 / row_sum + 1.0 / column_sum) - partner_ref[1])[:rows]
    target = jnp.sum(partner_ref[0] * logits, axis=1, keepdims=True)
    loss = jnp.log(row_sum) - target
    own = loss_ref.shape[0]
    index = lax.broadcasted_iota(jnp.int32, (count, 1), 0)
    for i in range(own):
        loss_ref[i] = jnp.sum(jnp.where(index == me * own + i, loss, 0.0))
    inner = jnp.sum(weights * cosines[:rows], axis=1, keepdims=True)
    scaled_weights = weights * column_scale
    upper = scaled_weights.astype(jnp.bfloat16)
    lower = (scaled_weights - upper.astype(jnp.float32)).astype(jnp.bfloat16)
    own_scale = row_scale[:rows]
    pooled_scale = lax.rsqrt(squares / model_width + EPSILON)
    grad_gain = gain_ref[...] * (model_width**0.5 / SOFTMAX_WARMTH)

    def write(vectors, scaled):
        gradient = jnp.dot(upper, vectors, preferred_element_type=jnp.float32) + jnp.dot(
            lower, vectors, preferred_element_type=jnp.float32
        )
        gradient = (gradient - scaled * (own_scale * inner)) * own_scale
        grad_ref[...] = (gradient * grad_gain).astype(jnp.bfloat16)
        pooled_ref[...] = (scaled * pooled_scale).astype(jnp.bfloat16)

    @pl.when(first_core)
    def _():
        write(near_ref[...], other_scaled_ref[...])

    @pl.when(core_number() == 1)
    def _():
        vectors = jnp.concatenate((sent_ref[:, width : 2 * width], other_far_ref[...]), axis=0)
        write(vectors, scaled_ref[...])


def core_roles(
    hidden_in,
    attn_gain,
    w_query,
    query_gain,
    cached_keys,
    cached_values,
    w_out,
    final_gain,
    lengths,
    pack_order,
    partner,
):
    pack_size = lax.axis_size("pack")
    stmts, width = hidden_in.shape
    model_width = width * pack_size
    head_dim = query_gain.shape[0]
    tokens = cached_keys.shape[0]
    chips = pack_size // 2
    others = range(1, chips)
    total = partner.shape[0]
    bf16 = jnp.bfloat16
    f32 = jnp.float32
    final_gain = final_gain[None]
    query_gain = query_gain[None]
    half = np.arange(head_dim // 2)
    frequency = (ROPE_BASE ** (-half * 2.0 / head_dim)).astype(np.float32)
    frequency = jnp.asarray(np.concatenate([frequency, frequency])[None])
    whole = pl.BlockSpec(memory_space=pltpu.VMEM)

    window = pl.pallas_call(
        open_window,
        out_shape=shaped((8, 128), f32),
        out_specs=whole,
        compiler_params=pltpu.CompilerParams(vmem_limit_bytes=1 << 20),
        cost_estimate=pl.CostEstimate(flops=1 << 34, bytes_accessed=0, transcendentals=0),
    )()
    attn_gain = attn_gain[None]
    other_hidden_in = flip(hidden_in, "pack", 1)
    pair = in_vmem(
        prepare_pair,
        shaped((stmts, 2 * width + 128), bf16),
        window,
        hidden_in,
        other_hidden_in,
        attn_gain,
        flip(attn_gain, "pack", 1),
    )
    received = [send_across(pair, "pack", k, 0) for k in others]
    own_projected = in_vmem(
        project_own_pair, shaped((stmts, width), f32), pair, w_query, limit=16, flops=1 << 26
    )
    rope, ranges = in_vmem(
        positions_and_ranges,
        (shaped((stmts, 2 * head_dim), f32), shaped((stmts, 256), f32)),
        pair,
        frequency,
        lengths,
        pack_order,
    )
    other_gain = flip(final_gain, "pack", 1)

    def project_on(core, parts, *after):
        first, second, third = parts
        early = in_vmem(
            lambda *refs: project_early(*refs, core=core),
            shaped((stmts, width), f32),
            third,
            second,
            own_projected,
            w_query,
            *after[:1],
            limit=16,
            flops=1 << 30,
        )
        return in_vmem(
            lambda *refs: make_queries(*refs, core=core, model_width=model_width),
            shaped((stmts, width), bf16),
            third,
            second,
            first,
            pair,
            early,
            w_query,
            query_gain,
            rope,
            *after[1:],
            limit=16,
            flops=1 << 36 if core == 0 else 1 << 27,
        )

    late_queries = project_on(1, received, rope)
    handed = [flip(part, "pack", 1) for part in received]
    held = in_vmem(
        copy_tokens,
        shaped((2,) + cached_keys.shape, bf16),
        handed[0],
        cached_keys,
        cached_values,
    )
    other_held = flip(held, "pack", 1)
    second_queries = flip(late_queries, "pack", 1)
    first_queries = project_on(0, handed)
    queries = in_vmem(
        join_queries, shaped((stmts, 2 * width), bf16), first_queries, second_queries
    )
    other_weights = flip(
        in_vmem(copy_weights, shaped(w_out.shape, bf16), queries, w_out, limit=16), "pack", 1
    )
    received = [send_across(queries, "pack", k, 0) for k in others]
    group_rows = stmts * (width // head_dim)
    own_part, own_stats = in_vmem(
        attend_own,
        (shaped((2, group_rows, head_dim), f32), shaped((2, group_rows, 256), f32)),
        queries,
        cached_keys,
        cached_values,
        other_held,
        ranges,
        other_gain,
        flops=1 << 27,
    )
    partials = []
    for k, part in zip(others[::-1], received[::-1]):
        partials.append(
            in_vmem(
                lambda *refs, offset=k: attend_remote(*refs, offset=offset),
                shaped((stmts, 2 * width + 128), bf16),
                part,
                cached_keys,
                cached_values,
                other_held,
                ranges,
                *(partials[-1:] or (own_stats,)),
                flops=1 << 34,
            )
        )
    received = [send_across(part, "pack", k, 1) for k, part in zip(others, partials[::-1])]
    attended = in_vmem(
        merge_partials,
        shaped((stmts, 2 * width), bf16),
        *received[::-1],
        own_part,
        own_stats,
    )

    def projected_to(offset, kind, *after):
        return in_vmem(
            lambda *refs: project_out(*refs, offset=offset),
            shaped((stmts, 2 * width), kind),
            attended,
            w_out,
            other_weights,
            *after,
            limit=16,
            flops=1 << 27,
        )

    third = projected_to(3, bf16)
    second = projected_to(2, bf16, third)
    first = projected_to(1, bf16, second)
    kept = projected_to(0, bf16, first)
    received = [send_across(part, "pack", k, 0) for k, part in zip(others, (first, second, third))]
    vector, scaled, far_scaled = in_vmem(
        finish_hidden,
        (shaped((stmts, 2 * width + 128), bf16),) + (shaped((stmts, width), f32),) * 2,
        *received[::-1],
        flip(kept, "pack", 1),
        hidden_in,
        other_hidden_in,
        final_gain,
        other_gain,
    )
    received = [send_across(vector, "dp", k, 1) for k in range(1, lax.axis_size("dp"))]
    other_scaled = flip(far_scaled, "pack", 1)
    gram, near, far = in_vmem(
        gram_part,
        (
            shaped((total // 2 + stmts, 128), f32),
            shaped((total, width), bf16),
            shaped((total - stmts, width), bf16),
        ),
        *received[::-1],
        flip(vector, "pack", 1),
        other_scaled,
    )
    received = [send_across(gram, "pack", k, 0) for k in others]
    other_far = flip(far, "pack", 1)
    summed = in_vmem(
        sum_grams,
        shaped(gram.shape, f32),
        *received[::-1],
        flip(gram, "pack", 1),
    )
    masks = in_vmem(
        lambda *refs: partner_masks(*refs, rows=stmts),
        shaped((2, total, total), f32),
        partner[None],
    )
    pooled, loss_rows, grad_hidden = pl.pallas_call(
        lambda *refs: losses_and_gradient(*refs, model_width=model_width),
        out_shape=(
            shaped((stmts, width), bf16),
            shaped((stmts // pack_size,), f32),
            shaped((stmts, width), bf16),
        ),
        in_specs=[whole] * 9,
        out_specs=(whole, pl.BlockSpec(memory_space=pltpu.SMEM), whole),
        compiler_params=pltpu.CompilerParams(vmem_limit_bytes=8 << 20),
    )(
        summed,
        flip(summed, "pack", 1),
        near,
        vector,
        other_far,
        scaled,
        other_scaled,
        final_gain,
        masks,
    )
    return (pooled, loss_rows, grad_hidden)


def local(
    hidden_in,
    attn_gain,
    w_query,
    query_gain,
    cached_keys,
    cached_values,
    w_out,
    final_gain,
    lengths,
    pack_order,
    partner,
):
    pack_size = lax.axis_size("pack")
    pack_index = lax.axis_index("pack")
    group_index = lax.axis_index("dp")
    stmt_count, feature_count = hidden_in.shape
    model_width = feature_count * pack_size
    head_dim = query_gain.shape[0]
    local_heads = w_query.shape[1] // head_dim
    token_count = cached_keys.shape[0]
    total_stmts = partner.shape[0]
    lengths_row = lengths[0]
    order_row = pack_order[0]
    inputs32 = hidden_in.astype(jnp.float32)

    scaled = (inputs32 * attn_gain[None, :]).astype(jnp.bfloat16)
    squares = split_float(jnp.sum(inputs32 * inputs32, axis=1), 3)
    extra = jnp.stack(squares + [jnp.zeros_like(squares[0])] * 125, axis=1)
    arrived = gather_blocks(jnp.concatenate([scaled, extra], axis=1), "pack")
    input_squares = jnp.sum(arrived[:, :, feature_count : feature_count + 3].astype(jnp.float32), axis=(0, 2))
    input_rms = lax.rsqrt(input_squares / model_width + EPSILON)
    features = jnp.moveaxis(arrived[:, :, :feature_count], 0, 1).reshape(stmt_count, model_width)
    projected = jnp.dot(features, w_query, preferred_element_type=jnp.float32)
    queries = (projected * input_rms[:, None]).reshape(stmt_count, local_heads, head_dim)
    queries = (
        queries
        * lax.rsqrt(jnp.mean(queries * queries, axis=2, keepdims=True) + EPSILON)
        * query_gain
    )
    queries = rotate_heads(queries, (lengths_row - 1).astype(jnp.float32)).astype(jnp.bfloat16)
    all_queries = jnp.moveaxis(gather_blocks(queries, "pack"), 0, 1).reshape(
        stmt_count, pack_size * local_heads, head_dim
    )
    start, end = statement_ranges(lengths_row, order_row)
    tokens = pack_index * token_count + jnp.arange(token_count, dtype=jnp.int32)
    token_mask = (tokens[None, :] >= start[:, None]) & (tokens[None, :] < end[:, None])
    block_max, block_sum, numerators = block_attention(
        all_queries, cached_keys, cached_values, token_mask, head_dim ** (-0.5)
    )

    def by_owner(part):
        return jnp.moveaxis(part.reshape((stmt_count, pack_size, -1)), 1, 0)

    message = jnp.concatenate(
        [by_owner(numerators.astype(jnp.bfloat16))]
        + [by_owner(piece) for piece in split_float(block_max, 3) + split_float(block_sum, 2)],
        axis=2,
    )
    message = lax.all_to_all(message, "pack", 0, 0)
    width = local_heads * head_dim
    stats = message[:, :, width:].astype(jnp.float32).reshape(pack_size, stmt_count, 5, local_heads)
    maxima = stats[:, :, 0] + stats[:, :, 1] + stats[:, :, 2]
    factor = jnp.exp(maxima - jnp.max(maxima, axis=0, keepdims=True))
    denominator = jnp.sum((stats[:, :, 3] + stats[:, :, 4]) * factor, axis=0)
    numerators = message[:, :, :width].astype(jnp.float32).reshape(pack_size, stmt_count, local_heads, head_dim)
    summed = jnp.sum(numerators * factor[..., None], axis=0)
    attended = (summed / denominator[..., None]).astype(jnp.bfloat16)
    partial_out = jnp.dot(
        attended.reshape(stmt_count, width), w_out, preferred_element_type=jnp.float32
    )
    partial_out = jnp.moveaxis(
        partial_out.astype(jnp.bfloat16).reshape(stmt_count, pack_size, feature_count), 1, 0
    )
    partial_out = lax.all_to_all(partial_out, "pack", 0, 0)
    hidden = inputs32 + jnp.sum(partial_out.astype(jnp.float32), axis=0)
    scaled_out = hidden * final_gain[None, :]
    vectors = lax.all_gather(scaled_out.astype(jnp.bfloat16), "dp", axis=0, tiled=True)
    gram = lax.dot_general(
        vectors, vectors, (((1,), (1,)), ((), ())), preferred_element_type=jnp.float32
    )
    own_squares = jnp.sum(hidden * hidden, axis=1)
    extra = jnp.zeros((total_stmts,), jnp.float32).at[:stmt_count].set(own_squares)
    gram = jnp.concatenate([gram, extra[:, None]], axis=1)
    if total_stmts <= 128:
        gram = jnp.sum(gather_blocks(gram, "pack"), axis=0)
    else:
        gram = lax.psum(gram, "pack")
    hidden_rms = jnp.sqrt(gram[:stmt_count, total_stmts] / model_width + EPSILON)
    gram = gram[:, :total_stmts]
    column_ids = jnp.arange(total_stmts, dtype=jnp.int32)
    diagonal = column_ids[:, None] == column_ids[None, :]
    norms_row = lax.rsqrt(jnp.sum(jnp.where(diagonal, gram, 0.0), axis=0))
    norms_column = lax.rsqrt(jnp.sum(jnp.where(diagonal, gram, 0.0), axis=1))
    cosines = gram * norms_column[:, None] * norms_row[None, :]
    logits = jnp.where(diagonal, MASKED_LOGIT, cosines / SOFTMAX_WARMTH)
    highest = jnp.max(logits, axis=1)
    all_lse = highest + jnp.log(jnp.sum(jnp.exp(logits - highest[:, None]), axis=1))
    is_partner = column_ids[None, :] == partner[:, None]
    all_loss = all_lse - jnp.sum(jnp.where(is_partner, logits, 0.0), axis=1)
    own_count = stmt_count // pack_size
    row_base = group_index * stmt_count
    loss_rows = lax.dynamic_slice_in_dim(all_loss, row_base + pack_index * own_count, own_count, 0)
    weights = (
        jnp.exp(logits - all_lse[:, None])
        + jnp.exp(logits - all_lse[None, :])
        - is_partner.astype(jnp.float32)
        - is_partner.T.astype(jnp.float32)
    ).astype(jnp.bfloat16)
    own_weights = lax.dynamic_slice_in_dim(weights, row_base, stmt_count, 0)
    own_cosines = lax.dynamic_slice_in_dim(cosines, row_base, stmt_count, 0)
    own_norm = lax.dynamic_slice_in_dim(norms_column, row_base, stmt_count, 0)
    inner = jnp.sum(own_weights.astype(jnp.float32) * own_cosines, axis=1)
    own_norm = own_norm[:, None]
    embeddings = (vectors.astype(jnp.float32) * norms_column[:, None]).astype(jnp.bfloat16)
    gradient = jnp.dot(own_weights, embeddings, preferred_element_type=jnp.float32)
    scale = model_width**0.5 / SOFTMAX_WARMTH
    pooled = (scaled_out / hidden_rms[:, None]).astype(jnp.bfloat16)
    grad_hidden = (
        scale * final_gain[None, :] * (gradient - scaled_out * own_norm * inner[:, None]) * own_norm
    ).astype(jnp.bfloat16)
    return (pooled, loss_rows, grad_hidden)


def solution(mesh):
    body = core_roles if mesh.shape["pack"] == 8 and mesh.shape["dp"] == 4 else local
    in_specs = (
        P("dp", "pack"),
        P("pack"),
        P(None, "pack"),
        P(),
        P(("dp", "pack"), None),
        P(("dp", "pack"), None),
        P("pack", None),
        P("pack"),
        P("dp", None),
        P("dp", None),
        P(),
    )
    out_specs = (P("dp", "pack"), P(("dp", "pack")), P("dp", "pack"))
    return jax.shard_map(body, mesh=mesh, in_specs=in_specs, out_specs=out_specs, check_vma=False)
```

```python
import numpy as np
import jax
import jax.numpy as jnp
from jax import lax
from jax.experimental import pallas as pl
from jax.experimental.pallas import tpu as pltpu
from jax.sharding import PartitionSpec as P

EPSILON = 1e-06
SOFTMAX_WARMTH = 0.05
ROPE_BASE = 1000000.0
MASKED_LOGIT = -1e30


def gather_blocks(block, axis):
    size = lax.axis_size(axis)
    return lax.all_to_all(jnp.broadcast_to(block[None], (size,) + block.shape), axis, 0, 0)


def split_float(value, pieces):
    out = []
    for _ in range(pieces):
        piece = lax.reduce_precision(value, 8, 7)
        out.append(piece.astype(jnp.bfloat16))
        value = value - piece
    return out


def cosine_and_sine(angles):
    turns = jnp.round(angles * np.float32(2.0 / np.pi))
    rest = angles - turns * np.float32(1.5703125)
    rest = rest - turns * np.float32(4.837512969970703125e-4)
    rest = rest - turns * np.float32(7.549789948768648e-8)
    square = rest * rest
    sine = rest + rest * square * (
        np.float32(-1.6666654611e-1)
        + square * (np.float32(8.3321608736e-3) + square * np.float32(-1.9515295891e-4))
    )
    cosine = (
        1.0
        - 0.5 * square
        + square
        * square
        * (
            np.float32(4.166664568298827e-2)
            + square
            * (np.float32(-1.388731625493765e-3) + square * np.float32(2.443315711809948e-5))
        )
    )
    quarter = turns.astype(jnp.int32) & 3
    swap = (quarter & 1) == 1
    cos_out = jnp.where(swap, sine, cosine)
    sin_out = jnp.where(swap, cosine, sine)
    cos_out = jnp.where((quarter == 1) | (quarter == 2), -cos_out, cos_out)
    sin_out = jnp.where(quarter >= 2, -sin_out, sin_out)
    return cos_out, sin_out


def rotate_heads(queries, position):
    head_dim = queries.shape[-1]
    half_dim = head_dim // 2
    frequency = (ROPE_BASE ** (-np.arange(half_dim) * 2.0 / head_dim)).astype(np.float32)
    cosine, sine = cosine_and_sine(position[:, None] * frequency[None, :])
    cosine = jnp.concatenate([cosine, cosine], axis=1)[:, None, :]
    sine = jnp.concatenate([-sine, sine], axis=1)[:, None, :]
    turned = jnp.concatenate([queries[..., half_dim:], queries[..., :half_dim]], axis=-1)
    return queries * cosine + turned * sine


def statement_ranges(lengths_row, order_row):
    stmt_count = order_row.shape[0]
    index = jnp.arange(stmt_count, dtype=jnp.int32)
    slot = jnp.sum(jnp.where(order_row[None, :] == index[:, None], index[None, :], 0), axis=1)
    start = jnp.sum(jnp.where(slot[None, :] < slot[:, None], lengths_row[None, :], 0), axis=1)
    return start, start + lengths_row


def block_attention(all_queries, cached_keys, cached_values, token_mask, score_scale):
    stmt_count, head_count, head_dim = all_queries.shape
    kv_heads = cached_keys.shape[1] // head_dim
    group_size = head_count // kv_heads
    grouped = all_queries.reshape(stmt_count, kv_heads, group_size, head_dim)
    key_heads = cached_keys.reshape(-1, kv_heads, head_dim)
    value_heads = cached_values.reshape(-1, kv_heads, head_dim)
    scores = (
        jnp.einsum("skgd,tkd->skgt", grouped, key_heads, preferred_element_type=jnp.float32)
        * score_scale
    )
    token_mask = token_mask[:, None, None, :]
    block_max = jnp.max(jnp.where(token_mask, scores, MASKED_LOGIT), axis=3)
    softmax_weights = jnp.where(token_mask, jnp.exp(scores - block_max[..., None]), 0.0)
    block_sum = jnp.sum(softmax_weights, axis=3)
    numerators = jnp.einsum(
        "skgt,tkd->skgd",
        softmax_weights.astype(jnp.bfloat16),
        value_heads,
        preferred_element_type=jnp.float32,
    )
    return (
        block_max.reshape(stmt_count, head_count),
        block_sum.reshape(stmt_count, head_count),
        numerators.reshape(stmt_count, head_count, head_dim),
    )


def flip(array, axis, offset):
    size = lax.axis_size(axis)
    return lax.ppermute(array, axis, [(i, i ^ offset) for i in range(size)])


def in_vmem(body, outputs, *operands, limit=8, flops=1_000_000):
    whole = pl.BlockSpec(memory_space=pltpu.VMEM)
    moved = sum(operand.size * operand.dtype.itemsize for operand in operands)
    return pl.pallas_call(
        body,
        out_shape=outputs,
        in_specs=[whole] * len(operands),
        out_specs=jax.tree.map(lambda _: whole, outputs),
        compiler_params=pltpu.CompilerParams(vmem_limit_bytes=limit << 20),
        cost_estimate=pl.CostEstimate(flops=flops, bytes_accessed=moved, transcendentals=0),
    )(*operands)


def shaped(shape, kind):
    return jax.ShapeDtypeStruct(shape, kind)


def open_window(out_ref):
    out_ref[...] = jnp.zeros_like(out_ref)


def prepare_inputs(window_ref, hidden_ref, gain_ref, message_ref):
    del window_ref
    inputs = hidden_ref[...].astype(jnp.float32)
    width = inputs.shape[1]
    message_ref[:, :width] = (inputs * gain_ref[...]).astype(jnp.bfloat16)
    message_ref[:, width:] = pack_statistics(
        [jnp.sum(inputs * inputs, axis=1, keepdims=True)], core_number()
    )


def positions_and_ranges(
    message_ref, frequency_ref, lengths_ref, order_ref, rope_ref, range_ref
):
    del message_ref
    count = lengths_ref.shape[1]
    half = frequency_ref.shape[1] // 2
    row = lax.broadcasted_iota(jnp.int32, (count, count), 0)
    column = lax.broadcasted_iota(jnp.int32, (count, count), 1)
    lengths = jnp.broadcast_to(lengths_ref[...], (count, count)).astype(jnp.float32)
    length = jnp.sum(jnp.where(row == column, lengths, 0.0), axis=1, keepdims=True)
    order = jnp.broadcast_to(order_ref[...], (count, count))
    placed = order == row
    slot = jnp.sum(jnp.where(placed, column, 0).astype(jnp.float32), axis=1, keepdims=True)
    packed = jnp.sum(jnp.where(placed, length, 0.0), axis=0, keepdims=True)
    earlier = column.astype(jnp.float32) < slot
    start = jnp.sum(jnp.where(earlier, packed, 0.0), axis=1, keepdims=True)
    range_ref[:, :128] = jnp.broadcast_to(start, (count, 128))
    range_ref[:, 128:] = jnp.broadcast_to(start + length, (count, 128))
    cosine, sine = cosine_and_sine((length - 1.0) * frequency_ref[...])
    lane = lax.broadcasted_iota(jnp.int32, cosine.shape, 1)
    rope_ref[:, : 2 * half] = cosine
    rope_ref[:, 2 * half :] = jnp.where(lane < half, -sine, sine)


LOG2_E = 1.4426950408889634


def pack_statistics(values, first=0):
    rows = values[0].shape[0]
    lane = lax.broadcasted_iota(jnp.int32, (rows, 128), 1)
    rest = jnp.zeros((rows, 128), jnp.float32)
    for place, value in enumerate(values):
        rest = jnp.where(lane == first + place, value, rest)
    out = rest.astype(jnp.bfloat16).astype(jnp.float32)
    for part in (1, 2):
        rest = rest - rest.astype(jnp.bfloat16).astype(jnp.float32)
        out = out + pltpu.roll(rest.astype(jnp.bfloat16).astype(jnp.float32), 32 * part, 1)
    return out.astype(jnp.bfloat16)


def read_statistic(block, first, count=1):
    lane = lax.broadcasted_iota(jnp.int32, block.shape, 1)
    place = (lane & 31) - first
    mine = (place >= 0) & (place < count) & (lane < 96)
    return jnp.sum(jnp.where(mine, block.astype(jnp.float32), 0.0), axis=1, keepdims=True)


def core_number():
    return lax.axis_index("pack") & 1


def chip_number():
    return lax.axis_index("pack") >> 1


def send_across(array, axis, offset, sender):
    groups, pack = lax.axis_size("dp"), lax.axis_size("pack")
    pairs = []
    for group in range(groups):
        for place in range(pack):
            if place % 2 != sender:
                target = (group, place ^ 1)
            elif axis == "dp":
                target = (group ^ offset, place ^ 1)
            else:
                target = (group, place ^ (2 * offset) ^ 1)
            pairs.append((group * pack + place, target[0] * pack + target[1]))
    return lax.ppermute(array, ("dp", "pack"), pairs)


def copy_tokens(_, key_ref, value_ref, out_ref):
    out_ref[0] = key_ref[...]
    out_ref[1] = value_ref[...]


def prepare_pair(_, own_ref, other_ref, own_gain_ref, other_gain_ref, pair_ref):
    width = own_ref.shape[1]
    squares = 0.0
    scaled = []
    for ref, factor_ref in ((own_ref, own_gain_ref), (other_ref, other_gain_ref)):
        inputs = ref[...].astype(jnp.float32)
        squares = squares + jnp.sum(inputs * inputs, axis=1, keepdims=True)
        scaled.append((inputs * factor_ref[...]).astype(jnp.bfloat16))
    pair_ref[:, 2 * width :] = pack_statistics([squares])
    for first in range(2):

        @pl.when(core_number() == first)
        def _():
            pair_ref[:, :width] = scaled[first]
            pair_ref[:, width : 2 * width] = scaled[1 - first]


def project_pair(pair_ref, offset, weight_ref):
    chip = chip_number() ^ offset
    width = 2 * weight_ref.shape[1]
    rows = pl.ds(pl.multiple_of(chip * width, width), width)
    return jnp.dot(
        pair_ref[:, :width], weight_ref[rows, :], preferred_element_type=jnp.float32
    )


def project_own_pair(pair_ref, weight_ref, total_ref):
    total_ref[...] = project_pair(pair_ref, 0, weight_ref)


def make_queries(
    third_ref,
    second_ref,
    first_ref,
    pair_ref,
    weight_ref,
    gain_ref,
    rope_ref,
    *refs,
    model_width,
):
    query_ref = refs[-1]
    width = query_ref.shape[1]
    head_dim = gain_ref.shape[1]

    @pl.when(core_number() == 1)
    def _():
        blocks = (pair_ref, first_ref, second_ref, third_ref)
        if len(refs) == 2:
            projected = refs[0][...]
        else:
            projected = project_pair(pair_ref, 0, weight_ref)
        squares = pair_ref[:, 2 * width :].astype(jnp.float32)
        for offset in (3, 2, 1):
            projected = projected + project_pair(blocks[offset], offset, weight_ref)
            squares = squares + blocks[offset][:, 2 * width :].astype(jnp.float32)
        squares = read_statistic(squares, 0)
        projected = projected * lax.rsqrt(squares / model_width + EPSILON)
        cosine = rope_ref[:, :head_dim]
        sine = rope_ref[:, head_dim:]
        for head in range(width // head_dim):
            place = slice(head * head_dim, (head + 1) * head_dim)
            query = projected[:, place]
            mean = jnp.mean(query * query, axis=1, keepdims=True)
            query = query * lax.rsqrt(mean + EPSILON) * gain_ref[...]
            turned = pltpu.roll(query, head_dim // 2, 1)
            query_ref[:, place] = (query * cosine + turned * sine).astype(jnp.bfloat16)


def join_queries(first_ref, second_ref, out_ref):
    width = first_ref.shape[1]
    out_ref[:, :width] = first_ref[...]
    out_ref[:, width:] = second_ref[...]


def token_masks(range_ref, tokens, group):
    me = lax.axis_index("pack")
    masks = []
    for owner in (me, me ^ 1):
        index = lax.broadcasted_iota(jnp.int32, (range_ref.shape[0], tokens), 1) + owner * tokens
        index = index.astype(jnp.float32)
        mask = (index >= range_ref[:, :1]) & (index < range_ref[:, 128:129])
        masks.append(jnp.concatenate([mask.astype(jnp.float32)] * group, axis=0) > 0.5)
    return masks


def attend_heads(queries, heads, key_ref, value_ref, other_ref, masks):
    head_dim = 128
    scale = head_dim**-0.5
    scores = []
    columns = []
    for query, head in zip(queries, heads):
        grouped = jnp.concatenate(
            [query[:, i : i + head_dim] for i in range(0, query.shape[1], head_dim)], axis=0
        )
        column = pl.ds(pl.multiple_of(head * head_dim, head_dim), head_dim)
        columns.append(column)
        raw = [
            lax.dot_general(
                grouped, keys, (((1,), (1,)), ((), ())), preferred_element_type=jnp.float32
            )
            for keys in (key_ref[:, column], other_ref[0, :, column])
        ]
        scores.append([jnp.where(mask, part, MASKED_LOGIT) for mask, part in zip(masks, raw)])
    maxima = [
        jnp.maximum(
            jnp.max(first, axis=1, keepdims=True), jnp.max(second, axis=1, keepdims=True)
        )
        for first, second in scores
    ]
    weights = [
        [jnp.exp2((part - highest) * (scale * LOG2_E)) for part in parts]
        for parts, highest in zip(scores, maxima)
    ]
    out = []
    for parts, highest, column in zip(weights, maxima, columns):
        total = jnp.sum(parts[0], axis=1, keepdims=True) + jnp.sum(
            parts[1], axis=1, keepdims=True
        )
        numerators = jnp.dot(
            parts[0].astype(jnp.bfloat16), value_ref[:, column], preferred_element_type=jnp.float32
        ) + jnp.dot(
            parts[1].astype(jnp.bfloat16),
            other_ref[1, :, column],
            preferred_element_type=jnp.float32,
        )
        out.append((highest * scale + jnp.log(total), numerators / total))
    return out


def attend_remote(query_ref, key_ref, value_ref, other_ref, range_ref, *refs, offset):
    out_ref = refs[-1]

    @pl.when(core_number() == 0)
    def _():
        rows = query_ref.shape[0]
        width = query_ref.shape[1] // 2
        masks = token_masks(range_ref, key_ref.shape[0], width // 128)
        chip = chip_number() ^ offset
        queries = [query_ref[:, :width], query_ref[:, width:]]
        heads = (2 * chip, 2 * chip + 1)
        parts = attend_heads(queries, heads, key_ref, value_ref, other_ref, masks)
        stats = []
        for j, (level, averages) in enumerate(parts):
            for h in range(width // 128):
                part = slice(h * rows, (h + 1) * rows)
                place = slice(j * width + h * 128, j * width + (h + 1) * 128)
                out_ref[:, place] = averages[part].astype(jnp.bfloat16)
                stats.append(level[part])
        out_ref[:, 2 * width :] = pack_statistics(stats)


def attend_own(query_ref, key_ref, value_ref, other_ref, range_ref, out_ref, stats_ref):
    @pl.when(core_number() == 1)
    def _():
        width = query_ref.shape[1] // 2
        masks = token_masks(range_ref, key_ref.shape[0], width // 128)
        chip = chip_number()
        parts = attend_heads(
            [query_ref[:, :width], query_ref[:, width:]],
            (2 * chip, 2 * chip + 1),
            key_ref,
            value_ref,
            other_ref,
            masks,
        )
        for j, (level, averages) in enumerate(parts):
            out_ref[j] = averages
            stats_ref[j] = jnp.broadcast_to(level, averages.shape)


def merge_partials(third_ref, second_ref, first_ref, own_ref, stats_ref, *refs):
    attended_ref = refs[-1]

    @pl.when(core_number() == 1)
    def _():
        rows = attended_ref.shape[0]
        width = attended_ref.shape[1] // 2
        others = (first_ref, second_ref, third_ref)
        stats = [ref[:, 2 * width :] for ref in others]
        for j in range(2):
            for h in range(width // 128):
                part = slice(h * rows, (h + 1) * rows)
                place = slice(j * width + h * 128, j * width + (h + 1) * 128)
                slot = j * (width // 128) + h
                levels = [stats_ref[j, part]] + [read_statistic(s, slot) for s in stats]
                averages = [own_ref[j, part]]
                averages += [ref[:, place].astype(jnp.float32) for ref in others]
                highest = levels[0]
                for level in levels[1:]:
                    highest = jnp.maximum(highest, level)
                factors = [jnp.exp(level - highest) for level in levels]
                summed = sum(factor * average for factor, average in zip(factors, averages))
                attended_ref[:, place] = (summed / sum(factors)).astype(jnp.bfloat16)


def copy_weights(_, weight_ref, out_ref):
    out_ref[...] = weight_ref[...]


def project_out(attended_ref, weight_ref, other_weight_ref, *refs, offset):
    out_ref = refs[-1]

    @pl.when(core_number() == 1)
    def _():
        width = attended_ref.shape[1] // 2
        column = pl.ds(pl.multiple_of((chip_number() ^ offset) * 2 * width, 2 * width), 2 * width)
        total = jnp.dot(
            attended_ref[:, width:], weight_ref[:, column], preferred_element_type=jnp.float32
        ) + jnp.dot(
            attended_ref[:, :width], other_weight_ref[:, column], preferred_element_type=jnp.float32
        )
        out_ref[...] = total.astype(out_ref.dtype)


def finish_hidden(
    third_ref,
    second_ref,
    first_ref,
    kept_ref,
    own_ref,
    other_ref,
    own_gain_ref,
    other_gain_ref,
    sent_ref,
    scaled_ref,
    other_scaled_ref,
):
    width = own_ref.shape[1]

    @pl.when(core_number() == 0)
    def _():
        squares = 0.0
        inputs = (own_ref, other_ref)
        gains = (own_gain_ref, other_gain_ref)
        for core in range(2):
            place = slice(core * width, (core + 1) * width)
            hidden = inputs[core][...].astype(jnp.float32)
            for ref in (kept_ref, first_ref, second_ref, third_ref):
                hidden = hidden + ref[:, place].astype(jnp.float32)
            scaled = hidden * gains[core][...]
            (scaled_ref, other_scaled_ref)[core][...] = scaled
            sent_ref[:, place] = scaled.astype(jnp.bfloat16)
            squares = squares + jnp.sum(hidden * hidden, axis=1, keepdims=True)
        sent_ref[:, 2 * width :] = pack_statistics([squares])


def gram_part(third_ref, second_ref, first_ref, own_ref, _, out_ref, near_ref, far_ref):
    @pl.when(core_number() == 1)
    def _():
        rows = own_ref.shape[0]
        width = far_ref.shape[1]
        refs = (own_ref, first_ref, second_ref, third_ref)
        for i, ref in enumerate(refs):
            near_ref[i * rows : (i + 1) * rows] = ref[:, width : 2 * width]
        for i, ref in enumerate(refs[1:]):
            far_ref[i * rows : (i + 1) * rows] = ref[:, :width]
        far = jnp.concatenate([ref[:, :width] for ref in refs], axis=0)
        squares = read_statistic(own_ref[:, 2 * width :], 0)
        gram = 0.0
        for vectors in (near_ref[...], far):
            gram = gram + lax.dot_general(
                vectors, vectors, (((1,), (1,)), ((), ())), preferred_element_type=jnp.float32
            )
        half = gram.shape[0] // 2
        out_ref[:half, : 2 * half] = gram[:half]
        out_ref[:half, 2 * half :] = gram[half:]
        out_ref[half:, :] = jnp.broadcast_to(squares, (rows, 128))


def sum_grams(third_ref, second_ref, first_ref, own_ref, *refs):
    out_ref = refs[-1]
    out_ref[...] = own_ref[...] + first_ref[...] + second_ref[...] + third_ref[...]


def partner_masks(partner_ref, out_ref, *, rows):
    group = lax.axis_index("dp")
    shape = out_ref.shape[1:]
    row = lax.broadcasted_iota(jnp.int32, shape, 0)
    column = lax.broadcasted_iota(jnp.int32, shape, 1)
    row_id = ((group ^ (row // rows)) * rows) + row % rows
    column_id = ((group ^ (column // rows)) * rows) + column % rows
    partners = jnp.broadcast_to(partner_ref[...], shape)
    row_partner = jnp.sum(
        jnp.where(column == row_id, partners, 0).astype(jnp.float32), axis=1, keepdims=True
    )
    column_partner = jnp.sum(
        jnp.where(row_id == column_id, row_partner, 0.0), axis=0, keepdims=True
    )
    own_partner = column_id.astype(jnp.float32) == row_partner
    other_partner = row_id.astype(jnp.float32) == column_partner
    own_partner = own_partner.astype(jnp.float32)
    out_ref[0] = own_partner
    out_ref[1] = own_partner + other_partner.astype(jnp.float32)


def losses_and_gradient(
    summed_ref,
    other_summed_ref,
    near_ref,
    sent_ref,
    other_far_ref,
    scaled_ref,
    other_scaled_ref,
    gain_ref,
    partner_ref,
    pooled_ref,
    loss_ref,
    grad_ref,
    *,
    model_width,
):
    me = lax.axis_index("pack")
    leads = core_number() == 1
    count, width = near_ref.shape
    rows = scaled_ref.shape[0]
    half = count // 2
    summed = jnp.where(leads, other_summed_ref[...], summed_ref[...])
    gram = jnp.concatenate([summed[:half, :count], summed[:half, count:]], axis=0)
    squares = summed[half:, :1]
    shape = (count, count)
    row = lax.broadcasted_iota(jnp.int32, shape, 0)
    column = lax.broadcasted_iota(jnp.int32, shape, 1)
    diagonal = row == column
    on_diagonal = jnp.where(diagonal, gram, 0.0)
    row_scale = lax.rsqrt(jnp.sum(on_diagonal, axis=1, keepdims=True))
    column_scale = lax.rsqrt(jnp.sum(on_diagonal, axis=0, keepdims=True))
    cosines = gram * row_scale * column_scale
    logits = cosines * (1.0 / SOFTMAX_WARMTH)
    powers = jnp.where(diagonal, 0.0, jnp.exp(logits))
    row_sum = jnp.sum(powers, axis=1, keepdims=True)
    column_sum = jnp.sum(powers, axis=0, keepdims=True)
    weights = (powers * (1.0 / row_sum + 1.0 / column_sum) - partner_ref[1])[:rows]
    target = jnp.sum(partner_ref[0] * logits, axis=1, keepdims=True)
    loss = jnp.log(row_sum) - target
    own = loss_ref.shape[0]
    index = lax.broadcasted_iota(jnp.int32, (count, 1), 0)
    for i in range(own):
        loss_ref[i] = jnp.sum(jnp.where(index == me * own + i, loss, 0.0))
    inner = jnp.sum(weights * cosines[:rows], axis=1, keepdims=True)
    scaled_weights = weights * column_scale
    upper = scaled_weights.astype(jnp.bfloat16)
    lower = (scaled_weights - upper.astype(jnp.float32)).astype(jnp.bfloat16)
    own_scale = row_scale[:rows]
    pooled_scale = lax.rsqrt(squares / model_width + EPSILON)
    grad_gain = gain_ref[...] * (model_width**0.5 / SOFTMAX_WARMTH)

    def write(vectors, scaled):
        gradient = jnp.dot(upper, vectors, preferred_element_type=jnp.float32) + jnp.dot(
            lower, vectors, preferred_element_type=jnp.float32
        )
        gradient = (gradient - scaled * (own_scale * inner)) * own_scale
        grad_ref[...] = (gradient * grad_gain).astype(jnp.bfloat16)
        pooled_ref[...] = (scaled * pooled_scale).astype(jnp.bfloat16)

    @pl.when(leads)
    def _():
        write(near_ref[...], other_scaled_ref[...])

    @pl.when(core_number() == 0)
    def _():
        vectors = jnp.concatenate((sent_ref[:, :width], other_far_ref[...]), axis=0)
        write(vectors, scaled_ref[...])


def core_roles(
    hidden_in,
    attn_gain,
    w_query,
    query_gain,
    cached_keys,
    cached_values,
    w_out,
    final_gain,
    lengths,
    pack_order,
    partner,
):
    pack_size = lax.axis_size("pack")
    stmts, width = hidden_in.shape
    model_width = width * pack_size
    head_dim = query_gain.shape[0]
    tokens = cached_keys.shape[0]
    chips = pack_size // 2
    others = range(1, chips)
    total = partner.shape[0]
    bf16 = jnp.bfloat16
    f32 = jnp.float32
    final_gain = final_gain[None]
    query_gain = query_gain[None]
    half = np.arange(head_dim // 2)
    frequency = (ROPE_BASE ** (-half * 2.0 / head_dim)).astype(np.float32)
    frequency = jnp.asarray(np.concatenate([frequency, frequency])[None])
    whole = pl.BlockSpec(memory_space=pltpu.VMEM)

    window = pl.pallas_call(
        open_window,
        out_shape=shaped((8, 128), f32),
        out_specs=whole,
        compiler_params=pltpu.CompilerParams(vmem_limit_bytes=1 << 20),
        cost_estimate=pl.CostEstimate(flops=1 << 34, bytes_accessed=0, transcendentals=0),
    )()
    attn_gain = attn_gain[None]
    other_hidden_in = flip(hidden_in, "pack", 1)
    other_w_query = flip(w_query, "pack", 1)
    pair = in_vmem(
        prepare_pair,
        shaped((stmts, 2 * width + 128), bf16),
        window,
        hidden_in,
        other_hidden_in,
        attn_gain,
        flip(attn_gain, "pack", 1),
        flops=1 << 34,
    )
    received = [send_across(pair, "pack", k, 0) for k in others]
    own_projected = in_vmem(
        project_own_pair, shaped((stmts, width), f32), pair, w_query, limit=16, flops=1 << 26
    )
    rope, ranges = in_vmem(
        positions_and_ranges,
        (shaped((stmts, 2 * head_dim), f32), shaped((stmts, 256), f32)),
        pair,
        frequency,
        lengths,
        pack_order,
    )
    held = in_vmem(
        copy_tokens,
        shaped((2,) + cached_keys.shape, bf16),
        own_projected,
        cached_keys,
        cached_values,
    )
    other_held = flip(held, "pack", 1)
    other_gain = flip(final_gain, "pack", 1)

    def queries_from(weights, flops, *own):
        return in_vmem(
            lambda *refs: make_queries(*refs, model_width=model_width),
            shaped((stmts, width), bf16),
            *received[::-1],
            pair,
            weights,
            query_gain,
            rope,
            *own,
            limit=16,
            flops=flops,
        )

    second_queries = queries_from(w_query, 1 << 34, own_projected)
    first_queries = queries_from(other_w_query, 1 << 27)
    queries = in_vmem(
        join_queries, shaped((stmts, 2 * width), bf16), first_queries, second_queries
    )
    other_weights = flip(
        in_vmem(copy_weights, shaped(w_out.shape, bf16), queries, w_out, limit=16), "pack", 1
    )
    received = [send_across(queries, "pack", k, 1) for k in others]
    group_rows = stmts * (width // head_dim)
    own_part, own_stats = in_vmem(
        attend_own,
        (shaped((2, group_rows, head_dim), f32),) * 2,
        queries,
        cached_keys,
        cached_values,
        other_held,
        ranges,
        flops=1 << 27,
    )
    partials = []
    for k, part in zip(others[::-1], received[::-1]):
        partials.append(
            in_vmem(
                lambda *refs, offset=k: attend_remote(*refs, offset=offset),
                shaped((stmts, 2 * width + 128), bf16),
                part,
                cached_keys,
                cached_values,
                other_held,
                ranges,
                *(partials[-1:] or (own_stats,)),
                flops=1 << 34,
            )
        )
    received = [send_across(part, "pack", k, 0) for k, part in zip(others, partials[::-1])]
    attended = in_vmem(
        merge_partials,
        shaped((stmts, 2 * width), bf16),
        *received[::-1],
        own_part,
        own_stats,
    )

    def projected_to(offset, kind, *after):
        return in_vmem(
            lambda *refs: project_out(*refs, offset=offset),
            shaped((stmts, 2 * width), kind),
            attended,
            w_out,
            other_weights,
            *after,
            limit=16,
            flops=1 << 27,
        )

    third = projected_to(3, bf16)
    second = projected_to(2, bf16, third)
    first = projected_to(1, bf16, second)
    kept = projected_to(0, bf16, first)
    received = [send_across(part, "pack", k, 1) for k, part in zip(others, (first, second, third))]
    vector, scaled, far_scaled = in_vmem(
        finish_hidden,
        (shaped((stmts, 2 * width + 128), bf16),) + (shaped((stmts, width), f32),) * 2,
        *received[::-1],
        flip(kept, "pack", 1),
        hidden_in,
        other_hidden_in,
        final_gain,
        other_gain,
    )
    received = [send_across(vector, "dp", k, 0) for k in range(1, lax.axis_size("dp"))]
    other_scaled = flip(far_scaled, "pack", 1)
    gram, near, far = in_vmem(
        gram_part,
        (
            shaped((total // 2 + stmts, 128), f32),
            shaped((total, width), bf16),
            shaped((total - stmts, width), bf16),
        ),
        *received[::-1],
        flip(vector, "pack", 1),
        other_scaled,
    )
    received = [send_across(gram, "pack", k, 1) for k in others]
    other_far = flip(far, "pack", 1)
    summed = in_vmem(
        sum_grams,
        shaped(gram.shape, f32),
        *received[::-1],
        flip(gram, "pack", 1),
    )
    masks = in_vmem(
        lambda *refs: partner_masks(*refs, rows=stmts),
        shaped((2, total, total), f32),
        partner[None],
    )
    pooled, loss_rows, grad_hidden = pl.pallas_call(
        lambda *refs: losses_and_gradient(*refs, model_width=model_width),
        out_shape=(
            shaped((stmts, width), bf16),
            shaped((stmts // pack_size,), f32),
            shaped((stmts, width), bf16),
        ),
        in_specs=[whole] * 9,
        out_specs=(whole, pl.BlockSpec(memory_space=pltpu.SMEM), whole),
        compiler_params=pltpu.CompilerParams(vmem_limit_bytes=8 << 20),
    )(
        summed,
        flip(summed, "pack", 1),
        near,
        vector,
        other_far,
        scaled,
        other_scaled,
        final_gain,
        masks,
    )
    return (pooled, loss_rows, grad_hidden)


def local(
    hidden_in,
    attn_gain,
    w_query,
    query_gain,
    cached_keys,
    cached_values,
    w_out,
    final_gain,
    lengths,
    pack_order,
    partner,
):
    pack_size = lax.axis_size("pack")
    pack_index = lax.axis_index("pack")
    group_index = lax.axis_index("dp")
    stmt_count, feature_count = hidden_in.shape
    model_width = feature_count * pack_size
    head_dim = query_gain.shape[0]
    local_heads = w_query.shape[1] // head_dim
    token_count = cached_keys.shape[0]
    total_stmts = partner.shape[0]
    lengths_row = lengths[0]
    order_row = pack_order[0]
    inputs32 = hidden_in.astype(jnp.float32)

    scaled = (inputs32 * attn_gain[None, :]).astype(jnp.bfloat16)
    squares = split_float(jnp.sum(inputs32 * inputs32, axis=1), 3)
    extra = jnp.stack(squares + [jnp.zeros_like(squares[0])] * 125, axis=1)
    arrived = gather_blocks(jnp.concatenate([scaled, extra], axis=1), "pack")
    input_squares = jnp.sum(arrived[:, :, feature_count : feature_count + 3].astype(jnp.float32), axis=(0, 2))
    input_rms = lax.rsqrt(input_squares / model_width + EPSILON)
    features = jnp.moveaxis(arrived[:, :, :feature_count], 0, 1).reshape(stmt_count, model_width)
    projected = jnp.dot(features, w_query, preferred_element_type=jnp.float32)
    queries = (projected * input_rms[:, None]).reshape(stmt_count, local_heads, head_dim)
    queries = (
        queries
        * lax.rsqrt(jnp.mean(queries * queries, axis=2, keepdims=True) + EPSILON)
        * query_gain
    )
    queries = rotate_heads(queries, (lengths_row - 1).astype(jnp.float32)).astype(jnp.bfloat16)
    all_queries = jnp.moveaxis(gather_blocks(queries, "pack"), 0, 1).reshape(
        stmt_count, pack_size * local_heads, head_dim
    )
    start, end = statement_ranges(lengths_row, order_row)
    tokens = pack_index * token_count + jnp.arange(token_count, dtype=jnp.int32)
    token_mask = (tokens[None, :] >= start[:, None]) & (tokens[None, :] < end[:, None])
    block_max, block_sum, numerators = block_attention(
        all_queries, cached_keys, cached_values, token_mask, head_dim ** (-0.5)
    )

    def by_owner(part):
        return jnp.moveaxis(part.reshape((stmt_count, pack_size, -1)), 1, 0)

    message = jnp.concatenate(
        [by_owner(numerators.astype(jnp.bfloat16))]
        + [by_owner(piece) for piece in split_float(block_max, 3) + split_float(block_sum, 2)],
        axis=2,
    )
    message = lax.all_to_all(message, "pack", 0, 0)
    width = local_heads * head_dim
    stats = message[:, :, width:].astype(jnp.float32).reshape(pack_size, stmt_count, 5, local_heads)
    maxima = stats[:, :, 0] + stats[:, :, 1] + stats[:, :, 2]
    factor = jnp.exp(maxima - jnp.max(maxima, axis=0, keepdims=True))
    denominator = jnp.sum((stats[:, :, 3] + stats[:, :, 4]) * factor, axis=0)
    numerators = message[:, :, :width].astype(jnp.float32).reshape(pack_size, stmt_count, local_heads, head_dim)
    summed = jnp.sum(numerators * factor[..., None], axis=0)
    attended = (summed / denominator[..., None]).astype(jnp.bfloat16)
    partial_out = jnp.dot(
        attended.reshape(stmt_count, width), w_out, preferred_element_type=jnp.float32
    )
    partial_out = jnp.moveaxis(
        partial_out.astype(jnp.bfloat16).reshape(stmt_count, pack_size, feature_count), 1, 0
    )
    partial_out = lax.all_to_all(partial_out, "pack", 0, 0)
    hidden = inputs32 + jnp.sum(partial_out.astype(jnp.float32), axis=0)
    scaled_out = hidden * final_gain[None, :]
    vectors = lax.all_gather(scaled_out.astype(jnp.bfloat16), "dp", axis=0, tiled=True)
    gram = lax.dot_general(
        vectors, vectors, (((1,), (1,)), ((), ())), preferred_element_type=jnp.float32
    )
    own_squares = jnp.sum(hidden * hidden, axis=1)
    extra = jnp.zeros((total_stmts,), jnp.float32).at[:stmt_count].set(own_squares)
    gram = jnp.concatenate([gram, extra[:, None]], axis=1)
    if total_stmts <= 128:
        gram = jnp.sum(gather_blocks(gram, "pack"), axis=0)
    else:
        gram = lax.psum(gram, "pack")
    hidden_rms = jnp.sqrt(gram[:stmt_count, total_stmts] / model_width + EPSILON)
    gram = gram[:, :total_stmts]
    column_ids = jnp.arange(total_stmts, dtype=jnp.int32)
    diagonal = column_ids[:, None] == column_ids[None, :]
    norms_row = lax.rsqrt(jnp.sum(jnp.where(diagonal, gram, 0.0), axis=0))
    norms_column = lax.rsqrt(jnp.sum(jnp.where(diagonal, gram, 0.0), axis=1))
    cosines = gram * norms_column[:, None] * norms_row[None, :]
    logits = jnp.where(diagonal, MASKED_LOGIT, cosines / SOFTMAX_WARMTH)
    highest = jnp.max(logits, axis=1)
    all_lse = highest + jnp.log(jnp.sum(jnp.exp(logits - highest[:, None]), axis=1))
    is_partner = column_ids[None, :] == partner[:, None]
    all_loss = all_lse - jnp.sum(jnp.where(is_partner, logits, 0.0), axis=1)
    own_count = stmt_count // pack_size
    row_base = group_index * stmt_count
    loss_rows = lax.dynamic_slice_in_dim(all_loss, row_base + pack_index * own_count, own_count, 0)
    weights = (
        jnp.exp(logits - all_lse[:, None])
        + jnp.exp(logits - all_lse[None, :])
        - is_partner.astype(jnp.float32)
        - is_partner.T.astype(jnp.float32)
    ).astype(jnp.bfloat16)
    own_weights = lax.dynamic_slice_in_dim(weights, row_base, stmt_count, 0)
    own_cosines = lax.dynamic_slice_in_dim(cosines, row_base, stmt_count, 0)
    own_norm = lax.dynamic_slice_in_dim(norms_column, row_base, stmt_count, 0)
    inner = jnp.sum(own_weights.astype(jnp.float32) * own_cosines, axis=1)
    own_norm = own_norm[:, None]
    embeddings = (vectors.astype(jnp.float32) * norms_column[:, None]).astype(jnp.bfloat16)
    gradient = jnp.dot(own_weights, embeddings, preferred_element_type=jnp.float32)
    scale = model_width**0.5 / SOFTMAX_WARMTH
    pooled = (scaled_out / hidden_rms[:, None]).astype(jnp.bfloat16)
    grad_hidden = (
        scale * final_gain[None, :] * (gradient - scaled_out * own_norm * inner[:, None]) * own_norm
    ).astype(jnp.bfloat16)
    return (pooled, loss_rows, grad_hidden)


def solution(mesh):
    body = core_roles if mesh.shape["pack"] == 8 and mesh.shape["dp"] == 4 else local
    in_specs = (
        P("dp", "pack"),
        P("pack"),
        P(None, "pack"),
        P(),
        P(("dp", "pack"), None),
        P(("dp", "pack"), None),
        P("pack", None),
        P("pack"),
        P("dp", None),
        P("dp", None),
        P(),
    )
    out_specs = (P("dp", "pack"), P(("dp", "pack")), P("dp", "pack"))
    return jax.shard_map(body, mesh=mesh, in_specs=in_specs, out_specs=out_specs, check_vma=False)
```

```python
import numpy as np
import jax
import jax.numpy as jnp
from jax import lax
from jax.experimental import pallas as pl
from jax.experimental.pallas import tpu as pltpu
from jax.sharding import PartitionSpec as P

EPSILON = 1e-06
SOFTMAX_WARMTH = 0.05
ROPE_BASE = 1000000.0
MASKED_LOGIT = -1e30


def gather_blocks(block, axis):
    size = lax.axis_size(axis)
    return lax.all_to_all(jnp.broadcast_to(block[None], (size,) + block.shape), axis, 0, 0)


def split_float(value, pieces):
    out = []
    for _ in range(pieces):
        piece = lax.reduce_precision(value, 8, 7)
        out.append(piece.astype(jnp.bfloat16))
        value = value - piece
    return out


def cosine_and_sine(angles):
    turns = jnp.round(angles * np.float32(2.0 / np.pi))
    rest = angles - turns * np.float32(1.5703125)
    rest = rest - turns * np.float32(4.837512969970703125e-4)
    rest = rest - turns * np.float32(7.549789948768648e-8)
    square = rest * rest
    sine = rest + rest * square * (
        np.float32(-1.6666654611e-1)
        + square * (np.float32(8.3321608736e-3) + square * np.float32(-1.9515295891e-4))
    )
    cosine = (
        1.0
        - 0.5 * square
        + square
        * square
        * (
            np.float32(4.166664568298827e-2)
            + square
            * (np.float32(-1.388731625493765e-3) + square * np.float32(2.443315711809948e-5))
        )
    )
    quarter = turns.astype(jnp.int32) & 3
    swap = (quarter & 1) == 1
    cos_out = jnp.where(swap, sine, cosine)
    sin_out = jnp.where(swap, cosine, sine)
    cos_out = jnp.where((quarter == 1) | (quarter == 2), -cos_out, cos_out)
    sin_out = jnp.where(quarter >= 2, -sin_out, sin_out)
    return cos_out, sin_out


def rotate_heads(queries, position):
    head_dim = queries.shape[-1]
    half_dim = head_dim // 2
    frequency = (ROPE_BASE ** (-np.arange(half_dim) * 2.0 / head_dim)).astype(np.float32)
    cosine, sine = cosine_and_sine(position[:, None] * frequency[None, :])
    cosine = jnp.concatenate([cosine, cosine], axis=1)[:, None, :]
    sine = jnp.concatenate([-sine, sine], axis=1)[:, None, :]
    turned = jnp.concatenate([queries[..., half_dim:], queries[..., :half_dim]], axis=-1)
    return queries * cosine + turned * sine


def statement_ranges(lengths_row, order_row):
    stmt_count = order_row.shape[0]
    index = jnp.arange(stmt_count, dtype=jnp.int32)
    slot = jnp.sum(jnp.where(order_row[None, :] == index[:, None], index[None, :], 0), axis=1)
    start = jnp.sum(jnp.where(slot[None, :] < slot[:, None], lengths_row[None, :], 0), axis=1)
    return start, start + lengths_row


def block_attention(all_queries, cached_keys, cached_values, token_mask, score_scale):
    stmt_count, head_count, head_dim = all_queries.shape
    kv_heads = cached_keys.shape[1] // head_dim
    group_size = head_count // kv_heads
    grouped = all_queries.reshape(stmt_count, kv_heads, group_size, head_dim)
    key_heads = cached_keys.reshape(-1, kv_heads, head_dim)
    value_heads = cached_values.reshape(-1, kv_heads, head_dim)
    scores = (
        jnp.einsum("skgd,tkd->skgt", grouped, key_heads, preferred_element_type=jnp.float32)
        * score_scale
    )
    token_mask = token_mask[:, None, None, :]
    block_max = jnp.max(jnp.where(token_mask, scores, MASKED_LOGIT), axis=3)
    softmax_weights = jnp.where(token_mask, jnp.exp(scores - block_max[..., None]), 0.0)
    block_sum = jnp.sum(softmax_weights, axis=3)
    numerators = jnp.einsum(
        "skgt,tkd->skgd",
        softmax_weights.astype(jnp.bfloat16),
        value_heads,
        preferred_element_type=jnp.float32,
    )
    return (
        block_max.reshape(stmt_count, head_count),
        block_sum.reshape(stmt_count, head_count),
        numerators.reshape(stmt_count, head_count, head_dim),
    )


def flip(array, axis, offset):
    size = lax.axis_size(axis)
    return lax.ppermute(array, axis, [(i, i ^ offset) for i in range(size)])


def in_vmem(body, outputs, *operands, limit=8, flops=1_000_000):
    whole = pl.BlockSpec(memory_space=pltpu.VMEM)
    moved = sum(operand.size * operand.dtype.itemsize for operand in operands)
    return pl.pallas_call(
        body,
        out_shape=outputs,
        in_specs=[whole] * len(operands),
        out_specs=jax.tree.map(lambda _: whole, outputs),
        compiler_params=pltpu.CompilerParams(vmem_limit_bytes=limit << 20),
        cost_estimate=pl.CostEstimate(flops=flops, bytes_accessed=moved, transcendentals=0),
    )(*operands)


def shaped(shape, kind):
    return jax.ShapeDtypeStruct(shape, kind)


def open_window(out_ref):
    out_ref[...] = jnp.zeros_like(out_ref)


def prepare_inputs(window_ref, hidden_ref, gain_ref, message_ref):
    del window_ref
    inputs = hidden_ref[...].astype(jnp.float32)
    width = inputs.shape[1]
    message_ref[:, :width] = (inputs * gain_ref[...]).astype(jnp.bfloat16)
    message_ref[:, width:] = pack_statistics(
        [jnp.sum(inputs * inputs, axis=1, keepdims=True)], core_number()
    )


def positions_and_ranges(
    message_ref, frequency_ref, lengths_ref, order_ref, rope_ref, range_ref
):
    del message_ref
    count = lengths_ref.shape[1]
    half = frequency_ref.shape[1] // 2
    row = lax.broadcasted_iota(jnp.int32, (count, count), 0)
    column = lax.broadcasted_iota(jnp.int32, (count, count), 1)
    lengths = jnp.broadcast_to(lengths_ref[...], (count, count)).astype(jnp.float32)
    length = jnp.sum(jnp.where(row == column, lengths, 0.0), axis=1, keepdims=True)
    order = jnp.broadcast_to(order_ref[...], (count, count))
    placed = order == row
    slot = jnp.sum(jnp.where(placed, column, 0).astype(jnp.float32), axis=1, keepdims=True)
    packed = jnp.sum(jnp.where(placed, length, 0.0), axis=0, keepdims=True)
    earlier = column.astype(jnp.float32) < slot
    start = jnp.sum(jnp.where(earlier, packed, 0.0), axis=1, keepdims=True)
    range_ref[:, :128] = jnp.broadcast_to(start, (count, 128))
    range_ref[:, 128:] = jnp.broadcast_to(start + length, (count, 128))
    cosine, sine = cosine_and_sine((length - 1.0) * frequency_ref[...])
    lane = lax.broadcasted_iota(jnp.int32, cosine.shape, 1)
    rope_ref[:, : 2 * half] = cosine
    rope_ref[:, 2 * half :] = jnp.where(lane < half, -sine, sine)


LOG2_E = 1.4426950408889634


def pack_statistics(values, first=0):
    rows = values[0].shape[0]
    lane = lax.broadcasted_iota(jnp.int32, (rows, 128), 1)
    rest = jnp.zeros((rows, 128), jnp.float32)
    for place, value in enumerate(values):
        rest = jnp.where(lane == first + place, value, rest)
    out = rest.astype(jnp.bfloat16).astype(jnp.float32)
    for part in (1, 2):
        rest = rest - rest.astype(jnp.bfloat16).astype(jnp.float32)
        out = out + pltpu.roll(rest.astype(jnp.bfloat16).astype(jnp.float32), 32 * part, 1)
    return out.astype(jnp.bfloat16)


def read_statistic(block, first, count=1):
    lane = lax.broadcasted_iota(jnp.int32, block.shape, 1)
    place = (lane & 31) - first
    mine = (place >= 0) & (place < count) & (lane < 96)
    return jnp.sum(jnp.where(mine, block.astype(jnp.float32), 0.0), axis=1, keepdims=True)


def core_number():
    return lax.axis_index("pack") & 1


def chip_number():
    return lax.axis_index("pack") >> 1


def send_across(array, axis, offset, sender):
    groups, pack = lax.axis_size("dp"), lax.axis_size("pack")
    pairs = []
    for group in range(groups):
        for place in range(pack):
            if place % 2 != sender:
                target = (group, place ^ 1)
            elif axis == "dp":
                target = (group ^ offset, place ^ 1)
            else:
                target = (group, place ^ (2 * offset) ^ 1)
            pairs.append((group * pack + place, target[0] * pack + target[1]))
    return lax.ppermute(array, ("dp", "pack"), pairs)


def copy_tokens(_, key_ref, value_ref, out_ref):
    out_ref[0] = key_ref[...]
    out_ref[1] = value_ref[...]


def prepare_pair(_, own_ref, other_ref, own_gain_ref, other_gain_ref, pair_ref):
    width = own_ref.shape[1]
    squares = 0.0
    scaled = []
    for ref, factor_ref in ((own_ref, own_gain_ref), (other_ref, other_gain_ref)):
        inputs = ref[...].astype(jnp.float32)
        squares = squares + jnp.sum(inputs * inputs, axis=1, keepdims=True)
        scaled.append((inputs * factor_ref[...]).astype(jnp.bfloat16))
    pair_ref[:, 2 * width :] = pack_statistics([squares])
    for first in range(2):

        @pl.when(core_number() == first)
        def _():
            pair_ref[:, :width] = scaled[first]
            pair_ref[:, width : 2 * width] = scaled[1 - first]


def project_pair(pair_ref, offset, weight_ref):
    chip = chip_number() ^ offset
    width = 2 * weight_ref.shape[1]
    rows = pl.ds(pl.multiple_of(chip * width, width), width)
    return jnp.dot(
        pair_ref[:, :width], weight_ref[rows, :], preferred_element_type=jnp.float32
    )


def project_own_pair(pair_ref, weight_ref, total_ref):
    total_ref[...] = project_pair(pair_ref, 0, weight_ref)


def make_queries(
    third_ref,
    second_ref,
    first_ref,
    pair_ref,
    weight_ref,
    gain_ref,
    rope_ref,
    *refs,
    model_width,
):
    query_ref = refs[-1]
    width = query_ref.shape[1]
    head_dim = gain_ref.shape[1]

    @pl.when(core_number() == 1)
    def _():
        blocks = (pair_ref, first_ref, second_ref, third_ref)
        if len(refs) == 2:
            projected = refs[0][...]
        else:
            projected = project_pair(pair_ref, 0, weight_ref)
        squares = pair_ref[:, 2 * width :].astype(jnp.float32)
        for offset in (3, 2, 1):
            projected = projected + project_pair(blocks[offset], offset, weight_ref)
            squares = squares + blocks[offset][:, 2 * width :].astype(jnp.float32)
        squares = read_statistic(squares, 0)
        projected = projected * lax.rsqrt(squares / model_width + EPSILON)
        cosine = rope_ref[:, :head_dim]
        sine = rope_ref[:, head_dim:]
        for head in range(width // head_dim):
            place = slice(head * head_dim, (head + 1) * head_dim)
            query = projected[:, place]
            mean = jnp.mean(query * query, axis=1, keepdims=True)
            query = query * lax.rsqrt(mean + EPSILON) * gain_ref[...]
            turned = pltpu.roll(query, head_dim // 2, 1)
            query_ref[:, place] = (query * cosine + turned * sine).astype(jnp.bfloat16)


def join_queries(first_ref, second_ref, out_ref):
    width = first_ref.shape[1]
    out_ref[:, :width] = first_ref[...]
    out_ref[:, width:] = second_ref[...]


def token_masks(range_ref, tokens, group):
    me = lax.axis_index("pack")
    masks = []
    for owner in (me, me ^ 1):
        index = lax.broadcasted_iota(jnp.int32, (range_ref.shape[0], tokens), 1) + owner * tokens
        index = index.astype(jnp.float32)
        mask = (index >= range_ref[:, :1]) & (index < range_ref[:, 128:129])
        masks.append(jnp.concatenate([mask.astype(jnp.float32)] * group, axis=0) > 0.5)
    return masks


def attend_heads(queries, heads, key_ref, value_ref, other_ref, masks):
    head_dim = 128
    scale = head_dim**-0.5
    scores = []
    columns = []
    for query, head in zip(queries, heads):
        grouped = jnp.concatenate(
            [query[:, i : i + head_dim] for i in range(0, query.shape[1], head_dim)], axis=0
        )
        column = pl.ds(pl.multiple_of(head * head_dim, head_dim), head_dim)
        columns.append(column)
        raw = [
            lax.dot_general(
                grouped, keys, (((1,), (1,)), ((), ())), preferred_element_type=jnp.float32
            )
            for keys in (key_ref[:, column], other_ref[0, :, column])
        ]
        scores.append([jnp.where(mask, part, MASKED_LOGIT) for mask, part in zip(masks, raw)])
    maxima = [
        jnp.maximum(
            jnp.max(first, axis=1, keepdims=True), jnp.max(second, axis=1, keepdims=True)
        )
        for first, second in scores
    ]
    weights = [
        [jnp.exp2((part - highest) * (scale * LOG2_E)) for part in parts]
        for parts, highest in zip(scores, maxima)
    ]
    out = []
    for parts, highest, column in zip(weights, maxima, columns):
        total = jnp.sum(parts[0], axis=1, keepdims=True) + jnp.sum(
            parts[1], axis=1, keepdims=True
        )
        numerators = jnp.dot(
            parts[0].astype(jnp.bfloat16), value_ref[:, column], preferred_element_type=jnp.float32
        ) + jnp.dot(
            parts[1].astype(jnp.bfloat16),
            other_ref[1, :, column],
            preferred_element_type=jnp.float32,
        )
        out.append((highest * scale + jnp.log(total), numerators / total))
    return out


def attend_remote(query_ref, key_ref, value_ref, other_ref, range_ref, *refs, offset):
    out_ref = refs[-1]

    @pl.when(core_number() == 0)
    def _():
        rows = query_ref.shape[0]
        width = query_ref.shape[1] // 2
        masks = token_masks(range_ref, key_ref.shape[0], width // 128)
        chip = chip_number() ^ offset
        queries = [query_ref[:, :width], query_ref[:, width:]]
        heads = (2 * chip, 2 * chip + 1)
        parts = attend_heads(queries, heads, key_ref, value_ref, other_ref, masks)
        stats = []
        for j, (level, averages) in enumerate(parts):
            for h in range(width // 128):
                part = slice(h * rows, (h + 1) * rows)
                place = slice(j * width + h * 128, j * width + (h + 1) * 128)
                out_ref[:, place] = averages[part].astype(jnp.bfloat16)
                stats.append(level[part])
        out_ref[:, 2 * width :] = pack_statistics(stats)


def attend_own(query_ref, key_ref, value_ref, other_ref, range_ref, out_ref, stats_ref):
    @pl.when(core_number() == 1)
    def _():
        width = query_ref.shape[1] // 2
        masks = token_masks(range_ref, key_ref.shape[0], width // 128)
        chip = chip_number()
        parts = attend_heads(
            [query_ref[:, :width], query_ref[:, width:]],
            (2 * chip, 2 * chip + 1),
            key_ref,
            value_ref,
            other_ref,
            masks,
        )
        for j, (level, averages) in enumerate(parts):
            out_ref[j] = averages
            stats_ref[j] = jnp.broadcast_to(level, averages.shape)


def merge_partials(third_ref, second_ref, first_ref, own_ref, stats_ref, *refs):
    attended_ref = refs[-1]

    @pl.when(core_number() == 1)
    def _():
        rows = attended_ref.shape[0]
        width = attended_ref.shape[1] // 2
        others = (first_ref, second_ref, third_ref)
        stats = [ref[:, 2 * width :] for ref in others]
        for j in range(2):
            for h in range(width // 128):
                part = slice(h * rows, (h + 1) * rows)
                place = slice(j * width + h * 128, j * width + (h + 1) * 128)
                slot = j * (width // 128) + h
                levels = [stats_ref[j, part]] + [read_statistic(s, slot) for s in stats]
                averages = [own_ref[j, part]]
                averages += [ref[:, place].astype(jnp.float32) for ref in others]
                highest = levels[0]
                for level in levels[1:]:
                    highest = jnp.maximum(highest, level)
                factors = [jnp.exp(level - highest) for level in levels]
                summed = sum(factor * average for factor, average in zip(factors, averages))
                attended_ref[:, place] = (summed / sum(factors)).astype(jnp.bfloat16)


def copy_weights(_, weight_ref, out_ref):
    out_ref[...] = weight_ref[...]


def project_out(attended_ref, weight_ref, other_weight_ref, *refs, offset):
    out_ref = refs[-1]

    @pl.when(core_number() == 1)
    def _():
        width = attended_ref.shape[1] // 2
        column = pl.ds(pl.multiple_of((chip_number() ^ offset) * 2 * width, 2 * width), 2 * width)
        total = jnp.dot(
            attended_ref[:, width:], weight_ref[:, column], preferred_element_type=jnp.float32
        ) + jnp.dot(
            attended_ref[:, :width], other_weight_ref[:, column], preferred_element_type=jnp.float32
        )
        out_ref[...] = total.astype(out_ref.dtype)


def finish_hidden(
    third_ref,
    second_ref,
    first_ref,
    kept_ref,
    own_ref,
    other_ref,
    own_gain_ref,
    other_gain_ref,
    sent_ref,
    scaled_ref,
    other_scaled_ref,
):
    width = own_ref.shape[1]

    @pl.when(core_number() == 0)
    def _():
        squares = 0.0
        inputs = (own_ref, other_ref)
        gains = (own_gain_ref, other_gain_ref)
        for core in range(2):
            place = slice(core * width, (core + 1) * width)
            hidden = inputs[core][...].astype(jnp.float32)
            for ref in (kept_ref, first_ref, second_ref, third_ref):
                hidden = hidden + ref[:, place].astype(jnp.float32)
            scaled = hidden * gains[core][...]
            (scaled_ref, other_scaled_ref)[core][...] = scaled
            sent_ref[:, place] = scaled.astype(jnp.bfloat16)
            squares = squares + jnp.sum(hidden * hidden, axis=1, keepdims=True)
        sent_ref[:, 2 * width :] = pack_statistics([squares])


def gram_part(third_ref, second_ref, first_ref, own_ref, _, out_ref, near_ref, far_ref):
    @pl.when(core_number() == 1)
    def _():
        rows = own_ref.shape[0]
        width = far_ref.shape[1]
        refs = (own_ref, first_ref, second_ref, third_ref)
        for i, ref in enumerate(refs):
            near_ref[i * rows : (i + 1) * rows] = ref[:, width : 2 * width]
        for i, ref in enumerate(refs[1:]):
            far_ref[i * rows : (i + 1) * rows] = ref[:, :width]
        far = jnp.concatenate([ref[:, :width] for ref in refs], axis=0)
        squares = read_statistic(own_ref[:, 2 * width :], 0)
        gram = 0.0
        for vectors in (near_ref[...], far):
            gram = gram + lax.dot_general(
                vectors, vectors, (((1,), (1,)), ((), ())), preferred_element_type=jnp.float32
            )
        half = gram.shape[0] // 2
        lane = lax.broadcasted_iota(jnp.int32, (half, 2 * half), 1)
        squares = jnp.concatenate([squares] * (half // rows), axis=0)
        out_ref[:, : 2 * half] = gram[:half]
        out_ref[:, 2 * half :] = jnp.where(lane < half, squares, gram[half:])


def sum_grams(third_ref, second_ref, first_ref, own_ref, *refs):
    out_ref = refs[-1]
    out_ref[...] = own_ref[...] + first_ref[...] + second_ref[...] + third_ref[...]


def partner_masks(partner_ref, out_ref, *, rows):
    group = lax.axis_index("dp")
    shape = out_ref.shape[1:]
    row = lax.broadcasted_iota(jnp.int32, shape, 0)
    column = lax.broadcasted_iota(jnp.int32, shape, 1)
    row_id = ((group ^ (row // rows)) * rows) + row % rows
    column_id = ((group ^ (column // rows)) * rows) + column % rows
    partners = jnp.broadcast_to(partner_ref[...], shape)
    row_partner = jnp.sum(
        jnp.where(column == row_id, partners, 0).astype(jnp.float32), axis=1, keepdims=True
    )
    column_partner = jnp.sum(
        jnp.where(row_id == column_id, row_partner, 0.0), axis=0, keepdims=True
    )
    own_partner = column_id.astype(jnp.float32) == row_partner
    other_partner = row_id.astype(jnp.float32) == column_partner
    own_partner = own_partner.astype(jnp.float32)
    out_ref[0] = own_partner
    out_ref[1] = own_partner + other_partner.astype(jnp.float32)


def losses_and_gradient(
    summed_ref,
    other_summed_ref,
    near_ref,
    sent_ref,
    other_far_ref,
    scaled_ref,
    other_scaled_ref,
    gain_ref,
    partner_ref,
    pooled_ref,
    loss_ref,
    grad_ref,
    *,
    model_width,
):
    me = lax.axis_index("pack")
    leads = core_number() == 1
    count, width = near_ref.shape
    rows = scaled_ref.shape[0]
    half = count // 2
    summed = jnp.where(leads, other_summed_ref[...], summed_ref[...])
    upper, lower = summed[:, :count], summed[:, count:]
    squares = lower[:rows, :1]
    row = lax.broadcasted_iota(jnp.int32, upper.shape, 0)
    column = lax.broadcasted_iota(jnp.int32, upper.shape, 1)
    diagonal = row == column
    lower_diagonal = row + half == column
    lower = jnp.where(column >= half, lower, 0.0)
    upper_norms = jnp.where(diagonal, upper, 0.0)
    lower_norms = jnp.where(lower_diagonal, lower, 0.0)
    row_scale = lax.rsqrt(jnp.sum(upper_norms, axis=1, keepdims=True))
    lower_scale = lax.rsqrt(jnp.sum(lower_norms, axis=1, keepdims=True))
    column_scale = lax.rsqrt(jnp.sum(upper_norms + lower_norms, axis=0, keepdims=True))
    cosines = upper * row_scale * column_scale
    logits = cosines * (1.0 / SOFTMAX_WARMTH)
    powers = jnp.where(diagonal, 0.0, jnp.exp(logits))
    lower_powers = jnp.exp(lower * lower_scale * column_scale * (1.0 / SOFTMAX_WARMTH))
    lower_powers = jnp.where((column >= half) & ~lower_diagonal, lower_powers, 0.0)
    mirrored = jnp.sum(jnp.where(column >= half, powers, 0.0), axis=1, keepdims=True)
    column_sum = jnp.sum(
        powers + lower_powers + jnp.where(diagonal, mirrored, 0.0), axis=0, keepdims=True
    )
    cosines, logits, powers = cosines[:rows], logits[:rows], powers[:rows]
    row_sum = jnp.sum(powers, axis=1, keepdims=True)
    weights = powers * (1.0 / row_sum + 1.0 / column_sum) - partner_ref[1, :rows]
    target = jnp.sum(partner_ref[0, :rows] * logits, axis=1, keepdims=True)
    loss = jnp.log(row_sum) - target
    own = loss_ref.shape[0]
    index = lax.broadcasted_iota(jnp.int32, (rows, 1), 0)
    for i in range(own):
        loss_ref[i] = jnp.sum(jnp.where(index == me * own + i, loss, 0.0))
    inner = jnp.sum(weights * cosines, axis=1, keepdims=True)
    scaled_weights = weights * column_scale
    coarse = scaled_weights.astype(jnp.bfloat16)
    fine = (scaled_weights - coarse.astype(jnp.float32)).astype(jnp.bfloat16)
    own_scale = row_scale[:rows]
    pooled_scale = lax.rsqrt(squares / model_width + EPSILON)
    grad_gain = gain_ref[...] * (model_width**0.5 / SOFTMAX_WARMTH)

    def write(vectors, scaled):
        gradient = jnp.dot(coarse, vectors, preferred_element_type=jnp.float32) + jnp.dot(
            fine, vectors, preferred_element_type=jnp.float32
        )
        gradient = (gradient - scaled * (own_scale * inner)) * own_scale
        grad_ref[...] = (gradient * grad_gain).astype(jnp.bfloat16)
        pooled_ref[...] = (scaled * pooled_scale).astype(jnp.bfloat16)

    @pl.when(leads)
    def _():
        write(near_ref[...], other_scaled_ref[...])

    @pl.when(core_number() == 0)
    def _():
        vectors = jnp.concatenate((sent_ref[:, :width], other_far_ref[...]), axis=0)
        write(vectors, scaled_ref[...])


def core_roles(
    hidden_in,
    attn_gain,
    w_query,
    query_gain,
    cached_keys,
    cached_values,
    w_out,
    final_gain,
    lengths,
    pack_order,
    partner,
):
    pack_size = lax.axis_size("pack")
    stmts, width = hidden_in.shape
    model_width = width * pack_size
    head_dim = query_gain.shape[0]
    tokens = cached_keys.shape[0]
    chips = pack_size // 2
    others = range(1, chips)
    total = partner.shape[0]
    bf16 = jnp.bfloat16
    f32 = jnp.float32
    final_gain = final_gain[None]
    query_gain = query_gain[None]
    half = np.arange(head_dim // 2)
    frequency = (ROPE_BASE ** (-half * 2.0 / head_dim)).astype(np.float32)
    frequency = jnp.asarray(np.concatenate([frequency, frequency])[None])
    whole = pl.BlockSpec(memory_space=pltpu.VMEM)

    window = pl.pallas_call(
        open_window,
        out_shape=shaped((8, 128), f32),
        out_specs=whole,
        compiler_params=pltpu.CompilerParams(vmem_limit_bytes=1 << 20),
        cost_estimate=pl.CostEstimate(flops=1 << 34, bytes_accessed=0, transcendentals=0),
    )()
    attn_gain = attn_gain[None]
    other_hidden_in = flip(hidden_in, "pack", 1)
    other_w_query = flip(w_query, "pack", 1)
    pair = in_vmem(
        prepare_pair,
        shaped((stmts, 2 * width + 128), bf16),
        window,
        hidden_in,
        other_hidden_in,
        attn_gain,
        flip(attn_gain, "pack", 1),
        flops=1 << 34,
    )
    received = [send_across(pair, "pack", k, 0) for k in others]
    own_projected = in_vmem(
        project_own_pair, shaped((stmts, width), f32), pair, w_query, limit=16, flops=1 << 26
    )
    rope, ranges = in_vmem(
        positions_and_ranges,
        (shaped((stmts, 2 * head_dim), f32), shaped((stmts, 256), f32)),
        pair,
        frequency,
        lengths,
        pack_order,
    )
    held = in_vmem(
        copy_tokens,
        shaped((2,) + cached_keys.shape, bf16),
        own_projected,
        cached_keys,
        cached_values,
    )
    other_held = flip(held, "pack", 1)
    other_gain = flip(final_gain, "pack", 1)

    def queries_from(weights, flops, *own):
        return in_vmem(
            lambda *refs: make_queries(*refs, model_width=model_width),
            shaped((stmts, width), bf16),
            *received[::-1],
            pair,
            weights,
            query_gain,
            rope,
            *own,
            limit=16,
            flops=flops,
        )

    second_queries = queries_from(w_query, 1 << 34, own_projected)
    first_queries = queries_from(other_w_query, 1 << 27)
    queries = in_vmem(
        join_queries, shaped((stmts, 2 * width), bf16), first_queries, second_queries
    )
    other_weights = flip(
        in_vmem(copy_weights, shaped(w_out.shape, bf16), queries, w_out, limit=16), "pack", 1
    )
    received = [send_across(queries, "pack", k, 1) for k in others]
    group_rows = stmts * (width // head_dim)
    own_part, own_stats = in_vmem(
        attend_own,
        (shaped((2, group_rows, head_dim), f32),) * 2,
        queries,
        cached_keys,
        cached_values,
        other_held,
        ranges,
        flops=1 << 27,
    )
    partials = []
    for k, part in zip(others[::-1], received[::-1]):
        partials.append(
            in_vmem(
                lambda *refs, offset=k: attend_remote(*refs, offset=offset),
                shaped((stmts, 2 * width + 128), bf16),
                part,
                cached_keys,
                cached_values,
                other_held,
                ranges,
                *(partials[-1:] or (own_stats,)),
                flops=1 << 34,
            )
        )
    received = [send_across(part, "pack", k, 0) for k, part in zip(others, partials[::-1])]
    attended = in_vmem(
        merge_partials,
        shaped((stmts, 2 * width), bf16),
        *received[::-1],
        own_part,
        own_stats,
    )

    def projected_to(offset, kind, *after):
        return in_vmem(
            lambda *refs: project_out(*refs, offset=offset),
            shaped((stmts, 2 * width), kind),
            attended,
            w_out,
            other_weights,
            *after,
            limit=16,
            flops=1 << 27,
        )

    third = projected_to(3, bf16)
    second = projected_to(2, bf16, third)
    first = projected_to(1, bf16, second)
    kept = projected_to(0, bf16, first)
    received = [send_across(part, "pack", k, 1) for k, part in zip(others, (first, second, third))]
    vector, scaled, far_scaled = in_vmem(
        finish_hidden,
        (shaped((stmts, 2 * width + 128), bf16),) + (shaped((stmts, width), f32),) * 2,
        *received[::-1],
        flip(kept, "pack", 1),
        hidden_in,
        other_hidden_in,
        final_gain,
        other_gain,
    )
    received = [send_across(vector, "dp", k, 0) for k in range(1, lax.axis_size("dp"))]
    other_scaled = flip(far_scaled, "pack", 1)
    gram, near, far = in_vmem(
        gram_part,
        (
            shaped((total // 2, 128), f32),
            shaped((total, width), bf16),
            shaped((total - stmts, width), bf16),
        ),
        *received[::-1],
        flip(vector, "pack", 1),
        other_scaled,
    )
    received = [send_across(gram, "pack", k, 1) for k in others]
    other_far = flip(far, "pack", 1)
    summed = in_vmem(
        sum_grams,
        shaped(gram.shape, f32),
        *received[::-1],
        flip(gram, "pack", 1),
        flops=1 << 30,
    )
    masks = in_vmem(
        lambda *refs: partner_masks(*refs, rows=stmts),
        shaped((2, total, total), f32),
        partner[None],
    )
    pooled, loss_rows, grad_hidden = pl.pallas_call(
        lambda *refs: losses_and_gradient(*refs, model_width=model_width),
        out_shape=(
            shaped((stmts, width), bf16),
            shaped((stmts // pack_size,), f32),
            shaped((stmts, width), bf16),
        ),
        in_specs=[whole] * 9,
        out_specs=(whole, pl.BlockSpec(memory_space=pltpu.SMEM), whole),
        compiler_params=pltpu.CompilerParams(vmem_limit_bytes=8 << 20),
    )(
        summed,
        flip(summed, "pack", 1),
        near,
        vector,
        other_far,
        scaled,
        other_scaled,
        final_gain,
        masks,
    )
    return (pooled, loss_rows, grad_hidden)


def local(
    hidden_in,
    attn_gain,
    w_query,
    query_gain,
    cached_keys,
    cached_values,
    w_out,
    final_gain,
    lengths,
    pack_order,
    partner,
):
    pack_size = lax.axis_size("pack")
    pack_index = lax.axis_index("pack")
    group_index = lax.axis_index("dp")
    stmt_count, feature_count = hidden_in.shape
    model_width = feature_count * pack_size
    head_dim = query_gain.shape[0]
    local_heads = w_query.shape[1] // head_dim
    token_count = cached_keys.shape[0]
    total_stmts = partner.shape[0]
    lengths_row = lengths[0]
    order_row = pack_order[0]
    inputs32 = hidden_in.astype(jnp.float32)

    scaled = (inputs32 * attn_gain[None, :]).astype(jnp.bfloat16)
    squares = split_float(jnp.sum(inputs32 * inputs32, axis=1), 3)
    extra = jnp.stack(squares + [jnp.zeros_like(squares[0])] * 125, axis=1)
    arrived = gather_blocks(jnp.concatenate([scaled, extra], axis=1), "pack")
    input_squares = jnp.sum(arrived[:, :, feature_count : feature_count + 3].astype(jnp.float32), axis=(0, 2))
    input_rms = lax.rsqrt(input_squares / model_width + EPSILON)
    features = jnp.moveaxis(arrived[:, :, :feature_count], 0, 1).reshape(stmt_count, model_width)
    projected = jnp.dot(features, w_query, preferred_element_type=jnp.float32)
    queries = (projected * input_rms[:, None]).reshape(stmt_count, local_heads, head_dim)
    queries = (
        queries
        * lax.rsqrt(jnp.mean(queries * queries, axis=2, keepdims=True) + EPSILON)
        * query_gain
    )
    queries = rotate_heads(queries, (lengths_row - 1).astype(jnp.float32)).astype(jnp.bfloat16)
    all_queries = jnp.moveaxis(gather_blocks(queries, "pack"), 0, 1).reshape(
        stmt_count, pack_size * local_heads, head_dim
    )
    start, end = statement_ranges(lengths_row, order_row)
    tokens = pack_index * token_count + jnp.arange(token_count, dtype=jnp.int32)
    token_mask = (tokens[None, :] >= start[:, None]) & (tokens[None, :] < end[:, None])
    block_max, block_sum, numerators = block_attention(
        all_queries, cached_keys, cached_values, token_mask, head_dim ** (-0.5)
    )

    def by_owner(part):
        return jnp.moveaxis(part.reshape((stmt_count, pack_size, -1)), 1, 0)

    message = jnp.concatenate(
        [by_owner(numerators.astype(jnp.bfloat16))]
        + [by_owner(piece) for piece in split_float(block_max, 3) + split_float(block_sum, 2)],
        axis=2,
    )
    message = lax.all_to_all(message, "pack", 0, 0)
    width = local_heads * head_dim
    stats = message[:, :, width:].astype(jnp.float32).reshape(pack_size, stmt_count, 5, local_heads)
    maxima = stats[:, :, 0] + stats[:, :, 1] + stats[:, :, 2]
    factor = jnp.exp(maxima - jnp.max(maxima, axis=0, keepdims=True))
    denominator = jnp.sum((stats[:, :, 3] + stats[:, :, 4]) * factor, axis=0)
    numerators = message[:, :, :width].astype(jnp.float32).reshape(pack_size, stmt_count, local_heads, head_dim)
    summed = jnp.sum(numerators * factor[..., None], axis=0)
    attended = (summed / denominator[..., None]).astype(jnp.bfloat16)
    partial_out = jnp.dot(
        attended.reshape(stmt_count, width), w_out, preferred_element_type=jnp.float32
    )
    partial_out = jnp.moveaxis(
        partial_out.astype(jnp.bfloat16).reshape(stmt_count, pack_size, feature_count), 1, 0
    )
    partial_out = lax.all_to_all(partial_out, "pack", 0, 0)
    hidden = inputs32 + jnp.sum(partial_out.astype(jnp.float32), axis=0)
    scaled_out = hidden * final_gain[None, :]
    vectors = lax.all_gather(scaled_out.astype(jnp.bfloat16), "dp", axis=0, tiled=True)
    gram = lax.dot_general(
        vectors, vectors, (((1,), (1,)), ((), ())), preferred_element_type=jnp.float32
    )
    own_squares = jnp.sum(hidden * hidden, axis=1)
    extra = jnp.zeros((total_stmts,), jnp.float32).at[:stmt_count].set(own_squares)
    gram = jnp.concatenate([gram, extra[:, None]], axis=1)
    if total_stmts <= 128:
        gram = jnp.sum(gather_blocks(gram, "pack"), axis=0)
    else:
        gram = lax.psum(gram, "pack")
    hidden_rms = jnp.sqrt(gram[:stmt_count, total_stmts] / model_width + EPSILON)
    gram = gram[:, :total_stmts]
    column_ids = jnp.arange(total_stmts, dtype=jnp.int32)
    diagonal = column_ids[:, None] == column_ids[None, :]
    norms_row = lax.rsqrt(jnp.sum(jnp.where(diagonal, gram, 0.0), axis=0))
    norms_column = lax.rsqrt(jnp.sum(jnp.where(diagonal, gram, 0.0), axis=1))
    cosines = gram * norms_column[:, None] * norms_row[None, :]
    logits = jnp.where(diagonal, MASKED_LOGIT, cosines / SOFTMAX_WARMTH)
    highest = jnp.max(logits, axis=1)
    all_lse = highest + jnp.log(jnp.sum(jnp.exp(logits - highest[:, None]), axis=1))
    is_partner = column_ids[None, :] == partner[:, None]
    all_loss = all_lse - jnp.sum(jnp.where(is_partner, logits, 0.0), axis=1)
    own_count = stmt_count // pack_size
    row_base = group_index * stmt_count
    loss_rows = lax.dynamic_slice_in_dim(all_loss, row_base + pack_index * own_count, own_count, 0)
    weights = (
        jnp.exp(logits - all_lse[:, None])
        + jnp.exp(logits - all_lse[None, :])
        - is_partner.astype(jnp.float32)
        - is_partner.T.astype(jnp.float32)
    ).astype(jnp.bfloat16)
    own_weights = lax.dynamic_slice_in_dim(weights, row_base, stmt_count, 0)
    own_cosines = lax.dynamic_slice_in_dim(cosines, row_base, stmt_count, 0)
    own_norm = lax.dynamic_slice_in_dim(norms_column, row_base, stmt_count, 0)
    inner = jnp.sum(own_weights.astype(jnp.float32) * own_cosines, axis=1)
    own_norm = own_norm[:, None]
    embeddings = (vectors.astype(jnp.float32) * norms_column[:, None]).astype(jnp.bfloat16)
    gradient = jnp.dot(own_weights, embeddings, preferred_element_type=jnp.float32)
    scale = model_width**0.5 / SOFTMAX_WARMTH
    pooled = (scaled_out / hidden_rms[:, None]).astype(jnp.bfloat16)
    grad_hidden = (
        scale * final_gain[None, :] * (gradient - scaled_out * own_norm * inner[:, None]) * own_norm
    ).astype(jnp.bfloat16)
    return (pooled, loss_rows, grad_hidden)


def solution(mesh):
    body = core_roles if mesh.shape["pack"] == 8 and mesh.shape["dp"] == 4 else local
    in_specs = (
        P("dp", "pack"),
        P("pack"),
        P(None, "pack"),
        P(),
        P(("dp", "pack"), None),
        P(("dp", "pack"), None),
        P("pack", None),
        P("pack"),
        P("dp", None),
        P("dp", None),
        P(),
    )
    out_specs = (P("dp", "pack"), P(("dp", "pack")), P("dp", "pack"))
    return jax.shard_map(body, mesh=mesh, in_specs=in_specs, out_specs=out_specs, check_vma=False)
```

```python
import numpy as np
import jax
import jax.numpy as jnp
from jax import lax
from jax.experimental import pallas as pl
from jax.experimental.pallas import tpu as pltpu
from jax.sharding import PartitionSpec as P

EPSILON = 1e-06
SOFTMAX_WARMTH = 0.05
ROPE_BASE = 1000000.0
MASKED_LOGIT = -1e30


def gather_blocks(block, axis):
    size = lax.axis_size(axis)
    return lax.all_to_all(jnp.broadcast_to(block[None], (size,) + block.shape), axis, 0, 0)


def split_float(value, pieces):
    out = []
    for _ in range(pieces):
        piece = lax.reduce_precision(value, 8, 7)
        out.append(piece.astype(jnp.bfloat16))
        value = value - piece
    return out


def cosine_and_sine(angles):
    turns = jnp.round(angles * np.float32(2.0 / np.pi))
    rest = angles - turns * np.float32(1.5703125)
    rest = rest - turns * np.float32(4.837512969970703125e-4)
    rest = rest - turns * np.float32(7.549789948768648e-8)
    square = rest * rest
    sine = rest + rest * square * (
        np.float32(-1.6666654611e-1)
        + square * (np.float32(8.3321608736e-3) + square * np.float32(-1.9515295891e-4))
    )
    cosine = (
        1.0
        - 0.5 * square
        + square
        * square
        * (
            np.float32(4.166664568298827e-2)
            + square
            * (np.float32(-1.388731625493765e-3) + square * np.float32(2.443315711809948e-5))
        )
    )
    quarter = turns.astype(jnp.int32) & 3
    swap = (quarter & 1) == 1
    cos_out = jnp.where(swap, sine, cosine)
    sin_out = jnp.where(swap, cosine, sine)
    cos_out = jnp.where((quarter == 1) | (quarter == 2), -cos_out, cos_out)
    sin_out = jnp.where(quarter >= 2, -sin_out, sin_out)
    return cos_out, sin_out


def rotate_heads(queries, position):
    head_dim = queries.shape[-1]
    half_dim = head_dim // 2
    frequency = (ROPE_BASE ** (-np.arange(half_dim) * 2.0 / head_dim)).astype(np.float32)
    cosine, sine = cosine_and_sine(position[:, None] * frequency[None, :])
    cosine = jnp.concatenate([cosine, cosine], axis=1)[:, None, :]
    sine = jnp.concatenate([-sine, sine], axis=1)[:, None, :]
    turned = jnp.concatenate([queries[..., half_dim:], queries[..., :half_dim]], axis=-1)
    return queries * cosine + turned * sine


def statement_ranges(lengths_row, order_row):
    stmt_count = order_row.shape[0]
    index = jnp.arange(stmt_count, dtype=jnp.int32)
    slot = jnp.sum(jnp.where(order_row[None, :] == index[:, None], index[None, :], 0), axis=1)
    start = jnp.sum(jnp.where(slot[None, :] < slot[:, None], lengths_row[None, :], 0), axis=1)
    return start, start + lengths_row


def block_attention(all_queries, cached_keys, cached_values, token_mask, score_scale):
    stmt_count, head_count, head_dim = all_queries.shape
    kv_heads = cached_keys.shape[1] // head_dim
    group_size = head_count // kv_heads
    grouped = all_queries.reshape(stmt_count, kv_heads, group_size, head_dim)
    key_heads = cached_keys.reshape(-1, kv_heads, head_dim)
    value_heads = cached_values.reshape(-1, kv_heads, head_dim)
    scores = (
        jnp.einsum("skgd,tkd->skgt", grouped, key_heads, preferred_element_type=jnp.float32)
        * score_scale
    )
    token_mask = token_mask[:, None, None, :]
    block_max = jnp.max(jnp.where(token_mask, scores, MASKED_LOGIT), axis=3)
    softmax_weights = jnp.where(token_mask, jnp.exp(scores - block_max[..., None]), 0.0)
    block_sum = jnp.sum(softmax_weights, axis=3)
    numerators = jnp.einsum(
        "skgt,tkd->skgd",
        softmax_weights.astype(jnp.bfloat16),
        value_heads,
        preferred_element_type=jnp.float32,
    )
    return (
        block_max.reshape(stmt_count, head_count),
        block_sum.reshape(stmt_count, head_count),
        numerators.reshape(stmt_count, head_count, head_dim),
    )


def flip(array, axis, offset):
    size = lax.axis_size(axis)
    return lax.ppermute(array, axis, [(i, i ^ offset) for i in range(size)])


def in_vmem(body, outputs, *operands, limit=8, flops=1_000_000):
    whole = pl.BlockSpec(memory_space=pltpu.VMEM)
    moved = sum(operand.size * operand.dtype.itemsize for operand in operands)
    return pl.pallas_call(
        body,
        out_shape=outputs,
        in_specs=[whole] * len(operands),
        out_specs=jax.tree.map(lambda _: whole, outputs),
        compiler_params=pltpu.CompilerParams(vmem_limit_bytes=limit << 20),
        cost_estimate=pl.CostEstimate(flops=flops, bytes_accessed=moved, transcendentals=0),
    )(*operands)


def shaped(shape, kind):
    return jax.ShapeDtypeStruct(shape, kind)


def open_window(out_ref):
    out_ref[...] = jnp.zeros_like(out_ref)


def prepare_inputs(window_ref, hidden_ref, gain_ref, message_ref):
    del window_ref
    inputs = hidden_ref[...].astype(jnp.float32)
    width = inputs.shape[1]
    message_ref[:, :width] = (inputs * gain_ref[...]).astype(jnp.bfloat16)
    message_ref[:, width:] = pack_statistics(
        [jnp.sum(inputs * inputs, axis=1, keepdims=True)], core_number()
    )


def positions_and_ranges(
    message_ref, frequency_ref, lengths_ref, order_ref, rope_ref, range_ref
):
    del message_ref
    count = lengths_ref.shape[1]
    half = frequency_ref.shape[1] // 2
    row = lax.broadcasted_iota(jnp.int32, (count, count), 0)
    column = lax.broadcasted_iota(jnp.int32, (count, count), 1)
    lengths = jnp.broadcast_to(lengths_ref[...], (count, count)).astype(jnp.float32)
    length = jnp.sum(jnp.where(row == column, lengths, 0.0), axis=1, keepdims=True)
    order = jnp.broadcast_to(order_ref[...], (count, count))
    placed = order == row
    slot = jnp.sum(jnp.where(placed, column, 0).astype(jnp.float32), axis=1, keepdims=True)
    packed = jnp.sum(jnp.where(placed, length, 0.0), axis=0, keepdims=True)
    earlier = column.astype(jnp.float32) < slot
    start = jnp.sum(jnp.where(earlier, packed, 0.0), axis=1, keepdims=True)
    range_ref[:, :128] = jnp.broadcast_to(start, (count, 128))
    range_ref[:, 128:] = jnp.broadcast_to(start + length, (count, 128))
    cosine, sine = cosine_and_sine((length - 1.0) * frequency_ref[...])
    lane = lax.broadcasted_iota(jnp.int32, cosine.shape, 1)
    rope_ref[:, : 2 * half] = cosine
    rope_ref[:, 2 * half :] = jnp.where(lane < half, -sine, sine)


LOG2_E = 1.4426950408889634


def pack_statistics(values, first=0):
    rows = values[0].shape[0]
    lane = lax.broadcasted_iota(jnp.int32, (rows, 128), 1)
    rest = jnp.zeros((rows, 128), jnp.float32)
    for place, value in enumerate(values):
        rest = jnp.where(lane == first + place, value, rest)
    out = rest.astype(jnp.bfloat16).astype(jnp.float32)
    for part in (1, 2):
        rest = rest - rest.astype(jnp.bfloat16).astype(jnp.float32)
        out = out + pltpu.roll(rest.astype(jnp.bfloat16).astype(jnp.float32), 32 * part, 1)
    return out.astype(jnp.bfloat16)


def read_statistic(block, first, count=1):
    lane = lax.broadcasted_iota(jnp.int32, block.shape, 1)
    place = (lane & 31) - first
    mine = (place >= 0) & (place < count) & (lane < 96)
    return jnp.sum(jnp.where(mine, block.astype(jnp.float32), 0.0), axis=1, keepdims=True)


def core_number():
    return lax.axis_index("pack") & 1


def chip_number():
    return lax.axis_index("pack") >> 1


def send_across(array, axis, offset, sender):
    groups, pack = lax.axis_size("dp"), lax.axis_size("pack")
    pairs = []
    for group in range(groups):
        for place in range(pack):
            if place % 2 != sender:
                target = (group, place ^ 1)
            elif axis == "dp":
                target = (group ^ offset, place ^ 1)
            else:
                target = (group, place ^ (2 * offset) ^ 1)
            pairs.append((group * pack + place, target[0] * pack + target[1]))
    return lax.ppermute(array, ("dp", "pack"), pairs)


def copy_tokens(_, key_ref, value_ref, out_ref):
    out_ref[0] = key_ref[...]
    out_ref[1] = value_ref[...]


def prepare_pair(_, own_ref, other_ref, own_gain_ref, other_gain_ref, _last, pair_ref):
    width = own_ref.shape[1]
    squares = 0.0
    scaled = []
    for ref, factor_ref in ((own_ref, own_gain_ref), (other_ref, other_gain_ref)):
        inputs = ref[...].astype(jnp.float32)
        squares = squares + jnp.sum(inputs * inputs, axis=1, keepdims=True)
        scaled.append((inputs * factor_ref[...]).astype(jnp.bfloat16))
    pair_ref[:, 2 * width :] = pack_statistics([squares])
    for first in range(2):

        @pl.when(core_number() == first)
        def _():
            pair_ref[:, :width] = scaled[first]
            pair_ref[:, width : 2 * width] = scaled[1 - first]


def project_pair(pair_ref, offset, weight_ref):
    chip = chip_number() ^ offset
    width = 2 * weight_ref.shape[1]
    rows = pl.ds(pl.multiple_of(chip * width, width), width)
    return jnp.dot(
        pair_ref[:, :width], weight_ref[rows, :], preferred_element_type=jnp.float32
    )


def project_own_pair(pair_ref, weight_ref, total_ref):
    total_ref[...] = project_pair(pair_ref, 0, weight_ref)


def make_queries(
    third_ref,
    second_ref,
    first_ref,
    pair_ref,
    weight_ref,
    gain_ref,
    rope_ref,
    *refs,
    model_width,
):
    query_ref = refs[-1]
    width = query_ref.shape[1]
    head_dim = gain_ref.shape[1]

    @pl.when(core_number() == 1)
    def _():
        blocks = (pair_ref, first_ref, second_ref, third_ref)
        if len(refs) == 2:
            projected = refs[0][...]
        else:
            projected = project_pair(pair_ref, 0, weight_ref)
        squares = pair_ref[:, 2 * width :].astype(jnp.float32)
        for offset in (3, 2, 1):
            projected = projected + project_pair(blocks[offset], offset, weight_ref)
            squares = squares + blocks[offset][:, 2 * width :].astype(jnp.float32)
        squares = read_statistic(squares, 0)
        projected = projected * lax.rsqrt(squares / model_width + EPSILON)
        cosine = rope_ref[:, :head_dim]
        sine = rope_ref[:, head_dim:]
        for head in range(width // head_dim):
            place = slice(head * head_dim, (head + 1) * head_dim)
            query = projected[:, place]
            mean = jnp.mean(query * query, axis=1, keepdims=True)
            query = query * lax.rsqrt(mean + EPSILON) * gain_ref[...]
            turned = pltpu.roll(query, head_dim // 2, 1)
            query_ref[:, place] = (query * cosine + turned * sine).astype(jnp.bfloat16)


def join_queries(first_ref, second_ref, out_ref):
    width = first_ref.shape[1]
    out_ref[:, :width] = first_ref[...]
    out_ref[:, width:] = second_ref[...]


def token_masks(range_ref, tokens, group):
    me = lax.axis_index("pack")
    masks = []
    for owner in (me, me ^ 1):
        index = lax.broadcasted_iota(jnp.int32, (range_ref.shape[0], tokens), 1) + owner * tokens
        index = index.astype(jnp.float32)
        mask = (index >= range_ref[:, :1]) & (index < range_ref[:, 128:129])
        masks.append(jnp.concatenate([mask.astype(jnp.float32)] * group, axis=0) > 0.5)
    return masks


def attend_heads(queries, heads, key_ref, value_ref, other_ref, masks):
    head_dim = 128
    scale = head_dim**-0.5
    scores = []
    columns = []
    for query, head in zip(queries, heads):
        grouped = jnp.concatenate(
            [query[:, i : i + head_dim] for i in range(0, query.shape[1], head_dim)], axis=0
        )
        column = pl.ds(pl.multiple_of(head * head_dim, head_dim), head_dim)
        columns.append(column)
        raw = [
            lax.dot_general(
                grouped, keys, (((1,), (1,)), ((), ())), preferred_element_type=jnp.float32
            )
            for keys in (key_ref[:, column], other_ref[0, :, column])
        ]
        scores.append([jnp.where(mask, part, MASKED_LOGIT) for mask, part in zip(masks, raw)])
    maxima = [
        jnp.maximum(
            jnp.max(first, axis=1, keepdims=True), jnp.max(second, axis=1, keepdims=True)
        )
        for first, second in scores
    ]
    weights = [
        [jnp.exp2((part - highest) * (scale * LOG2_E)) for part in parts]
        for parts, highest in zip(scores, maxima)
    ]
    out = []
    for parts, highest, column in zip(weights, maxima, columns):
        total = jnp.sum(parts[0], axis=1, keepdims=True) + jnp.sum(
            parts[1], axis=1, keepdims=True
        )
        numerators = jnp.dot(
            parts[0].astype(jnp.bfloat16), value_ref[:, column], preferred_element_type=jnp.float32
        ) + jnp.dot(
            parts[1].astype(jnp.bfloat16),
            other_ref[1, :, column],
            preferred_element_type=jnp.float32,
        )
        out.append((highest * scale + jnp.log(total), numerators / total))
    return out


def attend_remote(query_ref, key_ref, value_ref, other_ref, range_ref, *refs, offset):
    out_ref = refs[-1]

    @pl.when(core_number() == 0)
    def _():
        rows = query_ref.shape[0]
        width = query_ref.shape[1] // 2
        masks = token_masks(range_ref, key_ref.shape[0], width // 128)
        chip = chip_number() ^ offset
        queries = [query_ref[:, :width], query_ref[:, width:]]
        heads = (2 * chip, 2 * chip + 1)
        parts = attend_heads(queries, heads, key_ref, value_ref, other_ref, masks)
        stats = []
        for j, (level, averages) in enumerate(parts):
            for h in range(width // 128):
                part = slice(h * rows, (h + 1) * rows)
                place = slice(j * width + h * 128, j * width + (h + 1) * 128)
                out_ref[:, place] = averages[part].astype(jnp.bfloat16)
                stats.append(level[part])
        out_ref[:, 2 * width :] = pack_statistics(stats)


def attend_own(query_ref, key_ref, value_ref, other_ref, range_ref, out_ref, stats_ref):
    @pl.when(core_number() == 1)
    def _():
        width = query_ref.shape[1] // 2
        masks = token_masks(range_ref, key_ref.shape[0], width // 128)
        chip = chip_number()
        parts = attend_heads(
            [query_ref[:, :width], query_ref[:, width:]],
            (2 * chip, 2 * chip + 1),
            key_ref,
            value_ref,
            other_ref,
            masks,
        )
        for j, (level, averages) in enumerate(parts):
            out_ref[j] = averages
            stats_ref[j] = jnp.broadcast_to(level, averages.shape)


def merge_partials(third_ref, second_ref, first_ref, own_ref, stats_ref, *refs):
    attended_ref = refs[-1]

    @pl.when(core_number() == 1)
    def _():
        rows = attended_ref.shape[0]
        width = attended_ref.shape[1] // 2
        others = (first_ref, second_ref, third_ref)
        stats = [ref[:, 2 * width :] for ref in others]
        for j in range(2):
            for h in range(width // 128):
                part = slice(h * rows, (h + 1) * rows)
                place = slice(j * width + h * 128, j * width + (h + 1) * 128)
                slot = j * (width // 128) + h
                levels = [stats_ref[j, part]] + [read_statistic(s, slot) for s in stats]
                averages = [own_ref[j, part]]
                averages += [ref[:, place].astype(jnp.float32) for ref in others]
                highest = levels[0]
                for level in levels[1:]:
                    highest = jnp.maximum(highest, level)
                factors = [jnp.exp(level - highest) for level in levels]
                summed = sum(factor * average for factor, average in zip(factors, averages))
                attended_ref[:, place] = (summed / sum(factors)).astype(jnp.bfloat16)


def copy_weights(_, weight_ref, out_ref, *, offsets):
    width = out_ref.shape[2]
    for i, offset in enumerate(offsets):
        column = pl.ds(pl.multiple_of((chip_number() ^ offset) * width, width), width)
        out_ref[i] = weight_ref[:, column]


def project_out(attended_ref, weight_ref, other_weight_ref, *refs, offset):
    out_ref = refs[-1]

    @pl.when(core_number() == 1)
    def _():
        width = attended_ref.shape[1] // 2
        column = pl.ds(pl.multiple_of((chip_number() ^ offset) * 2 * width, 2 * width), 2 * width)
        total = jnp.dot(
            attended_ref[:, width:], weight_ref[:, column], preferred_element_type=jnp.float32
        ) + jnp.dot(
            attended_ref[:, :width], other_weight_ref[1 - offset % 2], preferred_element_type=jnp.float32
        )
        out_ref[...] = total.astype(out_ref.dtype)


def finish_hidden(
    third_ref,
    second_ref,
    first_ref,
    kept_ref,
    own_ref,
    other_ref,
    own_gain_ref,
    other_gain_ref,
    sent_ref,
    scaled_ref,
    other_scaled_ref,
):
    width = own_ref.shape[1]

    @pl.when(core_number() == 0)
    def _():
        squares = 0.0
        inputs = (own_ref, other_ref)
        gains = (own_gain_ref, other_gain_ref)
        for core in range(2):
            place = slice(core * width, (core + 1) * width)
            hidden = inputs[core][...].astype(jnp.float32)
            for ref in (kept_ref, first_ref, second_ref, third_ref):
                hidden = hidden + ref[:, place].astype(jnp.float32)
            scaled = hidden * gains[core][...]
            (scaled_ref, other_scaled_ref)[core][...] = scaled
            sent_ref[:, place] = scaled.astype(jnp.bfloat16)
            squares = squares + jnp.sum(hidden * hidden, axis=1, keepdims=True)
        sent_ref[:, 2 * width :] = pack_statistics([squares])


def gram_part(third_ref, second_ref, first_ref, own_ref, _, out_ref, near_ref, far_ref):
    @pl.when(core_number() == 1)
    def _():
        rows = own_ref.shape[0]
        width = far_ref.shape[1]
        refs = (own_ref, first_ref, second_ref, third_ref)
        for i, ref in enumerate(refs):
            near_ref[i * rows : (i + 1) * rows] = ref[:, width : 2 * width]
        for i, ref in enumerate(refs[1:]):
            far_ref[i * rows : (i + 1) * rows] = ref[:, :width]
        far = jnp.concatenate([ref[:, :width] for ref in refs], axis=0)
        squares = read_statistic(own_ref[:, 2 * width :], 0)
        gram = 0.0
        for vectors in (near_ref[...], far):
            gram = gram + lax.dot_general(
                vectors, vectors, (((1,), (1,)), ((), ())), preferred_element_type=jnp.float32
            )
        half = gram.shape[0] // 2
        lane = lax.broadcasted_iota(jnp.int32, (half, 2 * half), 1)
        squares = jnp.concatenate([squares] * (half // rows), axis=0)
        out_ref[:, : 2 * half] = gram[:half]
        out_ref[:, 2 * half :] = jnp.where(lane < half, squares, gram[half:])


def sum_grams(third_ref, second_ref, first_ref, own_ref, *refs):
    out_ref = refs[-1]
    out_ref[...] = own_ref[...] + first_ref[...] + second_ref[...] + third_ref[...]


def partner_masks(partner_ref, out_ref, *, rows):
    group = lax.axis_index("dp")
    shape = out_ref.shape[1:]
    row = lax.broadcasted_iota(jnp.int32, shape, 0)
    column = lax.broadcasted_iota(jnp.int32, shape, 1)
    row_id = ((group ^ (row // rows)) * rows) + row % rows
    column_id = ((group ^ (column // rows)) * rows) + column % rows
    partners = jnp.broadcast_to(partner_ref[...], shape)
    row_partner = jnp.sum(
        jnp.where(column == row_id, partners, 0).astype(jnp.float32), axis=1, keepdims=True
    )
    column_partner = jnp.sum(
        jnp.where(row_id == column_id, row_partner, 0.0), axis=0, keepdims=True
    )
    own_partner = column_id.astype(jnp.float32) == row_partner
    other_partner = row_id.astype(jnp.float32) == column_partner
    own_partner = own_partner.astype(jnp.float32)
    out_ref[0] = own_partner
    out_ref[1] = own_partner + other_partner.astype(jnp.float32)


def losses_and_gradient(
    summed_ref,
    other_summed_ref,
    near_ref,
    sent_ref,
    other_far_ref,
    scaled_ref,
    other_scaled_ref,
    gain_ref,
    partner_ref,
    pooled_ref,
    loss_ref,
    grad_ref,
    *,
    model_width,
):
    me = lax.axis_index("pack")
    leads = core_number() == 1
    count, width = near_ref.shape
    rows = scaled_ref.shape[0]
    half = count // 2
    summed = jnp.where(leads, other_summed_ref[...], summed_ref[...])
    upper, lower = summed[:, :count], summed[:, count:]
    squares = lower[:rows, :1]
    row = lax.broadcasted_iota(jnp.int32, upper.shape, 0)
    column = lax.broadcasted_iota(jnp.int32, upper.shape, 1)
    diagonal = row == column
    lower_diagonal = row + half == column
    lower = jnp.where(column >= half, lower, 0.0)
    upper_norms = jnp.where(diagonal, upper, 0.0)
    lower_norms = jnp.where(lower_diagonal, lower, 0.0)
    row_scale = lax.rsqrt(jnp.sum(upper_norms, axis=1, keepdims=True))
    lower_scale = lax.rsqrt(jnp.sum(lower_norms, axis=1, keepdims=True))
    column_scale = lax.rsqrt(jnp.sum(upper_norms + lower_norms, axis=0, keepdims=True))
    cosines = upper * row_scale * column_scale
    logits = cosines * (1.0 / SOFTMAX_WARMTH)
    powers = jnp.where(diagonal, 0.0, jnp.exp(logits))
    lower_powers = jnp.exp(lower * lower_scale * column_scale * (1.0 / SOFTMAX_WARMTH))
    lower_powers = jnp.where((column >= half) & ~lower_diagonal, lower_powers, 0.0)
    mirrored = jnp.sum(jnp.where(column >= half, powers, 0.0), axis=1, keepdims=True)
    column_sum = jnp.sum(
        powers + lower_powers + jnp.where(diagonal, mirrored, 0.0), axis=0, keepdims=True
    )
    cosines, logits, powers = cosines[:rows], logits[:rows], powers[:rows]
    row_sum = jnp.sum(powers, axis=1, keepdims=True)
    weights = powers * (1.0 / row_sum + 1.0 / column_sum) - partner_ref[1, :rows]
    target = jnp.sum(partner_ref[0, :rows] * logits, axis=1, keepdims=True)
    loss = jnp.log(row_sum) - target
    own = loss_ref.shape[0]
    index = lax.broadcasted_iota(jnp.int32, (rows, 1), 0)
    for i in range(own):
        loss_ref[i] = jnp.sum(jnp.where(index == me * own + i, loss, 0.0))
    inner = jnp.sum(weights * cosines, axis=1, keepdims=True)
    scaled_weights = weights * column_scale
    coarse = scaled_weights.astype(jnp.bfloat16)
    fine = (scaled_weights - coarse.astype(jnp.float32)).astype(jnp.bfloat16)
    own_scale = row_scale[:rows]
    pooled_scale = lax.rsqrt(squares / model_width + EPSILON)
    grad_gain = gain_ref[...] * (model_width**0.5 / SOFTMAX_WARMTH)

    def write(vectors, scaled):
        gradient = jnp.dot(coarse, vectors, preferred_element_type=jnp.float32) + jnp.dot(
            fine, vectors, preferred_element_type=jnp.float32
        )
        gradient = (gradient - scaled * (own_scale * inner)) * own_scale
        grad_ref[...] = (gradient * grad_gain).astype(jnp.bfloat16)
        pooled_ref[...] = (scaled * pooled_scale).astype(jnp.bfloat16)

    @pl.when(leads)
    def _():
        write(near_ref[...], other_scaled_ref[...])

    @pl.when(core_number() == 0)
    def _():
        vectors = jnp.concatenate((sent_ref[:, :width], other_far_ref[...]), axis=0)
        write(vectors, scaled_ref[...])


def core_roles(
    hidden_in,
    attn_gain,
    w_query,
    query_gain,
    cached_keys,
    cached_values,
    w_out,
    final_gain,
    lengths,
    pack_order,
    partner,
):
    pack_size = lax.axis_size("pack")
    stmts, width = hidden_in.shape
    model_width = width * pack_size
    head_dim = query_gain.shape[0]
    tokens = cached_keys.shape[0]
    chips = pack_size // 2
    others = range(1, chips)
    total = partner.shape[0]
    bf16 = jnp.bfloat16
    f32 = jnp.float32
    final_gain = final_gain[None]
    query_gain = query_gain[None]
    half = np.arange(head_dim // 2)
    frequency = (ROPE_BASE ** (-half * 2.0 / head_dim)).astype(np.float32)
    frequency = jnp.asarray(np.concatenate([frequency, frequency])[None])
    whole = pl.BlockSpec(memory_space=pltpu.VMEM)

    window = pl.pallas_call(
        open_window,
        out_shape=shaped((8, 128), f32),
        out_specs=whole,
        compiler_params=pltpu.CompilerParams(vmem_limit_bytes=1 << 20),
        cost_estimate=pl.CostEstimate(flops=1 << 34, bytes_accessed=0, transcendentals=0),
    )()
    attn_gain = attn_gain[None]
    other_hidden_in = flip(hidden_in, "pack", 1)
    other_gain = flip(final_gain, "pack", 1)
    other_w_query = flip(w_query, "pack", 1)
    pair = in_vmem(
        prepare_pair,
        shaped((stmts, 2 * width + 128), bf16),
        window,
        hidden_in,
        other_hidden_in,
        attn_gain,
        flip(attn_gain, "pack", 1),
        other_gain,
        flops=1 << 34,
    )
    received = [send_across(pair, "pack", k, 0) for k in others]
    own_projected = in_vmem(
        project_own_pair, shaped((stmts, width), f32), pair, w_query, limit=16, flops=1 << 26
    )
    rope, ranges = in_vmem(
        positions_and_ranges,
        (shaped((stmts, 2 * head_dim), f32), shaped((stmts, 256), f32)),
        pair,
        frequency,
        lengths,
        pack_order,
    )
    held = in_vmem(
        copy_tokens,
        shaped((2,) + cached_keys.shape, bf16),
        own_projected,
        cached_keys,
        cached_values,
    )
    other_held = flip(held, "pack", 1)

    def queries_from(weights, flops, *own):
        return in_vmem(
            lambda *refs: make_queries(*refs, model_width=model_width),
            shaped((stmts, width), bf16),
            *received[::-1],
            pair,
            weights,
            query_gain,
            rope,
            *own,
            limit=16,
            flops=flops,
        )

    second_queries = queries_from(w_query, 1 << 34, own_projected)
    first_queries = queries_from(other_w_query, 1 << 27)
    queries = in_vmem(
        join_queries, shaped((stmts, 2 * width), bf16), first_queries, second_queries
    )

    def weights_to(offsets, after):
        part = in_vmem(
            lambda *refs: copy_weights(*refs, offsets=offsets),
            shaped((2, width, 2 * width), bf16),
            after,
            w_out,
            limit=16,
        )
        return flip(part, "pack", 1)

    far_weights = weights_to((3, 2), queries)
    received = [send_across(queries, "pack", k, 1) for k in others]
    group_rows = stmts * (width // head_dim)
    own_part, own_stats = in_vmem(
        attend_own,
        (shaped((2, group_rows, head_dim), f32),) * 2,
        queries,
        cached_keys,
        cached_values,
        other_held,
        ranges,
        flops=1 << 27,
    )
    partials = []
    for k, part in zip(others[::-1], received[::-1]):
        partials.append(
            in_vmem(
                lambda *refs, offset=k: attend_remote(*refs, offset=offset),
                shaped((stmts, 2 * width + 128), bf16),
                part,
                cached_keys,
                cached_values,
                other_held,
                ranges,
                *(partials[-1:] or (own_stats,)),
                flops=1 << 34,
            )
        )
    received = [send_across(part, "pack", k, 0) for k, part in zip(others, partials[::-1])]
    near_weights = weights_to((1, 0), partials[-1])
    attended = in_vmem(
        merge_partials,
        shaped((stmts, 2 * width), bf16),
        *received[::-1],
        own_part,
        own_stats,
    )

    def projected_to(offset, kind, *after):
        return in_vmem(
            lambda *refs: project_out(*refs, offset=offset),
            shaped((stmts, 2 * width), kind),
            attended,
            w_out,
            far_weights if offset > 1 else near_weights,
            *after,
            limit=16,
            flops=1 << (35 if offset == 2 else 27),
        )

    third = projected_to(3, bf16)
    second = projected_to(2, bf16, third)
    first = projected_to(1, bf16, second)
    kept = projected_to(0, bf16, first)
    received = [send_across(part, "pack", k, 1) for k, part in zip(others, (first, second, third))]
    vector, scaled, far_scaled = in_vmem(
        finish_hidden,
        (shaped((stmts, 2 * width + 128), bf16),) + (shaped((stmts, width), f32),) * 2,
        *received[::-1],
        flip(kept, "pack", 1),
        hidden_in,
        other_hidden_in,
        final_gain,
        other_gain,
    )
    received = [send_across(vector, "dp", k, 0) for k in range(1, lax.axis_size("dp"))]
    other_scaled = flip(far_scaled, "pack", 1)
    gram, near, far = in_vmem(
        gram_part,
        (
            shaped((total // 2, 128), f32),
            shaped((total, width), bf16),
            shaped((total - stmts, width), bf16),
        ),
        *received[::-1],
        flip(vector, "pack", 1),
        other_scaled,
    )
    received = [send_across(gram, "pack", k, 1) for k in others]
    other_far = flip(far, "pack", 1)
    summed = in_vmem(
        sum_grams,
        shaped(gram.shape, f32),
        *received[::-1],
        flip(gram, "pack", 1),
        flops=1 << 30,
    )
    masks = in_vmem(
        lambda *refs: partner_masks(*refs, rows=stmts),
        shaped((2, total, total), f32),
        partner[None],
    )
    pooled, loss_rows, grad_hidden = pl.pallas_call(
        lambda *refs: losses_and_gradient(*refs, model_width=model_width),
        out_shape=(
            shaped((stmts, width), bf16),
            shaped((stmts // pack_size,), f32),
            shaped((stmts, width), bf16),
        ),
        in_specs=[whole] * 9,
        out_specs=(whole, pl.BlockSpec(memory_space=pltpu.SMEM), whole),
        compiler_params=pltpu.CompilerParams(vmem_limit_bytes=8 << 20),
    )(
        summed,
        flip(summed, "pack", 1),
        near,
        vector,
        other_far,
        scaled,
        other_scaled,
        final_gain,
        masks,
    )
    return (pooled, loss_rows, grad_hidden)


def local(
    hidden_in,
    attn_gain,
    w_query,
    query_gain,
    cached_keys,
    cached_values,
    w_out,
    final_gain,
    lengths,
    pack_order,
    partner,
):
    pack_size = lax.axis_size("pack")
    pack_index = lax.axis_index("pack")
    group_index = lax.axis_index("dp")
    stmt_count, feature_count = hidden_in.shape
    model_width = feature_count * pack_size
    head_dim = query_gain.shape[0]
    local_heads = w_query.shape[1] // head_dim
    token_count = cached_keys.shape[0]
    total_stmts = partner.shape[0]
    lengths_row = lengths[0]
    order_row = pack_order[0]
    inputs32 = hidden_in.astype(jnp.float32)

    scaled = (inputs32 * attn_gain[None, :]).astype(jnp.bfloat16)
    squares = split_float(jnp.sum(inputs32 * inputs32, axis=1), 3)
    extra = jnp.stack(squares + [jnp.zeros_like(squares[0])] * 125, axis=1)
    arrived = gather_blocks(jnp.concatenate([scaled, extra], axis=1), "pack")
    input_squares = jnp.sum(arrived[:, :, feature_count : feature_count + 3].astype(jnp.float32), axis=(0, 2))
    input_rms = lax.rsqrt(input_squares / model_width + EPSILON)
    features = jnp.moveaxis(arrived[:, :, :feature_count], 0, 1).reshape(stmt_count, model_width)
    projected = jnp.dot(features, w_query, preferred_element_type=jnp.float32)
    queries = (projected * input_rms[:, None]).reshape(stmt_count, local_heads, head_dim)
    queries = (
        queries
        * lax.rsqrt(jnp.mean(queries * queries, axis=2, keepdims=True) + EPSILON)
        * query_gain
    )
    queries = rotate_heads(queries, (lengths_row - 1).astype(jnp.float32)).astype(jnp.bfloat16)
    all_queries = jnp.moveaxis(gather_blocks(queries, "pack"), 0, 1).reshape(
        stmt_count, pack_size * local_heads, head_dim
    )
    start, end = statement_ranges(lengths_row, order_row)
    tokens = pack_index * token_count + jnp.arange(token_count, dtype=jnp.int32)
    token_mask = (tokens[None, :] >= start[:, None]) & (tokens[None, :] < end[:, None])
    block_max, block_sum, numerators = block_attention(
        all_queries, cached_keys, cached_values, token_mask, head_dim ** (-0.5)
    )

    def by_owner(part):
        return jnp.moveaxis(part.reshape((stmt_count, pack_size, -1)), 1, 0)

    message = jnp.concatenate(
        [by_owner(numerators.astype(jnp.bfloat16))]
        + [by_owner(piece) for piece in split_float(block_max, 3) + split_float(block_sum, 2)],
        axis=2,
    )
    message = lax.all_to_all(message, "pack", 0, 0)
    width = local_heads * head_dim
    stats = message[:, :, width:].astype(jnp.float32).reshape(pack_size, stmt_count, 5, local_heads)
    maxima = stats[:, :, 0] + stats[:, :, 1] + stats[:, :, 2]
    factor = jnp.exp(maxima - jnp.max(maxima, axis=0, keepdims=True))
    denominator = jnp.sum((stats[:, :, 3] + stats[:, :, 4]) * factor, axis=0)
    numerators = message[:, :, :width].astype(jnp.float32).reshape(pack_size, stmt_count, local_heads, head_dim)
    summed = jnp.sum(numerators * factor[..., None], axis=0)
    attended = (summed / denominator[..., None]).astype(jnp.bfloat16)
    partial_out = jnp.dot(
        attended.reshape(stmt_count, width), w_out, preferred_element_type=jnp.float32
    )
    partial_out = jnp.moveaxis(
        partial_out.astype(jnp.bfloat16).reshape(stmt_count, pack_size, feature_count), 1, 0
    )
    partial_out = lax.all_to_all(partial_out, "pack", 0, 0)
    hidden = inputs32 + jnp.sum(partial_out.astype(jnp.float32), axis=0)
    scaled_out = hidden * final_gain[None, :]
    vectors = lax.all_gather(scaled_out.astype(jnp.bfloat16), "dp", axis=0, tiled=True)
    gram = lax.dot_general(
        vectors, vectors, (((1,), (1,)), ((), ())), preferred_element_type=jnp.float32
    )
    own_squares = jnp.sum(hidden * hidden, axis=1)
    extra = jnp.zeros((total_stmts,), jnp.float32).at[:stmt_count].set(own_squares)
    gram = jnp.concatenate([gram, extra[:, None]], axis=1)
    if total_stmts <= 128:
        gram = jnp.sum(gather_blocks(gram, "pack"), axis=0)
    else:
        gram = lax.psum(gram, "pack")
    hidden_rms = jnp.sqrt(gram[:stmt_count, total_stmts] / model_width + EPSILON)
    gram = gram[:, :total_stmts]
    column_ids = jnp.arange(total_stmts, dtype=jnp.int32)
    diagonal = column_ids[:, None] == column_ids[None, :]
    norms_row = lax.rsqrt(jnp.sum(jnp.where(diagonal, gram, 0.0), axis=0))
    norms_column = lax.rsqrt(jnp.sum(jnp.where(diagonal, gram, 0.0), axis=1))
    cosines = gram * norms_column[:, None] * norms_row[None, :]
    logits = jnp.where(diagonal, MASKED_LOGIT, cosines / SOFTMAX_WARMTH)
    highest = jnp.max(logits, axis=1)
    all_lse = highest + jnp.log(jnp.sum(jnp.exp(logits - highest[:, None]), axis=1))
    is_partner = column_ids[None, :] == partner[:, None]
    all_loss = all_lse - jnp.sum(jnp.where(is_partner, logits, 0.0), axis=1)
    own_count = stmt_count // pack_size
    row_base = group_index * stmt_count
    loss_rows = lax.dynamic_slice_in_dim(all_loss, row_base + pack_index * own_count, own_count, 0)
    weights = (
        jnp.exp(logits - all_lse[:, None])
        + jnp.exp(logits - all_lse[None, :])
        - is_partner.astype(jnp.float32)
        - is_partner.T.astype(jnp.float32)
    ).astype(jnp.bfloat16)
    own_weights = lax.dynamic_slice_in_dim(weights, row_base, stmt_count, 0)
    own_cosines = lax.dynamic_slice_in_dim(cosines, row_base, stmt_count, 0)
    own_norm = lax.dynamic_slice_in_dim(norms_column, row_base, stmt_count, 0)
    inner = jnp.sum(own_weights.astype(jnp.float32) * own_cosines, axis=1)
    own_norm = own_norm[:, None]
    embeddings = (vectors.astype(jnp.float32) * norms_column[:, None]).astype(jnp.bfloat16)
    gradient = jnp.dot(own_weights, embeddings, preferred_element_type=jnp.float32)
    scale = model_width**0.5 / SOFTMAX_WARMTH
    pooled = (scaled_out / hidden_rms[:, None]).astype(jnp.bfloat16)
    grad_hidden = (
        scale * final_gain[None, :] * (gradient - scaled_out * own_norm * inner[:, None]) * own_norm
    ).astype(jnp.bfloat16)
    return (pooled, loss_rows, grad_hidden)


def solution(mesh):
    body = core_roles if mesh.shape["pack"] == 8 and mesh.shape["dp"] == 4 else local
    in_specs = (
        P("dp", "pack"),
        P("pack"),
        P(None, "pack"),
        P(),
        P(("dp", "pack"), None),
        P(("dp", "pack"), None),
        P("pack", None),
        P("pack"),
        P("dp", None),
        P("dp", None),
        P(),
    )
    out_specs = (P("dp", "pack"), P(("dp", "pack")), P("dp", "pack"))
    return jax.shard_map(body, mesh=mesh, in_specs=in_specs, out_specs=out_specs, check_vma=False)
```

```python
import numpy as np
import jax
import jax.numpy as jnp
from jax import lax
from jax.experimental import pallas as pl
from jax.experimental.pallas import tpu as pltpu
from jax.sharding import PartitionSpec as P

EPSILON = 1e-06
SOFTMAX_WARMTH = 0.05
ROPE_BASE = 1000000.0
MASKED_LOGIT = -1e30


def gather_blocks(block, axis):
    size = lax.axis_size(axis)
    return lax.all_to_all(jnp.broadcast_to(block[None], (size,) + block.shape), axis, 0, 0)


def split_float(value, pieces):
    out = []
    for _ in range(pieces):
        piece = lax.reduce_precision(value, 8, 7)
        out.append(piece.astype(jnp.bfloat16))
        value = value - piece
    return out


def cosine_and_sine(angles):
    turns = jnp.round(angles * np.float32(2.0 / np.pi))
    rest = angles - turns * np.float32(1.5703125)
    rest = rest - turns * np.float32(4.837512969970703125e-4)
    rest = rest - turns * np.float32(7.549789948768648e-8)
    square = rest * rest
    sine = rest + rest * square * (
        np.float32(-1.6666654611e-1)
        + square * (np.float32(8.3321608736e-3) + square * np.float32(-1.9515295891e-4))
    )
    cosine = (
        1.0
        - 0.5 * square
        + square
        * square
        * (
            np.float32(4.166664568298827e-2)
            + square
            * (np.float32(-1.388731625493765e-3) + square * np.float32(2.443315711809948e-5))
        )
    )
    quarter = turns.astype(jnp.int32) & 3
    swap = (quarter & 1) == 1
    cos_out = jnp.where(swap, sine, cosine)
    sin_out = jnp.where(swap, cosine, sine)
    cos_out = jnp.where((quarter == 1) | (quarter == 2), -cos_out, cos_out)
    sin_out = jnp.where(quarter >= 2, -sin_out, sin_out)
    return cos_out, sin_out


def rotate_heads(queries, position):
    head_dim = queries.shape[-1]
    half_dim = head_dim // 2
    frequency = (ROPE_BASE ** (-np.arange(half_dim) * 2.0 / head_dim)).astype(np.float32)
    cosine, sine = cosine_and_sine(position[:, None] * frequency[None, :])
    cosine = jnp.concatenate([cosine, cosine], axis=1)[:, None, :]
    sine = jnp.concatenate([-sine, sine], axis=1)[:, None, :]
    turned = jnp.concatenate([queries[..., half_dim:], queries[..., :half_dim]], axis=-1)
    return queries * cosine + turned * sine


def statement_ranges(lengths_row, order_row):
    stmt_count = order_row.shape[0]
    index = jnp.arange(stmt_count, dtype=jnp.int32)
    slot = jnp.sum(jnp.where(order_row[None, :] == index[:, None], index[None, :], 0), axis=1)
    start = jnp.sum(jnp.where(slot[None, :] < slot[:, None], lengths_row[None, :], 0), axis=1)
    return start, start + lengths_row


def block_attention(all_queries, cached_keys, cached_values, token_mask, score_scale):
    stmt_count, head_count, head_dim = all_queries.shape
    kv_heads = cached_keys.shape[1] // head_dim
    group_size = head_count // kv_heads
    grouped = all_queries.reshape(stmt_count, kv_heads, group_size, head_dim)
    key_heads = cached_keys.reshape(-1, kv_heads, head_dim)
    value_heads = cached_values.reshape(-1, kv_heads, head_dim)
    scores = (
        jnp.einsum("skgd,tkd->skgt", grouped, key_heads, preferred_element_type=jnp.float32)
        * score_scale
    )
    token_mask = token_mask[:, None, None, :]
    block_max = jnp.max(jnp.where(token_mask, scores, MASKED_LOGIT), axis=3)
    softmax_weights = jnp.where(token_mask, jnp.exp(scores - block_max[..., None]), 0.0)
    block_sum = jnp.sum(softmax_weights, axis=3)
    numerators = jnp.einsum(
        "skgt,tkd->skgd",
        softmax_weights.astype(jnp.bfloat16),
        value_heads,
        preferred_element_type=jnp.float32,
    )
    return (
        block_max.reshape(stmt_count, head_count),
        block_sum.reshape(stmt_count, head_count),
        numerators.reshape(stmt_count, head_count, head_dim),
    )


def flip(array, axis, offset):
    size = lax.axis_size(axis)
    return lax.ppermute(array, axis, [(i, i ^ offset) for i in range(size)])


def in_vmem(body, outputs, *operands, limit=8, flops=1_000_000):
    whole = pl.BlockSpec(memory_space=pltpu.VMEM)
    moved = sum(operand.size * operand.dtype.itemsize for operand in operands)
    return pl.pallas_call(
        body,
        out_shape=outputs,
        in_specs=[whole] * len(operands),
        out_specs=jax.tree.map(lambda _: whole, outputs),
        compiler_params=pltpu.CompilerParams(vmem_limit_bytes=limit << 20),
        cost_estimate=pl.CostEstimate(flops=flops, bytes_accessed=moved, transcendentals=0),
    )(*operands)


def shaped(shape, kind):
    return jax.ShapeDtypeStruct(shape, kind)


def open_window(out_ref):
    out_ref[...] = jnp.zeros_like(out_ref)


def prepare_inputs(window_ref, hidden_ref, gain_ref, message_ref):
    del window_ref
    inputs = hidden_ref[...].astype(jnp.float32)
    width = inputs.shape[1]
    message_ref[:, :width] = (inputs * gain_ref[...]).astype(jnp.bfloat16)
    message_ref[:, width:] = pack_statistics(
        [jnp.sum(inputs * inputs, axis=1, keepdims=True)], core_number()
    )


def positions_and_ranges(
    message_ref, frequency_ref, lengths_ref, order_ref, rope_ref, range_ref
):
    del message_ref
    count = lengths_ref.shape[1]
    half = frequency_ref.shape[1] // 2
    row = lax.broadcasted_iota(jnp.int32, (count, count), 0)
    column = lax.broadcasted_iota(jnp.int32, (count, count), 1)
    lengths = jnp.broadcast_to(lengths_ref[...], (count, count)).astype(jnp.float32)
    length = jnp.sum(jnp.where(row == column, lengths, 0.0), axis=1, keepdims=True)
    order = jnp.broadcast_to(order_ref[...], (count, count))
    placed = order == row
    slot = jnp.sum(jnp.where(placed, column, 0).astype(jnp.float32), axis=1, keepdims=True)
    packed = jnp.sum(jnp.where(placed, length, 0.0), axis=0, keepdims=True)
    earlier = column.astype(jnp.float32) < slot
    start = jnp.sum(jnp.where(earlier, packed, 0.0), axis=1, keepdims=True)
    range_ref[:, :128] = jnp.broadcast_to(start, (count, 128))
    range_ref[:, 128:] = jnp.broadcast_to(start + length, (count, 128))
    cosine, sine = cosine_and_sine((length - 1.0) * frequency_ref[...])
    lane = lax.broadcasted_iota(jnp.int32, cosine.shape, 1)
    rope_ref[:, : 2 * half] = cosine
    rope_ref[:, 2 * half :] = jnp.where(lane < half, -sine, sine)


LOG2_E = 1.4426950408889634


def pack_statistics(values, first=0):
    rows = values[0].shape[0]
    lane = lax.broadcasted_iota(jnp.int32, (rows, 128), 1)
    rest = jnp.zeros((rows, 128), jnp.float32)
    for place, value in enumerate(values):
        rest = jnp.where(lane == first + place, value, rest)
    out = rest.astype(jnp.bfloat16).astype(jnp.float32)
    for part in (1, 2):
        rest = rest - rest.astype(jnp.bfloat16).astype(jnp.float32)
        out = out + pltpu.roll(rest.astype(jnp.bfloat16).astype(jnp.float32), 32 * part, 1)
    return out.astype(jnp.bfloat16)


def read_statistic(block, first, count=1):
    lane = lax.broadcasted_iota(jnp.int32, block.shape, 1)
    place = (lane & 31) - first
    mine = (place >= 0) & (place < count) & (lane < 96)
    return jnp.sum(jnp.where(mine, block.astype(jnp.float32), 0.0), axis=1, keepdims=True)


def core_number():
    return lax.axis_index("pack") & 1


def chip_number():
    return lax.axis_index("pack") >> 1


def send_across(array, axis, offset, sender):
    groups, pack = lax.axis_size("dp"), lax.axis_size("pack")
    pairs = []
    for group in range(groups):
        for place in range(pack):
            if place % 2 != sender:
                target = (group, place ^ 1)
            elif axis == "dp":
                target = (group ^ offset, place ^ 1)
            else:
                target = (group, place ^ (2 * offset) ^ 1)
            pairs.append((group * pack + place, target[0] * pack + target[1]))
    return lax.ppermute(array, ("dp", "pack"), pairs)


def copy_tokens(_, key_ref, value_ref, out_ref):
    out_ref[0] = key_ref[...]
    out_ref[1] = value_ref[...]


def prepare_pair(_, own_ref, other_ref, own_gain_ref, other_gain_ref, _last, pair_ref):
    width = own_ref.shape[1]
    squares = 0.0
    scaled = []
    for ref, factor_ref in ((own_ref, own_gain_ref), (other_ref, other_gain_ref)):
        inputs = ref[...].astype(jnp.float32)
        squares = squares + jnp.sum(inputs * inputs, axis=1, keepdims=True)
        scaled.append((inputs * factor_ref[...]).astype(jnp.bfloat16))
    pair_ref[:, 2 * width :] = pack_statistics([squares])
    for first in range(2):

        @pl.when(core_number() == first)
        def _():
            pair_ref[:, :width] = scaled[first]
            pair_ref[:, width : 2 * width] = scaled[1 - first]


def project_pair(pair_ref, offset, weight_ref):
    chip = chip_number() ^ offset
    width = 2 * weight_ref.shape[1]
    rows = pl.ds(pl.multiple_of(chip * width, width), width)
    return jnp.dot(
        pair_ref[:, :width], weight_ref[rows, :], preferred_element_type=jnp.float32
    )


def project_own_pair(pair_ref, weight_ref, total_ref):
    total_ref[...] = project_pair(pair_ref, 0, weight_ref)


def make_queries(
    third_ref,
    second_ref,
    first_ref,
    pair_ref,
    weight_ref,
    gain_ref,
    rope_ref,
    *refs,
    model_width,
):
    query_ref = refs[-1]
    width = query_ref.shape[1]
    head_dim = gain_ref.shape[1]

    @pl.when(core_number() == 1)
    def _():
        blocks = (pair_ref, first_ref, second_ref, third_ref)
        if len(refs) == 2:
            projected = refs[0][...]
        else:
            projected = project_pair(pair_ref, 0, weight_ref)
        squares = pair_ref[:, 2 * width :].astype(jnp.float32)
        for offset in (3, 2, 1):
            projected = projected + project_pair(blocks[offset], offset, weight_ref)
            squares = squares + blocks[offset][:, 2 * width :].astype(jnp.float32)
        squares = read_statistic(squares, 0)
        projected = projected * lax.rsqrt(squares / model_width + EPSILON)
        cosine = rope_ref[:, :head_dim]
        sine = rope_ref[:, head_dim:]
        for head in range(width // head_dim):
            place = slice(head * head_dim, (head + 1) * head_dim)
            query = projected[:, place]
            mean = jnp.mean(query * query, axis=1, keepdims=True)
            query = query * lax.rsqrt(mean + EPSILON) * gain_ref[...]
            turned = pltpu.roll(query, head_dim // 2, 1)
            query_ref[:, place] = (query * cosine + turned * sine).astype(jnp.bfloat16)


def join_queries(first_ref, second_ref, out_ref):
    width = first_ref.shape[1]
    out_ref[:, :width] = first_ref[...]
    out_ref[:, width:] = second_ref[...]


def token_masks(range_ref, tokens, group):
    me = lax.axis_index("pack")
    masks = []
    for owner in (me, me ^ 1):
        index = lax.broadcasted_iota(jnp.int32, (range_ref.shape[0], tokens), 1) + owner * tokens
        index = index.astype(jnp.float32)
        mask = (index >= range_ref[:, :1]) & (index < range_ref[:, 128:129])
        masks.append(jnp.concatenate([mask.astype(jnp.float32)] * group, axis=0) > 0.5)
    return masks


def attend_heads(queries, heads, key_ref, value_ref, other_ref, masks):
    head_dim = 128
    scale = head_dim**-0.5
    scores = []
    columns = []
    for query, head in zip(queries, heads):
        grouped = jnp.concatenate(
            [query[:, i : i + head_dim] for i in range(0, query.shape[1], head_dim)], axis=0
        )
        column = pl.ds(pl.multiple_of(head * head_dim, head_dim), head_dim)
        columns.append(column)
        raw = [
            lax.dot_general(
                grouped, keys, (((1,), (1,)), ((), ())), preferred_element_type=jnp.float32
            )
            for keys in (key_ref[:, column], other_ref[0, :, column])
        ]
        scores.append([jnp.where(mask, part, MASKED_LOGIT) for mask, part in zip(masks, raw)])
    maxima = [
        jnp.maximum(
            jnp.max(first, axis=1, keepdims=True), jnp.max(second, axis=1, keepdims=True)
        )
        for first, second in scores
    ]
    weights = [
        [jnp.exp2((part - highest) * (scale * LOG2_E)) for part in parts]
        for parts, highest in zip(scores, maxima)
    ]
    out = []
    for parts, highest, column in zip(weights, maxima, columns):
        total = jnp.sum(parts[0], axis=1, keepdims=True) + jnp.sum(
            parts[1], axis=1, keepdims=True
        )
        numerators = jnp.dot(
            parts[0].astype(jnp.bfloat16), value_ref[:, column], preferred_element_type=jnp.float32
        ) + jnp.dot(
            parts[1].astype(jnp.bfloat16),
            other_ref[1, :, column],
            preferred_element_type=jnp.float32,
        )
        out.append((highest * scale + jnp.log(total), numerators / total))
    return out


def attend_remote(query_ref, key_ref, value_ref, other_ref, range_ref, *refs, offset):
    out_ref = refs[-1]

    @pl.when(core_number() == 0)
    def _():
        rows = query_ref.shape[0]
        width = query_ref.shape[1] // 2
        masks = token_masks(range_ref, key_ref.shape[0], width // 128)
        chip = chip_number() ^ offset
        queries = [query_ref[:, :width], query_ref[:, width:]]
        heads = (2 * chip, 2 * chip + 1)
        parts = attend_heads(queries, heads, key_ref, value_ref, other_ref, masks)
        stats = []
        for j, (level, averages) in enumerate(parts):
            for h in range(width // 128):
                part = slice(h * rows, (h + 1) * rows)
                place = slice(j * width + h * 128, j * width + (h + 1) * 128)
                out_ref[:, place] = averages[part].astype(jnp.bfloat16)
                stats.append(level[part])
        out_ref[:, 2 * width :] = pack_statistics(stats)


def attend_own(query_ref, key_ref, value_ref, other_ref, range_ref, out_ref, stats_ref):
    @pl.when(core_number() == 1)
    def _():
        width = query_ref.shape[1] // 2
        masks = token_masks(range_ref, key_ref.shape[0], width // 128)
        chip = chip_number()
        parts = attend_heads(
            [query_ref[:, :width], query_ref[:, width:]],
            (2 * chip, 2 * chip + 1),
            key_ref,
            value_ref,
            other_ref,
            masks,
        )
        for j, (level, averages) in enumerate(parts):
            out_ref[j] = averages
            stats_ref[j] = jnp.broadcast_to(level, averages.shape)


def merge_partials(third_ref, second_ref, first_ref, own_ref, stats_ref, *refs):
    attended_ref = refs[-1]

    @pl.when(core_number() == 1)
    def _():
        rows = attended_ref.shape[0]
        width = attended_ref.shape[1] // 2
        others = (first_ref, second_ref, third_ref)
        stats = [ref[:, 2 * width :] for ref in others]
        for j in range(2):
            for h in range(width // 128):
                part = slice(h * rows, (h + 1) * rows)
                place = slice(j * width + h * 128, j * width + (h + 1) * 128)
                slot = j * (width // 128) + h
                levels = [stats_ref[j, part]] + [read_statistic(s, slot) for s in stats]
                averages = [own_ref[j, part]]
                averages += [ref[:, place].astype(jnp.float32) for ref in others]
                highest = levels[0]
                for level in levels[1:]:
                    highest = jnp.maximum(highest, level)
                factors = [jnp.exp(level - highest) for level in levels]
                summed = sum(factor * average for factor, average in zip(factors, averages))
                attended_ref[:, place] = (summed / sum(factors)).astype(jnp.bfloat16)


def copy_weights(_, weight_ref, out_ref, *, offsets):
    width = out_ref.shape[2]
    for i, offset in enumerate(offsets):
        column = pl.ds(pl.multiple_of((chip_number() ^ offset) * width, width), width)
        out_ref[i] = weight_ref[:, column]


def project_out(attended_ref, weight_ref, other_weight_ref, *refs, offset):
    out_ref = refs[-1]

    @pl.when(core_number() == 1)
    def _():
        width = attended_ref.shape[1] // 2
        column = pl.ds(pl.multiple_of((chip_number() ^ offset) * 2 * width, 2 * width), 2 * width)
        total = jnp.dot(
            attended_ref[:, width:], weight_ref[:, column], preferred_element_type=jnp.float32
        ) + jnp.dot(
            attended_ref[:, :width], other_weight_ref[1 - offset % 2], preferred_element_type=jnp.float32
        )
        out_ref[...] = total.astype(out_ref.dtype)


def finish_hidden(
    third_ref,
    second_ref,
    first_ref,
    kept_ref,
    own_ref,
    other_ref,
    own_gain_ref,
    other_gain_ref,
    sent_ref,
    scaled_ref,
    other_scaled_ref,
):
    width = own_ref.shape[1]

    @pl.when(core_number() == 0)
    def _():
        squares = 0.0
        inputs = (own_ref, other_ref)
        gains = (own_gain_ref, other_gain_ref)
        for core in range(2):
            place = slice(core * width, (core + 1) * width)
            hidden = inputs[core][...].astype(jnp.float32)
            for ref in (kept_ref, first_ref, second_ref, third_ref):
                hidden = hidden + ref[:, place].astype(jnp.float32)
            scaled = hidden * gains[core][...]
            (scaled_ref, other_scaled_ref)[core][...] = scaled
            sent_ref[:, place] = scaled.astype(jnp.bfloat16)
            squares = squares + jnp.sum(hidden * hidden, axis=1, keepdims=True)
        sent_ref[:, 2 * width :] = pack_statistics([squares])


def gram_part(third_ref, second_ref, first_ref, own_ref, _, out_ref, near_ref, far_ref):
    @pl.when(core_number() == 1)
    def _():
        rows = own_ref.shape[0]
        width = far_ref.shape[1]
        refs = (own_ref, first_ref, second_ref, third_ref)
        for i, ref in enumerate(refs):
            near_ref[i * rows : (i + 1) * rows] = ref[:, width : 2 * width]
        for i, ref in enumerate(refs[1:]):
            far_ref[i * rows : (i + 1) * rows] = ref[:, :width]
        far = jnp.concatenate([ref[:, :width] for ref in refs], axis=0)
        squares = read_statistic(own_ref[:, 2 * width :], 0)
        gram = 0.0
        for vectors in (near_ref[...], far):
            gram = gram + lax.dot_general(
                vectors, vectors, (((1,), (1,)), ((), ())), preferred_element_type=jnp.float32
            )
        half = gram.shape[0] // 2
        lane = lax.broadcasted_iota(jnp.int32, (half, 2 * half), 1)
        squares = jnp.concatenate([squares] * (half // rows), axis=0)
        out_ref[:, : 2 * half] = gram[:half]
        out_ref[:, 2 * half :] = jnp.where(lane < half, squares, gram[half:])


def sum_grams(third_ref, second_ref, first_ref, own_ref, *refs):
    out_ref = refs[-1]
    out_ref[...] = own_ref[...] + first_ref[...] + second_ref[...] + third_ref[...]


def partner_masks(partner_ref, out_ref, *, rows):
    group = lax.axis_index("dp")
    shape = out_ref.shape[1:]
    row = lax.broadcasted_iota(jnp.int32, shape, 0)
    column = lax.broadcasted_iota(jnp.int32, shape, 1)
    row_id = ((group ^ (row // rows)) * rows) + row % rows
    column_id = ((group ^ (column // rows)) * rows) + column % rows
    partners = jnp.broadcast_to(partner_ref[...], shape)
    row_partner = jnp.sum(
        jnp.where(column == row_id, partners, 0).astype(jnp.float32), axis=1, keepdims=True
    )
    column_partner = jnp.sum(
        jnp.where(row_id == column_id, row_partner, 0.0), axis=0, keepdims=True
    )
    own_partner = column_id.astype(jnp.float32) == row_partner
    other_partner = row_id.astype(jnp.float32) == column_partner
    own_partner = own_partner.astype(jnp.float32)
    out_ref[0] = own_partner
    out_ref[1] = own_partner + other_partner.astype(jnp.float32)


def losses_and_gradient(
    summed_ref,
    other_summed_ref,
    near_ref,
    sent_ref,
    other_far_ref,
    scaled_ref,
    other_scaled_ref,
    gain_ref,
    partner_ref,
    pooled_ref,
    loss_ref,
    grad_ref,
    *,
    model_width,
):
    me = lax.axis_index("pack")
    leads = core_number() == 1
    count, width = near_ref.shape
    rows = scaled_ref.shape[0]
    half = count // 2
    summed = jnp.where(leads, other_summed_ref[...], summed_ref[...])
    upper, lower = summed[:, :count], summed[:, count:]
    squares = lower[:rows, :1]
    row = lax.broadcasted_iota(jnp.int32, upper.shape, 0)
    column = lax.broadcasted_iota(jnp.int32, upper.shape, 1)
    diagonal = row == column
    lower_diagonal = row + half == column
    lower = jnp.where(column >= half, lower, 0.0)
    upper_norms = jnp.where(diagonal, upper, 0.0)
    lower_norms = jnp.where(lower_diagonal, lower, 0.0)
    row_scale = lax.rsqrt(jnp.sum(upper_norms, axis=1, keepdims=True))
    lower_scale = lax.rsqrt(jnp.sum(lower_norms, axis=1, keepdims=True))
    column_scale = lax.rsqrt(jnp.sum(upper_norms + lower_norms, axis=0, keepdims=True))
    cosines = upper * row_scale * column_scale
    logits = cosines * (1.0 / SOFTMAX_WARMTH)
    powers = jnp.where(diagonal, 0.0, jnp.exp(logits))
    lower_powers = jnp.exp(lower * lower_scale * column_scale * (1.0 / SOFTMAX_WARMTH))
    lower_powers = jnp.where((column >= half) & ~lower_diagonal, lower_powers, 0.0)
    mirrored = jnp.sum(jnp.where(column >= half, powers, 0.0), axis=1, keepdims=True)
    column_sum = jnp.sum(
        powers + lower_powers + jnp.where(diagonal, mirrored, 0.0), axis=0, keepdims=True
    )
    cosines, logits, powers = cosines[:rows], logits[:rows], powers[:rows]
    row_sum = jnp.sum(powers, axis=1, keepdims=True)
    weights = powers * (1.0 / row_sum + 1.0 / column_sum) - partner_ref[1, :rows]
    target = jnp.sum(partner_ref[0, :rows] * logits, axis=1, keepdims=True)
    loss = jnp.log(row_sum) - target
    own = loss_ref.shape[0]
    index = lax.broadcasted_iota(jnp.int32, (rows, 1), 0)
    for i in range(own):
        loss_ref[i] = jnp.sum(jnp.where(index == me * own + i, loss, 0.0))
    inner = jnp.sum(weights * cosines, axis=1, keepdims=True)
    scaled_weights = weights * column_scale
    coarse = scaled_weights.astype(jnp.bfloat16)
    own_scale = row_scale[:rows]
    pooled_scale = lax.rsqrt(squares / model_width + EPSILON)
    grad_gain = gain_ref[...] * (model_width**0.5 / SOFTMAX_WARMTH)

    def write(vectors, scaled):
        gradient = jnp.dot(coarse, vectors, preferred_element_type=jnp.float32)
        gradient = (gradient - scaled * (own_scale * inner)) * own_scale
        grad_ref[...] = (gradient * grad_gain).astype(jnp.bfloat16)
        pooled_ref[...] = (scaled * pooled_scale).astype(jnp.bfloat16)

    @pl.when(leads)
    def _():
        write(near_ref[...], other_scaled_ref[...])

    @pl.when(core_number() == 0)
    def _():
        vectors = jnp.concatenate((sent_ref[:, :width], other_far_ref[...]), axis=0)
        write(vectors, scaled_ref[...])


def core_roles(
    hidden_in,
    attn_gain,
    w_query,
    query_gain,
    cached_keys,
    cached_values,
    w_out,
    final_gain,
    lengths,
    pack_order,
    partner,
):
    pack_size = lax.axis_size("pack")
    stmts, width = hidden_in.shape
    model_width = width * pack_size
    head_dim = query_gain.shape[0]
    tokens = cached_keys.shape[0]
    chips = pack_size // 2
    others = range(1, chips)
    total = partner.shape[0]
    bf16 = jnp.bfloat16
    f32 = jnp.float32
    final_gain = final_gain[None]
    query_gain = query_gain[None]
    half = np.arange(head_dim // 2)
    frequency = (ROPE_BASE ** (-half * 2.0 / head_dim)).astype(np.float32)
    frequency = jnp.asarray(np.concatenate([frequency, frequency])[None])
    whole = pl.BlockSpec(memory_space=pltpu.VMEM)

    window = pl.pallas_call(
        open_window,
        out_shape=shaped((8, 128), f32),
        out_specs=whole,
        compiler_params=pltpu.CompilerParams(vmem_limit_bytes=1 << 20),
        cost_estimate=pl.CostEstimate(flops=1 << 34, bytes_accessed=0, transcendentals=0),
    )()
    attn_gain = attn_gain[None]
    other_hidden_in = flip(hidden_in, "pack", 1)
    other_gain = flip(final_gain, "pack", 1)
    other_w_query = flip(w_query, "pack", 1)
    pair = in_vmem(
        prepare_pair,
        shaped((stmts, 2 * width + 128), bf16),
        window,
        hidden_in,
        other_hidden_in,
        attn_gain,
        flip(attn_gain, "pack", 1),
        other_gain,
        flops=1 << 34,
    )
    received = [send_across(pair, "pack", k, 0) for k in others]
    own_projected = in_vmem(
        project_own_pair, shaped((stmts, width), f32), pair, w_query, limit=16, flops=1 << 26
    )
    rope, ranges = in_vmem(
        positions_and_ranges,
        (shaped((stmts, 2 * head_dim), f32), shaped((stmts, 256), f32)),
        pair,
        frequency,
        lengths,
        pack_order,
    )
    held = in_vmem(
        copy_tokens,
        shaped((2,) + cached_keys.shape, bf16),
        own_projected,
        cached_keys,
        cached_values,
    )
    other_held = flip(held, "pack", 1)

    def queries_from(weights, flops, *own):
        return in_vmem(
            lambda *refs: make_queries(*refs, model_width=model_width),
            shaped((stmts, width), bf16),
            *received[::-1],
            pair,
            weights,
            query_gain,
            rope,
            *own,
            limit=16,
            flops=flops,
        )

    second_queries = queries_from(w_query, 1 << 34, own_projected)
    first_queries = queries_from(other_w_query, 1 << 27)
    queries = in_vmem(
        join_queries, shaped((stmts, 2 * width), bf16), first_queries, second_queries
    )

    def weights_to(offsets, after):
        part = in_vmem(
            lambda *refs: copy_weights(*refs, offsets=offsets),
            shaped((2, width, 2 * width), bf16),
            after,
            w_out,
            limit=16,
        )
        return flip(part, "pack", 1)

    far_weights = weights_to((3, 2), queries)
    received = [send_across(queries, "pack", k, 1) for k in others]
    group_rows = stmts * (width // head_dim)
    own_part, own_stats = in_vmem(
        attend_own,
        (shaped((2, group_rows, head_dim), f32),) * 2,
        queries,
        cached_keys,
        cached_values,
        other_held,
        ranges,
        flops=1 << 27,
    )
    partials = []
    for k, part in zip(others[::-1], received[::-1]):
        partials.append(
            in_vmem(
                lambda *refs, offset=k: attend_remote(*refs, offset=offset),
                shaped((stmts, 2 * width + 128), bf16),
                part,
                cached_keys,
                cached_values,
                other_held,
                ranges,
                *(partials[-1:] or (own_stats,)),
                flops=1 << 34,
            )
        )
    received = [send_across(part, "pack", k, 0) for k, part in zip(others, partials[::-1])]
    near_weights = weights_to((1, 0), partials[-1])
    attended = in_vmem(
        merge_partials,
        shaped((stmts, 2 * width), bf16),
        *received[::-1],
        own_part,
        own_stats,
    )

    def projected_to(offset, kind, *after):
        return in_vmem(
            lambda *refs: project_out(*refs, offset=offset),
            shaped((stmts, 2 * width), kind),
            attended,
            w_out,
            far_weights if offset > 1 else near_weights,
            *after,
            limit=16,
            flops=1 << (35 if offset == 2 else 27),
        )

    third = projected_to(3, bf16)
    second = projected_to(2, bf16, third)
    first = projected_to(1, bf16, second)
    kept = projected_to(0, bf16, first)
    received = [send_across(part, "pack", k, 1) for k, part in zip(others, (first, second, third))]
    vector, scaled, far_scaled = in_vmem(
        finish_hidden,
        (shaped((stmts, 2 * width + 128), bf16),) + (shaped((stmts, width), f32),) * 2,
        *received[::-1],
        flip(kept, "pack", 1),
        hidden_in,
        other_hidden_in,
        final_gain,
        other_gain,
    )
    received = [send_across(vector, "dp", k, 0) for k in range(1, lax.axis_size("dp"))]
    other_scaled = flip(far_scaled, "pack", 1)
    gram, near, far = in_vmem(
        gram_part,
        (
            shaped((total // 2, 128), f32),
            shaped((total, width), bf16),
            shaped((total - stmts, width), bf16),
        ),
        *received[::-1],
        flip(vector, "pack", 1),
        other_scaled,
    )
    received = [send_across(gram, "pack", k, 1) for k in others]
    other_far = flip(far, "pack", 1)
    summed = in_vmem(
        sum_grams,
        shaped(gram.shape, f32),
        *received[::-1],
        flip(gram, "pack", 1),
        flops=1 << 30,
    )
    masks = in_vmem(
        lambda *refs: partner_masks(*refs, rows=stmts),
        shaped((2, total, total), f32),
        partner[None],
    )
    pooled, loss_rows, grad_hidden = pl.pallas_call(
        lambda *refs: losses_and_gradient(*refs, model_width=model_width),
        out_shape=(
            shaped((stmts, width), bf16),
            shaped((stmts // pack_size,), f32),
            shaped((stmts, width), bf16),
        ),
        in_specs=[whole] * 9,
        out_specs=(whole, pl.BlockSpec(memory_space=pltpu.SMEM), whole),
        compiler_params=pltpu.CompilerParams(vmem_limit_bytes=8 << 20),
    )(
        summed,
        flip(summed, "pack", 1),
        near,
        vector,
        other_far,
        scaled,
        other_scaled,
        final_gain,
        masks,
    )
    return (pooled, loss_rows, grad_hidden)


def local(
    hidden_in,
    attn_gain,
    w_query,
    query_gain,
    cached_keys,
    cached_values,
    w_out,
    final_gain,
    lengths,
    pack_order,
    partner,
):
    pack_size = lax.axis_size("pack")
    pack_index = lax.axis_index("pack")
    group_index = lax.axis_index("dp")
    stmt_count, feature_count = hidden_in.shape
    model_width = feature_count * pack_size
    head_dim = query_gain.shape[0]
    local_heads = w_query.shape[1] // head_dim
    token_count = cached_keys.shape[0]
    total_stmts = partner.shape[0]
    lengths_row = lengths[0]
    order_row = pack_order[0]
    inputs32 = hidden_in.astype(jnp.float32)

    scaled = (inputs32 * attn_gain[None, :]).astype(jnp.bfloat16)
    squares = split_float(jnp.sum(inputs32 * inputs32, axis=1), 3)
    extra = jnp.stack(squares + [jnp.zeros_like(squares[0])] * 125, axis=1)
    arrived = gather_blocks(jnp.concatenate([scaled, extra], axis=1), "pack")
    input_squares = jnp.sum(arrived[:, :, feature_count : feature_count + 3].astype(jnp.float32), axis=(0, 2))
    input_rms = lax.rsqrt(input_squares / model_width + EPSILON)
    features = jnp.moveaxis(arrived[:, :, :feature_count], 0, 1).reshape(stmt_count, model_width)
    projected = jnp.dot(features, w_query, preferred_element_type=jnp.float32)
    queries = (projected * input_rms[:, None]).reshape(stmt_count, local_heads, head_dim)
    queries = (
        queries
        * lax.rsqrt(jnp.mean(queries * queries, axis=2, keepdims=True) + EPSILON)
        * query_gain
    )
    queries = rotate_heads(queries, (lengths_row - 1).astype(jnp.float32)).astype(jnp.bfloat16)
    all_queries = jnp.moveaxis(gather_blocks(queries, "pack"), 0, 1).reshape(
        stmt_count, pack_size * local_heads, head_dim
    )
    start, end = statement_ranges(lengths_row, order_row)
    tokens = pack_index * token_count + jnp.arange(token_count, dtype=jnp.int32)
    token_mask = (tokens[None, :] >= start[:, None]) & (tokens[None, :] < end[:, None])
    block_max, block_sum, numerators = block_attention(
        all_queries, cached_keys, cached_values, token_mask, head_dim ** (-0.5)
    )

    def by_owner(part):
        return jnp.moveaxis(part.reshape((stmt_count, pack_size, -1)), 1, 0)

    message = jnp.concatenate(
        [by_owner(numerators.astype(jnp.bfloat16))]
        + [by_owner(piece) for piece in split_float(block_max, 3) + split_float(block_sum, 2)],
        axis=2,
    )
    message = lax.all_to_all(message, "pack", 0, 0)
    width = local_heads * head_dim
    stats = message[:, :, width:].astype(jnp.float32).reshape(pack_size, stmt_count, 5, local_heads)
    maxima = stats[:, :, 0] + stats[:, :, 1] + stats[:, :, 2]
    factor = jnp.exp(maxima - jnp.max(maxima, axis=0, keepdims=True))
    denominator = jnp.sum((stats[:, :, 3] + stats[:, :, 4]) * factor, axis=0)
    numerators = message[:, :, :width].astype(jnp.float32).reshape(pack_size, stmt_count, local_heads, head_dim)
    summed = jnp.sum(numerators * factor[..., None], axis=0)
    attended = (summed / denominator[..., None]).astype(jnp.bfloat16)
    partial_out = jnp.dot(
        attended.reshape(stmt_count, width), w_out, preferred_element_type=jnp.float32
    )
    partial_out = jnp.moveaxis(
        partial_out.astype(jnp.bfloat16).reshape(stmt_count, pack_size, feature_count), 1, 0
    )
    partial_out = lax.all_to_all(partial_out, "pack", 0, 0)
    hidden = inputs32 + jnp.sum(partial_out.astype(jnp.float32), axis=0)
    scaled_out = hidden * final_gain[None, :]
    vectors = lax.all_gather(scaled_out.astype(jnp.bfloat16), "dp", axis=0, tiled=True)
    gram = lax.dot_general(
        vectors, vectors, (((1,), (1,)), ((), ())), preferred_element_type=jnp.float32
    )
    own_squares = jnp.sum(hidden * hidden, axis=1)
    extra = jnp.zeros((total_stmts,), jnp.float32).at[:stmt_count].set(own_squares)
    gram = jnp.concatenate([gram, extra[:, None]], axis=1)
    if total_stmts <= 128:
        gram = jnp.sum(gather_blocks(gram, "pack"), axis=0)
    else:
        gram = lax.psum(gram, "pack")
    hidden_rms = jnp.sqrt(gram[:stmt_count, total_stmts] / model_width + EPSILON)
    gram = gram[:, :total_stmts]
    column_ids = jnp.arange(total_stmts, dtype=jnp.int32)
    diagonal = column_ids[:, None] == column_ids[None, :]
    norms_row = lax.rsqrt(jnp.sum(jnp.where(diagonal, gram, 0.0), axis=0))
    norms_column = lax.rsqrt(jnp.sum(jnp.where(diagonal, gram, 0.0), axis=1))
    cosines = gram * norms_column[:, None] * norms_row[None, :]
    logits = jnp.where(diagonal, MASKED_LOGIT, cosines / SOFTMAX_WARMTH)
    highest = jnp.max(logits, axis=1)
    all_lse = highest + jnp.log(jnp.sum(jnp.exp(logits - highest[:, None]), axis=1))
    is_partner = column_ids[None, :] == partner[:, None]
    all_loss = all_lse - jnp.sum(jnp.where(is_partner, logits, 0.0), axis=1)
    own_count = stmt_count // pack_size
    row_base = group_index * stmt_count
    loss_rows = lax.dynamic_slice_in_dim(all_loss, row_base + pack_index * own_count, own_count, 0)
    weights = (
        jnp.exp(logits - all_lse[:, None])
        + jnp.exp(logits - all_lse[None, :])
        - is_partner.astype(jnp.float32)
        - is_partner.T.astype(jnp.float32)
    ).astype(jnp.bfloat16)
    own_weights = lax.dynamic_slice_in_dim(weights, row_base, stmt_count, 0)
    own_cosines = lax.dynamic_slice_in_dim(cosines, row_base, stmt_count, 0)
    own_norm = lax.dynamic_slice_in_dim(norms_column, row_base, stmt_count, 0)
    inner = jnp.sum(own_weights.astype(jnp.float32) * own_cosines, axis=1)
    own_norm = own_norm[:, None]
    embeddings = (vectors.astype(jnp.float32) * norms_column[:, None]).astype(jnp.bfloat16)
    gradient = jnp.dot(own_weights, embeddings, preferred_element_type=jnp.float32)
    scale = model_width**0.5 / SOFTMAX_WARMTH
    pooled = (scaled_out / hidden_rms[:, None]).astype(jnp.bfloat16)
    grad_hidden = (
        scale * final_gain[None, :] * (gradient - scaled_out * own_norm * inner[:, None]) * own_norm
    ).astype(jnp.bfloat16)
    return (pooled, loss_rows, grad_hidden)


def solution(mesh):
    body = core_roles if mesh.shape["pack"] == 8 and mesh.shape["dp"] == 4 else local
    in_specs = (
        P("dp", "pack"),
        P("pack"),
        P(None, "pack"),
        P(),
        P(("dp", "pack"), None),
        P(("dp", "pack"), None),
        P("pack", None),
        P("pack"),
        P("dp", None),
        P("dp", None),
        P(),
    )
    out_specs = (P("dp", "pack"), P(("dp", "pack")), P("dp", "pack"))
    return jax.shard_map(body, mesh=mesh, in_specs=in_specs, out_specs=out_specs, check_vma=False)
```
